32 devices in a mesh: seq: 16 (over z, x, core), fsdp: 2 (over y).
Axes of the slice: x: 2, y: 2, z: 4, core: 2. Of those that a mesh axis runs over, the one named last changes fastest.
Arguments:
- tokens: bfloat16 [2, 4096, 1024], P('fsdp', 'seq'), may hold values from -6 to 6
- cotangent: bfloat16 [2, 4096, 1024], P('fsdp', 'seq'), may hold values from -6 to 6
- seq_lengths: int32 [2, 3], replicated, may hold values from 1 to 3840, as said below
- group_of_shard: int32 [2], replicated, may hold values from 0 to 1, each once
- gain_attn: bfloat16 [1024], P('fsdp'), may hold values from 0.5 to 1.5
- w_query: bfloat16 [1024, 1024], P('fsdp'), may hold values from -0.1875 to 0.1875
- w_key: bfloat16 [1024, 128], P('fsdp'), may hold values from -0.1875 to 0.1875
- w_value: bfloat16 [1024, 128], P('fsdp'), may hold values from -0.1875 to 0.1875
- w_out: bfloat16 [1024, 1024], P('fsdp'), may hold values from -3 to 3
- gain_ffn: bfloat16 [1024], P('fsdp'), may hold values from 0.5 to 1.5
- w_up: bfloat16 [1024, 4096], P('fsdp'), may hold values from -0.1875 to 0.1875
- w_down: bfloat16 [4096, 1024], P('fsdp'), may hold values from -0.09375 to 0.09375
Outputs:
- output: bfloat16 [2, 4096, 1024], P('fsdp', 'seq')
- grad_tokens: float32 [2, 4096, 1024], P('fsdp', 'seq')
- grad_gain_attn: float32 [1024], P('fsdp')
- grad_w_query: float32 [1024, 1024], P('fsdp')
- grad_w_key: float32 [1024, 128], P('fsdp')
- grad_w_value: float32 [1024, 128], P('fsdp')
- grad_w_out: float32 [1024, 1024], P('fsdp')
- grad_gain_ffn: float32 [1024], P('fsdp')
- grad_w_up: float32 [1024, 4096], P('fsdp')
- grad_w_down: float32 [4096, 1024], P('fsdp')
The draws below stay inside these ranges and needn't reach their ends.
Inputs may be any that keep to these rules, and one draw needn't show every extreme that they name: `seq_lengths`: row g lists the lengths of the 3 sequences of group g in the order in which they are packed; the middle one is exactly 3840, the first and the last add up to 256. `group_of_shard`: each group appears once.
All inputs are finite; a program needn't handle non-finite values.
Results may differ from the reference program's by a relative error of at most 0.015.
Values may be sent and summed in bfloat16 or wider, within the bound.
A program may use at most 192 MiB of HBM per device.

```python
import math
import jax
import jax.numpy as jnp
from jax import lax

D = 1024
H = 8
HS = 128
FF = 4096
TOK_DEV = 256
GROUP = 4096
SEQ_MAX = 3840
N_FSDP = 2


def draw_seq_lengths(key, part):
    firsts = jax.random.randint(key, (N_FSDP, 1), 1, TOK_DEV, dtype=jnp.int32)
    longest = jnp.full((N_FSDP, 1), SEQ_MAX, dtype=jnp.int32)
    return jnp.concatenate([firsts, longest, TOK_DEV - firsts], axis=1).astype(jnp.int32)


def levels(key, shape, pieces, smallest, high):
    def one(position, parts):
        draws = jax.random.uniform(jax.random.fold_in(jax.random.fold_in(key, 6), position), (parts,), jnp.float32, smallest / len(pieces), high / len(pieces))
        return jnp.repeat(jnp.exp(draws), shape[position] // parts).reshape((-1,) + (1,) * (len(shape) - position - 1))

    loudness = one(*pieces[0])
    for cut in pieces[1:]:
        loudness = loudness * one(*cut)
    return loudness


def centred(key, shape, spread, limit, split=(), held_as=jnp.bfloat16):
    result = spread * jax.random.normal(key, shape, jnp.float32)
    if split:
        result = result * levels(key, shape, split, -0.22, 0.18)
    return jnp.clip(result, -limit, limit).astype(held_as)


def setup_inputs(seed: int = 0) -> dict:
    keys = jax.random.split(jax.random.key(seed), 13)
    tokens = centred(keys[0], (N_FSDP, GROUP, D), 1.0, 6.0, ((0, 2), (1, 16)))
    cotangent = centred(keys[1], (N_FSDP, GROUP, D), 1.0, 6.0, ((0, 2), (1, 16)))
    seq_lengths = draw_seq_lengths(jax.random.fold_in(keys[12], 71), 0)
    group_of_shard = jax.random.permutation(keys[3], N_FSDP).astype(jnp.int32)
    gain_attn = jnp.clip(1.0 + 0.1 * jax.random.normal(keys[4], (D,), jnp.float32), 0.5, 1.5).astype(jnp.bfloat16)
    w_query = centred(keys[5], (D, H * HS), D ** -0.5, 0.1875, ((0, 2),))
    w_key = centred(keys[6], (D, HS), D ** -0.5, 0.1875, ((0, 2),))
    w_value = centred(keys[7], (D, HS), D ** -0.5, 0.1875, ((0, 2),))
    w_out = centred(keys[8], (H * HS, D), (H * HS // 256) ** -0.5, 3.0, ((0, 2),))
    gain_ffn = jnp.clip(1.0 + 0.1 * jax.random.normal(keys[9], (D,), jnp.float32), 0.5, 1.5).astype(jnp.bfloat16)
    w_up = centred(keys[10], (D, FF), D ** -0.5, 0.1875, ((0, 2),))
    w_down = centred(keys[11], (FF, D), FF ** -0.5, 0.09375, ((0, 2),))
    return dict(tokens=tokens, cotangent=cotangent, seq_lengths=seq_lengths, group_of_shard=group_of_shard, gain_attn=gain_attn, w_query=w_query, w_key=w_key, w_value=w_value, w_out=w_out, gain_ffn=gain_ffn, w_up=w_up, w_down=w_down)


@jax.custom_vjp
def low(v):
    return lax.optimization_barrier(v.astype(jnp.bfloat16)).astype(jnp.float32)

@jax.custom_vjp
def low_back(v):
    return v

def low_keep(v):
    return (low(v), None)

def low_pass(kept, grad):
    return (grad,)

def back_keep(v):
    return (v, None)

def back_low(kept, grad):
    return (low(grad),)
low.defvjp(low_keep, low_pass)
low_back.defvjp(back_keep, back_low)
epsilon = 1e-05
negative = -1e+30

def dot_high(left, right):
    return jnp.dot(left, right, precision=lax.Precision.HIGHEST, preferred_element_type=jnp.float32)

def attention(queries, key_rows, value_rows, segment):
    row_block = min(GROUP, 512)
    score_scale = 1.0 / math.sqrt(HS)
    positions = jnp.arange(GROUP, dtype=jnp.int32)

    def attend_block(block_index):
        first_row = (block_index * row_block).astype(jnp.int32)
        query_block = lax.dynamic_slice_in_dim(queries, first_row, row_block, 0).reshape(row_block, H, HS)
        query_pos = lax.dynamic_slice_in_dim(positions, first_row, row_block, 0)
        query_seg = lax.dynamic_slice_in_dim(segment, first_row, row_block, 0)
        allowed = (positions[None, :] <= query_pos[:, None]) & (segment[None, :] == query_seg[:, None])
        scores = low_back(jnp.einsum('thd,kd->thk', query_block, key_rows, precision=lax.Precision.HIGHEST) * score_scale)
        scores = jnp.where(allowed[:, None, :], scores, negative)
        row_max = lax.optimization_barrier(jnp.max(scores, axis=2, keepdims=True))
        raw_exp = jnp.exp(scores - row_max)
        prob_rows = raw_exp / lax.optimization_barrier(jnp.sum(raw_exp, axis=2, keepdims=True))
        mixed = jnp.einsum('thk,kd->thd', low(prob_rows), value_rows, precision=lax.Precision.HIGHEST)
        return mixed.reshape(row_block, H * HS)
    blocks = lax.map(jax.checkpoint(attend_block), jnp.arange(GROUP // row_block, dtype=jnp.int32))
    return blocks.reshape(GROUP, H * HS)

def forward(stream_all, segments, gain_first, query_weight, key_weight, value_weight, out_weight, gain_second, up_weight, down_weight):

    def group_layer(group_pair):
        stream, segment = group_pair
        inverse = lax.rsqrt(lax.optimization_barrier(jnp.mean(stream * stream, axis=1, keepdims=True)) + epsilon)
        normed = low(stream * inverse * gain_first)
        queries = low_back(low(dot_high(normed, query_weight)))
        key_rows = low_back(low(dot_high(normed, key_weight)))
        value_rows = low_back(low(dot_high(normed, value_weight)))
        attended = low_back(low(attention(queries, key_rows, value_rows, segment)))
        residual = stream + low_back(dot_high(attended, out_weight))
        inverse_second = lax.rsqrt(lax.optimization_barrier(jnp.mean(residual * residual, axis=1, keepdims=True)) + epsilon)
        normed_second = low(residual * inverse_second * gain_second)
        hidden = low(jax.nn.silu(low_back(dot_high(normed_second, up_weight))))
        return residual + dot_high(hidden, down_weight)
    return lax.map(jax.checkpoint(group_layer), (stream_all, segments))

def reference(tokens, cotangent, seq_lengths, group_of_shard, gain_attn, w_query, w_key, w_value, w_out, gain_ffn, w_up, w_down):
    group_lengths = seq_lengths[group_of_shard].astype(jnp.int32)
    seq_ends = jnp.cumsum(group_lengths, axis=1, dtype=jnp.int32)
    positions = jnp.arange(GROUP, dtype=jnp.int32)
    segments = lax.optimization_barrier(jnp.sum((positions[None, :, None] >= seq_ends[:, None, :]).astype(jnp.int32), axis=2, dtype=jnp.int32))

    def layer_of(stream_all, gain_first, query_weight, key_weight, value_weight, out_weight, gain_second, up_weight, down_weight):
        return forward(stream_all, segments, gain_first, query_weight, key_weight, value_weight, out_weight, gain_second, up_weight, down_weight)
    primal, pullback = jax.vjp(layer_of, tokens.astype(jnp.float32), gain_attn.astype(jnp.float32), w_query.astype(jnp.float32), w_key.astype(jnp.float32), w_value.astype(jnp.float32), w_out.astype(jnp.float32), gain_ffn.astype(jnp.float32), w_up.astype(jnp.float32), w_down.astype(jnp.float32))
    gradients = pullback(cotangent.astype(jnp.float32))
    return (primal.astype(jnp.bfloat16), gradients[0], gradients[1], gradients[2], gradients[3], gradients[4], gradients[5], gradients[6], gradients[7], gradients[8])
```

```python
import functools
import math

import jax
import jax.numpy as jnp
from jax import lax
from jax.experimental import pallas as pl
from jax.experimental.pallas import tpu as pltpu
from jax.sharding import PartitionSpec as P

H = 8
HS = 128
EPS = 1e-05
NEG = -1e30
CHUNK = 512
BF = jnp.bfloat16
F32 = jnp.float32


def nt(a, b):
    return lax.dot_general(a, b, (((1,), (1,)), ((), ())), preferred_element_type=F32)


def nn(a, b):
    return lax.dot_general(a, b, (((1,), (0,)), ((), ())), preferred_element_type=F32)


def tn(a, b):
    return lax.dot_general(a, b, (((0,), (0,)), ((), ())), preferred_element_type=F32)


def query_range(scal, tok):
    first = scal[0] * tok
    pos = first + lax.broadcasted_iota(jnp.int32, (1, tok), 1)
    start = jnp.zeros((1, tok), jnp.int32)
    latest = jnp.int32(0)
    for i in range(1, scal.shape[0]):
        end = scal[i]
        start = jnp.maximum(start, jnp.where(end <= pos, end, 0))
        latest = jnp.maximum(latest, jnp.where(end <= first + tok - 1, end, 0))
    return first, pos, start, latest


def chunk_loop(scal, tok, window, step):
    first, pos, start, latest = query_range(scal, tok)
    chunks = (first + tok + CHUNK - 1) // CHUNK

    def body(j, carry):
        low = j * CHUNK
        whole = jnp.logical_and(low >= latest, low + CHUNK - 1 <= first)

        @pl.when(whole)
        def _():
            step(j, None)

        @pl.when(jnp.logical_not(whole))
        def _():
            keys = low + lax.broadcasted_iota(jnp.int32, (CHUNK, tok), 0)
            step(j, jnp.logical_and(keys >= start, keys <= pos))

        return carry

    lax.fori_loop(0, chunks, body, 0)
    return chunks


def attend_kernel(scal, q_ref, kv_ref, out_ref, lse_ref, acc, top, total):
    tok = q_ref.shape[0]
    factor = math.log2(math.e) / math.sqrt(HS)
    top[...] = jnp.full(top.shape, -3e38, F32)
    total[...] = jnp.zeros(total.shape, F32)
    acc[...] = jnp.zeros(acc.shape, F32)

    def step(j, mask):
        rows = pl.ds(pl.multiple_of(j * CHUNK, CHUNK), CHUNK)
        keys = kv_ref[rows, :HS]
        values_t = kv_ref[rows, HS:].T
        for h in range(H):
            scores = nt(keys, q_ref[:, h * HS : (h + 1) * HS])
            if mask is not None:
                scores = jnp.where(mask, scores, NEG)
            old = top[h : h + 1, :]
            new = jnp.maximum(old, jnp.max(scores, axis=0, keepdims=True) * factor)
            shrink = jnp.exp2(old - new)
            probs = jnp.exp2(scores * factor - new)
            total[h : h + 1, :] = total[h : h + 1, :] * shrink + jnp.sum(probs, axis=0, keepdims=True)
            acc[h] = acc[h] * shrink + nn(values_t, probs.astype(BF))
            top[h : h + 1, :] = new

    chunk_loop(scal, tok, kv_ref.shape[0], step)
    for h in range(H):
        mixed = acc[h] * (1.0 / total[h : h + 1, :])
        out_ref[:, h * HS : (h + 1) * HS] = mixed.T.astype(BF)
    lse_ref[...] = top[...] + jnp.log2(total[...])


def attend_back_kernel(scal, q_ref, kv_ref, d_ref, out_ref, lse_ref, dq_ref, dkv_ref, acc, delta):
    tok = q_ref.shape[0]
    window = kv_ref.shape[0]
    scale = 1.0 / math.sqrt(HS)
    factor = math.log2(math.e) * scale
    acc[...] = jnp.zeros(acc.shape, F32)
    for h in range(H):
        cols = slice(h * HS, (h + 1) * HS)
        both = d_ref[:, cols].astype(F32) * out_ref[:, cols].astype(F32)
        delta[h : h + 1, :] = jnp.sum(both.T, axis=0, keepdims=True)

    def step(j, mask):
        rows = pl.ds(pl.multiple_of(j * CHUNK, CHUNK), CHUNK)
        keys = kv_ref[rows, :HS]
        values = kv_ref[rows, HS:]
        keys_t = keys.T
        d_keys = jnp.zeros((CHUNK, HS), F32)
        d_values = jnp.zeros((CHUNK, HS), F32)
        for h in range(H):
            cols = slice(h * HS, (h + 1) * HS)
            q = q_ref[:, cols]
            d = d_ref[:, cols]
            scores = nt(keys, q)
            if mask is not None:
                scores = jnp.where(mask, scores, NEG)
            probs = jnp.exp2(scores * factor - lse_ref[h : h + 1, :])
            d_probs = nt(values, d)
            d_scores = (probs * (d_probs - delta[h : h + 1, :])).astype(BF)
            d_values = d_values + nn(probs.astype(BF), d)
            d_keys = d_keys + nn(d_scores, q)
            acc[h] = acc[h] + nn(keys_t, d_scores)
        dkv_ref[rows, :HS] = (d_keys * scale).astype(BF)
        dkv_ref[rows, HS:] = d_values.astype(BF)

    done = chunk_loop(scal, tok, window, step)

    def clear(j, carry):
        rows = pl.ds(pl.multiple_of(j * CHUNK, CHUNK), CHUNK)
        dkv_ref[rows, :] = jnp.zeros((CHUNK, 2 * HS), BF)
        return carry

    lax.fori_loop(done, window // CHUNK, clear, 0)
    for h in range(H):
        dq_ref[:, h * HS : (h + 1) * HS] = (acc[h] * scale).T.astype(BF)


VMEM = pl.BlockSpec(memory_space=pltpu.VMEM)
SMEM = pl.BlockSpec(memory_space=pltpu.SMEM)
PARAMS = pltpu.CompilerParams(vmem_limit_bytes=40 * 2**20)


def attend(scal, queries, window_kv):
    tok = queries.shape[0]
    window = window_kv.shape[0]
    return pl.pallas_call(
        attend_kernel,
        out_shape=(
            jax.ShapeDtypeStruct((tok, H * HS), BF),
            jax.ShapeDtypeStruct((H, tok), F32),
        ),
        in_specs=[SMEM, VMEM, VMEM],
        out_specs=(VMEM, VMEM),
        scratch_shapes=[
            pltpu.VMEM((H, HS, tok), F32),
            pltpu.VMEM((H, tok), F32),
            pltpu.VMEM((H, tok), F32),
        ],
        compiler_params=PARAMS,
        cost_estimate=pl.CostEstimate(
            flops=8 * tok * window * H * HS, bytes_accessed=4 * window * HS, transcendentals=tok * window * H
        ),
        name="attend",
    )(scal, queries, window_kv)


def attend_back(scal, queries, window_kv, d_attended, attended, lse):
    tok = queries.shape[0]
    window = window_kv.shape[0]
    return pl.pallas_call(
        attend_back_kernel,
        out_shape=(
            jax.ShapeDtypeStruct((tok, H * HS), BF),
            jax.ShapeDtypeStruct((window, 2 * HS), BF),
        ),
        in_specs=[SMEM, VMEM, VMEM, VMEM, VMEM, VMEM],
        out_specs=(VMEM, VMEM),
        scratch_shapes=[pltpu.VMEM((H, HS, tok), F32), pltpu.VMEM((H, tok), F32)],
        compiler_params=PARAMS,
        cost_estimate=pl.CostEstimate(
            flops=20 * tok * window * H * HS, bytes_accessed=8 * window * HS, transcendentals=tok * window * H
        ),
        name="attend_back",
    )(scal, queries, window_kv, d_attended, attended, lse)


def after(value, *others):
    return lax.optimization_barrier((value, *others))[0]


class Grid:
    def __init__(self):
        seq = lax.axis_size("seq")
        self.F = lax.axis_size("fsdp")
        self.C = 2
        chips = seq // 2
        self.B = 2 if chips == 8 else chips // 2
        self.A = chips // self.B
        self.s = lax.axis_index("seq")
        self.f = lax.axis_index("fsdp")
        self.c = self.s % 2
        self.b = self.s // 2 % self.B
        self.a = self.s // (2 * self.B)

    def size(self, axis):
        return {"a": self.A, "b": self.B, "c": self.C, "f": self.F}[axis]

    def place(self, axis):
        return {"a": self.a, "b": self.b, "c": self.c, "f": self.f}[axis]

    def send(self, value, axis, step, upward=False):
        pairs = []
        for a in range(self.A):
            for b in range(self.B):
                for c in range(2):
                    for f in range(self.F):
                        at = {"a": a, "b": b, "c": c, "f": f}
                        to = dict(at)
                        to[axis] += step
                        if upward and not 0 <= to[axis] < self.size(axis):
                            continue
                        to[axis] %= self.size(axis)
                        line = [((d["a"] * self.B + d["b"]) * 2 + d["c"]) * self.F + d["f"] for d in (at, to)]
                        pairs.append(tuple(line))
        return lax.ppermute(value, ("seq", "fsdp"), pairs)

    def stack(self, parts, axis):
        n, me = len(parts), self.place(axis)
        if n == 2:
            low = me == 0
            return jnp.stack([jnp.where(low, parts[0], parts[1]), jnp.where(low, parts[1], parts[0])])
        twice = jnp.stack(parts + parts)
        return lax.dynamic_slice_in_dim(twice, (n - me) % n, n, 0)

    def gather(self, value, axis):
        n = self.size(axis)
        return self.stack([value] + [self.send(value, axis, -k) for k in range(1, n)], axis)

    def scatter(self, parts, axis):
        n, me = self.size(axis), self.place(axis)

        def pick(k):
            return lax.dynamic_index_in_dim(parts, (me + k) % n, 0, keepdims=False)

        got = [self.send(pick(k).astype(BF), axis, k) for k in range(1, n)]
        total = pick(0).astype(F32)
        for piece in got:
            total = total + piece.astype(F32)
        return total

    def plane_sum(self, parts):
        half = self.scatter(parts, "b").astype(BF)
        return self.scatter(half, "a")

    def plane_gather(self, share):
        rows = self.gather(share.astype(BF), "a")
        return self.gather(rows, "b")


def local(
    tokens,
    cotangent,
    seq_lengths,
    group_of_shard,
    gain_attn,
    w_query,
    w_key,
    w_value,
    w_out,
    gain_ffn,
    w_up,
    w_down,
):
    g = Grid()
    A, B, C, F = g.A, g.B, g.C, g.F
    tok, D = tokens.shape[1:]
    FF = w_up.shape[1]
    own_rows = D // F
    seq_parts = A * B * C
    shard = FF // (2 * F)

    group = lax.dynamic_index_in_dim(group_of_shard, g.f, 0, keepdims=False)
    lengths = lax.dynamic_index_in_dim(seq_lengths, group, 0, keepdims=False)
    running, ends = jnp.int32(0), []
    for i in range(seq_lengths.shape[1]):
        running = running + lengths[i]
        ends.append(running)
    scal = jnp.stack([g.s.astype(jnp.int32), *ends])

    gains = jnp.stack([gain_attn, gain_ffn])
    full_gains = g.gather(gains, "f").transpose(1, 0, 2).reshape(2, D).astype(F32)
    gain_first, gain_second = full_gains[0], full_gains[1]
    own_kv = jnp.concatenate([w_key, w_value], axis=1)
    full_kv = g.gather(own_kv, "f").reshape(D, 2 * HS)

    def gather_weight(weight, *late):
        half = own_rows // 2
        mine = lax.dynamic_slice_in_dim(weight, g.c * half, half, 0)
        if late:
            mine = after(mine, *late)
        pieces = [g.gather(g.send(mine, "f", -k), "c").reshape(weight.shape) for k in range(1, F)]
        return g.stack([weight] + pieces, "f").reshape(F * own_rows, -1)

    full_query = gather_weight(w_query)

    stream = tokens[0].astype(F32)
    inverse_first = lax.rsqrt(jnp.mean(stream * stream, axis=1, keepdims=True) + EPS)
    unit_first = stream * inverse_first
    normed_first = (unit_first * gain_first).astype(BF)
    key_value = nn(normed_first, full_kv).astype(BF)
    queries = nn(normed_first, full_query).astype(BF)

    column = [key_value] + [g.send(key_value, "a", k, upward=True) for k in range(1, A)]
    twice = jnp.stack(column[::-1] + column[::-1])
    column = lax.dynamic_slice_in_dim(twice, A - 1 - g.a, A, 0)
    plane = g.gather(column, "b")
    whole = g.gather(plane, "c")
    window_kv = whole.transpose(2, 1, 0, 3, 4).reshape(seq_parts * tok, 2 * HS)

    full_out = gather_weight(w_out, full_query)
    upstream = cotangent[0]
    cot = []
    for k in range(F):
        mine = upstream if k == 0 else g.send(after(upstream, full_query), "f", k)
        cot.append(jnp.concatenate([mine, g.send(mine, "c", 1)], axis=0))
    ups = w_up.reshape(own_rows, F, 2, shard)
    up_parts = []
    for k in range(F):
        block = lax.dynamic_slice(ups, (0, (g.f + k) % F, g.c, 0), (own_rows, 1, 1, shard)).reshape(own_rows, shard)
        up_parts.append(block if k == 0 else g.send(after(block, full_out), "f", k))
    up_parts = [up_parts[0]] + up_parts[1:][::-1]
    up = g.stack(up_parts, "f").reshape(D, shard)
    down = lax.dynamic_slice_in_dim(w_down, g.c * shard, shard, 0)

    attended, lse = attend(scal, queries, window_kv)

    residual = stream + nn(attended, full_out)
    inverse_second = lax.rsqrt(jnp.mean(residual * residual, axis=1, keepdims=True) + EPS)
    unit_second = residual * inverse_second
    normed_second = (unit_second * gain_second).astype(BF)

    out_sum, back_sum = residual, jnp.zeros((tok, D), F32)
    hiddens, d_pres, norms = [], [], []
    backs, outs = [], []
    for k in range(F):
        mine = normed_second if k == 0 else g.send(normed_second, "f", k)
        norm = jnp.concatenate([mine, g.send(mine, "c", 1)], axis=0)
        before = nn(norm, up)
        d_hidden = nt(cot[k], down)
        sig = jax.nn.sigmoid(before)
        hidden = (before * sig).astype(BF)
        d_pre = (d_hidden * sig * (1.0 + before * (1.0 - sig))).astype(BF)
        back = nt(d_pre, up)
        out = nn(hidden, down)
        hiddens.append(hidden)
        d_pres.append(d_pre)
        norms.append(norm)
        backs.append(back)
        outs.append(out)

    def give_back(parts):
        total = 0.0
        for k, part in enumerate(parts):
            other = g.send(part[tok:].astype(BF), "c", 1)
            chip = part[:tok] + other.astype(F32)
            if k:
                chip = g.send(chip.astype(BF), "f", -k).astype(F32)
            total = total + chip
        return total

    d_normed_second = give_back(backs)
    output = (residual + give_back(outs)).astype(BF)

    grad_down = sum(tn(h, c) for h, c in zip(hiddens, cot)).astype(BF)
    grad_up = sum(tn(n, d) for n, d in zip(norms, d_pres)).astype(BF)

    def norm_back(gradient, unit_rows, inverse, gain_vec):
        scaled = gradient * gain_vec
        gain_grad = jnp.sum(gradient * unit_rows, axis=0)
        return gain_grad, inverse * (scaled - unit_rows * jnp.mean(scaled * unit_rows, axis=1, keepdims=True))

    gain_second_grad, d_from_norm = norm_back(d_normed_second, unit_second, inverse_second, gain_second)
    d_residual = upstream.astype(F32) + d_from_norm
    d_branch = d_residual.astype(BF)
    d_attended = nt(d_branch, full_out).astype(BF)
    grad_out = tn(attended, d_branch).astype(BF)

    d_query, window_grad = attend_back(scal, queries, window_kv, d_attended, attended, lse)

    blocks = window_grad.reshape(A, B, C, tok, 2 * HS)
    chip_sum = g.scatter(blocks.transpose(2, 1, 0, 3, 4), "c").astype(BF)
    d_key_value = g.plane_sum(chip_sum).astype(BF)

    d_normed_first = nt(d_query, full_query) + nt(d_key_value, full_kv)
    gain_first_grad, d_stream = norm_back(d_normed_first, unit_first, inverse_first, gain_first)
    grad_tokens = (d_residual + d_stream)[None]

    def reduce_all(parts):
        chip = g.scatter(parts.transpose(1, 0, 2, 3, 4, 5), "c").astype(BF)
        own = g.scatter(chip, "f").astype(BF)
        return g.plane_sum(own)

    def gather_rows(share):
        return g.gather(g.plane_gather(share), "c")

    down_share = g.plane_sum(grad_down.reshape(B, A, shard // (A * B), D))
    grad_w_down = gather_rows(down_share).reshape(FF // F, D).astype(F32)

    up_rows = own_rows // (A * B)
    up_parts = grad_up.reshape(F, B, A, up_rows, shard).transpose(1, 2, 0, 3, 4)
    up_share = g.plane_sum(up_parts).astype(BF)
    pieces = []
    for k in range(F):
        piece = lax.dynamic_index_in_dim(up_share, (g.f + k) % F, 0, keepdims=False)
        pieces.append(piece if k == 0 else g.send(piece, "f", k))
    pieces = [pieces[0]] + pieces[1:][::-1]
    up_own = g.stack(pieces, "f")
    up_all = gather_rows(up_own)
    grad_w_up = up_all.transpose(1, 2, 4, 3, 0, 5).reshape(own_rows, FF).astype(F32)

    def attn_grad(grad):
        width = grad.shape[1]
        parts = grad.reshape(F, C, B, A, own_rows // (C * B * A), width)
        return gather_rows(reduce_all(parts)).reshape(own_rows, width).astype(F32)

    grad_w_out = attn_grad(grad_out)
    grad_w_query = attn_grad(tn(normed_first, d_query).astype(BF))

    pieces = C * B * A
    wide = own_rows * 2 * HS // 128
    kv_grad = tn(normed_first, d_key_value).reshape(F, wide, 128)
    gain_grads = jnp.stack([gain_first_grad, gain_second_grad]).reshape(2, F, own_rows).transpose(1, 0, 2)
    gain_grads = gain_grads.reshape(F, 2 * own_rows // 128, 128)
    both = jnp.concatenate([kv_grad, gain_grads], axis=1)
    rows = -(-both.shape[1] // (8 * pieces)) * 8
    both = jnp.pad(both, ((0, 0), (0, rows * pieces - both.shape[1]), (0, 0))).astype(BF)
    both = gather_rows(reduce_all(both.reshape(F, C, B, A, rows, 128))).reshape(pieces * rows, 128).astype(F32)
    grad_kv = both[:wide].reshape(own_rows, 2 * HS)
    gain_grads = both[wide : wide + 2 * own_rows // 128].reshape(2, own_rows)

    return (
        output[None],
        grad_tokens,
        gain_grads[0],
        grad_w_query,
        grad_kv[:, :HS],
        grad_kv[:, HS:],
        grad_w_out,
        gain_grads[1],
        grad_w_up,
        grad_w_down,
    )


def solution(mesh):
    placed = (
        P("fsdp", "seq", None),
        P("fsdp", "seq", None),
        P(),
        P(),
        P("fsdp"),
        P("fsdp", None),
        P("fsdp", None),
        P("fsdp", None),
        P("fsdp", None),
        P("fsdp"),
        P("fsdp", None),
        P("fsdp", None),
    )
    return jax.shard_map(
        local,
        mesh=mesh,
        in_specs=placed,
        out_specs=(
            P("fsdp", "seq", None),
            P("fsdp", "seq", None),
            P("fsdp"),
            P("fsdp", None),
            P("fsdp", None),
            P("fsdp", None),
            P("fsdp", None),
            P("fsdp"),
            P("fsdp", None),
            P("fsdp", None),
        ),
        check_vma=False,
    )
```

```python
import functools
import math

import jax
import jax.numpy as jnp
from jax import lax
from jax.experimental import pallas as pl
from jax.experimental.pallas import tpu as pltpu
from jax.sharding import PartitionSpec as P

H = 8
HS = 128
EPS = 1e-05
NEG = -1e30
CHUNK = 512
BF = jnp.bfloat16
F32 = jnp.float32


def nt(a, b):
    return lax.dot_general(a, b, (((1,), (1,)), ((), ())), preferred_element_type=F32)


def nn(a, b):
    return lax.dot_general(a, b, (((1,), (0,)), ((), ())), preferred_element_type=F32)


def tn(a, b):
    return lax.dot_general(a, b, (((0,), (0,)), ((), ())), preferred_element_type=F32)


def query_range(scal, tok):
    first = scal[0] * tok
    pos = first + lax.broadcasted_iota(jnp.int32, (1, tok), 1)
    start = jnp.zeros((1, tok), jnp.int32)
    latest = jnp.int32(0)
    for i in range(1, scal.shape[0]):
        end = scal[i]
        start = jnp.maximum(start, jnp.where(end <= pos, end, 0))
        latest = jnp.maximum(latest, jnp.where(end <= first + tok - 1, end, 0))
    return first, pos, start, latest


def chunk_loop(scal, tok, window, step):
    first, pos, start, latest = query_range(scal, tok)
    chunks = (first + tok + CHUNK - 1) // CHUNK

    def body(j, carry):
        low = j * CHUNK
        whole = jnp.logical_and(low >= latest, low + CHUNK - 1 <= first)

        @pl.when(whole)
        def _():
            step(j, None)

        @pl.when(jnp.logical_not(whole))
        def _():
            keys = low + lax.broadcasted_iota(jnp.int32, (CHUNK, tok), 0)
            step(j, jnp.logical_and(keys >= start, keys <= pos))

        return carry

    lax.fori_loop(0, chunks, body, 0)
    return chunks


def attend_kernel(scal, q_ref, kv_ref, out_ref, lse_ref, acc, top, total):
    tok = q_ref.shape[0]
    factor = math.log2(math.e) / math.sqrt(HS)
    top[...] = jnp.full(top.shape, -3e38, F32)
    total[...] = jnp.zeros(total.shape, F32)
    acc[...] = jnp.zeros(acc.shape, F32)

    def step(j, mask):
        rows = pl.ds(pl.multiple_of(j * CHUNK, CHUNK), CHUNK)
        keys = kv_ref[rows, :HS]
        values_t = kv_ref[rows, HS:].T
        for h in range(H):
            scores = nt(keys, q_ref[:, h * HS : (h + 1) * HS])
            if mask is not None:
                scores = jnp.where(mask, scores, NEG)
            old = top[h : h + 1, :]
            new = jnp.maximum(old, jnp.max(scores, axis=0, keepdims=True) * factor)
            shrink = jnp.exp2(old - new)
            probs = jnp.exp2(scores * factor - new)
            total[h : h + 1, :] = total[h : h + 1, :] * shrink + jnp.sum(probs, axis=0, keepdims=True)
            acc[h] = acc[h] * shrink + nn(values_t, probs.astype(BF))
            top[h : h + 1, :] = new

    chunk_loop(scal, tok, kv_ref.shape[0], step)
    for h in range(H):
        mixed = acc[h] * (1.0 / total[h : h + 1, :])
        out_ref[:, h * HS : (h + 1) * HS] = mixed.T.astype(BF)
    lse_ref[...] = top[...] + jnp.log2(total[...])


VMEM = pl.BlockSpec(memory_space=pltpu.VMEM)
SMEM = pl.BlockSpec(memory_space=pltpu.SMEM)
PARAMS = pltpu.CompilerParams(vmem_limit_bytes=40 * 2**20)


def attend(scal, queries, window_kv):
    tok = queries.shape[0]
    window = window_kv.shape[0]
    return pl.pallas_call(
        attend_kernel,
        out_shape=(
            jax.ShapeDtypeStruct((tok, H * HS), BF),
            jax.ShapeDtypeStruct((H, tok), F32),
        ),
        in_specs=[SMEM, VMEM, VMEM],
        out_specs=(VMEM, VMEM),
        scratch_shapes=[
            pltpu.VMEM((H, HS, tok), F32),
            pltpu.VMEM((H, tok), F32),
            pltpu.VMEM((H, tok), F32),
        ],
        compiler_params=PARAMS,
        cost_estimate=pl.CostEstimate(
            flops=8 * tok * window * H * HS, bytes_accessed=4 * window * HS, transcendentals=tok * window * H
        ),
        name="attend",
    )(scal, queries, window_kv)


MESH = pl.DeviceIdType.MESH


def tail_kernel(
    dims,
    ends,
    q_ref,
    kv_ref,
    d_ref,
    att_ref,
    lse_ref,
    gd_ref,
    gu_ref,
    go_ref,
    n1_ref,
    wq_ref,
    wkv_ref,
    unit_ref,
    inv_ref,
    gain_ref,
    dres_ref,
    gain2_ref,
    out_down,
    out_up,
    out_o,
    out_q,
    out_kv,
    grad_tokens,
    acc,
    delta,
    dq,
    dkv,
    dkv_c,
    dkv_x,
    dkv_z,
    d_kv,
    dn1,
    gq_ref,
    gkv_ref,
    xr_d,
    xr_u,
    zs_d,
    zs_u,
    zr_d,
    zr_u,
    sh_d,
    sh_u,
    yr_u,
    o_c,
    o_y,
    o_x,
    o_z,
    o_s,
    q_c,
    q_y,
    q_x,
    q_z,
    q_s,
    kv_c,
    kv_y,
    kv_x,
    kv_z,
    kv_s,
    gain_rows,
    send_sem,
    recv_sem,
    copy_sem,
):
    A, B, F = dims
    tok = q_ref.shape[0]
    window = kv_ref.shape[0]
    D = n1_ref.shape[1]
    own_rows = D // F
    shard = gd_ref.shape[0]
    s = lax.axis_index("seq")
    f = lax.axis_index("fsdp")
    c = lax.rem(s, 2)
    b = lax.rem(s // 2, B)
    a = s // (2 * B)

    def device(axis, step):
        at = {"a": a, "b": b, "c": c, "f": f}
        at[axis] = lax.rem(at[axis] + step, {"a": A, "b": B, "c": 2, "f": F}[axis])
        return ((at["a"] * B + at["b"]) * 2 + at["c"], at["f"])

    def lower(axis, step):
        return lax.rem({"a": a + A, "b": b + B, "f": f + F}[axis] - step, {"a": A, "b": B, "f": F}[axis])

    used = [0]

    def slots(n=1):
        used[0] += n
        assert used[0] <= send_sem.shape[0]
        return used[0] - n

    def remote(src, dst, slot, to):
        return pltpu.make_async_remote_copy(
            src_ref=src, dst_ref=dst, send_sem=send_sem.at[slot], recv_sem=recv_sem.at[slot], device_id=to, device_id_type=MESH
        )

    pending = []

    def start(src, dst, slot, to):
        copy = remote(src, dst, slot, to)
        copy.start()
        pending.append(copy)
        return copy

    barrier = pltpu.get_barrier_semaphore()
    partners = [("a", k) for k in range(1, A)] + [("b", k) for k in range(1, B)] + [("c", 1)] + [("f", k) for k in range(1, F)]
    for axis, k in partners:
        pl.semaphore_signal(barrier, inc=1, device_id=device(axis, k), device_id_type=MESH)
    pl.semaphore_wait(barrier, len(partners))

    r_d = shard // (A * B)
    r_u = own_rows // B
    w_u = shard // A
    x_d = slots(A * (B - 1))
    x_u = slots(A * (B - 1))
    z_d = slots(A - 1)
    z_u = slots(A - 1)

    def x_copies(i):
        at = lax.rem(a + 1 + i, A)
        copies = []
        for kb in range(B - 1):
            to = device("b", kb + 1)
            other = lax.rem(b + kb + 1, B)
            rows = pl.ds(pl.multiple_of((other * A + at) * r_d, r_d), r_d)
            copies.append(remote(gd_ref.at[rows, :], xr_d.at[kb, i], x_d + kb * A + i, to))
            rows = pl.ds(pl.multiple_of(other * r_u, r_u), r_u)
            cols = pl.ds(pl.multiple_of(at * w_u, w_u), w_u)
            copies.append(remote(gu_ref.at[:, rows, cols], xr_u.at[kb, i], x_u + kb * A + i, to))
        return copies

    def own_sums(i):
        at = lax.rem(a + 1 + i, A)
        rows = pl.ds(pl.multiple_of((b * A + at) * r_d, r_d), r_d)
        total_d = gd_ref[rows, :].astype(F32)
        rows = pl.ds(pl.multiple_of(b * r_u, r_u), r_u)
        cols = pl.ds(pl.multiple_of(at * w_u, w_u), w_u)
        total_u = gu_ref[:, rows, cols].astype(F32)
        for kb in range(B - 1):
            total_d = total_d + xr_d[kb, i].astype(F32)
            total_u = total_u + xr_u[kb, i].astype(F32)
        return total_d, total_u

    for copy in x_copies(0):
        copy.start()

    half = D // 2

    def reduce_c(ref, got, width):
        other = pl.ds(pl.multiple_of((1 - c) * width, width), width)
        return start(ref.at[:, :, other], got, slots(), device("c", 1))

    def reduce_y(ref, got, sent, width):
        mine = pl.ds(pl.multiple_of(c * width, width), width)

        def add(i, carry):
            sent[i] = (ref[i, :, mine].astype(F32) + got[i].astype(F32)).astype(BF)
            return carry

        lax.fori_loop(0, F, add, 0)

    o_c_copy = reduce_c(go_ref, o_c, half)

    scale = 1.0 / math.sqrt(HS)
    factor = math.log2(math.e) * scale
    acc[...] = jnp.zeros(acc.shape, F32)
    for h in range(H):
        cols = slice(h * HS, (h + 1) * HS)
        both = d_ref[:, cols].astype(F32) * att_ref[:, cols].astype(F32)
        delta[h : h + 1, :] = jnp.sum(both.T, axis=0, keepdims=True)
    first = s * tok
    pos = first + lax.broadcasted_iota(jnp.int32, (1, tok), 1)
    begin = jnp.zeros((1, tok), jnp.int32)
    for i in range(ends.shape[0]):
        begin = jnp.maximum(begin, jnp.where(ends[i] <= pos, ends[i], 0))

    def step(j, masked):
        rows = pl.ds(pl.multiple_of(j * CHUNK, CHUNK), CHUNK)
        keys = kv_ref[rows, :HS]
        values = kv_ref[rows, HS:]
        keys_t = keys.T
        if masked:
            at = j * CHUNK + lax.broadcasted_iota(jnp.int32, (CHUNK, tok), 0)
            mask = jnp.logical_and(at >= begin, at <= pos)
        d_keys = jnp.zeros((CHUNK, HS), F32)
        d_values = jnp.zeros((CHUNK, HS), F32)
        for h in range(H):
            cols = slice(h * HS, (h + 1) * HS)
            q = q_ref[:, cols]
            d = d_ref[:, cols]
            scores = nt(keys, q)
            if masked:
                scores = jnp.where(mask, scores, NEG)
            probs = jnp.exp2(scores * factor - lse_ref[h : h + 1, :])
            d_probs = nt(values, d)
            d_scores = (probs * (d_probs - delta[h : h + 1, :])).astype(BF)
            d_values = d_values + nn(probs.astype(BF), d)
            d_keys = d_keys + nn(d_scores, q)
            acc[h] = acc[h] + nn(keys_t, d_scores)
        for i in range(2):
            part = slice(i * tok, (i + 1) * tok)
            dkv[j, i, :, :HS] = (d_keys[part] * scale).astype(BF)
            dkv[j, i, :, HS:] = d_values[part].astype(BF)

    chunks = s // 2 + 1
    per = -(-(window // CHUNK) // max(1, A - 1))

    def attention_chunk(j, carry):
        plain = jnp.logical_and(jnp.logical_and(j > 0, j < chunks - 1), s < 2 * A * B - 1)

        @pl.when(plain)
        def _():
            step(j, False)

        @pl.when(jnp.logical_not(plain))
        def _():
            step(j, True)

        return carry

    def feed_forward_step(i, carry):
        for copy in x_copies(i + 1):
            copy.start()
        lax.fori_loop(i * per, jnp.minimum((i + 1) * per, chunks), attention_chunk, 0)
        for copy in x_copies(i):
            copy.wait()
        total_d, total_u = own_sums(i)
        to = lax.rem(a + 1 + i, A)
        to = ((to * B + b) * 2 + c, f)
        zs_d[i] = total_d.astype(BF)
        remote(zs_d.at[i], zr_d.at[i], z_d + i, to).start()
        zs_u[i] = total_u.astype(BF)
        remote(zs_u.at[i], zr_u.at[i], z_u + i, to).start()
        return carry

    lax.fori_loop(0, A - 1, feed_forward_step, 0)

    def clear(j, carry):
        dkv[j] = jnp.zeros(dkv.shape[1:], BF)
        return carry

    lax.fori_loop(chunks, window // CHUNK, clear, 0)

    class Gather:
        def __init__(self, share, view, planes=True):
            self.share, self.view, self.planes = share, view, planes
            n = B if planes else 1
            self.z = slots(A - 1)
            self.x = slots((n - 1) * A)
            self.s = slots(n * A)
            self.local = pltpu.make_async_copy(share, view(c, b, a), copy_sem.at[len(gathers)])
            gathers.append(self)

        def begin(self):
            self.local.start()
            mine = self.view(c, b, a)
            self.zs = [start(self.share, mine, self.z + k, device("a", k + 1)) for k in range(A - 1)]
            self.xs, self.cs = {}, {}
            self.pass_on(self.share, mine, 0)

        def pass_on(self, src, dst, j):
            for kb in range(B - 1 if self.planes else 0):
                self.xs[kb, j] = start(src, dst, self.x + kb * A + j, device("b", kb + 1))
            self.cs[0, j] = start(src, dst, self.s + j, device("c", 1))

        def from_a(self):
            for k in range(A - 1):
                self.zs[k].wait_recv()
                here = self.view(c, b, lower("a", k + 1))
                self.pass_on(here, here, k + 1)

        def from_b(self):
            for kb in range(B - 1 if self.planes else 0):
                for j in range(A):
                    self.xs[kb, j].wait_recv()
                    here = self.view(c, lower("b", kb + 1), lower("a", j) if j else a)
                    self.cs[kb + 1, j] = start(here, here, self.s + (kb + 1) * A + j, device("c", 1))

        def end(self):
            self.local.wait()
            for copy in self.zs + list(self.xs.values()):
                copy.wait_send()
            for copy in self.cs.values():
                copy.wait()

    gathers = []

    def view_down(c_, b_, a_):
        return out_down.at[pl.ds(pl.multiple_of(((c_ * B + b_) * A + a_) * r_d, r_d), r_d), :]

    def view_up(c_, b_, a_):
        rows = pl.ds(pl.multiple_of(b_ * r_u, r_u), r_u)
        return out_up.at[:, rows, pl.ds(pl.multiple_of(c_ * shard + a_ * w_u, w_u), w_u)]

    w_o = half // A

    def view_square(out):
        def view(c_, b_, a_):
            rows = pl.ds(pl.multiple_of(b_ * r_u, r_u), r_u)
            return out.at[rows, pl.ds(pl.multiple_of(c_ * half + a_ * w_o, w_o), w_o)]

        return view

    gather_down = Gather(sh_d, view_down)
    gather_up = Gather(sh_u, view_up)
    gather_o = Gather(o_s, view_square(out_o))
    gather_q = Gather(q_s, view_square(out_q))
    gather_kv = Gather(kv_s, lambda c_, b_, a_: out_kv.at[c_, a_], planes=False)

    dkv_c_copy = start(dkv.at[:, 1 - c], dkv_c, slots(), device("c", 1))

    for copy in x_copies(A - 1):
        copy.wait()
    total_d, total_u = own_sums(A - 1)

    def z_wait(i, carry):
        to = lax.rem(a + 1 + i, A)
        to = ((to * B + b) * 2 + c, f)
        remote(zs_d.at[i], zr_d.at[i], z_d + i, to).wait()
        remote(zs_u.at[i], zr_u.at[i], z_u + i, to).wait()
        return carry

    lax.fori_loop(0, A - 1, z_wait, 0)
    for i in range(A - 1):
        total_d = total_d + zr_d[i].astype(F32)
        total_u = total_u + zr_u[i].astype(F32)
    sh_d[...] = total_d.astype(BF)
    gather_down.begin()
    yr_u[...] = total_u.astype(BF)
    up_copies = []
    for kf in range(F - 1):
        up_copies.append(start(yr_u.at[lax.rem(f + kf + 1, F)], sh_u.at[f], slots(), device("f", kf + 1)))
    sh_u[f] = yr_u[f]

    class Square:
        def __init__(self, grad, got_c, got_y, got_x, got_z, share, gather):
            self.grad, self.got_c, self.got_y, self.got_x, self.got_z = grad, got_c, got_y, got_x, got_z
            self.share, self.gather = share, gather

        def over_c(self):
            self.copy_c = reduce_c(self.grad, self.got_c, half)

        def over_f(self):
            self.copy_c.wait()
            reduce_y(self.grad, self.got_c, self.got_c, half)
            self.copies = [
                start(self.got_c.at[lax.rem(f + kf + 1, F)], self.got_y.at[kf], slots(), device("f", kf + 1)) for kf in range(F - 1)
            ]

        def over_b(self):
            total = self.got_c[f].astype(F32)
            for kf in range(F - 1):
                self.copies[kf].wait()
                total = total + self.got_y[kf].astype(F32)
            self.got_y[F - 1] = total.astype(BF)
            self.copies = []
            for kb in range(B - 1):
                rows = pl.ds(pl.multiple_of(lax.rem(b + kb + 1, B) * r_u, r_u), r_u)
                self.copies.append(start(self.got_y.at[F - 1, rows, :], self.got_x.at[kb], slots(), device("b", kb + 1)))

        def over_a(self):
            rows = pl.ds(pl.multiple_of(b * r_u, r_u), r_u)
            total = self.got_y[F - 1, rows, :].astype(F32)
            for kb in range(B - 1):
                self.copies[kb].wait()
                total = total + self.got_x[kb].astype(F32)
            self.got_x[B - 1] = total.astype(BF)
            self.copies = []
            for ka in range(A - 1):
                cols = pl.ds(pl.multiple_of(lax.rem(a + ka + 1, A) * w_o, w_o), w_o)
                self.copies.append(start(self.got_x.at[B - 1, :, cols], self.got_z.at[ka], slots(), device("a", ka + 1)))

        def finish(self):
            cols = pl.ds(pl.multiple_of(a * w_o, w_o), w_o)
            total = self.got_x[B - 1, :, cols].astype(F32)
            for ka in range(A - 1):
                self.copies[ka].wait()
                total = total + self.got_z[ka].astype(F32)
            self.share[...] = total.astype(BF)
            self.gather.begin()

    square_o = Square(go_ref, o_c, o_y, o_x, o_z, o_s, gather_o)
    square_o.copy_c = o_c_copy
    square_q = Square(gq_ref, q_c, q_y, q_x, q_z, q_s, gather_q)

    square_o.over_f()

    for h in range(H):
        dq[:, h * HS : (h + 1) * HS] = (acc[h] * scale).T.astype(BF)
    n_rows = 128

    def query_grad(i, carry):
        col = pl.ds(pl.multiple_of(i * n_rows, n_rows), n_rows)
        fi = i // (own_rows // n_rows)
        row = lax.rem(i, own_rows // n_rows) * n_rows
        gq_ref[fi, pl.ds(pl.multiple_of(row, n_rows), n_rows), :] = nn(n1_ref[:, col].T, dq[...]).astype(BF)
        return carry

    lax.fori_loop(0, D // n_rows, query_grad, 0)
    square_q.over_c()

    dkv_c_copy.wait()

    def add_c(j, carry):
        dkv_c[j] = (dkv_c[j].astype(F32) + dkv[j, c].astype(F32)).astype(BF)
        return carry

    lax.fori_loop(0, A * B, add_c, 0)
    x_kv = []
    for kb in range(B - 1):
        other = lax.rem(b + kb + 1, B)
        for j in range(A):
            x_kv.append(start(dkv_c.at[j * B + other], dkv_x.at[kb, j], slots(), device("b", kb + 1)))

    square_o.over_b()
    for copy in up_copies:
        copy.wait()
    gather_up.begin()
    gather_down.from_a()
    square_q.over_f()

    for copy in x_kv:
        copy.wait()

    def add_x(j, carry):
        total = dkv_c[j * B + b].astype(F32)
        for kb in range(B - 1):
            total = total + dkv_x[kb, j].astype(F32)
        dkv_x[0, j] = total.astype(BF)
        return carry

    lax.fori_loop(0, A, add_x, 0)
    z_kv = slots(A - 1)
    for k in range(1, A):

        @pl.when(a - k >= 0)
        def _():
            to = (((a - k) * B + b) * 2 + c, f)
            remote(dkv_x.at[0, jnp.maximum(a - k, 0)], dkv_z.at[k - 1], z_kv + k - 1, to).start()

    square_o.over_a()
    square_q.over_b()
    gather_up.from_a()

    total = dkv_x[0, a].astype(F32)
    d_kv[...] = total
    for k in range(1, A):
        copy = remote(dkv_x.at[0, jnp.maximum(a - k, 0)], dkv_z.at[k - 1], z_kv + k - 1, device("a", A - k))

        @pl.when(a - k >= 0)
        def _():
            copy.wait_send()

        @pl.when(a + k < A)
        def _():
            copy.wait_recv()
            d_kv[...] = d_kv[...] + dkv_z[k - 1].astype(F32)

    d_kv_low = d_kv[...].astype(BF)

    n_cols = 256
    mean = jnp.zeros((tok, 1), F32)
    for i in range(D // n_cols):
        cols = slice(i * n_cols, (i + 1) * n_cols)
        part = nt(dq[...], wq_ref[cols, :]) + nt(d_kv_low, wkv_ref[cols, :])
        dn1[:, cols] = part
        weighted = part * unit_ref[:, cols]
        gain_rows[0:1, cols] = jnp.sum(weighted, axis=0, keepdims=True)
        mean = mean + jnp.sum(weighted * gain_ref[:, cols], axis=1, keepdims=True)
    gain_rows[1:2, :] = gain2_ref[...]
    mean = mean * (1.0 / D)

    r_kv = own_rows // A
    rows_kv = r_kv + 16
    for fi in range(F):
        for i in range(A):
            at = fi * own_rows + i * r_kv
            part = tn(n1_ref[:, at : at + r_kv], d_kv_low).astype(BF)
            gkv_ref[0, fi, i, :r_kv, :] = part[:, :HS]
            gkv_ref[1, fi, i, :r_kv, :] = part[:, HS:]
            for ci in range(2):
                rows = [gain_rows[ci : ci + 1, fi * own_rows + k * 128 : fi * own_rows + (k + 1) * 128] for k in range(own_rows // 128)]
                block = jnp.concatenate(rows + [jnp.zeros((16 - len(rows), 128), F32)], axis=0)
                gkv_ref[ci, fi, i, r_kv:, :] = block.astype(BF)
    kv_c_copy = start(gkv_ref.at[1 - c], kv_c, slots(), device("c", 1))

    square_o.finish()
    for i in range(D // n_cols):
        cols = slice(i * n_cols, (i + 1) * n_cols)
        grad_tokens[:, cols] = dres_ref[:, cols] + inv_ref[...] * (dn1[:, cols] * gain_ref[:, cols] - unit_ref[:, cols] * mean)
    square_q.over_a()
    kv_c_copy.wait()
    kv_c[...] = (kv_c[...].astype(F32) + gkv_ref[c].astype(F32)).astype(BF)
    kv_f = [start(kv_c.at[lax.rem(f + kf + 1, F)], kv_y.at[kf], slots(), device("f", kf + 1)) for kf in range(F - 1)]
    gather_down.from_b()
    gather_o.from_a()
    total = kv_c[f].astype(F32)
    for kf in range(F - 1):
        kv_f[kf].wait()
        total = total + kv_y[kf].astype(F32)
    kv_y[F - 1] = total.astype(BF)
    kv_b = [start(kv_y.at[F - 1], kv_x.at[kb], slots(), device("b", kb + 1)) for kb in range(B - 1)]
    square_q.finish()
    total = kv_y[F - 1].astype(F32)
    for kb in range(B - 1):
        kv_b[kb].wait()
        total = total + kv_x[kb].astype(F32)
    kv_x[B - 1] = total.astype(BF)
    kv_a = [start(kv_x.at[B - 1, lax.rem(a + ka + 1, A)], kv_z.at[ka], slots(), device("a", ka + 1)) for ka in range(A - 1)]
    gather_up.from_b()
    total = kv_x[B - 1, a].astype(F32)
    for ka in range(A - 1):
        kv_a[ka].wait()
        total = total + kv_z[ka].astype(F32)
    kv_s[...] = total.astype(BF)
    gather_kv.begin()
    gather_q.from_a()
    gather_o.from_b()
    gather_kv.from_a()
    gather_q.from_b()
    for gather in gathers:
        gather.end()


def tail(dims, ends, queries, window_kv, d_attended, attended, lse, grad_down, grad_up, grad_out, n1, wq, wkv, unit, inv, gain, dres, gain2):
    A, B, F = dims
    tok, D = n1.shape
    window = window_kv.shape[0]
    own_rows, shard = D // F, grad_down.shape[0]
    half, r_d, r_u, w_u = D // 2, shard // (A * B), own_rows // B, shard // A
    w_o, r_kv = half // A, own_rows // A + 16
    hbm = pl.BlockSpec(memory_space=pltpu.HBM)

    def low(*shape):
        return pltpu.VMEM(shape, BF)

    square = [low(F, own_rows, half), low(F, own_rows, half), low(B, r_u, half), low(A - 1, r_u, w_o), low(r_u, w_o)]
    n_sems = 2 * (A * (B - 1) + A - 1) + 4 * (A - 1 + (B - 1) * A + B * A) + (A - 1 + A) + 2 * (F + B + A) + F + (B - 1) * A + A + F + B + A + 8
    return pl.pallas_call(
        functools.partial(tail_kernel, dims),
        out_shape=(
            jax.ShapeDtypeStruct((2 * shard, D), BF),
            jax.ShapeDtypeStruct((F, own_rows, 2 * shard), BF),
            jax.ShapeDtypeStruct((own_rows, D), BF),
            jax.ShapeDtypeStruct((own_rows, D), BF),
            jax.ShapeDtypeStruct((2, A, r_kv, HS), BF),
            jax.ShapeDtypeStruct((tok, D), F32),
        ),
        in_specs=[SMEM] + [VMEM] * 16,
        out_specs=(hbm,) * 5 + (VMEM,),
        scratch_shapes=[
            pltpu.VMEM((H, HS, tok), F32),
            pltpu.VMEM((H, tok), F32),
            low(tok, D),
            low(A * B, 2, tok, 2 * HS),
            low(A * B, tok, 2 * HS),
            low(max(1, B - 1), A, tok, 2 * HS),
            low(max(1, A - 1), tok, 2 * HS),
            pltpu.VMEM((tok, 2 * HS), F32),
            pltpu.VMEM((tok, D), F32),
            low(F, own_rows, D),
            low(2, F, A, r_kv, HS),
            low(B - 1, A, r_d, D),
            low(B - 1, A, F, r_u, w_u),
            low(A - 1, r_d, D),
            low(A - 1, F, r_u, w_u),
            low(A - 1, r_d, D),
            low(A - 1, F, r_u, w_u),
            low(r_d, D),
            low(F, r_u, w_u),
            low(F, r_u, w_u),
            *square,
            *square,
            low(F, A, r_kv, HS),
            low(F, A, r_kv, HS),
            low(B, A, r_kv, HS),
            low(A - 1, r_kv, HS),
            low(r_kv, HS),
            pltpu.VMEM((8, D), F32),
            pltpu.SemaphoreType.DMA((n_sems,)),
            pltpu.SemaphoreType.DMA((n_sems,)),
            pltpu.SemaphoreType.DMA((5,)),
        ],
        compiler_params=pltpu.CompilerParams(vmem_limit_bytes=56 * 2**20, collective_id=1, has_side_effects=True),
        cost_estimate=pl.CostEstimate(flops=20 * tok * window * D, bytes_accessed=2**25, transcendentals=tok * window * H),
        name="tail",
    )(ends, queries, window_kv, d_attended, attended, lse, grad_down, grad_up, grad_out, n1, wq, wkv, unit, inv, gain, dres, gain2)


def after(value, *others):
    return lax.optimization_barrier((value, *others))[0]


class Grid:
    def __init__(self):
        seq = lax.axis_size("seq")
        self.F = lax.axis_size("fsdp")
        self.C = 2
        chips = seq // 2
        self.B = 2 if chips == 8 else chips // 2
        self.A = chips // self.B
        self.s = lax.axis_index("seq")
        self.f = lax.axis_index("fsdp")
        self.c = self.s % 2
        self.b = self.s // 2 % self.B
        self.a = self.s // (2 * self.B)

    def size(self, axis):
        return {"a": self.A, "b": self.B, "c": self.C, "f": self.F}[axis]

    def place(self, axis):
        return {"a": self.a, "b": self.b, "c": self.c, "f": self.f}[axis]

    def send(self, value, axis, step, upward=False):
        pairs = []
        for a in range(self.A):
            for b in range(self.B):
                for c in range(2):
                    for f in range(self.F):
                        at = {"a": a, "b": b, "c": c, "f": f}
                        to = dict(at)
                        to[axis] += step
                        if upward and not 0 <= to[axis] < self.size(axis):
                            continue
                        to[axis] %= self.size(axis)
                        line = [((d["a"] * self.B + d["b"]) * 2 + d["c"]) * self.F + d["f"] for d in (at, to)]
                        pairs.append(tuple(line))
        return lax.ppermute(value, ("seq", "fsdp"), pairs)

    def stack(self, parts, axis):
        n, me = len(parts), self.place(axis)
        if n == 2:
            low = me == 0
            return jnp.stack([jnp.where(low, parts[0], parts[1]), jnp.where(low, parts[1], parts[0])])
        twice = jnp.stack(parts + parts)
        return lax.dynamic_slice_in_dim(twice, (n - me) % n, n, 0)

    def gather(self, value, axis):
        n = self.size(axis)
        return self.stack([value] + [self.send(value, axis, -k) for k in range(1, n)], axis)

    def scatter(self, parts, axis):
        n, me = self.size(axis), self.place(axis)

        def pick(k):
            return lax.dynamic_index_in_dim(parts, (me + k) % n, 0, keepdims=False)

        got = [self.send(pick(k).astype(BF), axis, k) for k in range(1, n)]
        total = pick(0).astype(F32)
        for piece in got:
            total = total + piece.astype(F32)
        return total

    def plane_sum(self, parts):
        half = self.scatter(parts, "b").astype(BF)
        return self.scatter(half, "a")

    def plane_gather(self, share):
        rows = self.gather(share.astype(BF), "a")
        return self.gather(rows, "b")


def local(
    tokens,
    cotangent,
    seq_lengths,
    group_of_shard,
    gain_attn,
    w_query,
    w_key,
    w_value,
    w_out,
    gain_ffn,
    w_up,
    w_down,
):
    g = Grid()
    A, B, C, F = g.A, g.B, g.C, g.F
    tok, D = tokens.shape[1:]
    FF = w_up.shape[1]
    own_rows = D // F
    seq_parts = A * B * C
    shard = FF // (2 * F)

    group = lax.dynamic_index_in_dim(group_of_shard, g.f, 0, keepdims=False)
    lengths = lax.dynamic_index_in_dim(seq_lengths, group, 0, keepdims=False)
    running, ends = jnp.int32(0), []
    for i in range(seq_lengths.shape[1]):
        running = running + lengths[i]
        ends.append(running)
    scal = jnp.stack([g.s.astype(jnp.int32), *ends])

    gains = jnp.stack([gain_attn, gain_ffn])
    full_gains = g.gather(gains, "f").transpose(1, 0, 2).reshape(2, D).astype(F32)
    gain_first, gain_second = full_gains[0], full_gains[1]
    own_kv = jnp.concatenate([w_key, w_value], axis=1)
    full_kv = g.gather(own_kv, "f").reshape(D, 2 * HS)

    def gather_weight(weight, *late):
        half = own_rows // 2
        mine = lax.dynamic_slice_in_dim(weight, g.c * half, half, 0)
        if late:
            mine = after(mine, *late)
        pieces = [g.gather(g.send(mine, "f", -k), "c").reshape(weight.shape) for k in range(1, F)]
        return g.stack([weight] + pieces, "f").reshape(F * own_rows, -1)

    full_query = gather_weight(w_query)

    stream = tokens[0].astype(F32)
    inverse_first = lax.rsqrt(jnp.mean(stream * stream, axis=1, keepdims=True) + EPS)
    unit_first = stream * inverse_first
    normed_first = (unit_first * gain_first).astype(BF)
    key_value = nn(normed_first, full_kv).astype(BF)
    queries = nn(normed_first, full_query).astype(BF)

    column = [key_value] + [g.send(key_value, "a", k, upward=True) for k in range(1, A)]
    twice = jnp.stack(column[::-1] + column[::-1])
    column = lax.dynamic_slice_in_dim(twice, A - 1 - g.a, A, 0)
    plane = g.gather(column, "b")
    whole = g.gather(plane, "c")
    window_kv = whole.transpose(2, 1, 0, 3, 4).reshape(seq_parts * tok, 2 * HS)

    full_out = gather_weight(w_out, full_query)
    upstream = cotangent[0]
    cot = []
    for k in range(F):
        mine = upstream if k == 0 else g.send(after(upstream, full_query), "f", k)
        cot.append(jnp.concatenate([mine, g.send(mine, "c", 1)], axis=0))
    ups = w_up.reshape(own_rows, F, 2, shard)
    up_parts = []
    for k in range(F):
        block = lax.dynamic_slice(ups, (0, (g.f + k) % F, g.c, 0), (own_rows, 1, 1, shard)).reshape(own_rows, shard)
        up_parts.append(block if k == 0 else g.send(after(block, full_out), "f", k))
    up_parts = [up_parts[0]] + up_parts[1:][::-1]
    up = g.stack(up_parts, "f").reshape(D, shard)
    down = lax.dynamic_slice_in_dim(w_down, g.c * shard, shard, 0)

    attended, lse = attend(scal, queries, window_kv)

    residual = stream + nn(attended, full_out)
    inverse_second = lax.rsqrt(jnp.mean(residual * residual, axis=1, keepdims=True) + EPS)
    unit_second = residual * inverse_second
    normed_second = (unit_second * gain_second).astype(BF)

    out_sum, back_sum = residual, jnp.zeros((tok, D), F32)
    hiddens, d_pres, norms = [], [], []
    backs, outs = [], []
    for k in range(F):
        mine = normed_second if k == 0 else g.send(normed_second, "f", k)
        norm = jnp.concatenate([mine, g.send(mine, "c", 1)], axis=0)
        before = nn(norm, up)
        d_hidden = nt(cot[k], down)
        sig = jax.nn.sigmoid(before)
        hidden = (before * sig).astype(BF)
        d_pre = (d_hidden * sig * (1.0 + before * (1.0 - sig))).astype(BF)
        back = nt(d_pre, up)
        out = nn(hidden, down)
        hiddens.append(hidden)
        d_pres.append(d_pre)
        norms.append(norm)
        backs.append(back)
        outs.append(out)

    def give_back(parts):
        total = 0.0
        for k, part in enumerate(parts):
            other = g.send(part[tok:].astype(BF), "c", 1)
            chip = part[:tok] + other.astype(F32)
            if k:
                chip = g.send(chip.astype(BF), "f", -k).astype(F32)
            total = total + chip
        return total

    d_normed_second = give_back(backs)
    output = (residual + give_back(outs)).astype(BF)

    grad_down = sum(tn(h, c) for h, c in zip(hiddens, cot)).astype(BF)
    grad_up = sum(tn(n, d) for n, d in zip(norms, d_pres)).astype(BF)

    def norm_back(gradient, unit_rows, inverse, gain_vec):
        scaled = gradient * gain_vec
        gain_grad = jnp.sum(gradient * unit_rows, axis=0)
        return gain_grad, inverse * (scaled - unit_rows * jnp.mean(scaled * unit_rows, axis=1, keepdims=True))

    gain_second_grad, d_from_norm = norm_back(d_normed_second, unit_second, inverse_second, gain_second)
    d_residual = upstream.astype(F32) + d_from_norm
    d_branch = d_residual.astype(BF)
    d_attended = nt(d_branch, full_out).astype(BF)
    grad_out = tn(attended, d_branch).astype(BF)

    down_all, up_all, out_all, query_all, kv_all, grad_tokens = tail(
        (A, B, F),
        scal[1:],
        queries,
        window_kv,
        d_attended,
        attended,
        lse,
        grad_down,
        grad_up.reshape(F, own_rows, shard),
        grad_out.reshape(F, own_rows, D),
        normed_first,
        full_query,
        full_kv,
        unit_first,
        inverse_first,
        gain_first[None],
        d_residual,
        gain_second_grad[None],
    )
    grad_w_down = down_all.astype(F32)
    grad_w_up = jnp.concatenate([up_all[i].astype(F32) for i in range(F)], axis=1)
    grad_w_out = out_all.astype(F32)
    grad_w_query = query_all.astype(F32)
    r_kv = own_rows // A
    grad_kv = kv_all[:, :, :r_kv].astype(F32).reshape(2, own_rows, HS)
    gain_grads = kv_all[:, 0, r_kv : r_kv + own_rows // 128].astype(F32).reshape(2, own_rows)

    return (
        output[None],
        grad_tokens[None],
        gain_grads[0],
        grad_w_query,
        grad_kv[0],
        grad_kv[1],
        grad_w_out,
        gain_grads[1],
        grad_w_up,
        grad_w_down,
    )


def solution(mesh):
    placed = (
        P("fsdp", "seq", None),
        P("fsdp", "seq", None),
        P(),
        P(),
        P("fsdp"),
        P("fsdp", None),
        P("fsdp", None),
        P("fsdp", None),
        P("fsdp", None),
        P("fsdp"),
        P("fsdp", None),
        P("fsdp", None),
    )
    return jax.shard_map(
        local,
        mesh=mesh,
        in_specs=placed,
        out_specs=(
            P("fsdp", "seq", None),
            P("fsdp", "seq", None),
            P("fsdp"),
            P("fsdp", None),
            P("fsdp", None),
            P("fsdp", None),
            P("fsdp", None),
            P("fsdp"),
            P("fsdp", None),
            P("fsdp", None),
        ),
        check_vma=False,
    )
```

```python
import functools
import math
import types

import jax
import jax.numpy as jnp
from jax import lax
from jax.experimental import pallas as pl
from jax.experimental.pallas import tpu as pltpu
from jax.sharding import PartitionSpec as P

H = 8
HS = 128
EPS = 1e-05
NEG = -1e30
LIMIT = 60 * 2**20
CHUNK = 512
BF = jnp.bfloat16
F32 = jnp.float32


def nt(a, b):
    return lax.dot_general(a, b, (((1,), (1,)), ((), ())), preferred_element_type=F32)


def nn(a, b):
    return lax.dot_general(a, b, (((1,), (0,)), ((), ())), preferred_element_type=F32)


def tn(a, b):
    return lax.dot_general(a, b, (((0,), (0,)), ((), ())), preferred_element_type=F32)


def query_range(scal, tok):
    first = scal[0] * tok
    pos = first + lax.broadcasted_iota(jnp.int32, (1, tok), 1)
    start = jnp.zeros((1, tok), jnp.int32)
    latest = jnp.int32(0)
    for i in range(1, scal.shape[0]):
        end = scal[i]
        start = jnp.maximum(start, jnp.where(end <= pos, end, 0))
        latest = jnp.maximum(latest, jnp.where(end <= first + tok - 1, end, 0))
    return first, pos, start, latest


def chunk_loop(scal, tok, window, step):
    first, pos, start, latest = query_range(scal, tok)
    chunks = (first + tok + CHUNK - 1) // CHUNK

    def body(j, carry):
        low = j * CHUNK
        whole = jnp.logical_and(low >= latest, low + CHUNK - 1 <= first)

        @pl.when(whole)
        def _():
            step(j, None)

        @pl.when(jnp.logical_not(whole))
        def _():
            keys = low + lax.broadcasted_iota(jnp.int32, (CHUNK, tok), 0)
            step(j, jnp.logical_and(keys >= start, keys <= pos))

        return carry

    lax.fori_loop(0, chunks, body, 0)
    return chunks


def attend_kernel(scal, q_ref, kv_ref, out_ref, lse_ref, acc, top, total):
    tok = q_ref.shape[0]
    factor = math.log2(math.e) / math.sqrt(HS)
    top[...] = jnp.full(top.shape, -3e38, F32)
    total[...] = jnp.zeros(total.shape, F32)
    acc[...] = jnp.zeros(acc.shape, F32)

    def step(j, mask):
        rows = pl.ds(pl.multiple_of(j * CHUNK, CHUNK), CHUNK)
        keys = kv_ref[rows, :HS]
        values_t = kv_ref[rows, HS:].T
        for h in range(H):
            scores = nt(keys, q_ref[:, h * HS : (h + 1) * HS])
            if mask is not None:
                scores = jnp.where(mask, scores, NEG)
            old = top[h : h + 1, :]
            new = jnp.maximum(old, jnp.max(scores, axis=0, keepdims=True) * factor)
            shrink = jnp.exp2(old - new)
            probs = jnp.exp2(scores * factor - new)
            total[h : h + 1, :] = total[h : h + 1, :] * shrink + jnp.sum(probs, axis=0, keepdims=True)
            acc[h] = acc[h] * shrink + nn(values_t, probs.astype(BF))
            top[h : h + 1, :] = new

    chunk_loop(scal, tok, kv_ref.shape[0], step)
    for h in range(H):
        mixed = acc[h] * (1.0 / total[h : h + 1, :])
        out_ref[:, h * HS : (h + 1) * HS] = mixed.T.astype(BF)
    lse_ref[...] = top[...] + jnp.log2(total[...])


VMEM = pl.BlockSpec(memory_space=pltpu.VMEM)
SMEM = pl.BlockSpec(memory_space=pltpu.SMEM)
PARAMS = pltpu.CompilerParams(vmem_limit_bytes=40 * 2**20)


def attend(scal, queries, window_kv):
    tok = queries.shape[0]
    window = window_kv.shape[0]
    return pl.pallas_call(
        attend_kernel,
        out_shape=(
            jax.ShapeDtypeStruct((tok, H * HS), BF),
            jax.ShapeDtypeStruct((H, tok), F32),
        ),
        in_specs=[SMEM, VMEM, VMEM],
        out_specs=(VMEM, VMEM),
        scratch_shapes=[
            pltpu.VMEM((H, HS, tok), F32),
            pltpu.VMEM((H, tok), F32),
            pltpu.VMEM((H, tok), F32),
        ],
        compiler_params=PARAMS,
        cost_estimate=pl.CostEstimate(
            flops=8 * tok * window * H * HS, bytes_accessed=4 * window * HS, transcendentals=tok * window * H
        ),
        name="attend",
    )(scal, queries, window_kv)


MESH = pl.DeviceIdType.MESH


TAIL_IN = (
    "ends",
    "q_ref",
    "kv_ref",
    "d_ref",
    "att_ref",
    "lse_ref",
    "gd_ref",
    "gu_ref",
    "go_ref",
    "n1_ref",
    "wq_ref",
    "wkv_ref",
    "tok_ref",
    "inv_ref",
    "gain_ref",
    "dres_ref",
    "gain2_ref",
)
TAIL_OUT = (
    "out_down",
    "out_up",
    "out_o",
    "out_q",
    "out_kv",
    "grad_tokens",
)
TAIL_SCRATCH = (
    "acc",
    "delta",
    "dq",
    "dkv",
    "dkv_c",
    "dkv_x",
    "dkv_z",
    "d_kv",
    "dn1",
    "gq_ref",
    "gkv_ref",
    "xr_d",
    "xr_u",
    "zs_d",
    "zs_u",
    "zr_d",
    "zr_u",
    "sh_d",
    "sh_u",
    "yr_u",
    "o_c",
    "o_y",
    "o_x",
    "o_z",
    "o_s",
    "q_c",
    "q_y",
    "q_x",
    "q_z",
    "q_s",
    "kv_c",
    "kv_y",
    "kv_x",
    "kv_z",
    "kv_s",
    "gain_rows",
    "send_sem",
    "recv_sem",
    "copy_sem",
)


def tail_kernel(dims, head, names, *refs):
    A, B, F = dims
    r = types.SimpleNamespace(**dict(zip(names, refs, strict=True)))
    if head is not None:
        for name, held in AGAIN.items():
            setattr(r, name, getattr(r, held))
    ends = r.ends
    q_ref = r.q_ref
    kv_ref = r.kv_ref
    d_ref = r.d_ref
    att_ref = r.att_ref
    lse_ref = r.lse_ref
    gd_ref = r.gd_ref
    gu_ref = r.gu_ref
    go_ref = r.go_ref
    n1_ref = r.n1_ref
    wq_ref = r.wq_ref
    wkv_ref = r.wkv_ref
    tok_ref = r.tok_ref
    inv_ref = r.inv_ref
    gain_ref = r.gain_ref
    dres_ref = r.dres_ref
    gain2_ref = r.gain2_ref
    out_down = r.out_down
    out_up = r.out_up
    out_o = r.out_o
    out_q = r.out_q
    out_kv = r.out_kv
    grad_tokens = r.grad_tokens
    acc = r.acc
    delta = r.delta
    dq = r.dq
    dkv = r.dkv
    dkv_c = r.dkv_c
    dkv_x = r.dkv_x
    dkv_z = r.dkv_z
    d_kv = r.d_kv
    dn1 = r.dn1
    gq_ref = r.gq_ref
    gkv_ref = r.gkv_ref
    xr_d = r.xr_d
    xr_u = r.xr_u
    zs_d = r.zs_d
    zs_u = r.zs_u
    zr_d = r.zr_d
    zr_u = r.zr_u
    sh_d = r.sh_d
    sh_u = r.sh_u
    yr_u = r.yr_u
    o_c = r.o_c
    o_y = r.o_y
    o_x = r.o_x
    o_z = r.o_z
    o_s = r.o_s
    q_c = r.q_c
    q_y = r.q_y
    q_x = r.q_x
    q_z = r.q_z
    q_s = r.q_s
    kv_c = r.kv_c
    kv_y = r.kv_y
    kv_x = r.kv_x
    kv_z = r.kv_z
    kv_s = r.kv_s
    gain_rows = r.gain_rows
    send_sem = r.send_sem
    recv_sem = r.recv_sem
    copy_sem = r.copy_sem
    tok = q_ref.shape[0]
    window = kv_ref.shape[0]
    D = n1_ref.shape[1]
    own_rows = D // F
    shard = gd_ref.shape[0]
    s = lax.axis_index("seq")
    f = lax.axis_index("fsdp")
    c = lax.rem(s, 2)
    b = lax.rem(s // 2, B)
    a = s // (2 * B)

    def device(axis, step):
        at = {"a": a, "b": b, "c": c, "f": f}
        at[axis] = lax.rem(at[axis] + step, {"a": A, "b": B, "c": 2, "f": F}[axis])
        return ((at["a"] * B + at["b"]) * 2 + at["c"], at["f"])

    def lower(axis, step):
        return lax.rem({"a": a + A, "b": b + B, "f": f + F}[axis] - step, {"a": A, "b": B, "f": F}[axis])

    used = [0]

    def slots(n=1):
        used[0] += n
        assert used[0] <= send_sem.shape[0]
        return used[0] - n

    def remote(src, dst, slot, to):
        return pltpu.make_async_remote_copy(
            src_ref=src, dst_ref=dst, send_sem=send_sem.at[slot], recv_sem=recv_sem.at[slot], device_id=to, device_id_type=MESH
        )

    pending = []

    def start(src, dst, slot, to):
        copy = remote(src, dst, slot, to)
        copy.start()
        pending.append(copy)
        return copy

    barrier = pltpu.get_barrier_semaphore()
    partners = [("a", k) for k in range(1, A)] + [("b", k) for k in range(1, B)] + [("c", 1)] + [("f", k) for k in range(1, F)]
    for axis, k in partners:
        pl.semaphore_signal(barrier, inc=1, device_id=device(axis, k), device_id_type=MESH)
    pl.semaphore_wait(barrier, len(partners))

    r_d = shard // (A * B)
    r_u = own_rows // B
    w_u = shard // A
    x_d = slots(A * (B - 1))
    x_u = slots(A * (B - 1))
    z_d = slots(A - 1)
    z_u = slots(A - 1)

    def down_copies(i):
        at = lax.rem(a + 1 + i, A)
        copies = []
        for kb in range(B - 1):
            other = lax.rem(b + kb + 1, B)
            rows = pl.ds(pl.multiple_of((other * A + at) * r_d, r_d), r_d)
            copies.append(remote(gd_ref.at[rows, :], xr_d.at[kb, i], x_d + kb * A + i, device("b", kb + 1)))
        return copies

    def up_copies(i):
        at = lax.rem(a + 1 + i, A)
        copies = []
        for kb in range(B - 1):
            rows = pl.ds(pl.multiple_of(lax.rem(b + kb + 1, B) * r_u, r_u), r_u)
            cols = pl.ds(pl.multiple_of(at * w_u, w_u), w_u)
            copies.append(remote(gu_ref.at[:, rows, cols], xr_u.at[kb, i], x_u + kb * A + i, device("b", kb + 1)))
        return copies

    def send_down(first, last):
        for i in range(first, last):
            for copy in down_copies(i):
                copy.start()

    def send_up(first, last):
        for i in range(first, last):
            for copy in up_copies(i):
                copy.start()

    def own_sums(i):
        at = lax.rem(a + 1 + i, A)
        rows = pl.ds(pl.multiple_of((b * A + at) * r_d, r_d), r_d)
        total_d = gd_ref[rows, :].astype(F32)
        rows = pl.ds(pl.multiple_of(b * r_u, r_u), r_u)
        cols = pl.ds(pl.multiple_of(at * w_u, w_u), w_u)
        total_u = gu_ref[:, rows, cols].astype(F32)
        for kb in range(B - 1):
            total_d = total_d + xr_d[kb, i].astype(F32)
            total_u = total_u + xr_u[kb, i].astype(F32)
        return total_d, total_u

    if head is None:
        for i in range(A):
            send_down(i, i + 1)
            send_up(i, i + 1)
    else:
        own = types.SimpleNamespace(
            A=A, B=B, F=F, a=a, b=b, c=c, f=f, s=s, slots=slots, remote=remote, device=device, lower=lower,
            send_down=send_down, send_up=send_up,
        )
        finish_output, finish_head = head(r, own)

    half = D // 2

    def reduce_c(ref, got, width):
        other = pl.ds(pl.multiple_of((1 - c) * width, width), width)
        return start(ref.at[:, :, other], got, slots(), device("c", 1))

    def reduce_y(ref, got, sent, width):
        mine = pl.ds(pl.multiple_of(c * width, width), width)

        def add(i, carry):
            sent[i] = (ref[i, :, mine].astype(F32) + got[i].astype(F32)).astype(BF)
            return carry

        lax.fori_loop(0, F, add, 0)

    o_c_copy = reduce_c(go_ref, o_c, half)

    scale = 1.0 / math.sqrt(HS)
    factor = math.log2(math.e) * scale
    acc[...] = jnp.zeros(acc.shape, F32)
    for h in range(H):
        cols = slice(h * HS, (h + 1) * HS)
        both = d_ref[:, cols].astype(F32) * att_ref[:, cols].astype(F32)
        delta[h : h + 1, :] = jnp.sum(both.T, axis=0, keepdims=True)
    first = s * tok
    pos = first + lax.broadcasted_iota(jnp.int32, (1, tok), 1)
    begin = jnp.zeros((1, tok), jnp.int32)
    for i in range(ends.shape[0]):
        begin = jnp.maximum(begin, jnp.where(ends[i] <= pos, ends[i], 0))

    def step(j, masked):
        rows = pl.ds(pl.multiple_of(j * CHUNK, CHUNK), CHUNK)
        keys = kv_ref[rows, :HS]
        values = kv_ref[rows, HS:]
        keys_t = keys.T
        if masked:
            at = j * CHUNK + lax.broadcasted_iota(jnp.int32, (CHUNK, tok), 0)
            mask = jnp.logical_and(at >= begin, at <= pos)
        d_keys = jnp.zeros((CHUNK, HS), F32)
        d_values = jnp.zeros((CHUNK, HS), F32)
        for h in range(H):
            cols = slice(h * HS, (h + 1) * HS)
            q = q_ref[:, cols]
            d = d_ref[:, cols]
            scores = nt(keys, q)
            if masked:
                scores = jnp.where(mask, scores, NEG)
            probs = jnp.exp2(scores * factor - lse_ref[h : h + 1, :])
            d_probs = nt(values, d)
            d_scores = (probs * (d_probs - delta[h : h + 1, :])).astype(BF)
            d_values = d_values + nn(probs.astype(BF), d)
            d_keys = d_keys + nn(d_scores, q)
            acc[h] = acc[h] + nn(keys_t, d_scores)
        for i in range(2):
            part = slice(i * tok, (i + 1) * tok)
            dkv[j, i, :, :HS] = (d_keys[part] * scale).astype(BF)
            dkv[j, i, :, HS:] = d_values[part].astype(BF)

    chunks = s // 2 + 1
    per = -(-(window // CHUNK) // max(1, A - 1))

    def attention_chunk(j, carry):
        plain = jnp.logical_and(jnp.logical_and(j > 0, j < chunks - 1), s < 2 * A * B - 1)

        @pl.when(plain)
        def _():
            step(j, False)

        @pl.when(jnp.logical_not(plain))
        def _():
            step(j, True)

        return carry

    def feed_forward_step(i, carry):
        lax.fori_loop(i * per, jnp.minimum((i + 1) * per, chunks), attention_chunk, 0)
        for copy in down_copies(i) + up_copies(i):
            copy.wait()
        total_d, total_u = own_sums(i)
        to = lax.rem(a + 1 + i, A)
        to = ((to * B + b) * 2 + c, f)
        zs_d[i] = total_d.astype(BF)
        remote(zs_d.at[i], zr_d.at[i], z_d + i, to).start()
        zs_u[i] = total_u.astype(BF)
        remote(zs_u.at[i], zr_u.at[i], z_u + i, to).start()
        return carry

    lax.fori_loop(0, A - 1, feed_forward_step, 0)

    def clear(j, carry):
        dkv[j] = jnp.zeros(dkv.shape[1:], BF)
        return carry

    lax.fori_loop(chunks, window // CHUNK, clear, 0)

    class Gather:
        def __init__(self, share, view, planes=True):
            self.share, self.view, self.planes = share, view, planes
            n = B if planes else 1
            self.z = slots(A - 1)
            self.x = slots((n - 1) * A)
            self.s = slots(n * A)
            self.local = pltpu.make_async_copy(share, view(c, b, a), copy_sem.at[len(gathers)])
            gathers.append(self)

        def begin(self):
            self.local.start()
            mine = self.view(c, b, a)
            self.zs = [start(self.share, mine, self.z + k, device("a", k + 1)) for k in range(A - 1)]
            self.xs, self.cs = {}, {}
            self.pass_on(self.share, mine, 0)

        def pass_on(self, src, dst, j):
            for kb in range(B - 1 if self.planes else 0):
                self.xs[kb, j] = start(src, dst, self.x + kb * A + j, device("b", kb + 1))
            self.cs[0, j] = start(src, dst, self.s + j, device("c", 1))

        def from_a(self):
            for k in range(A - 1):
                self.zs[k].wait_recv()
                here = self.view(c, b, lower("a", k + 1))
                self.pass_on(here, here, k + 1)

        def from_b(self):
            for kb in range(B - 1 if self.planes else 0):
                for j in range(A):
                    self.xs[kb, j].wait_recv()
                    here = self.view(c, lower("b", kb + 1), lower("a", j) if j else a)
                    self.cs[kb + 1, j] = start(here, here, self.s + (kb + 1) * A + j, device("c", 1))

        def end(self):
            self.local.wait()
            for copy in self.zs + list(self.xs.values()):
                copy.wait_send()
            for copy in self.cs.values():
                copy.wait()

    gathers = []

    def view_down(c_, b_, a_):
        return out_down.at[pl.ds(pl.multiple_of(((c_ * B + b_) * A + a_) * r_d, r_d), r_d), :]

    def view_up(c_, b_, a_):
        rows = pl.ds(pl.multiple_of(b_ * r_u, r_u), r_u)
        return out_up.at[:, rows, pl.ds(pl.multiple_of(c_ * shard + a_ * w_u, w_u), w_u)]

    w_o = half // A

    def view_square(out):
        def view(c_, b_, a_):
            rows = pl.ds(pl.multiple_of(b_ * r_u, r_u), r_u)
            return out.at[rows, pl.ds(pl.multiple_of(c_ * half + a_ * w_o, w_o), w_o)]

        return view

    gather_down = Gather(sh_d, view_down)
    gather_up = Gather(sh_u, view_up)
    gather_o = Gather(o_s, view_square(out_o))
    gather_q = Gather(q_s, view_square(out_q))
    gather_kv = Gather(kv_s, lambda c_, b_, a_: out_kv.at[c_, a_], planes=False)

    dkv_c_copy = start(dkv.at[:, 1 - c], dkv_c, slots(), device("c", 1))

    for copy in down_copies(A - 1) + up_copies(A - 1):
        copy.wait()
    total_d, total_u = own_sums(A - 1)

    def z_wait(i, carry):
        to = lax.rem(a + 1 + i, A)
        to = ((to * B + b) * 2 + c, f)
        remote(zs_d.at[i], zr_d.at[i], z_d + i, to).wait()
        remote(zs_u.at[i], zr_u.at[i], z_u + i, to).wait()
        return carry

    lax.fori_loop(0, A - 1, z_wait, 0)
    for i in range(A - 1):
        total_d = total_d + zr_d[i].astype(F32)
        total_u = total_u + zr_u[i].astype(F32)
    sh_d[...] = total_d.astype(BF)
    gather_down.begin()
    yr_u[...] = total_u.astype(BF)
    up_y = []
    for kf in range(F - 1):
        up_y.append(start(yr_u.at[lax.rem(f + kf + 1, F)], sh_u.at[f], slots(), device("f", kf + 1)))
    sh_u[f] = yr_u[f]

    class Square:
        def __init__(self, grad, got_c, got_y, got_x, got_z, share, gather):
            self.grad, self.got_c, self.got_y, self.got_x, self.got_z = grad, got_c, got_y, got_x, got_z
            self.share, self.gather = share, gather

        def over_c(self):
            self.copy_c = reduce_c(self.grad, self.got_c, half)

        def over_f(self):
            self.copy_c.wait()
            reduce_y(self.grad, self.got_c, self.got_c, half)
            self.copies = [
                start(self.got_c.at[lax.rem(f + kf + 1, F)], self.got_y.at[kf], slots(), device("f", kf + 1)) for kf in range(F - 1)
            ]

        def over_b(self):
            total = self.got_c[f].astype(F32)
            for kf in range(F - 1):
                self.copies[kf].wait()
                total = total + self.got_y[kf].astype(F32)
            self.got_y[F - 1] = total.astype(BF)
            self.copies = []
            for kb in range(B - 1):
                rows = pl.ds(pl.multiple_of(lax.rem(b + kb + 1, B) * r_u, r_u), r_u)
                self.copies.append(start(self.got_y.at[F - 1, rows, :], self.got_x.at[kb], slots(), device("b", kb + 1)))

        def over_a(self):
            rows = pl.ds(pl.multiple_of(b * r_u, r_u), r_u)
            total = self.got_y[F - 1, rows, :].astype(F32)
            for kb in range(B - 1):
                self.copies[kb].wait()
                total = total + self.got_x[kb].astype(F32)
            self.got_x[B - 1] = total.astype(BF)
            self.copies = []
            for ka in range(A - 1):
                cols = pl.ds(pl.multiple_of(lax.rem(a + ka + 1, A) * w_o, w_o), w_o)
                self.copies.append(start(self.got_x.at[B - 1, :, cols], self.got_z.at[ka], slots(), device("a", ka + 1)))

        def finish(self):
            cols = pl.ds(pl.multiple_of(a * w_o, w_o), w_o)
            total = self.got_x[B - 1, :, cols].astype(F32)
            for ka in range(A - 1):
                self.copies[ka].wait()
                total = total + self.got_z[ka].astype(F32)
            self.share[...] = total.astype(BF)
            self.gather.begin()

    square_o = Square(go_ref, o_c, o_y, o_x, o_z, o_s, gather_o)
    square_o.copy_c = o_c_copy
    square_q = Square(gq_ref, q_c, q_y, q_x, q_z, q_s, gather_q)

    square_o.over_f()

    if head is not None:
        finish_output()
    for h in range(H):
        dq[:, h * HS : (h + 1) * HS] = (acc[h] * scale).T.astype(BF)
    n_rows = 128

    def query_grad(i, carry):
        col = pl.ds(pl.multiple_of(i * n_rows, n_rows), n_rows)
        fi = i // (own_rows // n_rows)
        row = lax.rem(i, own_rows // n_rows) * n_rows
        gq_ref[fi, pl.ds(pl.multiple_of(row, n_rows), n_rows), :] = nn(n1_ref[:, col].T, dq[...]).astype(BF)
        return carry

    lax.fori_loop(0, D // n_rows, query_grad, 0)
    square_q.over_c()

    dkv_c_copy.wait()

    def add_c(j, carry):
        dkv_c[j] = (dkv_c[j].astype(F32) + dkv[j, c].astype(F32)).astype(BF)
        return carry

    lax.fori_loop(0, A * B, add_c, 0)
    x_kv = []
    for kb in range(B - 1):
        other = lax.rem(b + kb + 1, B)
        for j in range(A):
            x_kv.append(start(dkv_c.at[j * B + other], dkv_x.at[kb, j], slots(), device("b", kb + 1)))

    square_o.over_b()
    for copy in up_y:
        copy.wait()
    gather_up.begin()
    gather_down.from_a()
    square_q.over_f()

    for copy in x_kv:
        copy.wait()

    def add_x(j, carry):
        total = dkv_c[j * B + b].astype(F32)
        for kb in range(B - 1):
            total = total + dkv_x[kb, j].astype(F32)
        dkv_x[0, j] = total.astype(BF)
        return carry

    lax.fori_loop(0, A, add_x, 0)
    z_kv = slots(A - 1)
    for k in range(1, A):

        @pl.when(a - k >= 0)
        def _():
            to = (((a - k) * B + b) * 2 + c, f)
            remote(dkv_x.at[0, jnp.maximum(a - k, 0)], dkv_z.at[k - 1], z_kv + k - 1, to).start()

    square_o.over_a()
    square_q.over_b()
    gather_up.from_a()

    total = dkv_x[0, a].astype(F32)
    d_kv[...] = total
    for k in range(1, A):
        copy = remote(dkv_x.at[0, jnp.maximum(a - k, 0)], dkv_z.at[k - 1], z_kv + k - 1, device("a", A - k))

        @pl.when(a - k >= 0)
        def _():
            copy.wait_send()

        @pl.when(a + k < A)
        def _():
            copy.wait_recv()
            d_kv[...] = d_kv[...] + dkv_z[k - 1].astype(F32)

    d_kv_low = d_kv[...].astype(BF)

    n_cols = 256
    mean = jnp.zeros((tok, 1), F32)
    for i in range(D // n_cols):
        cols = slice(i * n_cols, (i + 1) * n_cols)
        part = nt(dq[...], wq_ref[cols, :]) + nt(d_kv_low, wkv_ref[cols, :])
        dn1[:, cols] = part
        weighted = part * (tok_ref[:, cols].astype(F32) * inv_ref[...])
        gain_rows[0:1, cols] = jnp.sum(weighted, axis=0, keepdims=True)
        mean = mean + jnp.sum(weighted * gain_ref[:, cols], axis=1, keepdims=True)
    if head is None:
        gain_rows[1:2, :] = gain2_ref[...]
    mean = mean * (1.0 / D)

    r_kv = own_rows // A
    rows_kv = r_kv + 16
    for fi in range(F):
        for i in range(A):
            at = fi * own_rows + i * r_kv
            part = tn(n1_ref[:, at : at + r_kv], d_kv_low).astype(BF)
            gkv_ref[0, fi, i, :r_kv, :] = part[:, :HS]
            gkv_ref[1, fi, i, :r_kv, :] = part[:, HS:]
            for ci in range(2):
                rows = [gain_rows[ci : ci + 1, fi * own_rows + k * 128 : fi * own_rows + (k + 1) * 128] for k in range(own_rows // 128)]
                block = jnp.concatenate(rows + [jnp.zeros((16 - len(rows), 128), F32)], axis=0)
                gkv_ref[ci, fi, i, r_kv:, :] = block.astype(BF)
    kv_c_copy = start(gkv_ref.at[1 - c], kv_c, slots(), device("c", 1))

    square_o.finish()
    for i in range(D // n_cols):
        cols = slice(i * n_cols, (i + 1) * n_cols)
        grad_tokens[:, cols] = dres_ref[:, cols] + inv_ref[...] * (
            dn1[:, cols] * gain_ref[:, cols] - tok_ref[:, cols].astype(F32) * inv_ref[...] * mean
        )
    square_q.over_a()
    kv_c_copy.wait()
    kv_c[...] = (kv_c[...].astype(F32) + gkv_ref[c].astype(F32)).astype(BF)
    kv_f = [start(kv_c.at[lax.rem(f + kf + 1, F)], kv_y.at[kf], slots(), device("f", kf + 1)) for kf in range(F - 1)]
    gather_down.from_b()
    gather_o.from_a()
    total = kv_c[f].astype(F32)
    for kf in range(F - 1):
        kv_f[kf].wait()
        total = total + kv_y[kf].astype(F32)
    kv_y[F - 1] = total.astype(BF)
    kv_b = [start(kv_y.at[F - 1], kv_x.at[kb], slots(), device("b", kb + 1)) for kb in range(B - 1)]
    square_q.finish()
    total = kv_y[F - 1].astype(F32)
    for kb in range(B - 1):
        kv_b[kb].wait()
        total = total + kv_x[kb].astype(F32)
    kv_x[B - 1] = total.astype(BF)
    kv_a = [start(kv_x.at[B - 1, lax.rem(a + ka + 1, A)], kv_z.at[ka], slots(), device("a", ka + 1)) for ka in range(A - 1)]
    gather_up.from_b()
    total = kv_x[B - 1, a].astype(F32)
    for ka in range(A - 1):
        kv_a[ka].wait()
        total = total + kv_z[ka].astype(F32)
    kv_s[...] = total.astype(BF)
    gather_kv.begin()
    gather_q.from_a()
    gather_o.from_b()
    gather_kv.from_a()
    gather_q.from_b()
    for gather in gathers:
        gather.end()
    if head is not None:
        finish_head()


def tail_shapes(dims, tok, D, shard, window, extra):
    A, B, F = dims
    own_rows = D // F
    half, r_d, r_u, w_u = D // 2, shard // (A * B), own_rows // B, shard // A
    w_o, r_kv = half // A, own_rows // A + 16

    def low(*shape):
        return pltpu.VMEM(shape, BF)

    square = [low(F, own_rows, half), low(F, own_rows, half), low(B, r_u, half), low(A - 1, r_u, w_o), low(r_u, w_o)]
    n_sems = extra + 2 * (A * (B - 1) + A - 1) + 4 * (A - 1 + (B - 1) * A + B * A) + (A - 1 + A)
    n_sems += 2 * (F + B + A) + F + (B - 1) * A + A + F + B + A + 8
    outs = (
        jax.ShapeDtypeStruct((2 * shard, D), BF),
        jax.ShapeDtypeStruct((F, own_rows, 2 * shard), BF),
        jax.ShapeDtypeStruct((own_rows, D), BF),
        jax.ShapeDtypeStruct((own_rows, D), BF),
        jax.ShapeDtypeStruct((2, A, r_kv, HS), BF),
        jax.ShapeDtypeStruct((tok, D), F32),
    )
    scratch = [
        pltpu.VMEM((H, HS, tok), F32),
        pltpu.VMEM((H, tok), F32),
        low(tok, D),
        low(A * B, 2, tok, 2 * HS),
        low(A * B, tok, 2 * HS),
        low(max(1, B - 1), A, tok, 2 * HS),
        low(max(1, A - 1), tok, 2 * HS),
        pltpu.VMEM((tok, 2 * HS), F32),
        pltpu.VMEM((tok, D), F32),
        low(F, own_rows, D),
        low(2, F, A, r_kv, HS),
        low(B - 1, A, r_d, D),
        low(B - 1, A, F, r_u, w_u),
        low(A - 1, r_d, D),
        low(A - 1, F, r_u, w_u),
        low(A - 1, r_d, D),
        low(A - 1, F, r_u, w_u),
        low(r_d, D),
        low(F, r_u, w_u),
        low(F, r_u, w_u),
        *square,
        *square,
        low(F, A, r_kv, HS),
        low(F, A, r_kv, HS),
        low(B, A, r_kv, HS),
        low(A - 1, r_kv, HS),
        low(r_kv, HS),
        pltpu.VMEM((8, D), F32),
        pltpu.SemaphoreType.DMA((n_sems,)),
        pltpu.SemaphoreType.DMA((n_sems,)),
        pltpu.SemaphoreType.DMA((5,)),
    ]
    return outs, scratch


def tail(dims, ends, queries, window_kv, d_attended, attended, lse, grad_down, grad_up, grad_out, n1, wq, wkv, tokens, inv, gain, dres, gain2):
    A, B, F = dims
    tok, D = n1.shape
    window = window_kv.shape[0]
    outs, scratch = tail_shapes(dims, tok, D, grad_down.shape[0], window, 0)
    hbm = pl.BlockSpec(memory_space=pltpu.HBM)
    return pl.pallas_call(
        functools.partial(tail_kernel, dims, None, TAIL_IN + TAIL_OUT + TAIL_SCRATCH),
        out_shape=outs,
        in_specs=[SMEM] + [VMEM] * 16,
        out_specs=(hbm,) * 5 + (VMEM,),
        scratch_shapes=scratch,
        compiler_params=pltpu.CompilerParams(vmem_limit_bytes=56 * 2**20, collective_id=1, has_side_effects=True),
        cost_estimate=pl.CostEstimate(flops=20 * tok * window * D, bytes_accessed=2**25, transcendentals=tok * window * H),
        name="tail",
    )(ends, queries, window_kv, d_attended, attended, lse, grad_down, grad_up, grad_out, n1, wq, wkv, tokens, inv, gain, dres, gain2)


HEAD_IN = (
    "ends",
    "tokens",
    "gains_in",
    "wk_in",
    "wv_in",
    "cot_in",
    "wq_in",
    "wo_in",
    "up_in",
    "down_in",
)
HEAD_SCRATCH = (
    "q_ref",
    "kv_ref",
    "d_ref",
    "att_ref",
    "lse_ref",
    "gd_ref",
    "gu_ref",
    "n1_ref",
    "wq_ref",
    "wkv_ref",
    "inv_ref",
    "gain_ref",
    "dres_ref",
    "gain2_ref",
    "wo_ref",
    "up_ref",
    "down_ref",
    "gains_all",
    "cot_all",
    "n2_all",
    "hid_all",
    "dp_all",
    "res_ref",
    "inv2_ref",
    "dbr_ref",
    "back_s",
    "back_c",
    "back_y",
    "back_r",
    "out_s",
    "out_c",
    "out_y",
    "out_r",
    "top",
    "total",
    "loc_sem",
)


def head(r, x):
    A, B, F, a, b, c, f, s = x.A, x.B, x.F, x.a, x.b, x.c, x.f, x.s
    slots, remote, device, lower = x.slots, x.remote, x.device, x.lower
    tok, D = r.tokens.shape
    own_rows = D // F
    shard = r.down_ref.shape[0]
    half = own_rows // 2
    sent = []

    def start(src, dst, to, slot=None):
        copy = remote(src, dst, slots() if slot is None else slot, to)
        copy.start()
        sent.append(copy)
        return copy

    def done(copies):
        for copy in copies:
            copy.wait_send()
            sent[:] = [other for other in sent if other is not copy]

    def span(at, n):
        return pl.ds(pl.multiple_of(at, n), n)

    sibling = device("c", 1)
    mine, mine_half = span(f * own_rows, own_rows), span(c * half, half)
    full_half = span((f * 2 + c) * half, half)

    def to_f(src, dst):
        return [start(src(kf), dst(kf), device("f", kf)) for kf in range(1, F)]

    gains_f = to_f(lambda kf: r.gains_in, lambda kf: r.gains_all.at[f])
    wk_f = to_f(lambda kf: r.wk_in.at[mine_half, :], lambda kf: r.wkv_ref.at[full_half, :HS])
    wv_f = to_f(lambda kf: r.wv_in.at[mine_half, :], lambda kf: r.wkv_ref.at[full_half, HS:])
    wq_f = to_f(lambda kf: r.wq_in.at[mine_half, :], lambda kf: r.wq_ref.at[full_half, :])
    wo_f = to_f(lambda kf: r.wo_in.at[mine_half, :], lambda kf: r.wo_ref.at[full_half, :])
    up_f = to_f(
        lambda kf: r.up_in.at[:, span((lax.rem(f + kf, F) * 2 + c) * shard, shard)], lambda kf: r.up_ref.at[mine, :]
    )
    cot_f = to_f(lambda kf: r.cot_in, lambda kf: r.cot_all.at[kf, :tok])
    cot_c = [start(r.cot_in, r.cot_all.at[0, tok:], sibling)]

    local = [
        pltpu.make_async_copy(src, dst, r.loc_sem.at[i])
        for i, (src, dst) in enumerate(
            (
                (r.wq_in, r.wq_ref.at[mine, :]),
                (r.wo_in, r.wo_ref.at[mine, :]),
                (r.up_in.at[:, span((f * 2 + c) * shard, shard)], r.up_ref.at[mine, :]),
                (r.cot_in, r.cot_all.at[0, :tok]),
                (r.down_in.at[span(c * shard, shard), :], r.down_ref),
            )
        )
    ]
    for copy in local:
        copy.start()

    def weight_halves(copies, ref, cols):
        passed = []
        for kf in range(1, F):
            copies[kf - 1].wait_recv()
            rows = span((lower("f", kf) * 2 + c) * half, half)
            passed.append(start(ref.at[rows, cols], ref.at[rows, cols], sibling))
        return passed

    n_rows = 64

    def unit_rows(i, carry):
        rows = span(i * n_rows, n_rows)
        stream = r.tokens[rows, :].astype(F32)
        inverse = lax.rsqrt(jnp.mean(stream * stream, axis=1, keepdims=True) + EPS)
        r.inv_ref[rows, :] = inverse
        return carry

    lax.fori_loop(0, tok // n_rows, unit_rows, 0)
    r.wkv_ref[mine, :HS] = r.wk_in[...]
    r.wkv_ref[mine, HS:] = r.wv_in[...]
    r.gains_all[f] = r.gains_in[...]
    for copy in gains_f:
        copy.wait_recv()
    for i in range(F):
        both = r.gains_all[i].astype(F32)
        cols = slice(i * own_rows, (i + 1) * own_rows)
        r.gain_ref[0:1, cols] = both[0:1, :]
        r.gain2_ref[0:1, cols] = both[1:2, :]

    def normed_rows(i, carry):
        rows = span(i * n_rows, n_rows)
        r.n1_ref[rows, :] = (r.tokens[rows, :].astype(F32) * r.inv_ref[rows, :] * r.gain_ref[...]).astype(BF)
        return carry

    lax.fori_loop(0, tok // n_rows, normed_rows, 0)

    wkv_c = weight_halves(wk_f, r.wkv_ref, slice(0, HS)) + weight_halves(wv_f, r.wkv_ref, slice(HS, 2 * HS))
    for copy in wkv_c:
        copy.wait_recv()
    kv = r.kv_ref

    def block(a_, b_, c_):
        return kv.at[span(((a_ * B + b_) * 2 + c_) * tok, tok), :]

    kv[span(s * tok, tok), :] = nn(r.n1_ref[...], r.wkv_ref[...]).astype(BF)
    kv_z, kv_x, kv_c = slots(A - 1), slots((B - 1) * A), slots(B * A)
    own = block(a, b, c)
    z_copies = [remote(own, own, kv_z + k - 1, device("a", k)) for k in range(1, A)]

    def guarded(k, ok, act):
        if k == 0:
            act()
        else:
            pl.when(ok)(act)

    for k in range(1, A):
        guarded(k, a + k < A, z_copies[k - 1].start)

    def x_copy(kb, k):
        here = block(jnp.maximum(a - k, 0), b, c)
        return remote(here, here, kv_x + (kb - 1) * A + k, device("b", kb))

    def c_copy(kb, k):
        here = block(jnp.maximum(a - k, 0), lower("b", kb) if kb else b, c)
        return remote(here, here, kv_c + kb * A + k, sibling)

    def pass_on(k):
        for kb in range(1, B):
            x_copy(kb, k).start()
        c_copy(0, k).start()

    pass_on(0)

    local[0].wait()
    wq_c = weight_halves(wq_f, r.wq_ref, slice(0, D))
    for copy in wq_c:
        copy.wait_recv()
    n_cols = 256

    def columns(n, act):
        def body(i, carry):
            act(span(i * n_cols, n_cols))
            return carry

        lax.fori_loop(0, n // n_cols, body, 0)

    def query_cols(cols):
        r.q_ref[:, cols] = nn(r.n1_ref[...], r.wq_ref[:, cols]).astype(BF)

    columns(D, query_cols)

    for k in range(1, A):

        def arrived(k=k):
            z_copies[k - 1].wait_recv()
            pass_on(k)

        guarded(k, a - k >= 0, arrived)

    factor = math.log2(math.e) / math.sqrt(HS)
    r.top[...] = jnp.full(r.top.shape, -3e38, F32)
    r.total[...] = jnp.zeros(r.total.shape, F32)
    r.acc[...] = jnp.zeros(r.acc.shape, F32)
    pos = s * tok + lax.broadcasted_iota(jnp.int32, (1, tok), 1)
    begin = jnp.zeros((1, tok), jnp.int32)
    for i in range(r.ends.shape[0]):
        begin = jnp.maximum(begin, jnp.where(r.ends[i] <= pos, r.ends[i], 0))

    def step(j, masked):
        rows = span(j * CHUNK, CHUNK)
        keys = kv[rows, :HS]
        values_t = kv[rows, HS:].T
        if masked:
            at = j * CHUNK + lax.broadcasted_iota(jnp.int32, (CHUNK, tok), 0)
            mask = jnp.logical_and(at >= begin, at <= pos)
        for h in range(H):
            scores = nt(keys, r.q_ref[:, h * HS : (h + 1) * HS])
            if masked:
                scores = jnp.where(mask, scores, NEG)
            old = r.top[h : h + 1, :]
            new = jnp.maximum(old, jnp.max(scores, axis=0, keepdims=True) * factor)
            shrink = jnp.exp2(old - new)
            probs = jnp.exp2(scores * factor - new)
            r.total[h : h + 1, :] = r.total[h : h + 1, :] * shrink + jnp.sum(probs, axis=0, keepdims=True)
            r.acc[h] = r.acc[h] * shrink + nn(values_t, probs.astype(BF))
            r.top[h : h + 1, :] = new

    last = s // 2
    c_copy(0, 0).wait_recv()
    step(last, True)
    for kb in range(1, B):
        for k in range(A):

            def arrived(kb=kb, k=k):
                x_copy(kb, k).wait_recv()
                c_copy(kb, k).start()

            guarded(k, a - k >= 0, arrived)
    for kb in range(B):
        for k in range(A):
            if kb or k:
                guarded(k, a - k >= 0, c_copy(kb, k).wait_recv)

    def attention_chunk(j, carry):
        plain = jnp.logical_and(j > 0, s < 2 * A * B - 1)

        @pl.when(plain)
        def _():
            step(j, False)

        @pl.when(jnp.logical_not(plain))
        def _():
            step(j, True)

        return carry

    lax.fori_loop(0, last, attention_chunk, 0)
    for h in range(H):
        mixed = r.acc[h] * (1.0 / r.total[h : h + 1, :])
        r.att_ref[:, h * HS : (h + 1) * HS] = mixed.T.astype(BF)
    r.lse_ref[...] = r.top[...] + jnp.log2(r.total[...])

    local[1].wait()
    wo_c = weight_halves(wo_f, r.wo_ref, slice(0, D))
    for copy in wo_c:
        copy.wait_recv()
    squares = jnp.zeros((tok, 1), F32)
    for i in range(D // n_cols):
        cols = slice(i * n_cols, (i + 1) * n_cols)
        part = r.tokens[:, cols].astype(F32) + nn(r.att_ref[...], r.wo_ref[:, cols])
        r.res_ref[:, cols] = part
        squares = squares + jnp.sum(part * part, axis=1, keepdims=True)
    r.inv2_ref[...] = lax.rsqrt(squares * (1.0 / D) + EPS)

    def second_norm(i, carry):
        rows = span(i * n_rows, n_rows)
        r.n2_all[0, rows, :] = (r.res_ref[rows, :] * r.inv2_ref[rows, :] * r.gain2_ref[...]).astype(BF)
        return carry

    lax.fori_loop(0, tok // n_rows, second_norm, 0)

    n2_f = to_f(lambda kf: r.n2_all.at[0, :tok], lambda kf: r.n2_all.at[kf, :tok])
    n2_c = [start(r.n2_all.at[0, :tok], r.n2_all.at[0, tok:], sibling)]
    local[2].wait()
    local[3].wait()
    local[4].wait()
    for copy in up_f:
        copy.wait_recv()
    for kf in range(1, F):
        cot_f[kf - 1].wait_recv()
        cot_c.append(start(r.cot_all.at[kf, :tok], r.cot_all.at[kf, tok:], sibling))

    def feed_forward(kf):
        def hidden_cols(cols):
            before = nn(r.n2_all[kf], r.up_ref[:, cols])
            d_hidden = nt(r.cot_all[kf], r.down_ref[cols, :])
            sig = 1.0 / (1.0 + jnp.exp(-before))
            r.hid_all[kf, :, cols] = (before * sig).astype(BF)
            r.dp_all[kf, :, cols] = (d_hidden * sig * (1.0 + before * (1.0 - sig))).astype(BF)

        columns(shard, hidden_cols)

        def back_cols(cols):
            r.back_s[kf, :, cols] = nt(r.dp_all[kf], r.up_ref[cols, :]).astype(BF)

        columns(D, back_cols)
        return start(r.back_s.at[kf, tok:], r.back_c.at[kf], sibling)

    def out_part(kf):
        def out_cols(cols):
            r.out_s[kf, :, cols] = nn(r.hid_all[kf], r.down_ref[:, cols]).astype(BF)

        columns(D, out_cols)
        return start(r.out_s.at[kf, tok:], r.out_c.at[kf], sibling)

    def chip_sum(kf, part, other, ref):
        def rows_sum(i, carry):
            rows = span(i * n_rows, n_rows)
            ref[kf - 1, rows, :] = (part[kf, rows, :].astype(F32) + other[kf, rows, :].astype(F32)).astype(BF)
            return carry

        lax.fori_loop(0, tok // n_rows, rows_sum, 0)

    back_copies, out_copies, back_back, out_back = [None] * F, [None] * F, [], []
    n2_c[0].wait_recv()
    cot_c[0].wait_recv()
    back_copies[0] = feed_forward(0)
    for kf in range(1, F):
        n2_f[kf - 1].wait_recv()
        n2_c.append(start(r.n2_all.at[kf, :tok], r.n2_all.at[kf, tok:], sibling))
    for kf in range(1, F):
        n2_c[kf].wait_recv()
        cot_c[kf].wait_recv()
        back_copies[kf] = feed_forward(kf)
        out_copies[kf] = out_part(kf)
        back_copies[kf].wait_recv()
        chip_sum(kf, r.back_s, r.back_c, r.back_y)
        back_back.append(start(r.back_y.at[kf - 1], r.back_r.at[kf - 1], device("f", F - kf)))

    n_out = 128

    def down_grad(i, carry):
        cols = span(i * n_out, n_out)
        r.gd_ref[cols, :] = sum(tn(r.hid_all[kf, :, cols], r.cot_all[kf]) for kf in range(F)).astype(BF)
        return carry

    lax.fori_loop(0, shard // n_out, down_grad, 0)
    x.send_down(0, 1)

    def up_grad(i, carry):
        cols = span(i * n_out, n_out)
        rows = span(lax.rem(i, own_rows // n_out) * n_out, n_out)
        grad = sum(tn(r.n2_all[kf, :, cols], r.dp_all[kf]) for kf in range(F))
        r.gu_ref[i // (own_rows // n_out), rows, :] = grad.astype(BF)
        return carry

    lax.fori_loop(0, D // n_out, up_grad, 0)
    x.send_up(0, 1)
    for i in range(1, A):
        x.send_down(i, i + 1)
        x.send_up(i, i + 1)
    for kf in range(1, F):
        out_copies[kf].wait_recv()
        chip_sum(kf, r.out_s, r.out_c, r.out_y)
        out_back.append(start(r.out_y.at[kf - 1], r.out_r.at[kf - 1], device("f", F - kf)))
    out_copies[0] = out_part(0)

    back_copies[0].wait_recv()
    for copy in back_back:
        copy.wait_recv()

    def norm_back(i, gain_grad):
        rows = span(i * n_rows, n_rows)
        d_normed = r.back_s[0, rows, :].astype(F32) + r.back_c[0, rows, :].astype(F32)
        for kf in range(1, F):
            d_normed = d_normed + r.back_r[kf - 1, rows, :].astype(F32)
        inverse = r.inv2_ref[rows, :]
        unit = r.res_ref[rows, :] * inverse
        weighted = d_normed * unit
        scaled = d_normed * r.gain2_ref[...]
        mean = jnp.mean(scaled * unit, axis=1, keepdims=True)
        d_residual = r.cot_all[0, rows, :].astype(F32) + inverse * (scaled - unit * mean)
        r.dres_ref[rows, :] = d_residual
        r.dbr_ref[rows, :] = d_residual.astype(BF)
        return gain_grad + jnp.sum(weighted, axis=0, keepdims=True)

    r.gain_rows[1:2, :] = lax.fori_loop(0, tok // n_rows, norm_back, jnp.zeros((1, D), F32))

    def attended_cols(cols):
        r.d_ref[:, cols] = nt(r.dbr_ref[...], r.wo_ref[cols, :]).astype(BF)

    columns(D, attended_cols)

    done(n2_f + n2_c)

    def out_grad(i, carry):
        cols = span(i * n_out, n_out)
        rows = span(lax.rem(i, own_rows // n_out) * n_out, n_out)
        r.go_ref[i // (own_rows // n_out), rows, :] = tn(r.att_ref[:, cols], r.dbr_ref[...]).astype(BF)
        return carry

    lax.fori_loop(0, D // n_out, out_grad, 0)

    def finish_output():
        out_copies[0].wait_recv()
        for copy in out_back:
            copy.wait_recv()

        def output_rows(i, carry):
            rows = span(i * n_rows, n_rows)
            value = r.res_ref[rows, :] + r.out_s[0, rows, :].astype(F32) + r.out_c[0, rows, :].astype(F32)
            for kf in range(1, F):
                value = value + r.out_r[kf - 1, rows, :].astype(F32)
            r.out_ref[rows, :] = value.astype(BF)
            return carry

        lax.fori_loop(0, tok // n_rows, output_rows, 0)
        done(out_copies)
        results[0].start()

    results = [
        pltpu.make_async_copy(src, dst, r.loc_sem.at[5 + i])
        for i, (src, dst) in enumerate(((r.out_ref, r.out_hbm), (r.grad_tokens, r.grad_hbm)))
    ]

    def finish():
        results[1].start()
        for copy in results:
            copy.wait()
        for copy in sent:
            copy.wait_send()
        for k in range(1, A):
            guarded(k, a + k < A, z_copies[k - 1].wait_send)
        for k in range(A):
            for kb in range(B):
                if kb:
                    guarded(k, a - k >= 0, x_copy(kb, k).wait_send)
                guarded(k, a - k >= 0, c_copy(kb, k).wait_send)

    return finish_output, finish


AGAIN = {
    "go_ref": "n2_all",
    "gq_ref": "out_s",
    "dn1": "res_ref",
    "grad_tokens": "res_ref",
    "dq": "d_ref",
    "out_ref": "dbr_ref",
    "tok_ref": "tokens",
}


def layer_shapes(dims, tok, D, shard, window):
    A, B, F = dims
    own_rows = D // F
    outs, scratch = tail_shapes(dims, tok, D, shard, window, 16 * F + A - 1 + (B - 1) * A + B * A)

    def low(*shape):
        return pltpu.VMEM(shape, BF)

    def wide(*shape):
        return pltpu.VMEM(shape, F32)

    pair = [low(F, 2 * tok, D), low(F, tok, D), low(F - 1, tok, D), low(F - 1, tok, D)]
    first = [
        low(tok, D),
        low(window, 2 * HS),
        low(tok, D),
        low(tok, D),
        wide(H, tok),
        low(shard, D),
        low(F, own_rows, shard),
        low(tok, D),
        low(D, D),
        low(D, 2 * HS),
        wide(tok, 1),
        wide(1, D),
        wide(tok, D),
        wide(1, D),
        low(D, D),
        low(D, shard),
        low(shard, D),
        low(F, 16, own_rows),
        low(F, 2 * tok, D),
        low(F, 2 * tok, D),
        low(F, 2 * tok, shard),
        low(F, 2 * tok, shard),
        wide(tok, D),
        wide(tok, 1),
        low(tok, D),
        *pair,
        *pair,
        wide(H, tok),
        wide(H, tok),
        pltpu.SemaphoreType.DMA((7,)),
    ]
    sizes = dict(zip(HEAD_SCRATCH + TAIL_SCRATCH, first + scratch))
    fits = all(sizes[k].shape == sizes[AGAIN[k]].shape for k in ("gq_ref", "dn1", "dq")) and own_rows == 2 * tok
    scratch = [ref for name, ref in zip(TAIL_SCRATCH, scratch) if name not in AGAIN]
    fits = fits and vmem_bytes(first + scratch) + 4 * 2**20 < LIMIT
    return outs + (jax.ShapeDtypeStruct((tok, D), BF),), first + scratch, fits


def vmem_bytes(scratch):
    total = 0
    for ref in scratch:
        shape = getattr(ref, "shape", ())
        if len(shape) >= 2:
            lanes = -(-shape[-1] // 128) * 128
            rows = -(-shape[-2] // 8) * 8
            total += math.prod(shape[:-2]) * rows * lanes * jnp.dtype(ref.dtype).itemsize
    return total


def layer(dims, ends, tokens, gains, w_key, w_value, cotangent, w_query, w_out, w_up, w_down, outs, scratch):
    tok, D = tokens.shape
    hbm = pl.BlockSpec(memory_space=pltpu.HBM)
    names = HEAD_IN + TAIL_OUT[:5] + ("grad_hbm", "out_hbm") + HEAD_SCRATCH + tuple(n for n in TAIL_SCRATCH if n not in AGAIN)
    return pl.pallas_call(
        functools.partial(tail_kernel, dims, head, names),
        out_shape=outs,
        in_specs=[SMEM] + [VMEM] * 4 + [hbm] * 5,
        out_specs=(hbm,) * 7,
        scratch_shapes=scratch,
        compiler_params=pltpu.CompilerParams(vmem_limit_bytes=LIMIT, collective_id=2, has_side_effects=True),
        cost_estimate=pl.CostEstimate(flops=2**35, bytes_accessed=2**25, transcendentals=2**24),
        name="layer",
    )(ends, tokens, gains, w_key, w_value, cotangent, w_query, w_out, w_up, w_down)


def after(value, *others):
    return lax.optimization_barrier((value, *others))[0]


class Grid:
    def __init__(self):
        seq = lax.axis_size("seq")
        self.F = lax.axis_size("fsdp")
        self.C = 2
        chips = seq // 2
        self.B = 2 if chips == 8 else chips // 2
        self.A = chips // self.B
        self.s = lax.axis_index("seq")
        self.f = lax.axis_index("fsdp")
        self.c = self.s % 2
        self.b = self.s // 2 % self.B
        self.a = self.s // (2 * self.B)

    def size(self, axis):
        return {"a": self.A, "b": self.B, "c": self.C, "f": self.F}[axis]

    def place(self, axis):
        return {"a": self.a, "b": self.b, "c": self.c, "f": self.f}[axis]

    def send(self, value, axis, step, upward=False):
        pairs = []
        for a in range(self.A):
            for b in range(self.B):
                for c in range(2):
                    for f in range(self.F):
                        at = {"a": a, "b": b, "c": c, "f": f}
                        to = dict(at)
                        to[axis] += step
                        if upward and not 0 <= to[axis] < self.size(axis):
                            continue
                        to[axis] %= self.size(axis)
                        line = [((d["a"] * self.B + d["b"]) * 2 + d["c"]) * self.F + d["f"] for d in (at, to)]
                        pairs.append(tuple(line))
        return lax.ppermute(value, ("seq", "fsdp"), pairs)

    def stack(self, parts, axis):
        n, me = len(parts), self.place(axis)
        if n == 2:
            low = me == 0
            return jnp.stack([jnp.where(low, parts[0], parts[1]), jnp.where(low, parts[1], parts[0])])
        twice = jnp.stack(parts + parts)
        return lax.dynamic_slice_in_dim(twice, (n - me) % n, n, 0)

    def gather(self, value, axis):
        n = self.size(axis)
        return self.stack([value] + [self.send(value, axis, -k) for k in range(1, n)], axis)

    def scatter(self, parts, axis):
        n, me = self.size(axis), self.place(axis)

        def pick(k):
            return lax.dynamic_index_in_dim(parts, (me + k) % n, 0, keepdims=False)

        got = [self.send(pick(k).astype(BF), axis, k) for k in range(1, n)]
        total = pick(0).astype(F32)
        for piece in got:
            total = total + piece.astype(F32)
        return total

    def plane_sum(self, parts):
        half = self.scatter(parts, "b").astype(BF)
        return self.scatter(half, "a")

    def plane_gather(self, share):
        rows = self.gather(share.astype(BF), "a")
        return self.gather(rows, "b")


def local(
    tokens,
    cotangent,
    seq_lengths,
    group_of_shard,
    gain_attn,
    w_query,
    w_key,
    w_value,
    w_out,
    gain_ffn,
    w_up,
    w_down,
):
    g = Grid()
    A, B, C, F = g.A, g.B, g.C, g.F
    tok, D = tokens.shape[1:]
    FF = w_up.shape[1]
    own_rows = D // F
    seq_parts = A * B * C
    shard = FF // (2 * F)

    group = lax.dynamic_index_in_dim(group_of_shard, g.f, 0, keepdims=False)
    lengths = lax.dynamic_index_in_dim(seq_lengths, group, 0, keepdims=False)
    running, ends = jnp.int32(0), []
    for i in range(seq_lengths.shape[1]):
        running = running + lengths[i]
        ends.append(running)
    scal = jnp.stack([g.s.astype(jnp.int32), *ends])

    outs, scratch, fits = layer_shapes((A, B, F), tok, D, shard, seq_parts * tok)
    if fits:
        gains = jnp.pad(jnp.stack([gain_attn, gain_ffn]), ((0, 14), (0, 0)))
        *grads, grad_tokens, output = layer(
            (A, B, F), scal[1:], tokens[0], gains, w_key, w_value, cotangent[0], w_query, w_out, w_up, w_down, outs, scratch
        )
        return results(output, grad_tokens, *grads)

    gains = jnp.stack([gain_attn, gain_ffn])
    full_gains = g.gather(gains, "f").transpose(1, 0, 2).reshape(2, D).astype(F32)
    gain_first, gain_second = full_gains[0], full_gains[1]
    own_kv = jnp.concatenate([w_key, w_value], axis=1)
    full_kv = g.gather(own_kv, "f").reshape(D, 2 * HS)

    def gather_weight(weight, *late):
        half = own_rows // 2
        mine = lax.dynamic_slice_in_dim(weight, g.c * half, half, 0)
        if late:
            mine = after(mine, *late)
        pieces = [g.gather(g.send(mine, "f", -k), "c").reshape(weight.shape) for k in range(1, F)]
        return g.stack([weight] + pieces, "f").reshape(F * own_rows, -1)

    full_query = gather_weight(w_query)

    stream = tokens[0].astype(F32)
    inverse_first = lax.rsqrt(jnp.mean(stream * stream, axis=1, keepdims=True) + EPS)
    unit_first = stream * inverse_first
    normed_first = (unit_first * gain_first).astype(BF)
    key_value = nn(normed_first, full_kv).astype(BF)
    queries = nn(normed_first, full_query).astype(BF)

    column = [key_value] + [g.send(key_value, "a", k, upward=True) for k in range(1, A)]
    twice = jnp.stack(column[::-1] + column[::-1])
    column = lax.dynamic_slice_in_dim(twice, A - 1 - g.a, A, 0)
    plane = g.gather(column, "b")
    whole = g.gather(plane, "c")
    window_kv = whole.transpose(2, 1, 0, 3, 4).reshape(seq_parts * tok, 2 * HS)

    full_out = gather_weight(w_out, full_query)
    upstream = cotangent[0]
    cot = []
    for k in range(F):
        mine = upstream if k == 0 else g.send(after(upstream, full_query), "f", k)
        cot.append(jnp.concatenate([mine, g.send(mine, "c", 1)], axis=0))
    ups = w_up.reshape(own_rows, F, 2, shard)
    up_parts = []
    for k in range(F):
        block = lax.dynamic_slice(ups, (0, (g.f + k) % F, g.c, 0), (own_rows, 1, 1, shard)).reshape(own_rows, shard)
        up_parts.append(block if k == 0 else g.send(after(block, full_out), "f", k))
    up_parts = [up_parts[0]] + up_parts[1:][::-1]
    up = g.stack(up_parts, "f").reshape(D, shard)
    down = lax.dynamic_slice_in_dim(w_down, g.c * shard, shard, 0)

    attended, lse = attend(scal, queries, window_kv)

    residual = stream + nn(attended, full_out)
    inverse_second = lax.rsqrt(jnp.mean(residual * residual, axis=1, keepdims=True) + EPS)
    unit_second = residual * inverse_second
    normed_second = (unit_second * gain_second).astype(BF)

    out_sum, back_sum = residual, jnp.zeros((tok, D), F32)
    hiddens, d_pres, norms = [], [], []
    backs, outs = [], []
    for k in range(F):
        mine = normed_second if k == 0 else g.send(normed_second, "f", k)
        norm = jnp.concatenate([mine, g.send(mine, "c", 1)], axis=0)
        before = nn(norm, up)
        d_hidden = nt(cot[k], down)
        sig = jax.nn.sigmoid(before)
        hidden = (before * sig).astype(BF)
        d_pre = (d_hidden * sig * (1.0 + before * (1.0 - sig))).astype(BF)
        back = nt(d_pre, up)
        out = nn(hidden, down)
        hiddens.append(hidden)
        d_pres.append(d_pre)
        norms.append(norm)
        backs.append(back)
        outs.append(out)

    def give_back(parts):
        total = 0.0
        for k, part in enumerate(parts):
            other = g.send(part[tok:].astype(BF), "c", 1)
            chip = part[:tok] + other.astype(F32)
            if k:
                chip = g.send(chip.astype(BF), "f", -k).astype(F32)
            total = total + chip
        return total

    d_normed_second = give_back(backs)
    output = (residual + give_back(outs)).astype(BF)

    grad_down = sum(tn(h, c) for h, c in zip(hiddens, cot)).astype(BF)
    grad_up = sum(tn(n, d) for n, d in zip(norms, d_pres)).astype(BF)

    def norm_back(gradient, unit_rows, inverse, gain_vec):
        scaled = gradient * gain_vec
        gain_grad = jnp.sum(gradient * unit_rows, axis=0)
        return gain_grad, inverse * (scaled - unit_rows * jnp.mean(scaled * unit_rows, axis=1, keepdims=True))

    gain_second_grad, d_from_norm = norm_back(d_normed_second, unit_second, inverse_second, gain_second)
    d_residual = upstream.astype(F32) + d_from_norm
    d_branch = d_residual.astype(BF)
    d_attended = nt(d_branch, full_out).astype(BF)
    grad_out = tn(attended, d_branch).astype(BF)

    down_all, up_all, out_all, query_all, kv_all, grad_tokens = tail(
        (A, B, F),
        scal[1:],
        queries,
        window_kv,
        d_attended,
        attended,
        lse,
        grad_down,
        grad_up.reshape(F, own_rows, shard),
        grad_out.reshape(F, own_rows, D),
        normed_first,
        full_query,
        full_kv,
        tokens[0],
        inverse_first,
        gain_first[None],
        d_residual,
        gain_second_grad[None],
    )
    return results(output, grad_tokens, down_all, up_all, out_all, query_all, kv_all)


def results(output, grad_tokens, down_all, up_all, out_all, query_all, kv_all):
    F, own_rows = up_all.shape[:2]
    grad_w_up = jnp.concatenate([up_all[i].astype(F32) for i in range(F)], axis=1)
    r_kv = own_rows // kv_all.shape[1]
    grad_kv = kv_all[:, :, :r_kv].astype(F32).reshape(2, own_rows, HS)
    gain_grads = kv_all[:, 0, r_kv : r_kv + own_rows // 128].astype(F32).reshape(2, own_rows)
    return (
        output[None],
        grad_tokens[None],
        gain_grads[0],
        query_all.astype(F32),
        grad_kv[0],
        grad_kv[1],
        out_all.astype(F32),
        gain_grads[1],
        grad_w_up,
        down_all.astype(F32),
    )


def solution(mesh):
    placed = (
        P("fsdp", "seq", None),
        P("fsdp", "seq", None),
        P(),
        P(),
        P("fsdp"),
        P("fsdp", None),
        P("fsdp", None),
        P("fsdp", None),
        P("fsdp", None),
        P("fsdp"),
        P("fsdp", None),
        P("fsdp", None),
    )
    return jax.shard_map(
        local,
        mesh=mesh,
        in_specs=placed,
        out_specs=(
            P("fsdp", "seq", None),
            P("fsdp", "seq", None),
            P("fsdp"),
            P("fsdp", None),
            P("fsdp", None),
            P("fsdp", None),
            P("fsdp", None),
            P("fsdp"),
            P("fsdp", None),
            P("fsdp", None),
        ),
        check_vma=False,
    )
```

```python
import functools
import math
import types

import jax
import jax.numpy as jnp
from jax import lax
from jax.experimental import pallas as pl
from jax.experimental.pallas import tpu as pltpu
from jax.sharding import PartitionSpec as P

H = 8
HS = 128
EPS = 1e-05
NEG = -1e30
LIMIT = 60 * 2**20
CHUNK = 512
BF = jnp.bfloat16
F32 = jnp.float32


def nt(a, b):
    return lax.dot_general(a, b, (((1,), (1,)), ((), ())), preferred_element_type=F32)


def nn(a, b):
    return lax.dot_general(a, b, (((1,), (0,)), ((), ())), preferred_element_type=F32)


def tn(a, b):
    return lax.dot_general(a, b, (((0,), (0,)), ((), ())), preferred_element_type=F32)


def query_range(scal, tok):
    first = scal[0] * tok
    pos = first + lax.broadcasted_iota(jnp.int32, (1, tok), 1)
    start = jnp.zeros((1, tok), jnp.int32)
    latest = jnp.int32(0)
    for i in range(1, scal.shape[0]):
        end = scal[i]
        start = jnp.maximum(start, jnp.where(end <= pos, end, 0))
        latest = jnp.maximum(latest, jnp.where(end <= first + tok - 1, end, 0))
    return first, pos, start, latest


def chunk_loop(scal, tok, window, step):
    first, pos, start, latest = query_range(scal, tok)
    chunks = (first + tok + CHUNK - 1) // CHUNK

    def body(j, carry):
        low = j * CHUNK
        whole = jnp.logical_and(low >= latest, low + CHUNK - 1 <= first)

        @pl.when(whole)
        def _():
            step(j, None)

        @pl.when(jnp.logical_not(whole))
        def _():
            keys = low + lax.broadcasted_iota(jnp.int32, (CHUNK, tok), 0)
            step(j, jnp.logical_and(keys >= start, keys <= pos))

        return carry

    lax.fori_loop(0, chunks, body, 0)
    return chunks


def attend_kernel(scal, q_ref, kv_ref, out_ref, lse_ref, acc, top, total):
    tok = q_ref.shape[0]
    factor = math.log2(math.e) / math.sqrt(HS)
    top[...] = jnp.full(top.shape, -3e38, F32)
    total[...] = jnp.zeros(total.shape, F32)
    acc[...] = jnp.zeros(acc.shape, F32)

    def step(j, mask):
        rows = pl.ds(pl.multiple_of(j * CHUNK, CHUNK), CHUNK)
        keys = kv_ref[rows, :HS]
        values_t = kv_ref[rows, HS:].T
        for h in range(H):
            scores = nt(keys, q_ref[:, h * HS : (h + 1) * HS])
            if mask is not None:
                scores = jnp.where(mask, scores, NEG)
            old = top[h : h + 1, :]
            new = jnp.maximum(old, jnp.max(scores, axis=0, keepdims=True) * factor)
            shrink = jnp.exp2(old - new)
            probs = jnp.exp2(scores * factor - new)
            total[h : h + 1, :] = total[h : h + 1, :] * shrink + jnp.sum(probs, axis=0, keepdims=True)
            acc[h] = acc[h] * shrink + nn(values_t, probs.astype(BF))
            top[h : h + 1, :] = new

    chunk_loop(scal, tok, kv_ref.shape[0], step)
    for h in range(H):
        mixed = acc[h] * (1.0 / total[h : h + 1, :])
        out_ref[:, h * HS : (h + 1) * HS] = mixed.T.astype(BF)
    lse_ref[...] = top[...] + jnp.log2(total[...])


VMEM = pl.BlockSpec(memory_space=pltpu.VMEM)
SMEM = pl.BlockSpec(memory_space=pltpu.SMEM)
PARAMS = pltpu.CompilerParams(vmem_limit_bytes=40 * 2**20)


def attend(scal, queries, window_kv):
    tok = queries.shape[0]
    window = window_kv.shape[0]
    return pl.pallas_call(
        attend_kernel,
        out_shape=(
            jax.ShapeDtypeStruct((tok, H * HS), BF),
            jax.ShapeDtypeStruct((H, tok), F32),
        ),
        in_specs=[SMEM, VMEM, VMEM],
        out_specs=(VMEM, VMEM),
        scratch_shapes=[
            pltpu.VMEM((H, HS, tok), F32),
            pltpu.VMEM((H, tok), F32),
            pltpu.VMEM((H, tok), F32),
        ],
        compiler_params=PARAMS,
        cost_estimate=pl.CostEstimate(
            flops=8 * tok * window * H * HS, bytes_accessed=4 * window * HS, transcendentals=tok * window * H
        ),
        name="attend",
    )(scal, queries, window_kv)


MESH = pl.DeviceIdType.MESH


TAIL_IN = (
    "ends",
    "q_ref",
    "kv_ref",
    "d_ref",
    "att_ref",
    "lse_ref",
    "gd_ref",
    "gu_ref",
    "go_ref",
    "n1_ref",
    "wq_ref",
    "wkv_ref",
    "tok_ref",
    "inv_ref",
    "gain_ref",
    "dres_ref",
    "gain2_ref",
)
TAIL_OUT = (
    "out_down",
    "out_up",
    "out_o",
    "out_q",
    "out_kv",
    "grad_tokens",
)
TAIL_SCRATCH = (
    "acc",
    "delta",
    "dq",
    "dkv",
    "dkv_c",
    "dkv_x",
    "dkv_z",
    "d_kv",
    "dn1",
    "gq_ref",
    "gkv_ref",
    "xr_d",
    "xr_u",
    "zs_d",
    "zs_u",
    "zr_d",
    "zr_u",
    "sh_d",
    "sh_u",
    "yr_u",
    "o_c",
    "o_y",
    "o_x",
    "o_z",
    "o_s",
    "q_c",
    "q_y",
    "q_x",
    "q_z",
    "q_s",
    "kv_c",
    "kv_y",
    "kv_x",
    "kv_z",
    "kv_s",
    "gain_rows",
    "send_sem",
    "recv_sem",
    "copy_sem",
)


def head_block(h, tok):
    return slice(h % 2 * HS, (h % 2 + 1) * HS), slice(h // 2 * tok, (h // 2 + 1) * tok)


def tail_kernel(dims, head, names, *refs):
    A, B, F = dims
    r = types.SimpleNamespace(**dict(zip(names, refs, strict=True)))
    if head is not None:
        for name, held in AGAIN.items():
            setattr(r, name, getattr(r, held))
    ends = r.ends
    q_ref = r.q_ref
    kv_ref = r.kv_ref
    d_ref = r.d_ref
    att_ref = r.att_ref
    lse_ref = r.lse_ref
    gd_ref = r.gd_ref
    gu_ref = r.gu_ref
    go_ref = r.go_ref
    n1_ref = r.n1_ref
    wq_ref = r.wq_ref
    wkv_ref = r.wkv_ref
    tok_ref = r.tok_ref
    inv_ref = r.inv_ref
    gain_ref = r.gain_ref
    dres_ref = r.dres_ref
    gain2_ref = r.gain2_ref
    out_down = r.out_down
    out_up = r.out_up
    out_o = r.out_o
    out_q = r.out_q
    out_kv = r.out_kv
    grad_tokens = r.grad_tokens
    acc = r.acc
    delta = r.delta
    dq = r.dq
    dkv = r.dkv
    dkv_c = r.dkv_c
    dkv_x = r.dkv_x
    dkv_z = r.dkv_z
    d_kv = r.d_kv
    dn1 = r.dn1
    gq_ref = r.gq_ref
    gkv_ref = r.gkv_ref
    xr_d = r.xr_d
    xr_u = r.xr_u
    zs_d = r.zs_d
    zs_u = r.zs_u
    zr_d = r.zr_d
    zr_u = r.zr_u
    sh_d = r.sh_d
    sh_u = r.sh_u
    yr_u = r.yr_u
    o_c = r.o_c
    o_y = r.o_y
    o_x = r.o_x
    o_z = r.o_z
    o_s = r.o_s
    q_c = r.q_c
    q_y = r.q_y
    q_x = r.q_x
    q_z = r.q_z
    q_s = r.q_s
    kv_c = r.kv_c
    kv_y = r.kv_y
    kv_x = r.kv_x
    kv_z = r.kv_z
    kv_s = r.kv_s
    gain_rows = r.gain_rows
    send_sem = r.send_sem
    recv_sem = r.recv_sem
    copy_sem = r.copy_sem
    tok = q_ref.shape[0]
    window = kv_ref.shape[0]
    D = n1_ref.shape[1]
    own_rows = D // F
    shard = gd_ref.shape[0]
    s = lax.axis_index("seq")
    f = lax.axis_index("fsdp")
    c = lax.rem(s, 2)
    b = lax.rem(s // 2, B)
    a = s // (2 * B)

    def device(axis, step):
        at = {"a": a, "b": b, "c": c, "f": f}
        at[axis] = lax.rem(at[axis] + step, {"a": A, "b": B, "c": 2, "f": F}[axis])
        return ((at["a"] * B + at["b"]) * 2 + at["c"], at["f"])

    def lower(axis, step):
        return lax.rem({"a": a + A, "b": b + B, "f": f + F}[axis] - step, {"a": A, "b": B, "f": F}[axis])

    def flip(axis_bit, place=None):
        place = a if place is None else place
        return place + axis_bit - 2 * axis_bit * lax.rem(place // axis_bit, 2) if axis_bit else place

    def offset(o):
        place = a
        for bit in bits:
            if o // bit % 2:
                place = flip(bit, place)
        return place

    def along_a(bit):
        return ((flip(bit) * B + b) * 2 + c, f)

    bits = [2**i for i in range(A.bit_length() - 1)]
    assert 2 ** len(bits) == A
    order = [o for bit in bits for o in range(A) if o // bit % 2 and o % bit == 0] + [0]

    def low_bit(o):
        return next((bit for bit in bits if o // bit % 2), A)

    used = [0]

    def slots(n=1):
        used[0] += n
        assert used[0] <= send_sem.shape[0]
        return used[0] - n

    def remote(src, dst, slot, to):
        return pltpu.make_async_remote_copy(
            src_ref=src, dst_ref=dst, send_sem=send_sem.at[slot], recv_sem=recv_sem.at[slot], device_id=to, device_id_type=MESH
        )

    pending = []

    def start(src, dst, slot, to):
        copy = remote(src, dst, slot, to)
        copy.start()
        pending.append(copy)
        return copy

    barrier = pltpu.get_barrier_semaphore()
    partners = [("a", k) for k in range(1, A)] + [("b", k) for k in range(1, B)] + [("c", 1)] + [("f", k) for k in range(1, F)]
    for axis, k in partners:
        pl.semaphore_signal(barrier, inc=1, device_id=device(axis, k), device_id_type=MESH)
    pl.semaphore_wait(barrier, len(partners))

    r_d = shard // (A * B)
    r_u = own_rows // B
    w_u = shard // A
    x_d = slots(A * (B - 1))
    x_u = slots(A * (B - 1))
    z_d = slots(A - 1)
    z_u = slots(A - 1)

    def down_copies(i):
        at = offset(order[i])
        copies = []
        for kb in range(B - 1):
            other = lax.rem(b + kb + 1, B)
            rows = pl.ds(pl.multiple_of((other * A + at) * r_d, r_d), r_d)
            copies.append(remote(gd_ref.at[rows, :], xr_d.at[kb, i], x_d + kb * A + i, device("b", kb + 1)))
        return copies

    def up_copies(i):
        at = offset(order[i])
        copies = []
        for kb in range(B - 1):
            rows = pl.ds(pl.multiple_of(lax.rem(b + kb + 1, B) * r_u, r_u), r_u)
            cols = pl.ds(pl.multiple_of(at * w_u, w_u), w_u)
            copies.append(remote(gu_ref.at[:, rows, cols], xr_u.at[kb, i], x_u + kb * A + i, device("b", kb + 1)))
        return copies

    def send_down(first, last):
        for i in range(first, last):
            for copy in down_copies(i):
                copy.start()

    def send_up(first, last):
        for i in range(first, last):
            for copy in up_copies(i):
                copy.start()

    def down_sum(i):
        for copy in down_copies(i):
            copy.wait()
        at = offset(order[i])
        rows = pl.ds(pl.multiple_of((b * A + at) * r_d, r_d), r_d)
        total = gd_ref[rows, :].astype(F32)
        for kb in range(B - 1):
            total = total + xr_d[kb, i].astype(F32)
        return total

    def up_sum(i):
        for copy in up_copies(i):
            copy.wait()
        at = offset(order[i])
        rows = pl.ds(pl.multiple_of(b * r_u, r_u), r_u)
        cols = pl.ds(pl.multiple_of(at * w_u, w_u), w_u)
        total = gu_ref[:, rows, cols].astype(F32)
        for kb in range(B - 1):
            total = total + xr_u[kb, i].astype(F32)
        return total

    def z_index(o, bit):
        return order.index(o + bit)

    def down_z(i):
        return remote(zs_d.at[i], zr_d.at[i], z_d + i, along_a(low_bit(order[i])))

    def up_z(i):
        return remote(zs_u.at[i], zr_u.at[i], z_u + i, along_a(low_bit(order[i])))

    def z_added(i, total, copy, got):
        o = order[i]
        for bit in bits:
            if bit < low_bit(o):
                k = z_index(o, bit)
                copy(k).wait()
                total = total + got[k].astype(F32)
        return total

    def down_step(i):
        zs_d[i] = z_added(i, down_sum(i), down_z, zr_d).astype(BF)
        down_z(i).start()

    def up_step(i):
        zs_u[i] = z_added(i, up_sum(i), up_z, zr_u).astype(BF)
        up_z(i).start()

    def down_share():
        sh_d[...] = z_added(A - 1, down_sum(A - 1), down_z, zr_d).astype(BF)
        gather_down.begin()

    up_y = slots(F - 1)

    def up_y_copy(kf):
        return remote(yr_u.at[lax.rem(f + kf + 1, F)], sh_u.at[f], up_y + kf, device("f", kf + 1))

    def up_share():
        total = z_added(A - 1, up_sum(A - 1), up_z, zr_u)
        yr_u[...] = total.astype(BF)
        for kf in range(F - 1):
            up_y_copy(kf).start()
        sh_u[f] = yr_u[f]

    def up_gather():
        for kf in range(F - 1):
            up_y_copy(kf).wait()
        gather_up.begin()

    gathers = []

    class Gather:
        def __init__(self, share, view, planes=True):
            self.share, self.view, self.n = share, view, B if planes else 1
            self.z_slot = slots(A)
            self.x_slot = slots((self.n - 1) * A)
            self.c_slot = slots(self.n * A)
            self.place = len(gathers)
            gathers.append(self)

        def local(self):
            return pltpu.make_async_copy(self.share, self.view(c, b, a), copy_sem.at[self.place])

        def at(self, o, kb=0):
            return self.view(c, lower("b", kb) if kb else b, offset(o))

        def z(self, bit, o):
            here = self.at(o)
            return remote(here if o else self.share, here, self.z_slot + A - A // bit + o // (2 * bit), along_a(bit))

        def x(self, kb, o):
            here = self.at(o)
            return remote(here if o else self.share, here, self.x_slot + kb * A + o, device("b", kb + 1))

        def c(self, kb, o):
            here = self.at(o, kb)
            return remote(here if kb or o else self.share, here, self.c_slot + kb * A + o, device("c", 1))

        def begin(self):
            self.local().start()
            for bit in bits[::-1]:
                self.z(bit, 0).start()
            self.pass_on(0)

        def pass_on(self, o):
            for kb in range(self.n - 1):
                self.x(kb, o).start()
            self.c(0, o).start()

        def from_a(self, stages=None):
            for i, bit in enumerate(bits[::-1]):
                if stages is not None and i not in stages:
                    continue
                for o in range(0, A, 2 * bit):
                    self.z(bit, o).wait_recv()
                    for lower_bit in bits[: len(bits) - 1 - i][::-1]:
                        self.z(lower_bit, o + bit).start()
                    self.pass_on(o + bit)

        def from_b(self):
            for kb in range(self.n - 1):
                for o in self.offsets():
                    self.x(kb, o).wait_recv()
                    self.c(kb + 1, o).start()

        def offsets(self):
            found = [0]
            for bit in bits[::-1]:
                found += [o + bit for o in found]
            return found

        def end(self):
            self.local().wait()
            for bit in bits:
                for o in range(0, A, 2 * bit):
                    self.z(bit, o).wait_send()
            for o in range(A):
                for kb in range(self.n - 1):
                    self.x(kb, o).wait_send()
                for kb in range(self.n):
                    self.c(kb, o).wait()

    def view_down(c_, b_, a_):
        return out_down.at[pl.ds(pl.multiple_of(((c_ * B + b_) * A + a_) * r_d, r_d), r_d), :]

    def view_up(c_, b_, a_):
        rows = pl.ds(pl.multiple_of(b_ * r_u, r_u), r_u)
        return out_up.at[:, rows, pl.ds(pl.multiple_of(c_ * shard + a_ * w_u, w_u), w_u)]

    half = D // 2
    w_o = half // A

    def view_square(out):
        def view(c_, b_, a_):
            rows = pl.ds(pl.multiple_of(b_ * r_u, r_u), r_u)
            return out.at[rows, pl.ds(pl.multiple_of(c_ * half + a_ * w_o, w_o), w_o)]

        return view

    gather_down = Gather(sh_d, view_down)
    gather_up = Gather(sh_u, view_up)
    gather_o = Gather(o_s, view_square(out_o))
    gather_q = Gather(q_s, view_square(out_q))
    gather_kv = Gather(kv_s, lambda c_, b_, a_: out_kv.at[c_, a_], planes=False)

    if head is None:
        send_down(0, A)
        send_up(0, A)
    else:
        own = types.SimpleNamespace(
            A=A, B=B, F=F, a=a, b=b, c=c, f=f, s=s, slots=slots, remote=remote, device=device, lower=lower,
            send_down=send_down, send_up=send_up, down_step=down_step,
        )
        finish_output, finish_head = head(r, own)

    def reduce_y(ref, got, sent, width):
        mine = pl.ds(pl.multiple_of(c * width, width), width)

        def add(i, carry):
            sent[i] = (ref[i, :, mine].astype(F32) + got[i].astype(F32)).astype(BF)
            return carry

        lax.fori_loop(0, F, add, 0)

    class Square:
        def __init__(self, grad, got_c, got_y, got_x, got_z, share, gather):
            self.grad, self.got_c, self.got_y, self.got_x, self.got_z = grad, got_c, got_y, got_x, got_z
            self.share, self.gather = share, gather
            self.c_slot, self.y_slot, self.x_slot = slots(), slots(F - 1), slots(B - 1)

        def c(self):
            other = pl.ds(pl.multiple_of((1 - c) * half, half), half)
            return remote(self.grad.at[:, :, other], self.got_c, self.c_slot, device("c", 1))

        def y(self, kf):
            return remote(self.got_c.at[lax.rem(f + kf + 1, F)], self.got_y.at[kf], self.y_slot + kf, device("f", kf + 1))

        def over_c(self):
            self.c().start()

        def over_f(self):
            self.c().wait()
            reduce_y(self.grad, self.got_c, self.got_c, half)
            for kf in range(F - 1):
                self.y(kf).start()

        def over_b(self):
            total = self.got_c[f].astype(F32)
            for kf in range(F - 1):
                self.y(kf).wait()
                total = total + self.got_y[kf].astype(F32)
            self.got_y[F - 1] = total.astype(BF)
            for kb in range(B - 1):
                self.x(kb).start()

        def x(self, kb):
            rows = pl.ds(pl.multiple_of(lax.rem(b + kb + 1, B) * r_u, r_u), r_u)
            return remote(self.got_y.at[F - 1, rows, :], self.got_x.at[kb], self.x_slot + kb, device("b", kb + 1))

        def over_a(self):
            rows = pl.ds(pl.multiple_of(b * r_u, r_u), r_u)
            total = self.got_y[F - 1, rows, :].astype(F32)
            for kb in range(B - 1):
                self.x(kb).wait()
                total = total + self.got_x[kb].astype(F32)
            self.got_x[B - 1] = total.astype(BF)
            self.copies = []
            for ka in range(A - 1):
                cols = pl.ds(pl.multiple_of(lax.rem(a + ka + 1, A) * w_o, w_o), w_o)
                self.copies.append(start(self.got_x.at[B - 1, :, cols], self.got_z.at[ka], slots(), device("a", ka + 1)))

        def finish(self):
            cols = pl.ds(pl.multiple_of(a * w_o, w_o), w_o)
            total = self.got_x[B - 1, :, cols].astype(F32)
            for ka in range(A - 1):
                self.copies[ka].wait()
                total = total + self.got_z[ka].astype(F32)
            self.share[...] = total.astype(BF)
            self.gather.begin()

    square_o = Square(go_ref, o_c, o_y, o_x, o_z, o_s, gather_o)
    square_q = Square(gq_ref, q_c, q_y, q_x, q_z, q_s, gather_q)

    square_o.over_c()

    scale = 1.0 / math.sqrt(HS)
    factor = math.log2(math.e) * scale
    acc[...] = jnp.zeros(acc.shape, F32)
    for h in range(H):
        cols = slice(h * HS, (h + 1) * HS)
        both = d_ref[:, cols].astype(F32) * att_ref[:, cols].astype(F32)
        delta[h : h + 1, :] = jnp.sum(both.T, axis=0, keepdims=True)
    first = s * tok
    pos = first + lax.broadcasted_iota(jnp.int32, (1, tok), 1)
    begin = jnp.zeros((1, tok), jnp.int32)
    for i in range(ends.shape[0]):
        begin = jnp.maximum(begin, jnp.where(ends[i] <= pos, ends[i], 0))

    def step(j, masked):
        rows = pl.ds(pl.multiple_of(j * CHUNK, CHUNK), CHUNK)
        keys = kv_ref[rows, :HS]
        values = kv_ref[rows, HS:]
        keys_t = keys.T
        if masked:
            at = j * CHUNK + lax.broadcasted_iota(jnp.int32, (CHUNK, tok), 0)
            mask = jnp.logical_and(at >= begin, at <= pos)
        d_keys = jnp.zeros((CHUNK, HS), F32)
        d_values = jnp.zeros((CHUNK, HS), F32)
        for h in range(H):
            cols = slice(h * HS, (h + 1) * HS)
            q = q_ref[:, cols]
            d = d_ref[:, cols]
            scores = nt(keys, q)
            if masked:
                scores = jnp.where(mask, scores, NEG)
            probs = jnp.exp2(scores * factor - lse_ref[h : h + 1, :])
            d_probs = nt(values, d)
            d_scores = (probs * (d_probs - delta[h : h + 1, :])).astype(BF)
            d_values = d_values + nn(probs.astype(BF), d)
            d_keys = d_keys + nn(d_scores, q)
            acc[head_block(h, tok)] += nn(keys_t, d_scores)
        for i in range(2):
            part = slice(i * tok, (i + 1) * tok)
            dkv[j, i, :, :HS] = (d_keys[part] * scale).astype(BF)
            dkv[j, i, :, HS:] = d_values[part].astype(BF)

    chunks = s // 2 + 1
    def attention_chunk(j, carry):
        plain = jnp.logical_and(jnp.logical_and(j > 0, j < chunks - 1), s < 2 * A * B - 1)

        @pl.when(plain)
        def _():
            step(j, False)

        @pl.when(jnp.logical_not(plain))
        def _():
            step(j, True)

        return carry

    first = 0 if head is None else min(2, A - 1)
    steps = [functools.partial(down_step, i) for i in range(first, A - 1)]
    steps += [functools.partial(up_step, i) for i in range(A - 2)] + [down_share]
    if A == 4:
        times = (1, 3, 5, 4) if head is not None else (0, 1, 2, 3, 4, 5)
        at_chunk = dict(zip(times, steps))
        at_chunk[2] = square_o.over_f
        at_chunk[6 if head is not None else 7] = square_o.over_b
    else:
        at_chunk = {0: square_o.over_f, 1: lambda: [step() for step in steps], 2: square_o.over_b}

    def chunk_and_step(j, carry):
        @pl.when(j < chunks)
        def _():
            attention_chunk(j, 0)

        for time, act in at_chunk.items():
            pl.when(j == time)(lambda act=act: act() and None)
        return carry

    lax.fori_loop(0, window // CHUNK, chunk_and_step, 0)

    def clear(j, carry):
        dkv[j] = jnp.zeros(dkv.shape[1:], BF)
        return carry

    lax.fori_loop(chunks, window // CHUNK, clear, 0)

    dkv_c_copy = start(dkv.at[:, 1 - c], dkv_c, slots(), device("c", 1))


    if head is not None:
        finish_output()
    for h in range(H):
        dq[:, h * HS : (h + 1) * HS] = (acc[head_block(h, tok)] * scale).T.astype(BF)
    n_rows = 128

    def query_grad(i, carry):
        col = pl.ds(pl.multiple_of(i * n_rows, n_rows), n_rows)
        fi = i // (own_rows // n_rows)
        row = lax.rem(i, own_rows // n_rows) * n_rows
        gq_ref[fi, pl.ds(pl.multiple_of(row, n_rows), n_rows), :] = nn(n1_ref[:, col].T, dq[...]).astype(BF)
        return carry

    lax.fori_loop(0, D // n_rows, query_grad, 0)
    square_q.over_c()

    dkv_c_copy.wait()

    def add_c(j, carry):
        dkv_c[j] = (dkv_c[j].astype(F32) + dkv[j, c].astype(F32)).astype(BF)
        return carry

    lax.fori_loop(0, A * B, add_c, 0)
    x_kv = []
    for kb in range(B - 1):
        other = lax.rem(b + kb + 1, B)
        for j in range(A):
            x_kv.append(start(dkv_c.at[j * B + other], dkv_x.at[kb, j], slots(), device("b", kb + 1)))

    up_step(A - 2)
    gather_down.from_a()
    up_share()
    square_q.over_f()

    for copy in x_kv:
        copy.wait()

    def add_x(j, carry):
        total = dkv_c[j * B + b].astype(F32)
        for kb in range(B - 1):
            total = total + dkv_x[kb, j].astype(F32)
        dkv_x[0, j] = total.astype(BF)
        return carry

    lax.fori_loop(0, A, add_x, 0)
    z_kv = slots(A - 1)
    for k in range(1, A):

        @pl.when(a - k >= 0)
        def _():
            to = (((a - k) * B + b) * 2 + c, f)
            remote(dkv_x.at[0, jnp.maximum(a - k, 0)], dkv_z.at[k - 1], z_kv + k - 1, to).start()

    up_gather()
    square_o.over_a()
    square_q.over_b()

    total = dkv_x[0, a].astype(F32)
    d_kv[...] = total
    for k in range(1, A):
        copy = remote(dkv_x.at[0, jnp.maximum(a - k, 0)], dkv_z.at[k - 1], z_kv + k - 1, device("a", A - k))

        @pl.when(a - k >= 0)
        def _():
            copy.wait_send()

        @pl.when(a + k < A)
        def _():
            copy.wait_recv()
            d_kv[...] = d_kv[...] + dkv_z[k - 1].astype(F32)

    d_kv_low = d_kv[...].astype(BF)

    n_cols = 256
    mean = jnp.zeros((tok, 1), F32)
    for i in range(D // n_cols):
        cols = slice(i * n_cols, (i + 1) * n_cols)
        part = nt(dq[...], wq_ref[cols, :]) + nt(d_kv_low, wkv_ref[cols, :])
        dn1[:, cols] = part
        weighted = part * (tok_ref[:, cols].astype(F32) * inv_ref[...])
        gain_rows[0:1, cols] = jnp.sum(weighted, axis=0, keepdims=True)
        mean = mean + jnp.sum(weighted * gain_ref[:, cols], axis=1, keepdims=True)
    if head is None:
        gain_rows[1:2, :] = gain2_ref[...]
    mean = mean * (1.0 / D)

    r_kv = own_rows // A
    rows_kv = r_kv + 16
    for fi in range(F):
        for i in range(A):
            at = fi * own_rows + i * r_kv
            part = tn(n1_ref[:, at : at + r_kv], d_kv_low).astype(BF)
            gkv_ref[0, fi, i, :r_kv, :] = part[:, :HS]
            gkv_ref[1, fi, i, :r_kv, :] = part[:, HS:]
            for ci in range(2):
                rows = [gain_rows[ci : ci + 1, fi * own_rows + k * 128 : fi * own_rows + (k + 1) * 128] for k in range(own_rows // 128)]
                block = jnp.concatenate(rows + [jnp.zeros((16 - len(rows), 128), F32)], axis=0)
                gkv_ref[ci, fi, i, r_kv:, :] = block.astype(BF)
    kv_c_copy = start(gkv_ref.at[1 - c], kv_c, slots(), device("c", 1))

    gather_up.from_a()
    for i in range(D // n_cols):
        cols = slice(i * n_cols, (i + 1) * n_cols)
        grad_tokens[:, cols] = dres_ref[:, cols] + inv_ref[...] * (
            dn1[:, cols] * gain_ref[:, cols] - tok_ref[:, cols].astype(F32) * inv_ref[...] * mean
        )
    square_q.over_a()
    kv_c_copy.wait()
    kv_c[...] = (kv_c[...].astype(F32) + gkv_ref[c].astype(F32)).astype(BF)
    kv_f = [start(kv_c.at[lax.rem(f + kf + 1, F)], kv_y.at[kf], slots(), device("f", kf + 1)) for kf in range(F - 1)]
    square_o.finish()
    total = kv_c[f].astype(F32)
    for kf in range(F - 1):
        kv_f[kf].wait()
        total = total + kv_y[kf].astype(F32)
    kv_y[F - 1] = total.astype(BF)
    kv_b = [start(kv_y.at[F - 1], kv_x.at[kb], slots(), device("b", kb + 1)) for kb in range(B - 1)]
    gather_o.from_a()
    square_q.finish()
    total = kv_y[F - 1].astype(F32)
    for kb in range(B - 1):
        kv_b[kb].wait()
        total = total + kv_x[kb].astype(F32)
    kv_x[B - 1] = total.astype(BF)
    kv_a = [start(kv_x.at[B - 1, lax.rem(a + ka + 1, A)], kv_z.at[ka], slots(), device("a", ka + 1)) for ka in range(A - 1)]
    gather_down.from_b()
    total = kv_x[B - 1, a].astype(F32)
    for ka in range(A - 1):
        kv_a[ka].wait()
        total = total + kv_z[ka].astype(F32)
    kv_s[...] = total.astype(BF)
    gather_kv.begin()
    gather_q.from_a()
    gather_up.from_b()
    gather_kv.from_a()
    gather_o.from_b()
    gather_q.from_b()
    for gather in gathers:
        gather.end()
    if head is not None:
        finish_head()


def tail_shapes(dims, tok, D, shard, window, extra):
    A, B, F = dims
    own_rows = D // F
    half, r_d, r_u, w_u = D // 2, shard // (A * B), own_rows // B, shard // A
    w_o, r_kv = half // A, own_rows // A + 16

    def low(*shape):
        return pltpu.VMEM(shape, BF)

    square = [low(F, own_rows, half), low(F, own_rows, half), low(B, r_u, half), low(A - 1, r_u, w_o), low(r_u, w_o)]
    n_sems = extra + 2 * (A * (B - 1) + A - 1) + 4 * (A + (B - 1) * A + B * A) + 2 * A
    n_sems += 2 * (F + B + A) + 2 * F + (B - 1) * A + A + F + B + A + 8
    outs = (
        jax.ShapeDtypeStruct((2 * shard, D), BF),
        jax.ShapeDtypeStruct((F, own_rows, 2 * shard), BF),
        jax.ShapeDtypeStruct((own_rows, D), BF),
        jax.ShapeDtypeStruct((own_rows, D), BF),
        jax.ShapeDtypeStruct((2, A, r_kv, HS), BF),
        jax.ShapeDtypeStruct((tok, D), F32),
    )
    scratch = [
        pltpu.VMEM((2 * HS, H // 2 * tok), F32),
        pltpu.VMEM((H, tok), F32),
        low(tok, D),
        low(A * B, 2, tok, 2 * HS),
        low(A * B, tok, 2 * HS),
        low(max(1, B - 1), A, tok, 2 * HS),
        low(max(1, A - 1), tok, 2 * HS),
        pltpu.VMEM((tok, 2 * HS), F32),
        pltpu.VMEM((tok, D), F32),
        low(F, own_rows, D),
        low(2, F, A, r_kv, HS),
        low(B - 1, A, r_d, D),
        low(B - 1, A, F, r_u, w_u),
        low(A - 1, r_d, D),
        low(A - 1, F, r_u, w_u),
        low(A - 1, r_d, D),
        low(A - 1, F, r_u, w_u),
        low(r_d, D),
        low(F, r_u, w_u),
        low(F, r_u, w_u),
        *square,
        *square,
        low(F, A, r_kv, HS),
        low(F, A, r_kv, HS),
        low(B, A, r_kv, HS),
        low(A - 1, r_kv, HS),
        low(r_kv, HS),
        pltpu.VMEM((8, D), F32),
        pltpu.SemaphoreType.DMA((n_sems,)),
        pltpu.SemaphoreType.DMA((n_sems,)),
        pltpu.SemaphoreType.DMA((5,)),
    ]
    return outs, scratch


def tail(dims, ends, queries, window_kv, d_attended, attended, lse, grad_down, grad_up, grad_out, n1, wq, wkv, tokens, inv, gain, dres, gain2):
    A, B, F = dims
    tok, D = n1.shape
    window = window_kv.shape[0]
    outs, scratch = tail_shapes(dims, tok, D, grad_down.shape[0], window, 0)
    hbm = pl.BlockSpec(memory_space=pltpu.HBM)
    return pl.pallas_call(
        functools.partial(tail_kernel, dims, None, TAIL_IN + TAIL_OUT + TAIL_SCRATCH),
        out_shape=outs,
        in_specs=[SMEM] + [VMEM] * 16,
        out_specs=(hbm,) * 5 + (VMEM,),
        scratch_shapes=scratch,
        compiler_params=pltpu.CompilerParams(vmem_limit_bytes=56 * 2**20, collective_id=1, has_side_effects=True),
        cost_estimate=pl.CostEstimate(flops=20 * tok * window * D, bytes_accessed=2**25, transcendentals=tok * window * H),
        name="tail",
    )(ends, queries, window_kv, d_attended, attended, lse, grad_down, grad_up, grad_out, n1, wq, wkv, tokens, inv, gain, dres, gain2)


HEAD_IN = (
    "lengths",
    "groups",
    "tokens",
    "gains_in",
    "wk_in",
    "wv_in",
    "cot_in",
    "wq_in",
    "wo_in",
    "up_in",
    "down_in",
)
HEAD_SCRATCH = (
    "q_ref",
    "kv_ref",
    "d_ref",
    "att_ref",
    "lse_ref",
    "gd_ref",
    "gu_ref",
    "n1_ref",
    "wq_ref",
    "wkv_ref",
    "inv_ref",
    "gain_ref",
    "dres_ref",
    "gain2_ref",
    "wo_ref",
    "up_ref",
    "down_ref",
    "gains_all",
    "cot_all",
    "n2_all",
    "hid_all",
    "dp_all",
    "res_ref",
    "inv2_ref",
    "dbr_ref",
    "back_s",
    "back_c",
    "back_y",
    "back_r",
    "out_s",
    "out_c",
    "out_y",
    "out_r",
    "loc_sem",
    "ends",
)


def head(r, x):
    A, B, F, a, b, c, f, s = x.A, x.B, x.F, x.a, x.b, x.c, x.f, x.s
    slots, remote, device, lower = x.slots, x.remote, x.device, x.lower
    tok, D = r.tokens.shape
    own_rows = D // F
    shard = r.down_ref.shape[0]
    half = own_rows // 2
    sent = []

    def start(src, dst, to, slot=None):
        copy = remote(src, dst, slots() if slot is None else slot, to)
        copy.start()
        sent.append(copy)
        return copy

    def done(copies):
        for copy in copies:
            copy.wait_send()
            sent[:] = [other for other in sent if other is not copy]

    def span(at, n):
        return pl.ds(pl.multiple_of(at, n), n)

    sibling = device("c", 1)
    mine, mine_half = span(f * own_rows, own_rows), span(c * half, half)
    full_half = span((f * 2 + c) * half, half)

    def to_f(src, dst):
        return [start(src(kf), dst(kf), device("f", kf)) for kf in range(1, F)]

    gains_f = to_f(lambda kf: r.gains_in, lambda kf: r.gains_all.at[f])
    wk_f = to_f(lambda kf: r.wk_in.at[mine_half, :], lambda kf: r.wkv_ref.at[full_half, :HS])
    wv_f = to_f(lambda kf: r.wv_in.at[mine_half, :], lambda kf: r.wkv_ref.at[full_half, HS:])
    wq_f = to_f(lambda kf: r.wq_in.at[mine_half, :], lambda kf: r.wq_ref.at[full_half, :])
    part, up_part = half // B, own_rows // B

    def wo_rows(f_, c_, b_):
        return span(((f_ * 2 + c_) * B + b_) * part, part)

    def up_rows(f_, b_):
        return span((f_ * B + b_) * up_part, up_part)

    wo_f = to_f(lambda kf: r.wo_in.at[span((c * B + b) * part, part), :], lambda kf: r.wo_ref.at[wo_rows(f, c, b), :])
    up_f = to_f(
        lambda kf: r.up_in.at[span(b * up_part, up_part), span((lax.rem(f + kf, F) * 2 + c) * shard, shard)],
        lambda kf: r.up_ref.at[up_rows(f, b), :],
    )
    cot_f = to_f(lambda kf: r.cot_in, lambda kf: r.cot_all.at[kf, :tok])
    cot_c = [start(r.cot_in, r.cot_all.at[0, tok:], sibling)]

    local = [
        pltpu.make_async_copy(src, dst, r.loc_sem.at[i])
        for i, (src, dst) in enumerate(
            (
                (r.wq_in, r.wq_ref.at[mine, :]),
                (r.wo_in, r.wo_ref.at[mine, :]),
                (r.up_in.at[:, span((f * 2 + c) * shard, shard)], r.up_ref.at[mine, :]),
                (r.cot_in, r.cot_all.at[0, :tok]),
                (r.down_in.at[span(c * shard, shard), :], r.down_ref),
            )
        )
    ]
    for copy in local:
        copy.start()

    def weight_halves(copies, ref, cols):
        passed = []
        for kf in range(1, F):
            copies[kf - 1].wait_recv()
            rows = span((lower("f", kf) * 2 + c) * half, half)
            passed.append(start(ref.at[rows, cols], ref.at[rows, cols], sibling))
        return passed

    def along_b(copies, ref, rows):
        passed = []
        for kf in range(1, F):
            copies[kf - 1].wait_recv()
            here = ref.at[rows(lower("f", kf)), :]
            passed += [start(here, here, device("b", kb)) for kb in range(1, B)]
        return passed

    group = r.groups[f]
    end = jnp.int32(0)
    for i in range(r.ends.shape[0]):
        end = end + r.lengths[group, i]
        r.ends[i] = end
    n_rows = 64

    def unit_rows(i, carry):
        rows = span(i * n_rows, n_rows)
        stream = r.tokens[rows, :].astype(F32)
        inverse = lax.rsqrt(jnp.mean(stream * stream, axis=1, keepdims=True) + EPS)
        r.inv_ref[rows, :] = inverse
        return carry

    lax.fori_loop(0, tok // n_rows, unit_rows, 0)
    r.wkv_ref[mine, :HS] = r.wk_in[...]
    r.wkv_ref[mine, HS:] = r.wv_in[...]
    r.gains_all[f] = r.gains_in[...]
    for copy in gains_f:
        copy.wait_recv()
    for i in range(F):
        both = r.gains_all[i].astype(F32)
        cols = slice(i * own_rows, (i + 1) * own_rows)
        r.gain_ref[0:1, cols] = both[0:1, :]
        r.gain2_ref[0:1, cols] = both[1:2, :]

    def normed_rows(i, carry):
        rows = span(i * n_rows, n_rows)
        r.n1_ref[rows, :] = (r.tokens[rows, :].astype(F32) * r.inv_ref[rows, :] * r.gain_ref[...]).astype(BF)
        return carry

    lax.fori_loop(0, tok // n_rows, normed_rows, 0)

    wkv_c = weight_halves(wk_f, r.wkv_ref, slice(0, HS)) + weight_halves(wv_f, r.wkv_ref, slice(HS, 2 * HS))
    for copy in wkv_c:
        copy.wait_recv()
    kv = r.kv_ref

    def block(a_, b_, c_):
        return kv.at[span(((a_ * B + b_) * 2 + c_) * tok, tok), :]

    kv[span(s * tok, tok), :] = nn(r.n1_ref[...], r.wkv_ref[...]).astype(BF)
    kv_z, kv_x, kv_c = slots(A - 1), slots((B - 1) * A), slots(B * A)
    own = block(a, b, c)
    z_copies = [remote(own, own, kv_z + k - 1, device("a", k)) for k in range(1, A)]

    def guarded(k, ok, act):
        if k == 0:
            act()
        else:
            pl.when(ok)(act)

    for k in range(1, A):
        guarded(k, a + k < A, z_copies[k - 1].start)

    def x_copy(kb, k):
        here = block(jnp.maximum(a - k, 0), b, c)
        return remote(here, here, kv_x + (kb - 1) * A + k, device("b", kb))

    def c_copy(kb, k):
        here = block(jnp.maximum(a - k, 0), lower("b", kb) if kb else b, c)
        return remote(here, here, kv_c + kb * A + k, sibling)

    def pass_on(k):
        for kb in range(1, B):
            x_copy(kb, k).start()
        c_copy(0, k).start()

    pass_on(0)

    local[0].wait()
    wq_c = weight_halves(wq_f, r.wq_ref, slice(0, D))
    for copy in wq_c:
        copy.wait_recv()
    n_cols = 256

    def columns(n, act):
        def body(i, carry):
            act(span(i * n_cols, n_cols))
            return carry

        lax.fori_loop(0, n // n_cols, body, 0)

    def query_cols(cols):
        r.q_ref[:, cols] = nn(r.n1_ref[...], r.wq_ref[:, cols]).astype(BF)

    columns(D, query_cols)

    for k in range(1, A):

        def arrived(k=k):
            z_copies[k - 1].wait_recv()
            pass_on(k)

        guarded(k, a - k >= 0, arrived)
    wo_b = along_b(wo_f, r.wo_ref, lambda f_: wo_rows(f_, c, b))

    factor = math.log2(math.e) / math.sqrt(HS)
    top, mixed, total = r.dres_ref, r.res_ref, r.acc
    top[...] = jnp.full(top.shape, -3e38, F32)
    mixed[...] = jnp.zeros(mixed.shape, F32)
    total[...] = jnp.zeros(total.shape, F32)
    pos = s * tok + lax.broadcasted_iota(jnp.int32, (tok, 1), 0)
    begin = jnp.zeros((tok, 1), jnp.int32)
    for i in range(r.ends.shape[0]):
        begin = jnp.maximum(begin, jnp.where(r.ends[i] <= pos, r.ends[i], 0))

    def step(j, masked):
        rows = span(j * CHUNK, CHUNK)
        keys = kv[rows, :HS]
        values = jnp.concatenate([kv[rows, HS:], jnp.ones((CHUNK, HS), BF)], axis=1)
        if masked:
            at = j * CHUNK + lax.broadcasted_iota(jnp.int32, (tok, CHUNK), 1)
            mask = jnp.logical_and(at >= begin, at <= pos)
        for h in range(H):
            cols = slice(h * HS, (h + 1) * HS)
            scores = nt(r.q_ref[:, cols], keys)
            if masked:
                scores = jnp.where(mask, scores, NEG)
            old = top[:, cols]
            new = jnp.maximum(old, jnp.max(scores, axis=1, keepdims=True) * factor)
            shrink = jnp.exp2(old - new)
            probs = jnp.exp2(scores * factor - jnp.concatenate([new] * (CHUNK // HS), axis=1))
            both = nn(probs.astype(BF), values)
            mixed[:, cols] = mixed[:, cols] * shrink + both[:, :HS]
            total[:, cols] = total[:, cols] * shrink + both[:, HS:]
            top[:, cols] = new

    last = s // 2
    c_copy(0, 0).wait_recv()
    step(last, True)
    for kb in range(1, B):
        for k in range(A):

            def arrived(kb=kb, k=k):
                x_copy(kb, k).wait_recv()
                c_copy(kb, k).start()

            guarded(k, a - k >= 0, arrived)
    for kb in range(B):
        for k in range(A):
            if kb or k:
                guarded(k, a - k >= 0, c_copy(kb, k).wait_recv)

    up_b = along_b(up_f, r.up_ref, lambda f_: up_rows(f_, b))

    def attention_chunk(j, carry):
        plain = jnp.logical_and(j > 0, s < 2 * A * B - 1)

        @pl.when(plain)
        def _():
            step(j, False)

        @pl.when(jnp.logical_not(plain))
        def _():
            step(j, True)

        return carry

    lax.fori_loop(0, last, attention_chunk, 0)
    for h in range(H):
        cols = slice(h * HS, (h + 1) * HS)
        r.att_ref[:, cols] = (mixed[:, cols] * (1.0 / total[:, cols])).astype(BF)
        r.lse_ref[h : h + 1, :] = (top[:, cols] + jnp.log2(total[:, cols])).T[0:1, :]

    local[1].wait()
    wo_c = []
    for copy in wo_b:
        copy.wait_recv()
    for kf in range(1, F):
        here = r.wo_ref.at[span((lower("f", kf) * 2 + c) * half, half), :]
        wo_c.append(start(here, here, sibling))
    for copy in wo_c:
        copy.wait_recv()
    squares = jnp.zeros((tok, 1), F32)
    for i in range(D // n_cols):
        cols = slice(i * n_cols, (i + 1) * n_cols)
        part = r.tokens[:, cols].astype(F32) + nn(r.att_ref[...], r.wo_ref[:, cols])
        r.res_ref[:, cols] = part
        squares = squares + jnp.sum(part * part, axis=1, keepdims=True)
    r.inv2_ref[...] = lax.rsqrt(squares * (1.0 / D) + EPS)

    def second_norm(i, carry):
        rows = span(i * n_rows, n_rows)
        r.n2_all[0, rows, :] = (r.res_ref[rows, :] * r.inv2_ref[rows, :] * r.gain2_ref[...]).astype(BF)
        return carry

    lax.fori_loop(0, tok // n_rows, second_norm, 0)

    n2_f = to_f(lambda kf: r.n2_all.at[0, :tok], lambda kf: r.n2_all.at[kf, :tok])
    n2_c = [start(r.n2_all.at[0, :tok], r.n2_all.at[0, tok:], sibling)]
    local[2].wait()
    local[3].wait()
    local[4].wait()
    for copy in up_b:
        copy.wait_recv()
    for kf in range(1, F):
        cot_f[kf - 1].wait_recv()
        cot_c.append(start(r.cot_all.at[kf, :tok], r.cot_all.at[kf, tok:], sibling))

    def feed_forward(kf):
        def hidden_cols(cols):
            before = nn(r.n2_all[kf], r.up_ref[:, cols])
            d_hidden = nt(r.cot_all[kf], r.down_ref[cols, :])
            sig = 1.0 / (1.0 + jnp.exp(-before))
            r.hid_all[kf, :, cols] = (before * sig).astype(BF)
            r.dp_all[kf, :, cols] = (d_hidden * sig * (1.0 + before * (1.0 - sig))).astype(BF)

        columns(shard, hidden_cols)

        def back_cols(cols):
            r.back_s[kf, :, cols] = nt(r.dp_all[kf], r.up_ref[cols, :]).astype(BF)

        columns(D, back_cols)
        return start(r.back_s.at[kf, tok:], r.back_c.at[kf], sibling)

    def out_part(kf):
        def out_cols(cols):
            r.out_s[kf, :, cols] = nn(r.hid_all[kf], r.down_ref[:, cols]).astype(BF)

        columns(D, out_cols)
        return start(r.out_s.at[kf, tok:], r.out_c.at[kf], sibling)

    def chip_sum(kf, part, other, ref):
        def rows_sum(i, carry):
            rows = span(i * n_rows, n_rows)
            ref[kf - 1, rows, :] = (part[kf, rows, :].astype(F32) + other[kf, rows, :].astype(F32)).astype(BF)
            return carry

        lax.fori_loop(0, tok // n_rows, rows_sum, 0)

    n_out = 128

    def down_grad(kf):
        def rows_of(i, carry):
            cols = span(i * n_out, n_out)
            grad = tn(r.hid_all[kf, :, cols], r.cot_all[kf])
            r.gd_ref[cols, :] = (grad + r.gd_ref[cols, :].astype(F32) if kf else grad).astype(BF)
            return carry

        lax.fori_loop(0, shard // n_out, rows_of, 0)

    def up_grad(kf):
        def rows_of(i, carry):
            cols = span(i * n_out, n_out)
            rows = span(lax.rem(i, own_rows // n_out) * n_out, n_out)
            at = i // (own_rows // n_out)
            grad = tn(r.n2_all[kf, :, cols], r.dp_all[kf])
            r.gu_ref[at, rows, :] = (grad + r.gu_ref[at, rows, :].astype(F32) if kf else grad).astype(BF)
            return carry

        lax.fori_loop(0, D // n_out, rows_of, 0)

    back_copies, out_copies, back_back, out_back = [None] * F, [None] * F, [], []
    n2_c[0].wait_recv()
    cot_c[0].wait_recv()
    back_copies[0] = feed_forward(0)
    down_grad(0)
    up_grad(0)
    out_copies[0] = out_part(0)
    for kf in range(1, F):
        n2_f[kf - 1].wait_recv()
        n2_c.append(start(r.n2_all.at[kf, :tok], r.n2_all.at[kf, tok:], sibling))
    for kf in range(1, F):
        n2_c[kf].wait_recv()
        cot_c[kf].wait_recv()
        back_copies[kf] = feed_forward(kf)
        if kf == F - 1:
            down_grad(kf)
            x.send_down(0, A)
        back_copies[kf].wait_recv()
        chip_sum(kf, r.back_s, r.back_c, r.back_y)
        back_back.append(start(r.back_y.at[kf - 1], r.back_r.at[kf - 1], device("f", F - kf)))
        if kf < F - 1:
            down_grad(kf)
        up_grad(kf)
        out_copies[kf] = out_part(kf)
    x.send_up(0, A)
    for kf in range(1, F):
        out_copies[kf].wait_recv()
        chip_sum(kf, r.out_s, r.out_c, r.out_y)
        out_back.append(start(r.out_y.at[kf - 1], r.out_r.at[kf - 1], device("f", F - kf)))
    x.down_step(0)

    back_copies[0].wait_recv()
    for copy in back_back:
        copy.wait_recv()

    def norm_back(i, gain_grad):
        rows = span(i * n_rows, n_rows)
        d_normed = r.back_s[0, rows, :].astype(F32) + r.back_c[0, rows, :].astype(F32)
        for kf in range(1, F):
            d_normed = d_normed + r.back_r[kf - 1, rows, :].astype(F32)
        inverse = r.inv2_ref[rows, :]
        unit = r.res_ref[rows, :] * inverse
        weighted = d_normed * unit
        scaled = d_normed * r.gain2_ref[...]
        mean = jnp.mean(scaled * unit, axis=1, keepdims=True)
        d_residual = r.cot_all[0, rows, :].astype(F32) + inverse * (scaled - unit * mean)
        r.dres_ref[rows, :] = d_residual
        r.dbr_ref[rows, :] = d_residual.astype(BF)
        return gain_grad + jnp.sum(weighted, axis=0, keepdims=True)

    r.gain_rows[1:2, :] = lax.fori_loop(0, tok // n_rows, norm_back, jnp.zeros((1, D), F32))

    def attended_cols(cols):
        r.d_ref[:, cols] = nt(r.dbr_ref[...], r.wo_ref[cols, :]).astype(BF)

    columns(D, attended_cols)

    done(n2_f + n2_c)

    def out_grad(i, carry):
        cols = span(i * n_out, n_out)
        rows = span(lax.rem(i, own_rows // n_out) * n_out, n_out)
        r.go_ref[i // (own_rows // n_out), rows, :] = tn(r.att_ref[:, cols], r.dbr_ref[...]).astype(BF)
        return carry

    lax.fori_loop(0, D // n_out, out_grad, 0)
    if A > 2:
        x.down_step(1)

    def finish_output():
        out_copies[0].wait_recv()
        for copy in out_back:
            copy.wait_recv()

        def output_rows(i, carry):
            rows = span(i * n_rows, n_rows)
            value = r.res_ref[rows, :] + r.out_s[0, rows, :].astype(F32) + r.out_c[0, rows, :].astype(F32)
            for kf in range(1, F):
                value = value + r.out_r[kf - 1, rows, :].astype(F32)
            r.out_ref[rows, :] = value.astype(BF)
            return carry

        lax.fori_loop(0, tok // n_rows, output_rows, 0)
        done(out_copies)
        results[0].start()

    results = [
        pltpu.make_async_copy(src, dst, r.loc_sem.at[5 + i])
        for i, (src, dst) in enumerate(((r.out_ref, r.out_hbm), (r.grad_tokens, r.grad_hbm)))
    ]

    def finish():
        results[1].start()
        for copy in results:
            copy.wait()
        for copy in sent:
            copy.wait_send()
        for k in range(1, A):
            guarded(k, a + k < A, z_copies[k - 1].wait_send)
        for k in range(A):
            for kb in range(B):
                if kb:
                    guarded(k, a - k >= 0, x_copy(kb, k).wait_send)
                guarded(k, a - k >= 0, c_copy(kb, k).wait_send)

    return finish_output, finish


AGAIN = {
    "go_ref": "n2_all",
    "gq_ref": "out_s",
    "dn1": "res_ref",
    "grad_tokens": "res_ref",
    "dq": "d_ref",
    "out_ref": "dbr_ref",
    "tok_ref": "tokens",
}


def layer_shapes(dims, tok, D, shard, window, sequences):
    A, B, F = dims
    own_rows = D // F
    outs, scratch = tail_shapes(dims, tok, D, shard, window, 16 * F + A - 1 + (B - 1) * A + B * A)

    def low(*shape):
        return pltpu.VMEM(shape, BF)

    def wide(*shape):
        return pltpu.VMEM(shape, F32)

    pair = [low(F, 2 * tok, D), low(F, tok, D), low(F - 1, tok, D), low(F - 1, tok, D)]
    first = [
        low(tok, D),
        low(window, 2 * HS),
        low(tok, D),
        low(tok, D),
        wide(H, tok),
        low(shard, D),
        low(F, own_rows, shard),
        low(tok, D),
        low(D, D),
        low(D, 2 * HS),
        wide(tok, 1),
        wide(1, D),
        wide(tok, D),
        wide(1, D),
        low(D, D),
        low(D, shard),
        low(shard, D),
        low(F, 16, own_rows),
        low(F, 2 * tok, D),
        low(F, 2 * tok, D),
        low(F, 2 * tok, shard),
        low(F, 2 * tok, shard),
        wide(tok, D),
        wide(tok, 1),
        low(tok, D),
        *pair,
        *pair,
        pltpu.SemaphoreType.DMA((7,)),
        pltpu.SMEM((sequences,), jnp.int32),
    ]
    sizes = dict(zip(HEAD_SCRATCH + TAIL_SCRATCH, first + scratch))
    fits = all(sizes[k].shape == sizes[AGAIN[k]].shape for k in ("gq_ref", "dn1", "dq")) and tok == 2 * HS and own_rows == 2 * tok
    scratch = [ref for name, ref in zip(TAIL_SCRATCH, scratch) if name not in AGAIN]
    fits = fits and vmem_bytes(first + scratch) + 4 * 2**20 < LIMIT
    return outs + (jax.ShapeDtypeStruct((tok, D), BF),), first + scratch, fits


def vmem_bytes(scratch):
    total = 0
    for ref in scratch:
        shape = getattr(ref, "shape", ())
        if len(shape) >= 2:
            lanes = -(-shape[-1] // 128) * 128
            rows = -(-shape[-2] // 8) * 8
            total += math.prod(shape[:-2]) * rows * lanes * jnp.dtype(ref.dtype).itemsize
    return total


def layer(dims, lengths, groups, tokens, gains, w_key, w_value, cotangent, w_query, w_out, w_up, w_down, outs, scratch):
    tok, D = tokens.shape
    hbm = pl.BlockSpec(memory_space=pltpu.HBM)
    names = HEAD_IN + TAIL_OUT[:5] + ("grad_hbm", "out_hbm") + HEAD_SCRATCH + tuple(n for n in TAIL_SCRATCH if n not in AGAIN)
    return pl.pallas_call(
        functools.partial(tail_kernel, dims, head, names),
        out_shape=outs,
        in_specs=[SMEM] * 2 + [VMEM] * 4 + [hbm] * 5,
        out_specs=(hbm,) * 7,
        scratch_shapes=scratch,
        compiler_params=pltpu.CompilerParams(vmem_limit_bytes=LIMIT, collective_id=2, has_side_effects=True),
        cost_estimate=pl.CostEstimate(flops=2**35, bytes_accessed=2**25, transcendentals=2**24),
        name="layer",
    )(lengths, groups, tokens, gains, w_key, w_value, cotangent, w_query, w_out, w_up, w_down)


def after(value, *others):
    return lax.optimization_barrier((value, *others))[0]


class Grid:
    def __init__(self):
        seq = lax.axis_size("seq")
        self.F = lax.axis_size("fsdp")
        self.C = 2
        chips = seq // 2
        self.B = 2 if chips == 8 else chips // 2
        self.A = chips // self.B
        self.s = lax.axis_index("seq")
        self.f = lax.axis_index("fsdp")
        self.c = self.s % 2
        self.b = self.s // 2 % self.B
        self.a = self.s // (2 * self.B)

    def size(self, axis):
        return {"a": self.A, "b": self.B, "c": self.C, "f": self.F}[axis]

    def place(self, axis):
        return {"a": self.a, "b": self.b, "c": self.c, "f": self.f}[axis]

    def send(self, value, axis, step, upward=False):
        pairs = []
        for a in range(self.A):
            for b in range(self.B):
                for c in range(2):
                    for f in range(self.F):
                        at = {"a": a, "b": b, "c": c, "f": f}
                        to = dict(at)
                        to[axis] += step
                        if upward and not 0 <= to[axis] < self.size(axis):
                            continue
                        to[axis] %= self.size(axis)
                        line = [((d["a"] * self.B + d["b"]) * 2 + d["c"]) * self.F + d["f"] for d in (at, to)]
                        pairs.append(tuple(line))
        return lax.ppermute(value, ("seq", "fsdp"), pairs)

    def stack(self, parts, axis):
        n, me = len(parts), self.place(axis)
        if n == 2:
            low = me == 0
            return jnp.stack([jnp.where(low, parts[0], parts[1]), jnp.where(low, parts[1], parts[0])])
        twice = jnp.stack(parts + parts)
        return lax.dynamic_slice_in_dim(twice, (n - me) % n, n, 0)

    def gather(self, value, axis):
        n = self.size(axis)
        return self.stack([value] + [self.send(value, axis, -k) for k in range(1, n)], axis)

    def scatter(self, parts, axis):
        n, me = self.size(axis), self.place(axis)

        def pick(k):
            return lax.dynamic_index_in_dim(parts, (me + k) % n, 0, keepdims=False)

        got = [self.send(pick(k).astype(BF), axis, k) for k in range(1, n)]
        total = pick(0).astype(F32)
        for piece in got:
            total = total + piece.astype(F32)
        return total

    def plane_sum(self, parts):
        half = self.scatter(parts, "b").astype(BF)
        return self.scatter(half, "a")

    def plane_gather(self, share):
        rows = self.gather(share.astype(BF), "a")
        return self.gather(rows, "b")


def local(
    tokens,
    cotangent,
    seq_lengths,
    group_of_shard,
    gain_attn,
    w_query,
    w_key,
    w_value,
    w_out,
    gain_ffn,
    w_up,
    w_down,
):
    g = Grid()
    A, B, C, F = g.A, g.B, g.C, g.F
    tok, D = tokens.shape[1:]
    FF = w_up.shape[1]
    own_rows = D // F
    seq_parts = A * B * C
    shard = FF // (2 * F)

    outs, scratch, fits = layer_shapes((A, B, F), tok, D, shard, seq_parts * tok, seq_lengths.shape[1])
    if fits:
        row = lax.broadcasted_iota(jnp.int32, (16, own_rows), 0)
        gains = jnp.where(row == 0, gain_attn[None], gain_ffn[None])
        *grads, grad_tokens, output = layer(
            (A, B, F),
            seq_lengths,
            group_of_shard,
            tokens[0],
            gains,
            w_key,
            w_value,
            cotangent[0],
            w_query,
            w_out,
            w_up,
            w_down,
            outs,
            scratch,
        )
        return results(output, grad_tokens, *grads)

    group = lax.dynamic_index_in_dim(group_of_shard, g.f, 0, keepdims=False)
    lengths = lax.dynamic_index_in_dim(seq_lengths, group, 0, keepdims=False)
    running, ends = jnp.int32(0), []
    for i in range(seq_lengths.shape[1]):
        running = running + lengths[i]
        ends.append(running)
    scal = jnp.stack([g.s.astype(jnp.int32), *ends])

    gains = jnp.stack([gain_attn, gain_ffn])
    full_gains = g.gather(gains, "f").transpose(1, 0, 2).reshape(2, D).astype(F32)
    gain_first, gain_second = full_gains[0], full_gains[1]
    own_kv = jnp.concatenate([w_key, w_value], axis=1)
    full_kv = g.gather(own_kv, "f").reshape(D, 2 * HS)

    def gather_weight(weight, *late):
        half = own_rows // 2
        mine = lax.dynamic_slice_in_dim(weight, g.c * half, half, 0)
        if late:
            mine = after(mine, *late)
        pieces = [g.gather(g.send(mine, "f", -k), "c").reshape(weight.shape) for k in range(1, F)]
        return g.stack([weight] + pieces, "f").reshape(F * own_rows, -1)

    full_query = gather_weight(w_query)

    stream = tokens[0].astype(F32)
    inverse_first = lax.rsqrt(jnp.mean(stream * stream, axis=1, keepdims=True) + EPS)
    unit_first = stream * inverse_first
    normed_first = (unit_first * gain_first).astype(BF)
    key_value = nn(normed_first, full_kv).astype(BF)
    queries = nn(normed_first, full_query).astype(BF)

    column = [key_value] + [g.send(key_value, "a", k, upward=True) for k in range(1, A)]
    twice = jnp.stack(column[::-1] + column[::-1])
    column = lax.dynamic_slice_in_dim(twice, A - 1 - g.a, A, 0)
    plane = g.gather(column, "b")
    whole = g.gather(plane, "c")
    window_kv = whole.transpose(2, 1, 0, 3, 4).reshape(seq_parts * tok, 2 * HS)

    full_out = gather_weight(w_out, full_query)
    upstream = cotangent[0]
    cot = []
    for k in range(F):
        mine = upstream if k == 0 else g.send(after(upstream, full_query), "f", k)
        cot.append(jnp.concatenate([mine, g.send(mine, "c", 1)], axis=0))
    ups = w_up.reshape(own_rows, F, 2, shard)
    up_parts = []
    for k in range(F):
        block = lax.dynamic_slice(ups, (0, (g.f + k) % F, g.c, 0), (own_rows, 1, 1, shard)).reshape(own_rows, shard)
        up_parts.append(block if k == 0 else g.send(after(block, full_out), "f", k))
    up_parts = [up_parts[0]] + up_parts[1:][::-1]
    up = g.stack(up_parts, "f").reshape(D, shard)
    down = lax.dynamic_slice_in_dim(w_down, g.c * shard, shard, 0)

    attended, lse = attend(scal, queries, window_kv)

    residual = stream + nn(attended, full_out)
    inverse_second = lax.rsqrt(jnp.mean(residual * residual, axis=1, keepdims=True) + EPS)
    unit_second = residual * inverse_second
    normed_second = (unit_second * gain_second).astype(BF)

    out_sum, back_sum = residual, jnp.zeros((tok, D), F32)
    hiddens, d_pres, norms = [], [], []
    backs, outs = [], []
    for k in range(F):
        mine = normed_second if k == 0 else g.send(normed_second, "f", k)
        norm = jnp.concatenate([mine, g.send(mine, "c", 1)], axis=0)
        before = nn(norm, up)
        d_hidden = nt(cot[k], down)
        sig = jax.nn.sigmoid(before)
        hidden = (before * sig).astype(BF)
        d_pre = (d_hidden * sig * (1.0 + before * (1.0 - sig))).astype(BF)
        back = nt(d_pre, up)
        out = nn(hidden, down)
        hiddens.append(hidden)
        d_pres.append(d_pre)
        norms.append(norm)
        backs.append(back)
        outs.append(out)

    def give_back(parts):
        total = 0.0
        for k, part in enumerate(parts):
            other = g.send(part[tok:].astype(BF), "c", 1)
            chip = part[:tok] + other.astype(F32)
            if k:
                chip = g.send(chip.astype(BF), "f", -k).astype(F32)
            total = total + chip
        return total

    d_normed_second = give_back(backs)
    output = (residual + give_back(outs)).astype(BF)

    grad_down = sum(tn(h, c) for h, c in zip(hiddens, cot)).astype(BF)
    grad_up = sum(tn(n, d) for n, d in zip(norms, d_pres)).astype(BF)

    def norm_back(gradient, unit_rows, inverse, gain_vec):
        scaled = gradient * gain_vec
        gain_grad = jnp.sum(gradient * unit_rows, axis=0)
        return gain_grad, inverse * (scaled - unit_rows * jnp.mean(scaled * unit_rows, axis=1, keepdims=True))

    gain_second_grad, d_from_norm = norm_back(d_normed_second, unit_second, inverse_second, gain_second)
    d_residual = upstream.astype(F32) + d_from_norm
    d_branch = d_residual.astype(BF)
    d_attended = nt(d_branch, full_out).astype(BF)
    grad_out = tn(attended, d_branch).astype(BF)

    down_all, up_all, out_all, query_all, kv_all, grad_tokens = tail(
        (A, B, F),
        scal[1:],
        queries,
        window_kv,
        d_attended,
        attended,
        lse,
        grad_down,
        grad_up.reshape(F, own_rows, shard),
        grad_out.reshape(F, own_rows, D),
        normed_first,
        full_query,
        full_kv,
        tokens[0],
        inverse_first,
        gain_first[None],
        d_residual,
        gain_second_grad[None],
    )
    return results(output, grad_tokens, down_all, up_all, out_all, query_all, kv_all)


def widen_kernel(
    low_ref, grad_ref, down_ref, up_ref, o_ref, q_ref, kv_ref, output, grad_tokens, grad_down, grad_up, grad_o, grad_q, grad_k, grad_v, gains
):
    output[0] = low_ref[...]
    grad_tokens[0] = grad_ref[...]
    grad_down[...] = down_ref[...].astype(F32)
    width = up_ref.shape[2]
    for i in range(up_ref.shape[0]):
        grad_up[:, i * width : (i + 1) * width] = up_ref[i].astype(F32)
    grad_o[...] = o_ref[...].astype(F32)
    grad_q[...] = q_ref[...].astype(F32)

    @pl.when(pl.program_id(0) == 0)
    def _():
        rows = kv_ref.shape[2] - 16
        for i in range(kv_ref.shape[1]):
            grad_k[i * rows : (i + 1) * rows, :] = kv_ref[0, i, :rows, :].astype(F32)
            grad_v[i * rows : (i + 1) * rows, :] = kv_ref[1, i, :rows, :].astype(F32)
        for i in range(2):
            gains[i] = kv_ref[i, 0, rows:, :].astype(F32)


def results(output, grad_tokens, down_all, up_all, out_all, query_all, kv_all):
    tok, D = output.shape
    F, own_rows, width = up_all.shape
    steps = max(1, own_rows // 256)

    def rows(n, cols):
        return pl.BlockSpec((n // steps, cols), lambda i: (i, 0))

    def whole(*shape):
        return pl.BlockSpec(shape, lambda i: (0,) * len(shape))

    def first(n, cols):
        return pl.BlockSpec((1, n // steps, cols), lambda i: (0, i, 0))

    down_rows = down_all.shape[0]
    shapes = [(down_rows, D), (own_rows, F * width), (own_rows, D), (own_rows, D), (own_rows, HS), (own_rows, HS), (2, 16, HS)]
    out, grad_tokens, down, up, o, q, k, v, gains = pl.pallas_call(
        widen_kernel,
        grid=(steps,),
        out_shape=[jax.ShapeDtypeStruct((1, tok, D), BF), jax.ShapeDtypeStruct((1, tok, D), F32)]
        + [jax.ShapeDtypeStruct(shape, F32) for shape in shapes],
        in_specs=[
            rows(tok, D),
            rows(tok, D),
            rows(down_rows, D),
            pl.BlockSpec((F, own_rows // steps, width), lambda i: (0, i, 0)),
            rows(own_rows, D),
            rows(own_rows, D),
            whole(*kv_all.shape),
        ],
        out_specs=[
            first(tok, D),
            first(tok, D),
            rows(down_rows, D),
            rows(own_rows, F * width),
            rows(own_rows, D),
            rows(own_rows, D),
            whole(own_rows, HS),
            whole(own_rows, HS),
            whole(2, 16, HS),
        ],
        compiler_params=pltpu.CompilerParams(vmem_limit_bytes=LIMIT),
        name="widen",
    )(output, grad_tokens, down_all, up_all, out_all, query_all, kv_all)
    gains = gains[:, : own_rows // HS].reshape(2, own_rows)
    return out, grad_tokens, gains[0], q, k, v, o, gains[1], up, down


def solution(mesh):
    placed = (
        P("fsdp", "seq", None),
        P("fsdp", "seq", None),
        P(),
        P(),
        P("fsdp"),
        P("fsdp", None),
        P("fsdp", None),
        P("fsdp", None),
        P("fsdp", None),
        P("fsdp"),
        P("fsdp", None),
        P("fsdp", None),
    )
    return jax.shard_map(
        local,
        mesh=mesh,
        in_specs=placed,
        out_specs=(
            P("fsdp", "seq", None),
            P("fsdp", "seq", None),
            P("fsdp"),
            P("fsdp", None),
            P("fsdp", None),
            P("fsdp", None),
            P("fsdp", None),
            P("fsdp"),
            P("fsdp", None),
            P("fsdp", None),
        ),
        check_vma=False,
    )
```

```python
import functools
import math
import types

import jax
import jax.numpy as jnp
from jax import lax
from jax.experimental import pallas as pl
from jax.experimental.pallas import tpu as pltpu
from jax.sharding import PartitionSpec as P

H = 8
HS = 128
EPS = 1e-05
NEG = -1e30
LIMIT = 60 * 2**20
CHUNK = 512
BF = jnp.bfloat16
F32 = jnp.float32


def nt(a, b):
    return lax.dot_general(a, b, (((1,), (1,)), ((), ())), preferred_element_type=F32)


def nn(a, b):
    return lax.dot_general(a, b, (((1,), (0,)), ((), ())), preferred_element_type=F32)


def tn(a, b):
    return lax.dot_general(a, b, (((0,), (0,)), ((), ())), preferred_element_type=F32)


def query_range(scal, tok):
    first = scal[0] * tok
    pos = first + lax.broadcasted_iota(jnp.int32, (1, tok), 1)
    start = jnp.zeros((1, tok), jnp.int32)
    latest = jnp.int32(0)
    for i in range(1, scal.shape[0]):
        end = scal[i]
        start = jnp.maximum(start, jnp.where(end <= pos, end, 0))
        latest = jnp.maximum(latest, jnp.where(end <= first + tok - 1, end, 0))
    return first, pos, start, latest


def chunk_loop(scal, tok, window, step):
    first, pos, start, latest = query_range(scal, tok)
    chunks = (first + tok + CHUNK - 1) // CHUNK

    def body(j, carry):
        low = j * CHUNK
        whole = jnp.logical_and(low >= latest, low + CHUNK - 1 <= first)

        @pl.when(whole)
        def _():
            step(j, None)

        @pl.when(jnp.logical_not(whole))
        def _():
            keys = low + lax.broadcasted_iota(jnp.int32, (CHUNK, tok), 0)
            step(j, jnp.logical_and(keys >= start, keys <= pos))

        return carry

    lax.fori_loop(0, chunks, body, 0)
    return chunks


def attend_kernel(scal, q_ref, kv_ref, out_ref, lse_ref, acc, top, total):
    tok = q_ref.shape[0]
    factor = math.log2(math.e) / math.sqrt(HS)
    top[...] = jnp.full(top.shape, -3e38, F32)
    total[...] = jnp.zeros(total.shape, F32)
    acc[...] = jnp.zeros(acc.shape, F32)

    def step(j, mask):
        rows = pl.ds(pl.multiple_of(j * CHUNK, CHUNK), CHUNK)
        keys = kv_ref[rows, :HS]
        values_t = kv_ref[rows, HS:].T
        for h in range(H):
            scores = nt(keys, q_ref[:, h * HS : (h + 1) * HS])
            if mask is not None:
                scores = jnp.where(mask, scores, NEG)
            old = top[h : h + 1, :]
            new = jnp.maximum(old, jnp.max(scores, axis=0, keepdims=True) * factor)
            shrink = jnp.exp2(old - new)
            probs = jnp.exp2(scores * factor - new)
            total[h : h + 1, :] = total[h : h + 1, :] * shrink + jnp.sum(probs, axis=0, keepdims=True)
            acc[h] = acc[h] * shrink + nn(values_t, probs.astype(BF))
            top[h : h + 1, :] = new

    chunk_loop(scal, tok, kv_ref.shape[0], step)
    for h in range(H):
        mixed = acc[h] * (1.0 / total[h : h + 1, :])
        out_ref[:, h * HS : (h + 1) * HS] = mixed.T.astype(BF)
    lse_ref[...] = top[...] + jnp.log2(total[...])


VMEM = pl.BlockSpec(memory_space=pltpu.VMEM)
SMEM = pl.BlockSpec(memory_space=pltpu.SMEM)
PARAMS = pltpu.CompilerParams(vmem_limit_bytes=40 * 2**20)


def attend(scal, queries, window_kv):
    tok = queries.shape[0]
    window = window_kv.shape[0]
    return pl.pallas_call(
        attend_kernel,
        out_shape=(
            jax.ShapeDtypeStruct((tok, H * HS), BF),
            jax.ShapeDtypeStruct((H, tok), F32),
        ),
        in_specs=[SMEM, VMEM, VMEM],
        out_specs=(VMEM, VMEM),
        scratch_shapes=[
            pltpu.VMEM((H, HS, tok), F32),
            pltpu.VMEM((H, tok), F32),
            pltpu.VMEM((H, tok), F32),
        ],
        compiler_params=PARAMS,
        cost_estimate=pl.CostEstimate(
            flops=8 * tok * window * H * HS, bytes_accessed=4 * window * HS, transcendentals=tok * window * H
        ),
        name="attend",
    )(scal, queries, window_kv)


MESH = pl.DeviceIdType.MESH


TAIL_IN = (
    "ends",
    "q_ref",
    "kv_ref",
    "d_ref",
    "att_ref",
    "lse_ref",
    "gd_ref",
    "gu_ref",
    "go_ref",
    "n1_ref",
    "wq_ref",
    "wkv_ref",
    "tok_ref",
    "inv_ref",
    "gain_ref",
    "dres_ref",
    "gain2_ref",
)
TAIL_OUT = (
    "out_down",
    "out_up",
    "out_o",
    "out_q",
    "out_kv",
    "grad_tokens",
)
TAIL_SCRATCH = (
    "acc",
    "delta",
    "dq",
    "dkv",
    "dkv_c",
    "dkv_x",
    "dkv_z",
    "d_kv",
    "dn1",
    "gq_ref",
    "gkv_ref",
    "xr_d",
    "xr_u",
    "zs_d",
    "zs_u",
    "zr_d",
    "zr_u",
    "sh_d",
    "sh_u",
    "yr_u",
    "o_c",
    "o_y",
    "o_x",
    "o_z",
    "o_s",
    "q_c",
    "q_y",
    "q_x",
    "q_z",
    "q_s",
    "kv_c",
    "kv_y",
    "kv_x",
    "kv_z",
    "kv_s",
    "gain_rows",
    "send_sem",
    "recv_sem",
    "copy_sem",
)


def head_block(h, tok):
    return slice(h % 2 * HS, (h % 2 + 1) * HS), slice(h // 2 * tok, (h // 2 + 1) * tok)


def tail_kernel(dims, head, names, *refs):
    A, B, F = dims
    r = types.SimpleNamespace(**dict(zip(names, refs, strict=True)))
    if head is not None:
        for name, held in AGAIN.items():
            setattr(r, name, getattr(r, held))
    ends = r.ends
    q_ref = r.q_ref
    kv_ref = r.kv_ref
    d_ref = r.d_ref
    att_ref = r.att_ref
    lse_ref = r.lse_ref
    gd_ref = r.gd_ref
    gu_ref = r.gu_ref
    go_ref = r.go_ref
    n1_ref = r.n1_ref
    wq_ref = r.wq_ref
    wkv_ref = r.wkv_ref
    tok_ref = r.tok_ref
    inv_ref = r.inv_ref
    gain_ref = r.gain_ref
    dres_ref = r.dres_ref
    gain2_ref = r.gain2_ref
    out_down = r.out_down
    out_up = r.out_up
    out_o = r.out_o
    out_q = r.out_q
    out_kv = r.out_kv
    grad_tokens = r.grad_tokens
    acc = r.acc
    delta = r.delta
    dq = r.dq
    dkv = r.dkv
    dkv_c = r.dkv_c
    dkv_x = r.dkv_x
    dkv_z = r.dkv_z
    d_kv = r.d_kv
    dn1 = r.dn1
    gq_ref = r.gq_ref
    gkv_ref = r.gkv_ref
    xr_d = r.xr_d
    xr_u = r.xr_u
    zs_d = r.zs_d
    zs_u = r.zs_u
    zr_d = r.zr_d
    zr_u = r.zr_u
    sh_d = r.sh_d
    sh_u = r.sh_u
    yr_u = r.yr_u
    o_c = r.o_c
    o_y = r.o_y
    o_x = r.o_x
    o_z = r.o_z
    o_s = r.o_s
    q_c = r.q_c
    q_y = r.q_y
    q_x = r.q_x
    q_z = r.q_z
    q_s = r.q_s
    kv_c = r.kv_c
    kv_y = r.kv_y
    kv_x = r.kv_x
    kv_z = r.kv_z
    kv_s = r.kv_s
    gain_rows = r.gain_rows
    send_sem = r.send_sem
    recv_sem = r.recv_sem
    copy_sem = r.copy_sem
    tok = q_ref.shape[0]
    window = kv_ref.shape[0]
    D = n1_ref.shape[1]
    own_rows = D // F
    shard = gd_ref.shape[0]
    s = lax.axis_index("seq")
    f = lax.axis_index("fsdp")
    c = lax.rem(s, 2)
    b = lax.rem(s // 2, B)
    a = s // (2 * B)

    def device(axis, step):
        at = {"a": a, "b": b, "c": c, "f": f}
        at[axis] = lax.rem(at[axis] + step, {"a": A, "b": B, "c": 2, "f": F}[axis])
        return ((at["a"] * B + at["b"]) * 2 + at["c"], at["f"])

    def lower(axis, step):
        return lax.rem({"a": a + A, "b": b + B, "f": f + F}[axis] - step, {"a": A, "b": B, "f": F}[axis])

    def flip(axis_bit, place=None):
        place = a if place is None else place
        return place + axis_bit - 2 * axis_bit * lax.rem(place // axis_bit, 2) if axis_bit else place

    def offset(o):
        place = a
        for bit in bits:
            if o // bit % 2:
                place = flip(bit, place)
        return place

    def along_a(bit):
        return ((flip(bit) * B + b) * 2 + c, f)

    bits = [2**i for i in range(A.bit_length() - 1)]
    assert 2 ** len(bits) == A
    order = [o for bit in bits for o in range(A) if o // bit % 2 and o % bit == 0] + [0]

    def low_bit(o):
        return next((bit for bit in bits if o // bit % 2), A)

    used = [0]

    def slots(n=1):
        used[0] += n
        assert used[0] <= send_sem.shape[0]
        return used[0] - n

    def remote(src, dst, slot, to):
        return pltpu.make_async_remote_copy(
            src_ref=src, dst_ref=dst, send_sem=send_sem.at[slot], recv_sem=recv_sem.at[slot], device_id=to, device_id_type=MESH
        )

    pending = []

    def start(src, dst, slot, to):
        copy = remote(src, dst, slot, to)
        copy.start()
        pending.append(copy)
        return copy

    barrier = pltpu.get_barrier_semaphore()
    partners = [("a", k) for k in range(1, A)] + [("b", k) for k in range(1, B)] + [("c", 1)] + [("f", k) for k in range(1, F)]
    for axis, k in partners:
        pl.semaphore_signal(barrier, inc=1, device_id=device(axis, k), device_id_type=MESH)
    pl.semaphore_wait(barrier, len(partners))

    r_d = shard // (A * B)
    r_u = own_rows // B
    w_u = shard // A
    x_d = slots(A * (B - 1))
    x_u = slots(A * (B - 1))
    z_d = slots(A - 1)
    z_u = slots(A - 1)

    def down_copies(i):
        at = offset(order[i])
        copies = []
        for kb in range(B - 1):
            other = lax.rem(b + kb + 1, B)
            rows = pl.ds(pl.multiple_of((other * A + at) * r_d, r_d), r_d)
            copies.append(remote(gd_ref.at[rows, :], xr_d.at[kb, i], x_d + kb * A + i, device("b", kb + 1)))
        return copies

    def up_copies(i):
        at = offset(order[i])
        copies = []
        for kb in range(B - 1):
            rows = pl.ds(pl.multiple_of(lax.rem(b + kb + 1, B) * r_u, r_u), r_u)
            cols = pl.ds(pl.multiple_of(at * w_u, w_u), w_u)
            copies.append(remote(gu_ref.at[:, rows, cols], xr_u.at[kb, i], x_u + kb * A + i, device("b", kb + 1)))
        return copies

    def send_down(first, last):
        for i in range(first, last):
            for copy in down_copies(i):
                copy.start()

    def send_up(first, last):
        for i in range(first, last):
            for copy in up_copies(i):
                copy.start()

    def down_sum(i):
        for copy in down_copies(i):
            copy.wait()
        at = offset(order[i])
        rows = pl.ds(pl.multiple_of((b * A + at) * r_d, r_d), r_d)
        total = gd_ref[rows, :].astype(F32)
        for kb in range(B - 1):
            total = total + xr_d[kb, i].astype(F32)
        return total

    def up_sum(i):
        for copy in up_copies(i):
            copy.wait()
        at = offset(order[i])
        rows = pl.ds(pl.multiple_of(b * r_u, r_u), r_u)
        cols = pl.ds(pl.multiple_of(at * w_u, w_u), w_u)
        total = gu_ref[:, rows, cols].astype(F32)
        for kb in range(B - 1):
            total = total + xr_u[kb, i].astype(F32)
        return total

    def z_index(o, bit):
        return order.index(o + bit)

    def down_z(i):
        return remote(zs_d.at[i], zr_d.at[i], z_d + i, along_a(low_bit(order[i])))

    def up_z(i):
        return remote(zs_u.at[i], zr_u.at[i], z_u + i, along_a(low_bit(order[i])))

    def z_added(i, total, copy, got):
        o = order[i]
        for bit in bits:
            if bit < low_bit(o):
                k = z_index(o, bit)
                copy(k).wait()
                total = total + got[k].astype(F32)
        return total

    def down_step(i):
        zs_d[i] = z_added(i, down_sum(i), down_z, zr_d).astype(BF)
        down_z(i).start()

    def up_step(i):
        zs_u[i] = z_added(i, up_sum(i), up_z, zr_u).astype(BF)
        up_z(i).start()

    def down_share():
        sh_d[...] = z_added(A - 1, down_sum(A - 1), down_z, zr_d).astype(BF)
        gather_down.begin()

    up_y = slots(F - 1)

    def up_y_copy(kf):
        return remote(yr_u.at[lax.rem(f + kf + 1, F)], sh_u.at[f], up_y + kf, device("f", kf + 1))

    def up_share():
        total = z_added(A - 1, up_sum(A - 1), up_z, zr_u)
        yr_u[...] = total.astype(BF)
        for kf in range(F - 1):
            up_y_copy(kf).start()
        sh_u[f] = yr_u[f]

    def up_gather():
        for kf in range(F - 1):
            up_y_copy(kf).wait()
        gather_up.begin()

    gathers = []

    class Gather:
        def __init__(self, share, view, planes=True):
            self.share, self.view, self.n = share, view, B if planes else 1
            self.z_slot = slots(A)
            self.x_slot = slots((self.n - 1) * A)
            self.c_slot = slots(self.n * A)
            self.place = len(gathers)
            gathers.append(self)

        def local(self):
            return pltpu.make_async_copy(self.share, self.view(c, b, a), copy_sem.at[self.place])

        def at(self, o, kb=0):
            return self.view(c, lower("b", kb) if kb else b, offset(o))

        def z(self, bit, o):
            here = self.at(o)
            return remote(here if o else self.share, here, self.z_slot + A - A // bit + o // (2 * bit), along_a(bit))

        def x(self, kb, o):
            here = self.at(o)
            return remote(here if o else self.share, here, self.x_slot + kb * A + o, device("b", kb + 1))

        def c(self, kb, o):
            here = self.at(o, kb)
            return remote(here if kb or o else self.share, here, self.c_slot + kb * A + o, device("c", 1))

        def begin(self):
            self.local().start()
            for bit in bits[::-1]:
                self.z(bit, 0).start()
            self.pass_on(0)

        def pass_on(self, o):
            for kb in range(self.n - 1):
                self.x(kb, o).start()
            self.c(0, o).start()

        def from_a(self, stages=None):
            for i, bit in enumerate(bits[::-1]):
                if stages is not None and i not in stages:
                    continue
                for o in range(0, A, 2 * bit):
                    self.z(bit, o).wait_recv()
                    for lower_bit in bits[: len(bits) - 1 - i][::-1]:
                        self.z(lower_bit, o + bit).start()
                    self.pass_on(o + bit)

        def from_b(self):
            for kb in range(self.n - 1):
                for o in self.offsets():
                    self.x(kb, o).wait_recv()
                    self.c(kb + 1, o).start()

        def offsets(self):
            found = [0]
            for bit in bits[::-1]:
                found += [o + bit for o in found]
            return found

        def end(self):
            self.local().wait()
            for bit in bits:
                for o in range(0, A, 2 * bit):
                    self.z(bit, o).wait_send()
            for o in range(A):
                for kb in range(self.n - 1):
                    self.x(kb, o).wait_send()
                for kb in range(self.n):
                    self.c(kb, o).wait()

    def view_down(c_, b_, a_):
        return out_down.at[pl.ds(pl.multiple_of(((c_ * B + b_) * A + a_) * r_d, r_d), r_d), :]

    def view_up(c_, b_, a_):
        rows = pl.ds(pl.multiple_of(b_ * r_u, r_u), r_u)
        return out_up.at[:, rows, pl.ds(pl.multiple_of(c_ * shard + a_ * w_u, w_u), w_u)]

    half = D // 2
    w_o = half // A

    def view_square(out):
        def view(c_, b_, a_):
            rows = pl.ds(pl.multiple_of(b_ * r_u, r_u), r_u)
            return out.at[rows, pl.ds(pl.multiple_of(c_ * half + a_ * w_o, w_o), w_o)]

        return view

    gather_down = Gather(sh_d, view_down)
    gather_up = Gather(sh_u, view_up)
    gather_o = Gather(o_s, view_square(out_o))
    gather_q = Gather(q_s, view_square(out_q))
    gather_kv = Gather(kv_s, lambda c_, b_, a_: out_kv.at[c_, a_], planes=False)

    if head is None:
        send_down(0, A)
        send_up(0, A)
    else:
        own = types.SimpleNamespace(
            A=A, B=B, F=F, a=a, b=b, c=c, f=f, s=s, slots=slots, remote=remote, device=device, lower=lower,
            send_down=send_down, send_up=send_up, down_step=down_step, offset=offset, order=order,
        )
        finish_output, finish_head = head(r, own)

    def reduce_y(ref, got, sent, width):
        mine = pl.ds(pl.multiple_of(c * width, width), width)

        def add(i, carry):
            sent[i] = (ref[i, :, mine].astype(F32) + got[i].astype(F32)).astype(BF)
            return carry

        lax.fori_loop(0, F, add, 0)

    class Square:
        def __init__(self, grad, got_c, got_y, got_x, got_z, share, gather):
            self.grad, self.got_c, self.got_y, self.got_x, self.got_z = grad, got_c, got_y, got_x, got_z
            self.share, self.gather = share, gather
            self.c_slot, self.y_slot, self.x_slot = slots(), slots(F - 1), slots(B - 1)

        def c(self):
            other = pl.ds(pl.multiple_of((1 - c) * half, half), half)
            return remote(self.grad.at[:, :, other], self.got_c, self.c_slot, device("c", 1))

        def y(self, kf):
            return remote(self.got_c.at[lax.rem(f + kf + 1, F)], self.got_y.at[kf], self.y_slot + kf, device("f", kf + 1))

        def over_c(self):
            self.c().start()

        def over_f(self):
            self.c().wait()
            reduce_y(self.grad, self.got_c, self.got_c, half)
            for kf in range(F - 1):
                self.y(kf).start()

        def over_b(self):
            total = self.got_c[f].astype(F32)
            for kf in range(F - 1):
                self.y(kf).wait()
                total = total + self.got_y[kf].astype(F32)
            self.got_y[F - 1] = total.astype(BF)
            for kb in range(B - 1):
                self.x(kb).start()

        def x(self, kb):
            rows = pl.ds(pl.multiple_of(lax.rem(b + kb + 1, B) * r_u, r_u), r_u)
            return remote(self.got_y.at[F - 1, rows, :], self.got_x.at[kb], self.x_slot + kb, device("b", kb + 1))

        def over_a(self):
            rows = pl.ds(pl.multiple_of(b * r_u, r_u), r_u)
            total = self.got_y[F - 1, rows, :].astype(F32)
            for kb in range(B - 1):
                self.x(kb).wait()
                total = total + self.got_x[kb].astype(F32)
            self.got_x[B - 1] = total.astype(BF)
            self.copies = []
            for ka in range(A - 1):
                cols = pl.ds(pl.multiple_of(lax.rem(a + ka + 1, A) * w_o, w_o), w_o)
                self.copies.append(start(self.got_x.at[B - 1, :, cols], self.got_z.at[ka], slots(), device("a", ka + 1)))

        def finish(self):
            cols = pl.ds(pl.multiple_of(a * w_o, w_o), w_o)
            total = self.got_x[B - 1, :, cols].astype(F32)
            for ka in range(A - 1):
                self.copies[ka].wait()
                total = total + self.got_z[ka].astype(F32)
            self.share[...] = total.astype(BF)
            self.gather.begin()

    square_o = Square(go_ref, o_c, o_y, o_x, o_z, o_s, gather_o)
    square_q = Square(gq_ref, q_c, q_y, q_x, q_z, q_s, gather_q)

    square_o.over_c()

    scale = 1.0 / math.sqrt(HS)
    factor = math.log2(math.e) * scale
    acc[...] = jnp.zeros(acc.shape, F32)
    for h in range(H):
        cols = slice(h * HS, (h + 1) * HS)
        both = d_ref[:, cols].astype(F32) * att_ref[:, cols].astype(F32)
        delta[h : h + 1, :] = jnp.sum(both.T, axis=0, keepdims=True)
    first = s * tok
    pos = first + lax.broadcasted_iota(jnp.int32, (1, tok), 1)
    begin = jnp.zeros((1, tok), jnp.int32)
    for i in range(ends.shape[0]):
        begin = jnp.maximum(begin, jnp.where(ends[i] <= pos, ends[i], 0))

    def step(j, masked):
        rows = pl.ds(pl.multiple_of(j * CHUNK, CHUNK), CHUNK)
        keys = kv_ref[rows, :HS]
        values = kv_ref[rows, HS:]
        keys_t = keys.T
        if masked:
            at = j * CHUNK + lax.broadcasted_iota(jnp.int32, (CHUNK, tok), 0)
            mask = jnp.logical_and(at >= begin, at <= pos)
        d_keys = jnp.zeros((CHUNK, HS), F32)
        d_values = jnp.zeros((CHUNK, HS), F32)
        for h in range(H):
            cols = slice(h * HS, (h + 1) * HS)
            q = q_ref[:, cols]
            d = d_ref[:, cols]
            scores = nt(keys, q)
            if masked:
                scores = jnp.where(mask, scores, NEG)
            probs = jnp.exp2(scores * factor - lse_ref[h : h + 1, :])
            d_probs = nt(values, d)
            d_scores = (probs * (d_probs - delta[h : h + 1, :])).astype(BF)
            d_values = d_values + nn(probs.astype(BF), d)
            d_keys = d_keys + nn(d_scores, q)
            acc[head_block(h, tok)] += nn(keys_t, d_scores)
        for i in range(2):
            part = slice(i * tok, (i + 1) * tok)
            dkv[j, i, :, :HS] = (d_keys[part] * scale).astype(BF)
            dkv[j, i, :, HS:] = d_values[part].astype(BF)

    chunks = s // 2 + 1
    def attention_chunk(j, carry):
        plain = jnp.logical_and(jnp.logical_and(j > 0, j < chunks - 1), s < 2 * A * B - 1)

        @pl.when(plain)
        def _():
            step(j, False)

        @pl.when(jnp.logical_not(plain))
        def _():
            step(j, True)

        return carry

    first = 0 if head is None else min(3, A - 1)
    steps = [functools.partial(down_step, i) for i in range(first, A - 1)]
    steps += [functools.partial(up_step, i) for i in range(A - 2)] + [down_share, square_o.over_b]
    if A == 4:
        times = (3, 5, 6, 7) if head is not None else (0, 1, 2, 3, 4, 5, 6)
        at_chunk = dict(zip(times, steps))
        at_chunk[2 if head is not None else 7] = square_o.over_f
    else:
        at_chunk = {0: square_o.over_f, 1: lambda: [step() for step in steps]}

    def chunk_and_step(j, carry):
        @pl.when(j < chunks)
        def _():
            attention_chunk(j, 0)

        for time, act in at_chunk.items():
            pl.when(j == time)(lambda act=act: act() and None)
        return carry

    lax.fori_loop(0, window // CHUNK, chunk_and_step, 0)

    def clear(j, carry):
        dkv[j] = jnp.zeros(dkv.shape[1:], BF)
        return carry

    lax.fori_loop(chunks, window // CHUNK, clear, 0)

    dkv_c_copy = start(dkv.at[:, 1 - c], dkv_c, slots(), device("c", 1))


    if head is not None:
        finish_output()
    for h in range(H):
        dq[:, h * HS : (h + 1) * HS] = (acc[head_block(h, tok)] * scale).T.astype(BF)
    n_rows = 128

    def query_grad(i, carry):
        col = pl.ds(pl.multiple_of(i * n_rows, n_rows), n_rows)
        fi = i // (own_rows // n_rows)
        row = lax.rem(i, own_rows // n_rows) * n_rows
        gq_ref[fi, pl.ds(pl.multiple_of(row, n_rows), n_rows), :] = nn(n1_ref[:, col].T, dq[...]).astype(BF)
        return carry

    lax.fori_loop(0, D // n_rows, query_grad, 0)
    square_q.over_c()

    dkv_c_copy.wait()

    def add_c(j, carry):
        dkv_c[j] = (dkv_c[j].astype(F32) + dkv[j, c].astype(F32)).astype(BF)
        return carry

    lax.fori_loop(0, A * B, add_c, 0)
    x_kv = []
    for kb in range(B - 1):
        other = lax.rem(b + kb + 1, B)
        for j in range(A):
            x_kv.append(start(dkv_c.at[j * B + other], dkv_x.at[kb, j], slots(), device("b", kb + 1)))

    up_step(A - 2)
    square_q.over_f()
    gather_down.from_a((0,))
    up_share()
    square_q.over_b()
    for i in range(1, len(bits)):
        gather_down.from_a((i,))
    square_o.over_a()

    for copy in x_kv:
        copy.wait()

    def add_x(j, carry):
        total = dkv_c[j * B + b].astype(F32)
        for kb in range(B - 1):
            total = total + dkv_x[kb, j].astype(F32)
        dkv_x[0, j] = total.astype(BF)
        return carry

    lax.fori_loop(0, A, add_x, 0)
    z_kv = slots(A - 1)
    for k in range(1, A):

        @pl.when(a - k >= 0)
        def _():
            to = (((a - k) * B + b) * 2 + c, f)
            remote(dkv_x.at[0, jnp.maximum(a - k, 0)], dkv_z.at[k - 1], z_kv + k - 1, to).start()

    up_gather()

    total = dkv_x[0, a].astype(F32)
    d_kv[...] = total
    for k in range(1, A):
        copy = remote(dkv_x.at[0, jnp.maximum(a - k, 0)], dkv_z.at[k - 1], z_kv + k - 1, device("a", A - k))

        @pl.when(a - k >= 0)
        def _():
            copy.wait_send()

        @pl.when(a + k < A)
        def _():
            copy.wait_recv()
            d_kv[...] = d_kv[...] + dkv_z[k - 1].astype(F32)

    d_kv_low = d_kv[...].astype(BF)

    n_cols = 256
    mean = jnp.zeros((tok, 1), F32)
    for i in range(D // n_cols):
        cols = slice(i * n_cols, (i + 1) * n_cols)
        part = nt(dq[...], wq_ref[cols, :]) + nt(d_kv_low, wkv_ref[cols, :])
        dn1[:, cols] = part
        weighted = part * (tok_ref[:, cols].astype(F32) * inv_ref[...])
        gain_rows[0:1, cols] = jnp.sum(weighted, axis=0, keepdims=True)
        mean = mean + jnp.sum(weighted * gain_ref[:, cols], axis=1, keepdims=True)
    if head is None:
        gain_rows[1:2, :] = gain2_ref[...]
    mean = mean * (1.0 / D)

    r_kv = own_rows // A
    rows_kv = r_kv + 16
    for fi in range(F):
        for i in range(A):
            at = fi * own_rows + i * r_kv
            part = tn(n1_ref[:, at : at + r_kv], d_kv_low).astype(BF)
            gkv_ref[0, fi, i, :r_kv, :] = part[:, :HS]
            gkv_ref[1, fi, i, :r_kv, :] = part[:, HS:]
            for ci in range(2):
                rows = [gain_rows[ci : ci + 1, fi * own_rows + k * 128 : fi * own_rows + (k + 1) * 128] for k in range(own_rows // 128)]
                block = jnp.concatenate(rows + [jnp.zeros((16 - len(rows), 128), F32)], axis=0)
                gkv_ref[ci, fi, i, r_kv:, :] = block.astype(BF)
    kv_c_copy = start(gkv_ref.at[1 - c], kv_c, slots(), device("c", 1))

    square_q.over_a()
    for i in range(D // n_cols):
        cols = slice(i * n_cols, (i + 1) * n_cols)
        grad_tokens[:, cols] = dres_ref[:, cols] + inv_ref[...] * (
            dn1[:, cols] * gain_ref[:, cols] - tok_ref[:, cols].astype(F32) * inv_ref[...] * mean
        )
    kv_c_copy.wait()
    kv_c[...] = (kv_c[...].astype(F32) + gkv_ref[c].astype(F32)).astype(BF)
    kv_f = [start(kv_c.at[lax.rem(f + kf + 1, F)], kv_y.at[kf], slots(), device("f", kf + 1)) for kf in range(F - 1)]
    square_o.finish()
    gather_up.from_a((0,))
    total = kv_c[f].astype(F32)
    for kf in range(F - 1):
        kv_f[kf].wait()
        total = total + kv_y[kf].astype(F32)
    kv_y[F - 1] = total.astype(BF)
    kv_b = [start(kv_y.at[F - 1], kv_x.at[kb], slots(), device("b", kb + 1)) for kb in range(B - 1)]
    square_q.finish()
    for i in range(1, len(bits)):
        gather_up.from_a((i,))
    total = kv_y[F - 1].astype(F32)
    for kb in range(B - 1):
        kv_b[kb].wait()
        total = total + kv_x[kb].astype(F32)
    kv_x[B - 1] = total.astype(BF)
    kv_a = [start(kv_x.at[B - 1, lax.rem(a + ka + 1, A)], kv_z.at[ka], slots(), device("a", ka + 1)) for ka in range(A - 1)]
    gather_o.from_a()
    gather_q.from_a((0,))
    total = kv_x[B - 1, a].astype(F32)
    for ka in range(A - 1):
        kv_a[ka].wait()
        total = total + kv_z[ka].astype(F32)
    kv_s[...] = total.astype(BF)
    gather_kv.begin()
    for i in range(1, len(bits)):
        gather_q.from_a((i,))
    gather_down.from_b()
    gather_up.from_b()
    gather_kv.from_a()
    gather_o.from_b()
    gather_q.from_b()
    for gather in gathers:
        gather.end()
    if head is not None:
        finish_head()


def tail_shapes(dims, tok, D, shard, window, extra):
    A, B, F = dims
    own_rows = D // F
    half, r_d, r_u, w_u = D // 2, shard // (A * B), own_rows // B, shard // A
    w_o, r_kv = half // A, own_rows // A + 16

    def low(*shape):
        return pltpu.VMEM(shape, BF)

    square = [low(F, own_rows, half), low(F, own_rows, half), low(B, r_u, half), low(A - 1, r_u, w_o), low(r_u, w_o)]
    n_sems = extra + 2 * (A * (B - 1) + A - 1) + 4 * (A + (B - 1) * A + B * A) + 2 * A
    n_sems += 2 * (F + B + A) + 2 * F + (B - 1) * A + A + F + B + A + 8
    outs = (
        jax.ShapeDtypeStruct((2 * shard, D), BF),
        jax.ShapeDtypeStruct((F, own_rows, 2 * shard), BF),
        jax.ShapeDtypeStruct((own_rows, D), BF),
        jax.ShapeDtypeStruct((own_rows, D), BF),
        jax.ShapeDtypeStruct((2, A, r_kv, HS), BF),
        jax.ShapeDtypeStruct((tok, D), F32),
    )
    scratch = [
        pltpu.VMEM((2 * HS, H // 2 * tok), F32),
        pltpu.VMEM((H, tok), F32),
        low(tok, D),
        low(A * B, 2, tok, 2 * HS),
        low(A * B, tok, 2 * HS),
        low(max(1, B - 1), A, tok, 2 * HS),
        low(max(1, A - 1), tok, 2 * HS),
        pltpu.VMEM((tok, 2 * HS), F32),
        pltpu.VMEM((tok, D), F32),
        low(F, own_rows, D),
        low(2, F, A, r_kv, HS),
        low(B - 1, A, r_d, D),
        low(B - 1, A, F, r_u, w_u),
        low(A - 1, r_d, D),
        low(A - 1, F, r_u, w_u),
        low(A - 1, r_d, D),
        low(A - 1, F, r_u, w_u),
        low(r_d, D),
        low(F, r_u, w_u),
        low(F, r_u, w_u),
        *square,
        *square,
        low(F, A, r_kv, HS),
        low(F, A, r_kv, HS),
        low(B, A, r_kv, HS),
        low(A - 1, r_kv, HS),
        low(r_kv, HS),
        pltpu.VMEM((8, D), F32),
        pltpu.SemaphoreType.DMA((n_sems,)),
        pltpu.SemaphoreType.DMA((n_sems,)),
        pltpu.SemaphoreType.DMA((5,)),
    ]
    return outs, scratch


def tail(dims, ends, queries, window_kv, d_attended, attended, lse, grad_down, grad_up, grad_out, n1, wq, wkv, tokens, inv, gain, dres, gain2):
    A, B, F = dims
    tok, D = n1.shape
    window = window_kv.shape[0]
    outs, scratch = tail_shapes(dims, tok, D, grad_down.shape[0], window, 0)
    hbm = pl.BlockSpec(memory_space=pltpu.HBM)
    return pl.pallas_call(
        functools.partial(tail_kernel, dims, None, TAIL_IN + TAIL_OUT + TAIL_SCRATCH),
        out_shape=outs,
        in_specs=[SMEM] + [VMEM] * 16,
        out_specs=(hbm,) * 5 + (VMEM,),
        scratch_shapes=scratch,
        compiler_params=pltpu.CompilerParams(vmem_limit_bytes=56 * 2**20, collective_id=1, has_side_effects=True),
        cost_estimate=pl.CostEstimate(flops=20 * tok * window * D, bytes_accessed=2**25, transcendentals=tok * window * H),
        name="tail",
    )(ends, queries, window_kv, d_attended, attended, lse, grad_down, grad_up, grad_out, n1, wq, wkv, tokens, inv, gain, dres, gain2)


HEAD_IN = (
    "lengths",
    "groups",
    "tokens",
    "gains_in",
    "wk_in",
    "wv_in",
    "cot_in",
    "wq_in",
    "wo_in",
    "up_in",
    "down_in",
)
HEAD_SCRATCH = (
    "q_ref",
    "kv_ref",
    "d_ref",
    "att_ref",
    "lse_ref",
    "gd_ref",
    "gu_ref",
    "n1_ref",
    "wq_ref",
    "wkv_ref",
    "inv_ref",
    "gain_ref",
    "dres_ref",
    "gain2_ref",
    "wo_ref",
    "up_ref",
    "down_ref",
    "gains_all",
    "cot_all",
    "n2_all",
    "hid_all",
    "dp_all",
    "res_ref",
    "inv2_ref",
    "dbr_ref",
    "back_s",
    "back_c",
    "back_y",
    "back_r",
    "out_s",
    "out_c",
    "out_y",
    "out_r",
    "loc_sem",
    "ends",
)


def head(r, x):
    A, B, F, a, b, c, f, s = x.A, x.B, x.F, x.a, x.b, x.c, x.f, x.s
    slots, remote, device, lower = x.slots, x.remote, x.device, x.lower
    tok, D = r.tokens.shape
    own_rows = D // F
    shard = r.down_ref.shape[0]
    half = own_rows // 2
    sent = []

    def start(src, dst, to, slot=None):
        copy = remote(src, dst, slots() if slot is None else slot, to)
        copy.start()
        sent.append(copy)
        return copy

    def done(copies):
        for copy in copies:
            copy.wait_send()
            sent[:] = [other for other in sent if other is not copy]

    def span(at, n):
        return pl.ds(pl.multiple_of(at, n), n)

    sibling = device("c", 1)
    mine, mine_half = span(f * own_rows, own_rows), span(c * half, half)
    full_half = span((f * 2 + c) * half, half)

    def to_f(src, dst):
        return [start(src(kf), dst(kf), device("f", kf)) for kf in range(1, F)]

    gains_f = to_f(lambda kf: r.gains_in, lambda kf: r.gains_all.at[f])
    wk_f = to_f(lambda kf: r.wk_in.at[mine_half, :], lambda kf: r.wkv_ref.at[full_half, :HS])
    wv_f = to_f(lambda kf: r.wv_in.at[mine_half, :], lambda kf: r.wkv_ref.at[full_half, HS:])
    wq_f = to_f(lambda kf: r.wq_in.at[mine_half, :], lambda kf: r.wq_ref.at[full_half, :])
    part, up_part = half // B, own_rows // B

    def wo_rows(f_, c_, b_):
        return span(((f_ * 2 + c_) * B + b_) * part, part)

    def up_rows(f_, b_):
        return span((f_ * B + b_) * up_part, up_part)

    wo_f = to_f(lambda kf: r.wo_in.at[span((c * B + b) * part, part), :], lambda kf: r.wo_ref.at[wo_rows(f, c, b), :])
    up_f = to_f(
        lambda kf: r.up_in.at[span(b * up_part, up_part), span((lax.rem(f + kf, F) * 2 + c) * shard, shard)],
        lambda kf: r.up_ref.at[up_rows(f, b), :],
    )
    cot_f = to_f(lambda kf: r.cot_in, lambda kf: r.cot_all.at[kf, :tok])
    cot_c = [start(r.cot_in, r.cot_all.at[0, tok:], sibling)]

    local = [
        pltpu.make_async_copy(src, dst, r.loc_sem.at[i])
        for i, (src, dst) in enumerate(
            (
                (r.wq_in, r.wq_ref.at[mine, :]),
                (r.wo_in, r.wo_ref.at[mine, :]),
                (r.up_in.at[:, span((f * 2 + c) * shard, shard)], r.up_ref.at[mine, :]),
                (r.cot_in, r.cot_all.at[0, :tok]),
                (r.down_in.at[span(c * shard, shard), :], r.down_ref),
            )
        )
    ]
    for copy in local:
        copy.start()

    def weight_halves(copies, ref, cols):
        passed = []
        for kf in range(1, F):
            copies[kf - 1].wait_recv()
            rows = span((lower("f", kf) * 2 + c) * half, half)
            passed.append(start(ref.at[rows, cols], ref.at[rows, cols], sibling))
        return passed

    def along_b(copies, ref, rows):
        passed = []
        for kf in range(1, F):
            copies[kf - 1].wait_recv()
            here = ref.at[rows(lower("f", kf)), :]
            passed += [start(here, here, device("b", kb)) for kb in range(1, B)]
        return passed

    group = r.groups[f]
    end = jnp.int32(0)
    for i in range(r.ends.shape[0]):
        end = end + r.lengths[group, i]
        r.ends[i] = end
    n_rows = 64

    def unit_rows(i, carry):
        rows = span(i * n_rows, n_rows)
        stream = r.tokens[rows, :].astype(F32)
        inverse = lax.rsqrt(jnp.mean(stream * stream, axis=1, keepdims=True) + EPS)
        r.inv_ref[rows, :] = inverse
        return carry

    lax.fori_loop(0, tok // n_rows, unit_rows, 0)
    r.wkv_ref[mine, :HS] = r.wk_in[...]
    r.wkv_ref[mine, HS:] = r.wv_in[...]
    r.gains_all[f] = r.gains_in[...]
    for copy in gains_f:
        copy.wait_recv()
    for i in range(F):
        both = r.gains_all[i].astype(F32)
        cols = slice(i * own_rows, (i + 1) * own_rows)
        r.gain_ref[0:1, cols] = both[0:1, :]
        r.gain2_ref[0:1, cols] = both[1:2, :]

    def normed_rows(i, carry):
        rows = span(i * n_rows, n_rows)
        r.n1_ref[rows, :] = (r.tokens[rows, :].astype(F32) * r.inv_ref[rows, :] * r.gain_ref[...]).astype(BF)
        return carry

    lax.fori_loop(0, tok // n_rows, normed_rows, 0)

    wkv_c = weight_halves(wk_f, r.wkv_ref, slice(0, HS)) + weight_halves(wv_f, r.wkv_ref, slice(HS, 2 * HS))
    for copy in wkv_c:
        copy.wait_recv()
    kv = r.kv_ref

    def block(a_, b_, c_):
        return kv.at[span(((a_ * B + b_) * 2 + c_) * tok, tok), :]

    kv[span(s * tok, tok), :] = nn(r.n1_ref[...], r.wkv_ref[...]).astype(BF)
    kv_z, kv_x, kv_c = slots(A - 1), slots((B - 1) * A), slots(B * A)
    own = block(a, b, c)
    z_copies = [remote(own, own, kv_z + k - 1, device("a", k)) for k in range(1, A)]

    def guarded(k, ok, act):
        if k == 0:
            act()
        else:
            pl.when(ok)(act)

    for k in range(1, A):
        guarded(k, a + k < A, z_copies[k - 1].start)

    def x_copy(kb, k):
        here = block(jnp.maximum(a - k, 0), b, c)
        return remote(here, here, kv_x + (kb - 1) * A + k, device("b", kb))

    def c_copy(kb, k):
        here = block(jnp.maximum(a - k, 0), lower("b", kb) if kb else b, c)
        return remote(here, here, kv_c + kb * A + k, sibling)

    def pass_on(k):
        for kb in range(1, B):
            x_copy(kb, k).start()
        c_copy(0, k).start()

    pass_on(0)

    def from_a(k):
        z_copies[k - 1].wait_recv()
        pass_on(k)

    if A > 2:
        guarded(1, a >= 1, functools.partial(from_a, 1))

    local[0].wait()
    wq_c = weight_halves(wq_f, r.wq_ref, slice(0, D))
    for copy in wq_c:
        copy.wait_recv()
    n_cols = 256

    def columns(n, act):
        def body(i, carry):
            act(span(i * n_cols, n_cols))
            return carry

        lax.fori_loop(0, n // n_cols, body, 0)

    def query_cols(cols):
        r.q_ref[:, cols] = nn(r.n1_ref[...], r.wq_ref[:, cols]).astype(BF)

    columns(D, query_cols)

    for k in range(2 if A > 2 else 1, A):
        guarded(k, a - k >= 0, functools.partial(from_a, k))
    wo_b = along_b(wo_f, r.wo_ref, lambda f_: wo_rows(f_, c, b))

    factor = math.log2(math.e) / math.sqrt(HS)
    top, mixed, total = r.dres_ref, r.res_ref, r.acc
    top[...] = jnp.full(top.shape, -3e38, F32)
    mixed[...] = jnp.zeros(mixed.shape, F32)
    total[...] = jnp.zeros(total.shape, F32)
    pos = s * tok + lax.broadcasted_iota(jnp.int32, (tok, 1), 0)
    begin = jnp.zeros((tok, 1), jnp.int32)
    for i in range(r.ends.shape[0]):
        begin = jnp.maximum(begin, jnp.where(r.ends[i] <= pos, r.ends[i], 0))

    def step(j, masked):
        rows = span(j * CHUNK, CHUNK)
        keys = kv[rows, :HS]
        values = jnp.concatenate([kv[rows, HS:], jnp.ones((CHUNK, HS), BF)], axis=1)
        if masked:
            at = j * CHUNK + lax.broadcasted_iota(jnp.int32, (tok, CHUNK), 1)
            mask = jnp.logical_and(at >= begin, at <= pos)
        for h in range(H):
            cols = slice(h * HS, (h + 1) * HS)
            scores = nt(r.q_ref[:, cols], keys)
            if masked:
                scores = jnp.where(mask, scores, NEG)
            old = top[:, cols]
            new = jnp.maximum(old, jnp.max(scores, axis=1, keepdims=True) * factor)
            shrink = jnp.exp2(old - new)
            probs = jnp.exp2(scores * factor - jnp.concatenate([new] * (CHUNK // HS), axis=1))
            both = nn(probs.astype(BF), values)
            mixed[:, cols] = mixed[:, cols] * shrink + both[:, :HS]
            total[:, cols] = total[:, cols] * shrink + both[:, HS:]
            top[:, cols] = new

    last = s // 2
    c_copy(0, 0).wait_recv()
    step(last, True)

    def from_b(k):
        for kb in range(1, B):
            x_copy(kb, k).wait_recv()
            c_copy(kb, k).start()

    def from_c(k):
        for kb in range(B):
            if kb or k:
                c_copy(kb, k).wait_recv()

    wo_c, up_b = [], []
    for kf in range(1, F):
        here = r.wo_ref.at[span((lower("f", kf) * 2 + c) * half, half), :]
        wo_c.append(remote(here, here, slots(), sibling))
        here = r.up_ref.at[up_rows(lower("f", kf), b), :]
        up_b += [remote(here, here, slots(), device("b", kb)) for kb in range(1, B)]
    sent.extend(wo_c + up_b)

    def pass_weights():
        for copy in wo_b:
            copy.wait_recv()
        for copy in wo_c:
            copy.start()
        for copy in up_f:
            copy.wait_recv()
        for copy in up_b:
            copy.start()

    from_b(0)
    guarded(1, a >= 1, functools.partial(from_b, 1))
    from_c(0)

    def begin_group(k):
        for later in range(2, A) if k == 1 else ():
            guarded(later, a - later >= 0, functools.partial(from_b, later))
        from_c(k)
        if k == 2:
            pass_weights()

    def attention_chunk(j, carry):
        plain = jnp.logical_and(j > 0, s < 2 * A * B - 1)

        @pl.when(plain)
        def _():
            step(j, False)

        @pl.when(jnp.logical_not(plain))
        def _():
            step(j, True)

        return carry

    def attention_part(i, carry):
        j = last - 1 - i
        for k in range(1, A):
            pl.when(j == (a - k) * B + B - 1)(functools.partial(begin_group, k))
        return attention_chunk(j, carry)

    lax.fori_loop(0, last, attention_part, 0)
    guarded(1, a < 2, pass_weights)
    for h in range(H):
        cols = slice(h * HS, (h + 1) * HS)
        r.att_ref[:, cols] = (mixed[:, cols] * (1.0 / total[:, cols])).astype(BF)
        r.lse_ref[h : h + 1, :] = (top[:, cols] + jnp.log2(total[:, cols])).T[0:1, :]

    local[1].wait()
    for copy in wo_c:
        copy.wait_recv()
    squares = jnp.zeros((tok, 1), F32)
    for i in range(D // n_cols):
        cols = slice(i * n_cols, (i + 1) * n_cols)
        part = r.tokens[:, cols].astype(F32) + nn(r.att_ref[...], r.wo_ref[:, cols])
        r.res_ref[:, cols] = part
        squares = squares + jnp.sum(part * part, axis=1, keepdims=True)
    r.inv2_ref[...] = lax.rsqrt(squares * (1.0 / D) + EPS)

    def second_norm(i, carry):
        rows = span(i * n_rows, n_rows)
        r.n2_all[0, rows, :] = (r.res_ref[rows, :] * r.inv2_ref[rows, :] * r.gain2_ref[...]).astype(BF)
        return carry

    lax.fori_loop(0, tok // n_rows, second_norm, 0)

    n2_f = to_f(lambda kf: r.n2_all.at[0, :tok], lambda kf: r.n2_all.at[kf, :tok])
    n2_c = [start(r.n2_all.at[0, :tok], r.n2_all.at[0, tok:], sibling)]
    local[2].wait()
    local[3].wait()
    local[4].wait()
    for copy in up_b:
        copy.wait_recv()
    for kf in range(1, F):
        cot_f[kf - 1].wait_recv()
        cot_c.append(start(r.cot_all.at[kf, :tok], r.cot_all.at[kf, tok:], sibling))

    def feed_forward(kf):
        def hidden_cols(cols):
            before = nn(r.n2_all[kf], r.up_ref[:, cols])
            d_hidden = nt(r.cot_all[kf], r.down_ref[cols, :])
            sig = 1.0 / (1.0 + jnp.exp(-before))
            r.hid_all[kf, :, cols] = (before * sig).astype(BF)
            r.dp_all[kf, :, cols] = (d_hidden * sig * (1.0 + before * (1.0 - sig))).astype(BF)

        columns(shard, hidden_cols)

    def back_part(kf):
        def back_cols(cols):
            r.back_s[kf, :, cols] = nt(r.dp_all[kf], r.up_ref[cols, :]).astype(BF)

        columns(D, back_cols)
        return start(r.back_s.at[kf, tok:], r.back_c.at[kf], sibling)

    def out_part(kf):
        def out_cols(cols):
            r.out_s[kf, :, cols] = nn(r.hid_all[kf], r.down_ref[:, cols]).astype(BF)

        columns(D, out_cols)
        return start(r.out_s.at[kf, tok:], r.out_c.at[kf], sibling)

    def chip_sum(kf, part, other, ref):
        def rows_sum(i, carry):
            rows = span(i * n_rows, n_rows)
            ref[kf - 1, rows, :] = (part[kf, rows, :].astype(F32) + other[kf, rows, :].astype(F32)).astype(BF)
            return carry

        lax.fori_loop(0, tok // n_rows, rows_sum, 0)

    n_out = 128

    r_d = shard // (A * B)

    def down_rows(kf, place):
        cols = span(place * r_d, r_d)
        grad = tn(r.hid_all[kf, :, cols], r.cot_all[kf])
        r.gd_ref[cols, :] = (grad + r.gd_ref[cols, :].astype(F32) if kf else grad).astype(BF)

    def down_grad(kf):
        if kf < F - 1:

            def rows_of(i, carry):
                down_rows(kf, i)
                return carry

            lax.fori_loop(0, A * B, rows_of, 0)
            return
        for i in range(A):
            for kb in range(1, B):
                down_rows(kf, lax.rem(b + kb, B) * A + x.offset(x.order[i]))
            x.send_down(i, i + 1)

    def down_grad_own(kf):
        def rows_of(i, carry):
            down_rows(kf, b * A + i)
            return carry

        lax.fori_loop(0, A, rows_of, 0)

    def up_grad(kf):
        def rows_of(i, carry):
            cols = span(i * n_out, n_out)
            rows = span(lax.rem(i, own_rows // n_out) * n_out, n_out)
            at = i // (own_rows // n_out)
            grad = tn(r.n2_all[kf, :, cols], r.dp_all[kf])
            r.gu_ref[at, rows, :] = (grad + r.gu_ref[at, rows, :].astype(F32) if kf else grad).astype(BF)
            return carry

        lax.fori_loop(0, D // n_out, rows_of, 0)

    back_copies, out_copies, back_back, out_back = [None] * F, [None] * F, [], []
    n2_c[0].wait_recv()
    cot_c[0].wait_recv()
    feed_forward(0)
    back_copies[0] = back_part(0)
    down_grad(0)
    up_grad(0)
    for kf in range(1, F):
        n2_f[kf - 1].wait_recv()
        n2_c.append(start(r.n2_all.at[kf, :tok], r.n2_all.at[kf, tok:], sibling))
    for kf in range(1, F):
        n2_c[kf].wait_recv()
        cot_c[kf].wait_recv()
        feed_forward(kf)
        if kf == F - 1:
            down_grad(kf)
        back_copies[kf] = back_part(kf)
        if kf == F - 1:
            down_grad_own(kf)
        back_copies[kf].wait_recv()
        chip_sum(kf, r.back_s, r.back_c, r.back_y)
        back_back.append(start(r.back_y.at[kf - 1], r.back_r.at[kf - 1], device("f", F - kf)))
        if kf < F - 1:
            down_grad(kf)
        up_grad(kf)
        out_copies[kf] = out_part(kf)
    x.send_up(0, A)
    for kf in range(1, F):
        out_copies[kf].wait_recv()
        chip_sum(kf, r.out_s, r.out_c, r.out_y)
        out_back.append(start(r.out_y.at[kf - 1], r.out_r.at[kf - 1], device("f", F - kf)))
    out_copies[0] = out_part(0)
    x.down_step(0)
    if A > 2:
        x.down_step(1)

    back_copies[0].wait_recv()
    for copy in back_back:
        copy.wait_recv()

    def norm_back(i, gain_grad):
        rows = span(i * n_rows, n_rows)
        d_normed = r.back_s[0, rows, :].astype(F32) + r.back_c[0, rows, :].astype(F32)
        for kf in range(1, F):
            d_normed = d_normed + r.back_r[kf - 1, rows, :].astype(F32)
        inverse = r.inv2_ref[rows, :]
        unit = r.res_ref[rows, :] * inverse
        weighted = d_normed * unit
        scaled = d_normed * r.gain2_ref[...]
        mean = jnp.mean(scaled * unit, axis=1, keepdims=True)
        d_residual = r.cot_all[0, rows, :].astype(F32) + inverse * (scaled - unit * mean)
        r.dres_ref[rows, :] = d_residual
        r.dbr_ref[rows, :] = d_residual.astype(BF)
        return gain_grad + jnp.sum(weighted, axis=0, keepdims=True)

    r.gain_rows[1:2, :] = lax.fori_loop(0, tok // n_rows, norm_back, jnp.zeros((1, D), F32))

    def attended_cols(cols):
        r.d_ref[:, cols] = nt(r.dbr_ref[...], r.wo_ref[cols, :]).astype(BF)

    columns(D, attended_cols)

    done(n2_f + n2_c)

    def out_grad(i, carry):
        cols = span(i * n_out, n_out)
        rows = span(lax.rem(i, own_rows // n_out) * n_out, n_out)
        r.go_ref[i // (own_rows // n_out), rows, :] = tn(r.att_ref[:, cols], r.dbr_ref[...]).astype(BF)
        return carry

    lax.fori_loop(0, D // n_out, out_grad, 0)
    if A > 2:
        x.down_step(2)

    def finish_output():
        out_copies[0].wait_recv()
        for copy in out_back:
            copy.wait_recv()

        def output_rows(i, carry):
            rows = span(i * n_rows, n_rows)
            value = r.res_ref[rows, :] + r.out_s[0, rows, :].astype(F32) + r.out_c[0, rows, :].astype(F32)
            for kf in range(1, F):
                value = value + r.out_r[kf - 1, rows, :].astype(F32)
            r.out_ref[rows, :] = value.astype(BF)
            return carry

        lax.fori_loop(0, tok // n_rows, output_rows, 0)
        done(out_copies)
        results[0].start()

    results = [
        pltpu.make_async_copy(src, dst, r.loc_sem.at[5 + i])
        for i, (src, dst) in enumerate(((r.out_ref, r.out_hbm), (r.grad_tokens, r.grad_hbm)))
    ]

    def finish():
        results[1].start()
        for copy in results:
            copy.wait()
        for copy in sent:
            copy.wait_send()
        for k in range(1, A):
            guarded(k, a + k < A, z_copies[k - 1].wait_send)
        for k in range(A):
            for kb in range(B):
                if kb:
                    guarded(k, a - k >= 0, x_copy(kb, k).wait_send)
                guarded(k, a - k >= 0, c_copy(kb, k).wait_send)

    return finish_output, finish


AGAIN = {
    "go_ref": "n2_all",
    "gq_ref": "out_s",
    "dn1": "res_ref",
    "grad_tokens": "res_ref",
    "dq": "d_ref",
    "out_ref": "dbr_ref",
    "tok_ref": "tokens",
}


def layer_shapes(dims, tok, D, shard, window, sequences):
    A, B, F = dims
    own_rows = D // F
    outs, scratch = tail_shapes(dims, tok, D, shard, window, 16 * F + A - 1 + (B - 1) * A + B * A)

    def low(*shape):
        return pltpu.VMEM(shape, BF)

    def wide(*shape):
        return pltpu.VMEM(shape, F32)

    pair = [low(F, 2 * tok, D), low(F, tok, D), low(F - 1, tok, D), low(F - 1, tok, D)]
    first = [
        low(tok, D),
        low(window, 2 * HS),
        low(tok, D),
        low(tok, D),
        wide(H, tok),
        low(shard, D),
        low(F, own_rows, shard),
        low(tok, D),
        low(D, D),
        low(D, 2 * HS),
        wide(tok, 1),
        wide(1, D),
        wide(tok, D),
        wide(1, D),
        low(D, D),
        low(D, shard),
        low(shard, D),
        low(F, 16, own_rows),
        low(F, 2 * tok, D),
        low(F, 2 * tok, D),
        low(F, 2 * tok, shard),
        low(F, 2 * tok, shard),
        wide(tok, D),
        wide(tok, 1),
        low(tok, D),
        *pair,
        *pair,
        pltpu.SemaphoreType.DMA((7,)),
        pltpu.SMEM((sequences,), jnp.int32),
    ]
    sizes = dict(zip(HEAD_SCRATCH + TAIL_SCRATCH, first + scratch))
    fits = all(sizes[k].shape == sizes[AGAIN[k]].shape for k in ("gq_ref", "dn1", "dq")) and tok == 2 * HS and own_rows == 2 * tok
    scratch = [ref for name, ref in zip(TAIL_SCRATCH, scratch) if name not in AGAIN]
    fits = fits and vmem_bytes(first + scratch) + 4 * 2**20 < LIMIT
    return outs + (jax.ShapeDtypeStruct((tok, D), BF),), first + scratch, fits


def vmem_bytes(scratch):
    total = 0
    for ref in scratch:
        shape = getattr(ref, "shape", ())
        if len(shape) >= 2:
            lanes = -(-shape[-1] // 128) * 128
            rows = -(-shape[-2] // 8) * 8
            total += math.prod(shape[:-2]) * rows * lanes * jnp.dtype(ref.dtype).itemsize
    return total


def layer(dims, lengths, groups, tokens, gains, w_key, w_value, cotangent, w_query, w_out, w_up, w_down, outs, scratch):
    tok, D = tokens.shape
    hbm = pl.BlockSpec(memory_space=pltpu.HBM)
    names = HEAD_IN + TAIL_OUT[:5] + ("grad_hbm", "out_hbm") + HEAD_SCRATCH + tuple(n for n in TAIL_SCRATCH if n not in AGAIN)
    return pl.pallas_call(
        functools.partial(tail_kernel, dims, head, names),
        out_shape=outs,
        in_specs=[SMEM] * 2 + [VMEM] * 4 + [hbm] * 5,
        out_specs=(hbm,) * 7,
        scratch_shapes=scratch,
        compiler_params=pltpu.CompilerParams(vmem_limit_bytes=LIMIT, collective_id=2, has_side_effects=True),
        cost_estimate=pl.CostEstimate(flops=2**35, bytes_accessed=2**25, transcendentals=2**24),
        name="layer",
    )(lengths, groups, tokens, gains, w_key, w_value, cotangent, w_query, w_out, w_up, w_down)


def after(value, *others):
    return lax.optimization_barrier((value, *others))[0]


class Grid:
    def __init__(self):
        seq = lax.axis_size("seq")
        self.F = lax.axis_size("fsdp")
        self.C = 2
        chips = seq // 2
        self.B = 2 if chips == 8 else chips // 2
        self.A = chips // self.B
        self.s = lax.axis_index("seq")
        self.f = lax.axis_index("fsdp")
        self.c = self.s % 2
        self.b = self.s // 2 % self.B
        self.a = self.s // (2 * self.B)

    def size(self, axis):
        return {"a": self.A, "b": self.B, "c": self.C, "f": self.F}[axis]

    def place(self, axis):
        return {"a": self.a, "b": self.b, "c": self.c, "f": self.f}[axis]

    def send(self, value, axis, step, upward=False):
        pairs = []
        for a in range(self.A):
            for b in range(self.B):
                for c in range(2):
                    for f in range(self.F):
                        at = {"a": a, "b": b, "c": c, "f": f}
                        to = dict(at)
                        to[axis] += step
                        if upward and not 0 <= to[axis] < self.size(axis):
                            continue
                        to[axis] %= self.size(axis)
                        line = [((d["a"] * self.B + d["b"]) * 2 + d["c"]) * self.F + d["f"] for d in (at, to)]
                        pairs.append(tuple(line))
        return lax.ppermute(value, ("seq", "fsdp"), pairs)

    def stack(self, parts, axis):
        n, me = len(parts), self.place(axis)
        if n == 2:
            low = me == 0
            return jnp.stack([jnp.where(low, parts[0], parts[1]), jnp.where(low, parts[1], parts[0])])
        twice = jnp.stack(parts + parts)
        return lax.dynamic_slice_in_dim(twice, (n - me) % n, n, 0)

    def gather(self, value, axis):
        n = self.size(axis)
        return self.stack([value] + [self.send(value, axis, -k) for k in range(1, n)], axis)

    def scatter(self, parts, axis):
        n, me = self.size(axis), self.place(axis)

        def pick(k):
            return lax.dynamic_index_in_dim(parts, (me + k) % n, 0, keepdims=False)

        got = [self.send(pick(k).astype(BF), axis, k) for k in range(1, n)]
        total = pick(0).astype(F32)
        for piece in got:
            total = total + piece.astype(F32)
        return total

    def plane_sum(self, parts):
        half = self.scatter(parts, "b").astype(BF)
        return self.scatter(half, "a")

    def plane_gather(self, share):
        rows = self.gather(share.astype(BF), "a")
        return self.gather(rows, "b")


def local(
    tokens,
    cotangent,
    seq_lengths,
    group_of_shard,
    gain_attn,
    w_query,
    w_key,
    w_value,
    w_out,
    gain_ffn,
    w_up,
    w_down,
):
    g = Grid()
    A, B, C, F = g.A, g.B, g.C, g.F
    tok, D = tokens.shape[1:]
    FF = w_up.shape[1]
    own_rows = D // F
    seq_parts = A * B * C
    shard = FF // (2 * F)

    outs, scratch, fits = layer_shapes((A, B, F), tok, D, shard, seq_parts * tok, seq_lengths.shape[1])
    if fits:
        row = lax.broadcasted_iota(jnp.int32, (16, own_rows), 0)
        gains = jnp.where(row == 0, gain_attn[None], gain_ffn[None])
        *grads, grad_tokens, output = layer(
            (A, B, F),
            seq_lengths,
            group_of_shard,
            tokens[0],
            gains,
            w_key,
            w_value,
            cotangent[0],
            w_query,
            w_out,
            w_up,
            w_down,
            outs,
            scratch,
        )
        return results(output, grad_tokens, *grads)

    group = lax.dynamic_index_in_dim(group_of_shard, g.f, 0, keepdims=False)
    lengths = lax.dynamic_index_in_dim(seq_lengths, group, 0, keepdims=False)
    running, ends = jnp.int32(0), []
    for i in range(seq_lengths.shape[1]):
        running = running + lengths[i]
        ends.append(running)
    scal = jnp.stack([g.s.astype(jnp.int32), *ends])

    gains = jnp.stack([gain_attn, gain_ffn])
    full_gains = g.gather(gains, "f").transpose(1, 0, 2).reshape(2, D).astype(F32)
    gain_first, gain_second = full_gains[0], full_gains[1]
    own_kv = jnp.concatenate([w_key, w_value], axis=1)
    full_kv = g.gather(own_kv, "f").reshape(D, 2 * HS)

    def gather_weight(weight, *late):
        half = own_rows // 2
        mine = lax.dynamic_slice_in_dim(weight, g.c * half, half, 0)
        if late:
            mine = after(mine, *late)
        pieces = [g.gather(g.send(mine, "f", -k), "c").reshape(weight.shape) for k in range(1, F)]
        return g.stack([weight] + pieces, "f").reshape(F * own_rows, -1)

    full_query = gather_weight(w_query)

    stream = tokens[0].astype(F32)
    inverse_first = lax.rsqrt(jnp.mean(stream * stream, axis=1, keepdims=True) + EPS)
    unit_first = stream * inverse_first
    normed_first = (unit_first * gain_first).astype(BF)
    key_value = nn(normed_first, full_kv).astype(BF)
    queries = nn(normed_first, full_query).astype(BF)

    column = [key_value] + [g.send(key_value, "a", k, upward=True) for k in range(1, A)]
    twice = jnp.stack(column[::-1] + column[::-1])
    column = lax.dynamic_slice_in_dim(twice, A - 1 - g.a, A, 0)
    plane = g.gather(column, "b")
    whole = g.gather(plane, "c")
    window_kv = whole.transpose(2, 1, 0, 3, 4).reshape(seq_parts * tok, 2 * HS)

    full_out = gather_weight(w_out, full_query)
    upstream = cotangent[0]
    cot = []
    for k in range(F):
        mine = upstream if k == 0 else g.send(after(upstream, full_query), "f", k)
        cot.append(jnp.concatenate([mine, g.send(mine, "c", 1)], axis=0))
    ups = w_up.reshape(own_rows, F, 2, shard)
    up_parts = []
    for k in range(F):
        block = lax.dynamic_slice(ups, (0, (g.f + k) % F, g.c, 0), (own_rows, 1, 1, shard)).reshape(own_rows, shard)
        up_parts.append(block if k == 0 else g.send(after(block, full_out), "f", k))
    up_parts = [up_parts[0]] + up_parts[1:][::-1]
    up = g.stack(up_parts, "f").reshape(D, shard)
    down = lax.dynamic_slice_in_dim(w_down, g.c * shard, shard, 0)

    attended, lse = attend(scal, queries, window_kv)

    residual = stream + nn(attended, full_out)
    inverse_second = lax.rsqrt(jnp.mean(residual * residual, axis=1, keepdims=True) + EPS)
    unit_second = residual * inverse_second
    normed_second = (unit_second * gain_second).astype(BF)

    out_sum, back_sum = residual, jnp.zeros((tok, D), F32)
    hiddens, d_pres, norms = [], [], []
    backs, outs = [], []
    for k in range(F):
        mine = normed_second if k == 0 else g.send(normed_second, "f", k)
        norm = jnp.concatenate([mine, g.send(mine, "c", 1)], axis=0)
        before = nn(norm, up)
        d_hidden = nt(cot[k], down)
        sig = jax.nn.sigmoid(before)
        hidden = (before * sig).astype(BF)
        d_pre = (d_hidden * sig * (1.0 + before * (1.0 - sig))).astype(BF)
        back = nt(d_pre, up)
        out = nn(hidden, down)
        hiddens.append(hidden)
        d_pres.append(d_pre)
        norms.append(norm)
        backs.append(back)
        outs.append(out)

    def give_back(parts):
        total = 0.0
        for k, part in enumerate(parts):
            other = g.send(part[tok:].astype(BF), "c", 1)
            chip = part[:tok] + other.astype(F32)
            if k:
                chip = g.send(chip.astype(BF), "f", -k).astype(F32)
            total = total + chip
        return total

    d_normed_second = give_back(backs)
    output = (residual + give_back(outs)).astype(BF)

    grad_down = sum(tn(h, c) for h, c in zip(hiddens, cot)).astype(BF)
    grad_up = sum(tn(n, d) for n, d in zip(norms, d_pres)).astype(BF)

    def norm_back(gradient, unit_rows, inverse, gain_vec):
        scaled = gradient * gain_vec
        gain_grad = jnp.sum(gradient * unit_rows, axis=0)
        return gain_grad, inverse * (scaled - unit_rows * jnp.mean(scaled * unit_rows, axis=1, keepdims=True))

    gain_second_grad, d_from_norm = norm_back(d_normed_second, unit_second, inverse_second, gain_second)
    d_residual = upstream.astype(F32) + d_from_norm
    d_branch = d_residual.astype(BF)
    d_attended = nt(d_branch, full_out).astype(BF)
    grad_out = tn(attended, d_branch).astype(BF)

    down_all, up_all, out_all, query_all, kv_all, grad_tokens = tail(
        (A, B, F),
        scal[1:],
        queries,
        window_kv,
        d_attended,
        attended,
        lse,
        grad_down,
        grad_up.reshape(F, own_rows, shard),
        grad_out.reshape(F, own_rows, D),
        normed_first,
        full_query,
        full_kv,
        tokens[0],
        inverse_first,
        gain_first[None],
        d_residual,
        gain_second_grad[None],
    )
    return results(output, grad_tokens, down_all, up_all, out_all, query_all, kv_all)


def widen_kernel(
    low_ref, grad_ref, down_ref, up_ref, o_ref, q_ref, kv_ref, output, grad_tokens, grad_down, grad_up, grad_o, grad_q, grad_k, grad_v, gains
):
    output[0] = low_ref[...]
    grad_tokens[0] = grad_ref[...]
    grad_down[...] = down_ref[...].astype(F32)
    width = up_ref.shape[2]
    for i in range(up_ref.shape[0]):
        grad_up[:, i * width : (i + 1) * width] = up_ref[i].astype(F32)
    grad_o[...] = o_ref[...].astype(F32)
    grad_q[...] = q_ref[...].astype(F32)

    @pl.when(pl.program_id(0) == 0)
    def _():
        rows = kv_ref.shape[2] - 16
        for i in range(kv_ref.shape[1]):
            grad_k[i * rows : (i + 1) * rows, :] = kv_ref[0, i, :rows, :].astype(F32)
            grad_v[i * rows : (i + 1) * rows, :] = kv_ref[1, i, :rows, :].astype(F32)
        for i in range(2):
            gains[i] = kv_ref[i, 0, rows:, :].astype(F32)


def results(output, grad_tokens, down_all, up_all, out_all, query_all, kv_all):
    tok, D = output.shape
    F, own_rows, width = up_all.shape
    steps = max(1, own_rows // 256)

    def rows(n, cols):
        return pl.BlockSpec((n // steps, cols), lambda i: (i, 0))

    def whole(*shape):
        return pl.BlockSpec(shape, lambda i: (0,) * len(shape))

    def first(n, cols):
        return pl.BlockSpec((1, n // steps, cols), lambda i: (0, i, 0))

    down_rows = down_all.shape[0]
    shapes = [(down_rows, D), (own_rows, F * width), (own_rows, D), (own_rows, D), (own_rows, HS), (own_rows, HS), (2, 16, HS)]
    out, grad_tokens, down, up, o, q, k, v, gains = pl.pallas_call(
        widen_kernel,
        grid=(steps,),
        out_shape=[jax.ShapeDtypeStruct((1, tok, D), BF), jax.ShapeDtypeStruct((1, tok, D), F32)]
        + [jax.ShapeDtypeStruct(shape, F32) for shape in shapes],
        in_specs=[
            rows(tok, D),
            rows(tok, D),
            rows(down_rows, D),
            pl.BlockSpec((F, own_rows // steps, width), lambda i: (0, i, 0)),
            rows(own_rows, D),
            rows(own_rows, D),
            whole(*kv_all.shape),
        ],
        out_specs=[
            first(tok, D),
            first(tok, D),
            rows(down_rows, D),
            rows(own_rows, F * width),
            rows(own_rows, D),
            rows(own_rows, D),
            whole(own_rows, HS),
            whole(own_rows, HS),
            whole(2, 16, HS),
        ],
        compiler_params=pltpu.CompilerParams(vmem_limit_bytes=LIMIT),
        name="widen",
    )(output, grad_tokens, down_all, up_all, out_all, query_all, kv_all)
    gains = gains[:, : own_rows // HS].reshape(2, own_rows)
    return out, grad_tokens, gains[0], q, k, v, o, gains[1], up, down


def solution(mesh):
    placed = (
        P("fsdp", "seq", None),
        P("fsdp", "seq", None),
        P(),
        P(),
        P("fsdp"),
        P("fsdp", None),
        P("fsdp", None),
        P("fsdp", None),
        P("fsdp", None),
        P("fsdp"),
        P("fsdp", None),
        P("fsdp", None),
    )
    return jax.shard_map(
        local,
        mesh=mesh,
        in_specs=placed,
        out_specs=(
            P("fsdp", "seq", None),
            P("fsdp", "seq", None),
            P("fsdp"),
            P("fsdp", None),
            P("fsdp", None),
            P("fsdp", None),
            P("fsdp", None),
            P("fsdp"),
            P("fsdp", None),
            P("fsdp", None),
        ),
        check_vma=False,
    )
```

```python
import functools
import math
import types

import jax
import jax.numpy as jnp
from jax import lax
from jax.experimental import pallas as pl
from jax.experimental.pallas import tpu as pltpu
from jax.sharding import PartitionSpec as P

H = 8
HS = 128
EPS = 1e-05
NEG = -1e30
LIMIT = 60 * 2**20
CHUNK = 512
BF = jnp.bfloat16
F32 = jnp.float32


def nt(a, b):
    return lax.dot_general(a, b, (((1,), (1,)), ((), ())), preferred_element_type=F32)


def nn(a, b):
    return lax.dot_general(a, b, (((1,), (0,)), ((), ())), preferred_element_type=F32)


def tn(a, b):
    return lax.dot_general(a, b, (((0,), (0,)), ((), ())), preferred_element_type=F32)


def query_range(scal, tok):
    first = scal[0] * tok
    pos = first + lax.broadcasted_iota(jnp.int32, (1, tok), 1)
    start = jnp.zeros((1, tok), jnp.int32)
    latest = jnp.int32(0)
    for i in range(1, scal.shape[0]):
        end = scal[i]
        start = jnp.maximum(start, jnp.where(end <= pos, end, 0))
        latest = jnp.maximum(latest, jnp.where(end <= first + tok - 1, end, 0))
    return first, pos, start, latest


def chunk_loop(scal, tok, window, step):
    first, pos, start, latest = query_range(scal, tok)
    chunks = (first + tok + CHUNK - 1) // CHUNK

    def body(j, carry):
        low = j * CHUNK
        whole = jnp.logical_and(low >= latest, low + CHUNK - 1 <= first)

        @pl.when(whole)
        def _():
            step(j, None)

        @pl.when(jnp.logical_not(whole))
        def _():
            keys = low + lax.broadcasted_iota(jnp.int32, (CHUNK, tok), 0)
            step(j, jnp.logical_and(keys >= start, keys <= pos))

        return carry

    lax.fori_loop(0, chunks, body, 0)
    return chunks


def attend_kernel(scal, q_ref, kv_ref, out_ref, lse_ref, acc, top, total):
    tok = q_ref.shape[0]
    factor = math.log2(math.e) / math.sqrt(HS)
    top[...] = jnp.full(top.shape, -3e38, F32)
    total[...] = jnp.zeros(total.shape, F32)
    acc[...] = jnp.zeros(acc.shape, F32)

    def step(j, mask):
        rows = pl.ds(pl.multiple_of(j * CHUNK, CHUNK), CHUNK)
        keys = kv_ref[rows, :HS]
        values_t = kv_ref[rows, HS:].T
        for h in range(H):
            scores = nt(keys, q_ref[:, h * HS : (h + 1) * HS])
            if mask is not None:
                scores = jnp.where(mask, scores, NEG)
            old = top[h : h + 1, :]
            new = jnp.maximum(old, jnp.max(scores, axis=0, keepdims=True) * factor)
            shrink = jnp.exp2(old - new)
            probs = jnp.exp2(scores * factor - new)
            total[h : h + 1, :] = total[h : h + 1, :] * shrink + jnp.sum(probs, axis=0, keepdims=True)
            acc[h] = acc[h] * shrink + nn(values_t, probs.astype(BF))
            top[h : h + 1, :] = new

    chunk_loop(scal, tok, kv_ref.shape[0], step)
    for h in range(H):
        mixed = acc[h] * (1.0 / total[h : h + 1, :])
        out_ref[:, h * HS : (h + 1) * HS] = mixed.T.astype(BF)
    lse_ref[...] = top[...] + jnp.log2(total[...])


VMEM = pl.BlockSpec(memory_space=pltpu.VMEM)
SMEM = pl.BlockSpec(memory_space=pltpu.SMEM)
PARAMS = pltpu.CompilerParams(vmem_limit_bytes=40 * 2**20)


def attend(scal, queries, window_kv):
    tok = queries.shape[0]
    window = window_kv.shape[0]
    return pl.pallas_call(
        attend_kernel,
        out_shape=(
            jax.ShapeDtypeStruct((tok, H * HS), BF),
            jax.ShapeDtypeStruct((H, tok), F32),
        ),
        in_specs=[SMEM, VMEM, VMEM],
        out_specs=(VMEM, VMEM),
        scratch_shapes=[
            pltpu.VMEM((H, HS, tok), F32),
            pltpu.VMEM((H, tok), F32),
            pltpu.VMEM((H, tok), F32),
        ],
        compiler_params=PARAMS,
        cost_estimate=pl.CostEstimate(
            flops=8 * tok * window * H * HS, bytes_accessed=4 * window * HS, transcendentals=tok * window * H
        ),
        name="attend",
    )(scal, queries, window_kv)


MESH = pl.DeviceIdType.MESH


TAIL_IN = (
    "ends",
    "q_ref",
    "kv_ref",
    "d_ref",
    "att_ref",
    "lse_ref",
    "gd_ref",
    "gu_ref",
    "go_ref",
    "n1_ref",
    "wq_ref",
    "wkv_ref",
    "tok_ref",
    "inv_ref",
    "gain_ref",
    "dres_ref",
    "gain2_ref",
)
TAIL_OUT = (
    "out_down",
    "out_up",
    "out_o",
    "out_q",
    "out_kv",
    "grad_tokens",
)
TAIL_SCRATCH = (
    "acc",
    "delta",
    "dq",
    "dkv",
    "dkv_c",
    "dkv_x",
    "dkv_z",
    "d_kv",
    "dn1",
    "gq_ref",
    "gkv_ref",
    "xr_d",
    "xr_u",
    "zs_d",
    "zs_u",
    "zr_d",
    "zr_u",
    "sh_d",
    "sh_u",
    "yr_u",
    "o_c",
    "o_y",
    "o_x",
    "o_z",
    "o_s",
    "q_c",
    "q_y",
    "q_x",
    "q_z",
    "q_s",
    "kv_c",
    "kv_y",
    "kv_x",
    "kv_z",
    "kv_s",
    "gain_rows",
    "send_sem",
    "recv_sem",
    "copy_sem",
)


def head_block(h, tok):
    return slice(h % 2 * HS, (h % 2 + 1) * HS), slice(h // 2 * tok, (h // 2 + 1) * tok)


def tail_kernel(dims, head, names, *refs):
    A, B, F = dims
    r = types.SimpleNamespace(**dict(zip(names, refs, strict=True)))
    if head is not None:
        for name, held in AGAIN.items():
            setattr(r, name, getattr(r, held))
    ends = r.ends
    q_ref = r.q_ref
    kv_ref = r.kv_ref
    d_ref = r.d_ref
    att_ref = r.att_ref
    lse_ref = r.lse_ref
    gd_ref = r.gd_ref
    gu_ref = r.gu_ref
    go_ref = r.go_ref
    n1_ref = r.n1_ref
    wq_ref = r.wq_ref
    wkv_ref = r.wkv_ref
    tok_ref = r.tok_ref
    inv_ref = r.inv_ref
    gain_ref = r.gain_ref
    dres_ref = r.dres_ref
    gain2_ref = r.gain2_ref
    out_down = r.out_down
    out_up = r.out_up
    out_o = r.out_o
    out_q = r.out_q
    out_kv = r.out_kv
    grad_tokens = r.grad_tokens
    acc = r.acc
    delta = r.delta
    dq = r.dq
    dkv = r.dkv
    dkv_c = r.dkv_c
    dkv_x = r.dkv_x
    dkv_z = r.dkv_z
    d_kv = r.d_kv
    dn1 = r.dn1
    gq_ref = r.gq_ref
    gkv_ref = r.gkv_ref
    xr_d = r.xr_d
    xr_u = r.xr_u
    zs_d = r.zs_d
    zs_u = r.zs_u
    zr_d = r.zr_d
    zr_u = r.zr_u
    sh_d = r.sh_d
    sh_u = r.sh_u
    yr_u = r.yr_u
    o_c = r.o_c
    o_y = r.o_y
    o_x = r.o_x
    o_z = r.o_z
    o_s = r.o_s
    q_c = r.q_c
    q_y = r.q_y
    q_x = r.q_x
    q_z = r.q_z
    q_s = r.q_s
    kv_c = r.kv_c
    kv_y = r.kv_y
    kv_x = r.kv_x
    kv_z = r.kv_z
    kv_s = r.kv_s
    gain_rows = r.gain_rows
    send_sem = r.send_sem
    recv_sem = r.recv_sem
    copy_sem = r.copy_sem
    tok = q_ref.shape[0]
    window = kv_ref.shape[0]
    D = n1_ref.shape[1]
    own_rows = D // F
    shard = gd_ref.shape[0]
    s = lax.axis_index("seq")
    f = lax.axis_index("fsdp")
    c = lax.rem(s, 2)
    b = lax.rem(s // 2, B)
    a = s // (2 * B)

    def device(axis, step):
        at = {"a": a, "b": b, "c": c, "f": f}
        at[axis] = lax.rem(at[axis] + step, {"a": A, "b": B, "c": 2, "f": F}[axis])
        return ((at["a"] * B + at["b"]) * 2 + at["c"], at["f"])

    def lower(axis, step):
        return lax.rem({"a": a + A, "b": b + B, "f": f + F}[axis] - step, {"a": A, "b": B, "f": F}[axis])

    def flip(axis_bit, place=None):
        place = a if place is None else place
        return place + axis_bit - 2 * axis_bit * lax.rem(place // axis_bit, 2) if axis_bit else place

    def offset(o):
        place = a
        for bit in bits:
            if o // bit % 2:
                place = flip(bit, place)
        return place

    def along_a(bit):
        return ((flip(bit) * B + b) * 2 + c, f)

    bits = [2**i for i in range(A.bit_length() - 1)]
    assert 2 ** len(bits) == A
    order = [o for bit in bits for o in range(A) if o // bit % 2 and o % bit == 0] + [0]

    def low_bit(o):
        return next((bit for bit in bits if o // bit % 2), A)

    used = [0]

    def slots(n=1):
        used[0] += n
        assert used[0] <= send_sem.shape[0]
        return used[0] - n

    def remote(src, dst, slot, to):
        return pltpu.make_async_remote_copy(
            src_ref=src, dst_ref=dst, send_sem=send_sem.at[slot], recv_sem=recv_sem.at[slot], device_id=to, device_id_type=MESH
        )

    pending = []

    def start(src, dst, slot, to):
        copy = remote(src, dst, slot, to)
        copy.start()
        pending.append(copy)
        return copy

    barrier = pltpu.get_barrier_semaphore()
    partners = [("a", k) for k in range(1, A)] + [("b", k) for k in range(1, B)] + [("c", 1)] + [("f", k) for k in range(1, F)]
    for axis, k in partners:
        pl.semaphore_signal(barrier, inc=1, device_id=device(axis, k), device_id_type=MESH)
    pl.semaphore_wait(barrier, len(partners))

    r_d = shard // (A * B)
    r_u = own_rows // B
    w_u = shard // A
    x_d = slots(A * (B - 1))
    x_u = slots(A * (B - 1))
    z_d = slots(A - 1)
    z_u = slots(A - 1)

    def down_copies(i):
        at = offset(order[i])
        copies = []
        for kb in range(B - 1):
            other = lax.rem(b + kb + 1, B)
            rows = pl.ds(pl.multiple_of((other * A + at) * r_d, r_d), r_d)
            copies.append(remote(gd_ref.at[rows, :], xr_d.at[kb, i], x_d + kb * A + i, device("b", kb + 1)))
        return copies

    def up_copies(i):
        at = offset(order[i])
        copies = []
        for kb in range(B - 1):
            rows = pl.ds(pl.multiple_of(lax.rem(b + kb + 1, B) * r_u, r_u), r_u)
            cols = pl.ds(pl.multiple_of(at * w_u, w_u), w_u)
            copies.append(remote(gu_ref.at[:, rows, cols], xr_u.at[kb, i], x_u + kb * A + i, device("b", kb + 1)))
        return copies

    def send_down(first, last):
        for i in range(first, last):
            for copy in down_copies(i):
                copy.start()

    def send_up(first, last):
        for i in range(first, last):
            for copy in up_copies(i):
                copy.start()

    def down_sum(i):
        for copy in down_copies(i):
            copy.wait()
        at = offset(order[i])
        rows = pl.ds(pl.multiple_of((b * A + at) * r_d, r_d), r_d)
        total = gd_ref[rows, :].astype(F32)
        for kb in range(B - 1):
            total = total + xr_d[kb, i].astype(F32)
        return total

    def up_sum(i):
        for copy in up_copies(i):
            copy.wait()
        at = offset(order[i])
        rows = pl.ds(pl.multiple_of(b * r_u, r_u), r_u)
        cols = pl.ds(pl.multiple_of(at * w_u, w_u), w_u)
        total = gu_ref[:, rows, cols].astype(F32)
        for kb in range(B - 1):
            total = total + xr_u[kb, i].astype(F32)
        return total

    def z_index(o, bit):
        return order.index(o + bit)

    def down_z(i):
        return remote(zs_d.at[i], zr_d.at[i], z_d + i, along_a(low_bit(order[i])))

    def up_z(i):
        return remote(zs_u.at[i], zr_u.at[i], z_u + i, along_a(low_bit(order[i])))

    def z_added(i, total, copy, got):
        o = order[i]
        for bit in bits:
            if bit < low_bit(o):
                k = z_index(o, bit)
                copy(k).wait()
                total = total + got[k].astype(F32)
        return total

    def down_step(i):
        zs_d[i] = z_added(i, down_sum(i), down_z, zr_d).astype(BF)
        down_z(i).start()

    def up_step(i):
        zs_u[i] = z_added(i, up_sum(i), up_z, zr_u).astype(BF)
        up_z(i).start()

    def down_share():
        sh_d[...] = z_added(A - 1, down_sum(A - 1), down_z, zr_d).astype(BF)
        gather_down.begin()

    up_y = slots(F - 1)

    def up_y_copy(kf):
        return remote(yr_u.at[lax.rem(f + kf + 1, F)], sh_u.at[f], up_y + kf, device("f", kf + 1))

    def up_share():
        total = z_added(A - 1, up_sum(A - 1), up_z, zr_u)
        yr_u[...] = total.astype(BF)
        for kf in range(F - 1):
            up_y_copy(kf).start()
        sh_u[f] = yr_u[f]

    def up_gather():
        for kf in range(F - 1):
            up_y_copy(kf).wait()
        gather_up.begin()

    gathers = []

    class Gather:
        def __init__(self, share, view, planes=True):
            self.share, self.view, self.n = share, view, B if planes else 1
            self.z_slot = slots(A)
            self.x_slot = slots((self.n - 1) * A)
            self.c_slot = slots(self.n * A)
            self.place = len(gathers)
            gathers.append(self)

        def local(self):
            return pltpu.make_async_copy(self.share, self.view(c, b, a), copy_sem.at[self.place])

        def at(self, o, kb=0):
            return self.view(c, lower("b", kb) if kb else b, offset(o))

        def z(self, bit, o):
            here = self.at(o)
            return remote(here if o else self.share, here, self.z_slot + A - A // bit + o // (2 * bit), along_a(bit))

        def x(self, kb, o):
            here = self.at(o)
            return remote(here if o else self.share, here, self.x_slot + kb * A + o, device("b", kb + 1))

        def c(self, kb, o):
            here = self.at(o, kb)
            return remote(here if kb or o else self.share, here, self.c_slot + kb * A + o, device("c", 1))

        def begin(self):
            self.local().start()
            for bit in bits[::-1]:
                self.z(bit, 0).start()
            self.pass_on(0)

        def pass_on(self, o):
            for kb in range(self.n - 1):
                self.x(kb, o).start()
            self.c(0, o).start()

        def from_a(self, stages=None):
            for i, bit in enumerate(bits[::-1]):
                if stages is not None and i not in stages:
                    continue
                for o in range(0, A, 2 * bit):
                    self.z(bit, o).wait_recv()
                    for lower_bit in bits[: len(bits) - 1 - i][::-1]:
                        self.z(lower_bit, o + bit).start()
                    self.pass_on(o + bit)

        def from_b(self):
            for kb in range(self.n - 1):
                for o in self.offsets():
                    self.x(kb, o).wait_recv()
                    self.c(kb + 1, o).start()

        def offsets(self):
            found = [0]
            for bit in bits[::-1]:
                found += [o + bit for o in found]
            return found

        def end(self):
            self.local().wait()
            for bit in bits:
                for o in range(0, A, 2 * bit):
                    self.z(bit, o).wait_send()
            for o in range(A):
                for kb in range(self.n - 1):
                    self.x(kb, o).wait_send()
                for kb in range(self.n):
                    self.c(kb, o).wait()

    def view_down(c_, b_, a_):
        return out_down.at[pl.ds(pl.multiple_of(((c_ * B + b_) * A + a_) * r_d, r_d), r_d), :]

    def view_up(c_, b_, a_):
        rows = pl.ds(pl.multiple_of(b_ * r_u, r_u), r_u)
        return out_up.at[:, rows, pl.ds(pl.multiple_of(c_ * shard + a_ * w_u, w_u), w_u)]

    half = D // 2
    w_o = half // A

    def view_square(out):
        def view(c_, b_, a_):
            rows = pl.ds(pl.multiple_of(b_ * r_u, r_u), r_u)
            return out.at[rows, pl.ds(pl.multiple_of(c_ * half + a_ * w_o, w_o), w_o)]

        return view

    gather_down = Gather(sh_d, view_down)
    gather_up = Gather(sh_u, view_up)
    gather_o = Gather(o_s, view_square(out_o))
    gather_q = Gather(q_s, view_square(out_q))
    gather_kv = Gather(kv_s, lambda c_, b_, a_: out_kv.at[c_, a_], planes=False)

    if head is None:
        send_down(0, A)
        send_up(0, A)
    else:
        own = types.SimpleNamespace(
            A=A, B=B, F=F, a=a, b=b, c=c, f=f, s=s, slots=slots, remote=remote, device=device, lower=lower,
            send_down=send_down, send_up=send_up, down_step=down_step, offset=offset, order=order,
        )
        finish_output, finish_head = head(r, own)

    def reduce_y(ref, got, sent, width):
        mine = pl.ds(pl.multiple_of(c * width, width), width)

        def add(i, carry):
            sent[i] = (ref[i, :, mine].astype(F32) + got[i].astype(F32)).astype(BF)
            return carry

        lax.fori_loop(0, F, add, 0)

    class Square:
        def __init__(self, grad, got_c, got_y, got_x, got_z, share, gather):
            self.grad, self.got_c, self.got_y, self.got_x, self.got_z = grad, got_c, got_y, got_x, got_z
            self.share, self.gather = share, gather
            self.c_slot, self.y_slot, self.x_slot = slots(), slots(F - 1), slots(B - 1)

        def c(self):
            other = pl.ds(pl.multiple_of((1 - c) * half, half), half)
            return remote(self.grad.at[:, :, other], self.got_c, self.c_slot, device("c", 1))

        def y(self, kf):
            return remote(self.got_c.at[lax.rem(f + kf + 1, F)], self.got_y.at[kf], self.y_slot + kf, device("f", kf + 1))

        def over_c(self):
            self.c().start()

        def over_f(self):
            self.c().wait()
            reduce_y(self.grad, self.got_c, self.got_c, half)
            for kf in range(F - 1):
                self.y(kf).start()

        def over_b(self):
            total = self.got_c[f].astype(F32)
            for kf in range(F - 1):
                self.y(kf).wait()
                total = total + self.got_y[kf].astype(F32)
            self.got_y[F - 1] = total.astype(BF)
            for kb in range(B - 1):
                self.x(kb).start()

        def x(self, kb):
            rows = pl.ds(pl.multiple_of(lax.rem(b + kb + 1, B) * r_u, r_u), r_u)
            return remote(self.got_y.at[F - 1, rows, :], self.got_x.at[kb], self.x_slot + kb, device("b", kb + 1))

        def over_a(self):
            rows = pl.ds(pl.multiple_of(b * r_u, r_u), r_u)
            total = self.got_y[F - 1, rows, :].astype(F32)
            for kb in range(B - 1):
                self.x(kb).wait()
                total = total + self.got_x[kb].astype(F32)
            self.got_x[B - 1] = total.astype(BF)
            self.copies = []
            for ka in range(A - 1):
                cols = pl.ds(pl.multiple_of(lax.rem(a + ka + 1, A) * w_o, w_o), w_o)
                self.copies.append(start(self.got_x.at[B - 1, :, cols], self.got_z.at[ka], slots(), device("a", ka + 1)))

        def finish(self):
            cols = pl.ds(pl.multiple_of(a * w_o, w_o), w_o)
            total = self.got_x[B - 1, :, cols].astype(F32)
            for ka in range(A - 1):
                self.copies[ka].wait()
                total = total + self.got_z[ka].astype(F32)
            self.share[...] = total.astype(BF)
            self.gather.begin()

    square_o = Square(go_ref, o_c, o_y, o_x, o_z, o_s, gather_o)
    square_q = Square(gq_ref, q_c, q_y, q_x, q_z, q_s, gather_q)

    square_o.over_c()

    scale = 1.0 / math.sqrt(HS)
    factor = math.log2(math.e) * scale
    acc[...] = jnp.zeros(acc.shape, F32)
    for h in range(H):
        cols = slice(h * HS, (h + 1) * HS)
        both = d_ref[:, cols].astype(F32) * att_ref[:, cols].astype(F32)
        delta[h : h + 1, :] = jnp.sum(both.T, axis=0, keepdims=True)
    first = s * tok
    pos = first + lax.broadcasted_iota(jnp.int32, (1, tok), 1)
    begin = jnp.zeros((1, tok), jnp.int32)
    for i in range(ends.shape[0]):
        begin = jnp.maximum(begin, jnp.where(ends[i] <= pos, ends[i], 0))

    def step(j, masked):
        rows = pl.ds(pl.multiple_of(j * CHUNK, CHUNK), CHUNK)
        keys = kv_ref[rows, :HS]
        values = kv_ref[rows, HS:]
        keys_t = keys.T
        if masked:
            at = j * CHUNK + lax.broadcasted_iota(jnp.int32, (CHUNK, tok), 0)
            mask = jnp.logical_and(at >= begin, at <= pos)
        else:
            seen = begin <= j * CHUNK
        d_keys = jnp.zeros((CHUNK, HS), F32)
        d_values = jnp.zeros((CHUNK, HS), F32)
        for h in range(H):
            cols = slice(h * HS, (h + 1) * HS)
            q = q_ref[:, cols]
            d = d_ref[:, cols]
            scores = nt(keys, q)
            if masked:
                scores = jnp.where(mask, scores, NEG)
            lse = lse_ref[h : h + 1, :]
            if not masked:
                lse = jnp.where(seen, lse, 3e38)
            probs = jnp.exp2(scores * factor - lse)
            d_probs = nt(values, d)
            d_scores = (probs * (d_probs - delta[h : h + 1, :])).astype(BF)
            d_values = d_values + nn(probs.astype(BF), d)
            d_keys = d_keys + nn(d_scores, q)
            acc[head_block(h, tok)] += nn(keys_t, d_scores)
        for i in range(2):
            part = slice(i * tok, (i + 1) * tok)
            dkv[j, i, :, :HS] = (d_keys[part] * scale).astype(BF)
            dkv[j, i, :, HS:] = d_values[part].astype(BF)

    chunks = s // 2 + 1
    def attention_chunk(j, carry):
        plain = jnp.logical_and(j > 0, j < chunks - 1)

        @pl.when(plain)
        def _():
            step(j, False)

        @pl.when(jnp.logical_not(plain))
        def _():
            step(j, True)

        return carry

    first = 0 if head is None else min(3, A - 1)
    steps = [functools.partial(down_step, i) for i in range(first, A - 1)]
    steps += [functools.partial(up_step, i) for i in range(A - 2)] + [down_share, functools.partial(up_step, A - 2), square_o.over_b]
    if A == 4 and head is not None:
        acts = [(1, steps[0]), (3, steps[1]), (4, steps[2]), (5, steps[4]), (2, square_o.over_f)]
    else:
        acts = [(0, square_o.over_f), *((1, act) for act in steps)]

    def chunk_and_step(j, carry):
        @pl.when(j < chunks)
        def _():
            attention_chunk(j, 0)

        for time, act in acts:
            pl.when(j == time)(act)
        return carry

    lax.fori_loop(0, window // CHUNK, chunk_and_step, 0)

    def clear(j, carry):
        dkv[j] = jnp.zeros(dkv.shape[1:], BF)
        return carry

    lax.fori_loop(chunks, window // CHUNK, clear, 0)

    dkv_c_copy = start(dkv.at[:, 1 - c], dkv_c, slots(), device("c", 1))


    if head is not None:
        finish_output()
    for h in range(H):
        dq[:, h * HS : (h + 1) * HS] = (acc[head_block(h, tok)] * scale).T.astype(BF)
    n_rows = 128

    def query_grad(i, carry):
        col = pl.ds(pl.multiple_of(i * n_rows, n_rows), n_rows)
        fi = i // (own_rows // n_rows)
        row = lax.rem(i, own_rows // n_rows) * n_rows
        gq_ref[fi, pl.ds(pl.multiple_of(row, n_rows), n_rows), :] = nn(n1_ref[:, col].T, dq[...]).astype(BF)
        return carry

    lax.fori_loop(0, D // n_rows, query_grad, 0)
    square_q.over_c()

    dkv_c_copy.wait()

    def add_c(j, carry):
        dkv_c[j] = (dkv_c[j].astype(F32) + dkv[j, c].astype(F32)).astype(BF)
        return carry

    lax.fori_loop(0, A * B, add_c, 0)
    x_kv = []
    for kb in range(B - 1):
        other = lax.rem(b + kb + 1, B)
        for j in range(A):
            x_kv.append(start(dkv_c.at[j * B + other], dkv_x.at[kb, j], slots(), device("b", kb + 1)))

    if A == 4 and head is not None:
        steps[3]()
    square_q.over_f()
    gather_down.from_a((0,))
    up_share()
    square_q.over_b()
    for i in range(1, len(bits)):
        gather_down.from_a((i,))
    square_o.over_a()

    for copy in x_kv:
        copy.wait()

    def add_x(j, carry):
        total = dkv_c[j * B + b].astype(F32)
        for kb in range(B - 1):
            total = total + dkv_x[kb, j].astype(F32)
        dkv_x[0, j] = total.astype(BF)
        return carry

    lax.fori_loop(0, A, add_x, 0)
    z_kv = slots(A - 1)
    for k in range(A - 1, 0, -1):

        @pl.when(a - k >= 0)
        def _():
            to = (((a - k) * B + b) * 2 + c, f)
            remote(dkv_x.at[0, jnp.maximum(a - k, 0)], dkv_z.at[k - 1], z_kv + k - 1, to).start()

    up_gather()

    total = dkv_x[0, a].astype(F32)
    d_kv[...] = total
    for k in range(1, A):
        copy = remote(dkv_x.at[0, jnp.maximum(a - k, 0)], dkv_z.at[k - 1], z_kv + k - 1, device("a", A - k))

        @pl.when(a - k >= 0)
        def _():
            copy.wait_send()

        @pl.when(a + k < A)
        def _():
            copy.wait_recv()
            d_kv[...] = d_kv[...] + dkv_z[k - 1].astype(F32)

    d_kv_low = d_kv[...].astype(BF)

    n_cols = 256
    mean = jnp.zeros((tok, 1), F32)
    for i in range(D // n_cols):
        cols = slice(i * n_cols, (i + 1) * n_cols)
        part = nt(dq[...], wq_ref[cols, :]) + nt(d_kv_low, wkv_ref[cols, :])
        dn1[:, cols] = part
        weighted = part * (tok_ref[:, cols].astype(F32) * inv_ref[...])
        gain_rows[0:1, cols] = jnp.sum(weighted, axis=0, keepdims=True)
        mean = mean + jnp.sum(weighted * gain_ref[:, cols], axis=1, keepdims=True)
    if head is None:
        gain_rows[1:2, :] = gain2_ref[...]
    mean = mean * (1.0 / D)

    r_kv = own_rows // A
    rows_kv = r_kv + 16
    for fi in range(F):
        for i in range(A):
            at = fi * own_rows + i * r_kv
            part = tn(n1_ref[:, at : at + r_kv], d_kv_low).astype(BF)
            gkv_ref[0, fi, i, :r_kv, :] = part[:, :HS]
            gkv_ref[1, fi, i, :r_kv, :] = part[:, HS:]
            for ci in range(2):
                rows = [gain_rows[ci : ci + 1, fi * own_rows + k * 128 : fi * own_rows + (k + 1) * 128] for k in range(own_rows // 128)]
                block = jnp.concatenate(rows + [jnp.zeros((16 - len(rows), 128), F32)], axis=0)
                gkv_ref[ci, fi, i, r_kv:, :] = block.astype(BF)
    kv_c_copy = start(gkv_ref.at[1 - c], kv_c, slots(), device("c", 1))

    square_q.over_a()
    for i in range(D // n_cols):
        cols = slice(i * n_cols, (i + 1) * n_cols)
        grad_tokens[:, cols] = dres_ref[:, cols] + inv_ref[...] * (
            dn1[:, cols] * gain_ref[:, cols] - tok_ref[:, cols].astype(F32) * inv_ref[...] * mean
        )
    kv_c_copy.wait()
    kv_c[...] = (kv_c[...].astype(F32) + gkv_ref[c].astype(F32)).astype(BF)
    kv_f = [start(kv_c.at[lax.rem(f + kf + 1, F)], kv_y.at[kf], slots(), device("f", kf + 1)) for kf in range(F - 1)]
    square_o.finish()
    gather_up.from_a((0,))
    total = kv_c[f].astype(F32)
    for kf in range(F - 1):
        kv_f[kf].wait()
        total = total + kv_y[kf].astype(F32)
    kv_y[F - 1] = total.astype(BF)
    kv_b = [start(kv_y.at[F - 1], kv_x.at[kb], slots(), device("b", kb + 1)) for kb in range(B - 1)]
    square_q.finish()
    for i in range(1, len(bits)):
        gather_up.from_a((i,))
    total = kv_y[F - 1].astype(F32)
    for kb in range(B - 1):
        kv_b[kb].wait()
        total = total + kv_x[kb].astype(F32)
    kv_x[B - 1] = total.astype(BF)
    kv_a = [start(kv_x.at[B - 1, lax.rem(a + ka + 1, A)], kv_z.at[ka], slots(), device("a", ka + 1)) for ka in range(A - 1)]
    gather_o.from_a()
    gather_q.from_a((0,))
    total = kv_x[B - 1, a].astype(F32)
    for ka in range(A - 1):
        kv_a[ka].wait()
        total = total + kv_z[ka].astype(F32)
    kv_s[...] = total.astype(BF)
    gather_kv.begin()
    for i in range(1, len(bits)):
        gather_q.from_a((i,))
    gather_down.from_b()
    gather_up.from_b()
    gather_kv.from_a()
    gather_o.from_b()
    gather_q.from_b()
    for gather in gathers:
        gather.end()
    if head is not None:
        finish_head()


def tail_shapes(dims, tok, D, shard, window, extra):
    A, B, F = dims
    own_rows = D // F
    half, r_d, r_u, w_u = D // 2, shard // (A * B), own_rows // B, shard // A
    w_o, r_kv = half // A, own_rows // A + 16

    def low(*shape):
        return pltpu.VMEM(shape, BF)

    square = [low(F, own_rows, half), low(F, own_rows, half), low(B, r_u, half), low(A - 1, r_u, w_o), low(r_u, w_o)]
    n_sems = extra + 2 * (A * (B - 1) + A - 1) + 4 * (A + (B - 1) * A + B * A) + 2 * A
    n_sems += 2 * (F + B + A) + 2 * F + (B - 1) * A + A + F + B + A + 8
    outs = (
        jax.ShapeDtypeStruct((2 * shard, D), BF),
        jax.ShapeDtypeStruct((F, own_rows, 2 * shard), BF),
        jax.ShapeDtypeStruct((own_rows, D), BF),
        jax.ShapeDtypeStruct((own_rows, D), BF),
        jax.ShapeDtypeStruct((2, A, r_kv, HS), BF),
        jax.ShapeDtypeStruct((tok, D), F32),
    )
    scratch = [
        pltpu.VMEM((2 * HS, H // 2 * tok), F32),
        pltpu.VMEM((H, tok), F32),
        low(tok, D),
        low(A * B, 2, tok, 2 * HS),
        low(A * B, tok, 2 * HS),
        low(max(1, B - 1), A, tok, 2 * HS),
        low(max(1, A - 1), tok, 2 * HS),
        pltpu.VMEM((tok, 2 * HS), F32),
        pltpu.VMEM((tok, D), F32),
        low(F, own_rows, D),
        low(2, F, A, r_kv, HS),
        low(B - 1, A, r_d, D),
        low(B - 1, A, F, r_u, w_u),
        low(A - 1, r_d, D),
        low(A - 1, F, r_u, w_u),
        low(A - 1, r_d, D),
        low(A - 1, F, r_u, w_u),
        low(r_d, D),
        low(F, r_u, w_u),
        low(F, r_u, w_u),
        *square,
        *square,
        low(F, A, r_kv, HS),
        low(F, A, r_kv, HS),
        low(B, A, r_kv, HS),
        low(A - 1, r_kv, HS),
        low(r_kv, HS),
        pltpu.VMEM((8, D), F32),
        pltpu.SemaphoreType.DMA((n_sems,)),
        pltpu.SemaphoreType.DMA((n_sems,)),
        pltpu.SemaphoreType.DMA((5,)),
    ]
    return outs, scratch


def tail(dims, ends, queries, window_kv, d_attended, attended, lse, grad_down, grad_up, grad_out, n1, wq, wkv, tokens, inv, gain, dres, gain2):
    A, B, F = dims
    tok, D = n1.shape
    window = window_kv.shape[0]
    outs, scratch = tail_shapes(dims, tok, D, grad_down.shape[0], window, 0)
    hbm = pl.BlockSpec(memory_space=pltpu.HBM)
    return pl.pallas_call(
        functools.partial(tail_kernel, dims, None, TAIL_IN + TAIL_OUT + TAIL_SCRATCH),
        out_shape=outs,
        in_specs=[SMEM] + [VMEM] * 16,
        out_specs=(hbm,) * 5 + (VMEM,),
        scratch_shapes=scratch,
        compiler_params=pltpu.CompilerParams(vmem_limit_bytes=56 * 2**20, collective_id=1, has_side_effects=True),
        cost_estimate=pl.CostEstimate(flops=20 * tok * window * D, bytes_accessed=2**25, transcendentals=tok * window * H),
        name="tail",
    )(ends, queries, window_kv, d_attended, attended, lse, grad_down, grad_up, grad_out, n1, wq, wkv, tokens, inv, gain, dres, gain2)


HEAD_IN = (
    "lengths",
    "groups",
    "tokens",
    "gains_in",
    "wk_in",
    "wv_in",
    "cot_in",
    "wq_in",
    "wo_in",
    "up_in",
    "down_in",
)
HEAD_SCRATCH = (
    "q_ref",
    "kv_ref",
    "d_ref",
    "att_ref",
    "lse_ref",
    "gd_ref",
    "gu_ref",
    "n1_ref",
    "wq_ref",
    "wkv_ref",
    "inv_ref",
    "gain_ref",
    "dres_ref",
    "gain2_ref",
    "wo_ref",
    "up_ref",
    "down_ref",
    "gains_all",
    "cot_all",
    "n2_all",
    "hid_all",
    "dp_all",
    "res_ref",
    "inv2_ref",
    "dbr_ref",
    "back_s",
    "back_c",
    "back_y",
    "back_r",
    "out_s",
    "out_c",
    "out_y",
    "out_r",
    "loc_sem",
    "ends",
)


def head(r, x):
    A, B, F, a, b, c, f, s = x.A, x.B, x.F, x.a, x.b, x.c, x.f, x.s
    slots, remote, device, lower = x.slots, x.remote, x.device, x.lower
    tok, D = r.tokens.shape
    own_rows = D // F
    shard = r.down_ref.shape[0]
    half = own_rows // 2
    sent = []

    def start(src, dst, to, slot=None):
        copy = remote(src, dst, slots() if slot is None else slot, to)
        copy.start()
        sent.append(copy)
        return copy

    def done(copies):
        for copy in copies:
            copy.wait_send()
            sent[:] = [other for other in sent if other is not copy]

    def span(at, n):
        return pl.ds(pl.multiple_of(at, n), n)

    sibling = device("c", 1)
    mine, mine_half = span(f * own_rows, own_rows), span(c * half, half)
    full_half = span((f * 2 + c) * half, half)

    def to_f(src, dst):
        return [start(src(kf), dst(kf), device("f", kf)) for kf in range(1, F)]

    gains_f = to_f(lambda kf: r.gains_in, lambda kf: r.gains_all.at[f])
    wk_f = to_f(lambda kf: r.wk_in.at[mine_half, :], lambda kf: r.wkv_ref.at[full_half, :HS])
    wv_f = to_f(lambda kf: r.wv_in.at[mine_half, :], lambda kf: r.wkv_ref.at[full_half, HS:])
    part, up_part = half // B, own_rows // B

    def wo_rows(f_, c_, b_):
        return span(((f_ * 2 + c_) * B + b_) * part, part)

    def up_rows(f_, b_):
        return span((f_ * B + b_) * up_part, up_part)

    wq_f = to_f(lambda kf: r.wq_in.at[span((c * B + b) * part, part), :], lambda kf: r.wq_ref.at[wo_rows(f, c, b), :])
    wo_f = to_f(lambda kf: r.wo_in.at[span((c * B + b) * part, part), :], lambda kf: r.wo_ref.at[wo_rows(f, c, b), :])
    up_f = to_f(
        lambda kf: r.up_in.at[span(b * up_part, up_part), span((lax.rem(f + kf, F) * 2 + c) * shard, shard)],
        lambda kf: r.up_ref.at[up_rows(f, b), :],
    )
    cot_f = to_f(lambda kf: r.cot_in, lambda kf: r.cot_all.at[kf, :tok])
    cot_c = [start(r.cot_in, r.cot_all.at[0, tok:], sibling)]

    local = [
        pltpu.make_async_copy(src, dst, r.loc_sem.at[i])
        for i, (src, dst) in enumerate(
            (
                (r.wq_in, r.wq_ref.at[mine, :]),
                (r.wo_in, r.wo_ref.at[mine, :]),
                (r.up_in.at[:, span((f * 2 + c) * shard, shard)], r.up_ref.at[mine, :]),
                (r.cot_in, r.cot_all.at[0, :tok]),
                (r.down_in.at[span(c * shard, shard), :], r.down_ref),
            )
        )
    ]
    for copy in local:
        copy.start()

    def weight_halves(copies, ref, cols):
        passed = []
        for kf in range(1, F):
            copies[kf - 1].wait_recv()
            rows = span((lower("f", kf) * 2 + c) * half, half)
            passed.append(start(ref.at[rows, cols], ref.at[rows, cols], sibling))
        return passed

    def along_b(copies, ref, rows):
        passed = []
        for kf in range(1, F):
            copies[kf - 1].wait_recv()
            here = ref.at[rows(lower("f", kf)), :]
            passed += [start(here, here, device("b", kb)) for kb in range(1, B)]
        return passed

    group = r.groups[f]
    end = jnp.int32(0)
    for i in range(r.ends.shape[0]):
        end = end + r.lengths[group, i]
        r.ends[i] = end
    n_rows = 64

    def unit_rows(i, carry):
        rows = span(i * n_rows, n_rows)
        stream = r.tokens[rows, :].astype(F32)
        inverse = lax.rsqrt(jnp.mean(stream * stream, axis=1, keepdims=True) + EPS)
        r.inv_ref[rows, :] = inverse
        return carry

    lax.fori_loop(0, tok // n_rows, unit_rows, 0)
    r.wkv_ref[mine, :HS] = r.wk_in[...]
    r.wkv_ref[mine, HS:] = r.wv_in[...]
    r.gains_all[f] = r.gains_in[...]
    for copy in gains_f:
        copy.wait_recv()
    for i in range(F):
        both = r.gains_all[i].astype(F32)
        cols = slice(i * own_rows, (i + 1) * own_rows)
        r.gain_ref[0:1, cols] = both[0:1, :]
        r.gain2_ref[0:1, cols] = both[1:2, :]

    def normed_rows(i, carry):
        rows = span(i * n_rows, n_rows)
        r.n1_ref[rows, :] = (r.tokens[rows, :].astype(F32) * r.inv_ref[rows, :] * r.gain_ref[...]).astype(BF)
        return carry

    lax.fori_loop(0, tok // n_rows, normed_rows, 0)

    wkv_c = weight_halves(wk_f, r.wkv_ref, slice(0, HS)) + weight_halves(wv_f, r.wkv_ref, slice(HS, 2 * HS))
    for copy in wkv_c:
        copy.wait_recv()
    kv = r.kv_ref

    def block(a_, b_, c_):
        return kv.at[span(((a_ * B + b_) * 2 + c_) * tok, tok), :]

    kv[span(s * tok, tok), :] = nn(r.n1_ref[...], r.wkv_ref[...]).astype(BF)
    kv_z, kv_x, kv_c = slots(A - 1), slots((B - 1) * A), slots(B * A)
    own = block(a, b, c)
    z_copies = [remote(own, own, kv_z + k - 1, device("a", k)) for k in range(1, A)]

    def guarded(k, ok, act):
        if k == 0:
            act()
        else:
            pl.when(ok)(act)

    for k in range(1, A):
        guarded(k, a + k < A, z_copies[k - 1].start)

    def x_copy(kb, k):
        here = block(jnp.maximum(a - k, 0), b, c)
        return remote(here, here, kv_x + (kb - 1) * A + k, device("b", kb))

    def c_copy(kb, k):
        here = block(jnp.maximum(a - k, 0), lower("b", kb) if kb else b, c)
        return remote(here, here, kv_c + kb * A + k, sibling)

    def pass_on(k):
        for kb in range(1, B):
            x_copy(kb, k).start()
        c_copy(0, k).start()

    pass_on(0)

    def from_a(k):
        z_copies[k - 1].wait_recv()
        pass_on(k)

    wq_b = along_b(wq_f, r.wq_ref, lambda f_: wo_rows(f_, c, b))
    if A > 2:
        guarded(1, a >= 1, functools.partial(from_a, 1))

    local[0].wait()
    for copy in wq_b:
        copy.wait_recv()
    wq_c = []
    for kf in range(1, F):
        here = r.wq_ref.at[span((lower("f", kf) * 2 + c) * half, half), :]
        wq_c.append(start(here, here, sibling))
    for copy in wq_c:
        copy.wait_recv()
    n_cols = 256

    def columns(n, act):
        def body(i, carry):
            act(span(i * n_cols, n_cols))
            return carry

        lax.fori_loop(0, n // n_cols, body, 0)

    def query_cols(cols):
        r.q_ref[:, cols] = nn(r.n1_ref[...], r.wq_ref[:, cols]).astype(BF)

    columns(D, query_cols)

    for k in range(2 if A > 2 else 1, A):
        guarded(k, a - k >= 0, functools.partial(from_a, k))
    wo_b = along_b(wo_f, r.wo_ref, lambda f_: wo_rows(f_, c, b))

    factor = math.log2(math.e) / math.sqrt(HS)
    top, mixed, total = r.dres_ref, r.res_ref, r.acc
    top[...] = jnp.full(top.shape, -3e38, F32)
    mixed[...] = jnp.zeros(mixed.shape, F32)
    total[...] = jnp.zeros(total.shape, F32)
    pos = s * tok + lax.broadcasted_iota(jnp.int32, (tok, 1), 0)
    begin = jnp.zeros((tok, 1), jnp.int32)
    for i in range(r.ends.shape[0]):
        begin = jnp.maximum(begin, jnp.where(r.ends[i] <= pos, r.ends[i], 0))

    def step(j, masked):
        rows = span(j * CHUNK, CHUNK)
        keys = kv[rows, :HS]
        values = jnp.concatenate([kv[rows, HS:], jnp.ones((CHUNK, HS), BF)], axis=1)
        if masked:
            at = j * CHUNK + lax.broadcasted_iota(jnp.int32, (tok, CHUNK), 1)
            mask = jnp.logical_and(at >= begin, at <= pos)
        else:
            seen = begin <= j * CHUNK
        for h in range(H):
            cols = slice(h * HS, (h + 1) * HS)
            scores = nt(r.q_ref[:, cols], keys)
            if masked:
                scores = jnp.where(mask, scores, NEG)
            old = top[:, cols]
            new = jnp.maximum(old, jnp.max(scores, axis=1, keepdims=True) * factor)
            if not masked:
                new = jnp.where(seen, new, old)
            shrink = jnp.exp2(old - new)
            probs = jnp.exp2(scores * factor - jnp.concatenate([new] * (CHUNK // HS), axis=1))
            both = nn(probs.astype(BF), values)
            if not masked:
                both = jnp.where(seen, both, 0.0)
            mixed[:, cols] = mixed[:, cols] * shrink + both[:, :HS]
            total[:, cols] = total[:, cols] * shrink + both[:, HS:]
            top[:, cols] = new

    last = s // 2
    c_copy(0, 0).wait_recv()
    step(last, True)

    def from_b(k):
        for kb in range(1, B):
            x_copy(kb, k).wait_recv()
            c_copy(kb, k).start()

    def from_c(k):
        for kb in range(B):
            if kb or k:
                c_copy(kb, k).wait_recv()

    wo_c, up_b = [], []
    for kf in range(1, F):
        here = r.wo_ref.at[span((lower("f", kf) * 2 + c) * half, half), :]
        wo_c.append(remote(here, here, slots(), sibling))
        here = r.up_ref.at[up_rows(lower("f", kf), b), :]
        up_b += [remote(here, here, slots(), device("b", kb)) for kb in range(1, B)]
    sent.extend(wo_c + up_b)

    def pass_weights():
        for copy in wo_b:
            copy.wait_recv()
        for copy in wo_c:
            copy.start()
        for copy in up_f:
            copy.wait_recv()
        for copy in up_b:
            copy.start()

    from_b(0)
    guarded(1, a >= 1, functools.partial(from_b, 1))
    from_c(0)

    def begin_group(k):
        if k + 1 < A:
            guarded(k + 1, a - (k + 1) >= 0, functools.partial(from_b, k + 1))
        from_c(k)
        if k == A - 1:
            pass_weights()

    def attention_chunk(j, carry):
        @pl.when(j > 0)
        def _():
            step(j, False)

        @pl.when(j == 0)
        def _():
            step(j, True)

        return carry

    def attention_part(i, carry):
        j = last - 1 - i
        for k in range(1, A):
            pl.when(j == (a - k) * B + B - 1)(functools.partial(begin_group, k))
        return attention_chunk(j, carry)

    lax.fori_loop(0, last, attention_part, 0)
    guarded(1, a < A - 1, pass_weights)
    for h in range(H):
        cols = slice(h * HS, (h + 1) * HS)
        r.att_ref[:, cols] = (mixed[:, cols] * (1.0 / total[:, cols])).astype(BF)
        r.lse_ref[h : h + 1, :] = (top[:, cols] + jnp.log2(total[:, cols])).T[0:1, :]

    local[1].wait()
    for copy in wo_c:
        copy.wait_recv()
    squares = jnp.zeros((tok, 1), F32)
    for i in range(D // n_cols):
        cols = slice(i * n_cols, (i + 1) * n_cols)
        part = r.tokens[:, cols].astype(F32) + nn(r.att_ref[...], r.wo_ref[:, cols])
        r.res_ref[:, cols] = part
        squares = squares + jnp.sum(part * part, axis=1, keepdims=True)
    r.inv2_ref[...] = lax.rsqrt(squares * (1.0 / D) + EPS)

    def second_norm(i, carry):
        rows = span(i * n_rows, n_rows)
        r.n2_all[0, rows, :] = (r.res_ref[rows, :] * r.inv2_ref[rows, :] * r.gain2_ref[...]).astype(BF)
        return carry

    lax.fori_loop(0, tok // n_rows, second_norm, 0)

    n2_f = to_f(lambda kf: r.n2_all.at[0, :tok], lambda kf: r.n2_all.at[kf, :tok])
    n2_c = [start(r.n2_all.at[0, :tok], r.n2_all.at[0, tok:], sibling)]
    local[2].wait()
    local[3].wait()
    local[4].wait()
    for copy in up_b:
        copy.wait_recv()
    for kf in range(1, F):
        cot_f[kf - 1].wait_recv()
        cot_c.append(start(r.cot_all.at[kf, :tok], r.cot_all.at[kf, tok:], sibling))

    def feed_forward(kf):
        def hidden_cols(cols):
            before = nn(r.n2_all[kf], r.up_ref[:, cols])
            d_hidden = nt(r.cot_all[kf], r.down_ref[cols, :])
            sig = 1.0 / (1.0 + jnp.exp(-before))
            r.hid_all[kf, :, cols] = (before * sig).astype(BF)
            r.dp_all[kf, :, cols] = (d_hidden * sig * (1.0 + before * (1.0 - sig))).astype(BF)

        columns(shard, hidden_cols)

    def back_part(kf):
        def back_cols(cols):
            r.back_s[kf, :, cols] = nt(r.dp_all[kf], r.up_ref[cols, :]).astype(BF)

        columns(D, back_cols)
        return start(r.back_s.at[kf, tok:], r.back_c.at[kf], sibling)

    def out_part(kf):
        def out_cols(cols):
            r.out_s[kf, :, cols] = nn(r.hid_all[kf], r.down_ref[:, cols]).astype(BF)

        columns(D, out_cols)
        return start(r.out_s.at[kf, tok:], r.out_c.at[kf], sibling)

    def chip_sum(kf, part, other, ref):
        def rows_sum(i, carry):
            rows = span(i * n_rows, n_rows)
            ref[kf - 1, rows, :] = (part[kf, rows, :].astype(F32) + other[kf, rows, :].astype(F32)).astype(BF)
            return carry

        lax.fori_loop(0, tok // n_rows, rows_sum, 0)

    n_out = 128

    r_d = shard // (A * B)

    def down_rows(kfs, place):
        cols = span(place * r_d, r_d)
        grad = sum(tn(r.hid_all[kf, :, cols], r.cot_all[kf]) for kf in kfs)
        if 0 not in kfs:
            grad = grad + r.gd_ref[cols, :].astype(F32)
        r.gd_ref[cols, :] = grad.astype(BF)

    def down_grad(kf):
        for i in range(A):
            for kb in range(1, B):
                down_rows((kf,), lax.rem(b + kb, B) * A + x.offset(x.order[i]))
            if kf == F - 1:
                x.send_down(i, i + 1)

    def down_grad_own():
        def rows_of(i, carry):
            down_rows(range(F), b * A + i)
            return carry

        lax.fori_loop(0, A, rows_of, 0)

    def up_grad():
        def rows_of(i, carry):
            cols = span(i * n_out, n_out)
            rows = span(lax.rem(i, own_rows // n_out) * n_out, n_out)
            grad = sum(tn(r.n2_all[kf, :, cols], r.dp_all[kf]) for kf in range(F))
            r.gu_ref[i // (own_rows // n_out), rows, :] = grad.astype(BF)
            return carry

        lax.fori_loop(0, D // n_out, rows_of, 0)

    back_copies, out_copies, back_back, out_back = [None] * F, [None] * F, [], []
    n2_c[0].wait_recv()
    cot_c[0].wait_recv()
    feed_forward(0)
    down_grad(0)
    back_copies[0] = back_part(0)
    for kf in range(1, F):
        n2_f[kf - 1].wait_recv()
        n2_c.append(start(r.n2_all.at[kf, :tok], r.n2_all.at[kf, tok:], sibling))
    for kf in range(1, F):
        n2_c[kf].wait_recv()
        cot_c[kf].wait_recv()
        feed_forward(kf)
        down_grad(kf)
        back_copies[kf] = back_part(kf)
        if kf == F - 1:
            down_grad_own()
        back_copies[kf].wait_recv()
        chip_sum(kf, r.back_s, r.back_c, r.back_y)
        back_back.append(start(r.back_y.at[kf - 1], r.back_r.at[kf - 1], device("f", F - kf)))
        if kf == F - 1:
            up_grad()
            x.send_up(0, A)
            x.down_step(0)
        out_copies[kf] = out_part(kf)
    for kf in range(1, F):
        out_copies[kf].wait_recv()
        chip_sum(kf, r.out_s, r.out_c, r.out_y)
        out_back.append(start(r.out_y.at[kf - 1], r.out_r.at[kf - 1], device("f", F - kf)))
    if A > 2:
        x.down_step(1)
    out_copies[0] = out_part(0)
    if A > 2:
        x.down_step(2)

    back_copies[0].wait_recv()
    for copy in back_back:
        copy.wait_recv()

    def norm_back(i, gain_grad):
        rows = span(i * n_rows, n_rows)
        d_normed = r.back_s[0, rows, :].astype(F32) + r.back_c[0, rows, :].astype(F32)
        for kf in range(1, F):
            d_normed = d_normed + r.back_r[kf - 1, rows, :].astype(F32)
        inverse = r.inv2_ref[rows, :]
        unit = r.res_ref[rows, :] * inverse
        weighted = d_normed * unit
        scaled = d_normed * r.gain2_ref[...]
        mean = jnp.mean(scaled * unit, axis=1, keepdims=True)
        d_residual = r.cot_all[0, rows, :].astype(F32) + inverse * (scaled - unit * mean)
        r.dres_ref[rows, :] = d_residual
        r.dbr_ref[rows, :] = d_residual.astype(BF)
        return gain_grad + jnp.sum(weighted, axis=0, keepdims=True)

    r.gain_rows[1:2, :] = lax.fori_loop(0, tok // n_rows, norm_back, jnp.zeros((1, D), F32))

    def attended_cols(cols):
        r.d_ref[:, cols] = nt(r.dbr_ref[...], r.wo_ref[cols, :]).astype(BF)

    columns(D, attended_cols)

    done(n2_f + n2_c)

    def out_grad(i, carry):
        cols = span(i * n_out, n_out)
        rows = span(lax.rem(i, own_rows // n_out) * n_out, n_out)
        r.go_ref[i // (own_rows // n_out), rows, :] = tn(r.att_ref[:, cols], r.dbr_ref[...]).astype(BF)
        return carry

    lax.fori_loop(0, D // n_out, out_grad, 0)

    def finish_output():
        out_copies[0].wait_recv()
        for copy in out_back:
            copy.wait_recv()

        def output_rows(i, carry):
            rows = span(i * n_rows, n_rows)
            value = r.res_ref[rows, :] + r.out_s[0, rows, :].astype(F32) + r.out_c[0, rows, :].astype(F32)
            for kf in range(1, F):
                value = value + r.out_r[kf - 1, rows, :].astype(F32)
            r.out_ref[rows, :] = value.astype(BF)
            return carry

        lax.fori_loop(0, tok // n_rows, output_rows, 0)
        done(out_copies)
        results[0].start()

    results = [
        pltpu.make_async_copy(src, dst, r.loc_sem.at[5 + i])
        for i, (src, dst) in enumerate(((r.out_ref, r.out_hbm), (r.grad_tokens, r.grad_hbm)))
    ]

    def finish():
        results[1].start()
        for copy in results:
            copy.wait()
        for copy in sent:
            copy.wait_send()
        for k in range(1, A):
            guarded(k, a + k < A, z_copies[k - 1].wait_send)
        for k in range(A):
            for kb in range(B):
                if kb:
                    guarded(k, a - k >= 0, x_copy(kb, k).wait_send)
                guarded(k, a - k >= 0, c_copy(kb, k).wait_send)

    return finish_output, finish


AGAIN = {
    "go_ref": "n2_all",
    "gq_ref": "out_s",
    "dn1": "res_ref",
    "grad_tokens": "res_ref",
    "dq": "d_ref",
    "out_ref": "dbr_ref",
    "tok_ref": "tokens",
}


def layer_shapes(dims, tok, D, shard, window, sequences):
    A, B, F = dims
    own_rows = D // F
    outs, scratch = tail_shapes(dims, tok, D, shard, window, 16 * F + A - 1 + (B - 1) * A + B * A)

    def low(*shape):
        return pltpu.VMEM(shape, BF)

    def wide(*shape):
        return pltpu.VMEM(shape, F32)

    pair = [low(F, 2 * tok, D), low(F, tok, D), low(F - 1, tok, D), low(F - 1, tok, D)]
    first = [
        low(tok, D),
        low(window, 2 * HS),
        low(tok, D),
        low(tok, D),
        wide(H, tok),
        low(shard, D),
        low(F, own_rows, shard),
        low(tok, D),
        low(D, D),
        low(D, 2 * HS),
        wide(tok, 1),
        wide(1, D),
        wide(tok, D),
        wide(1, D),
        low(D, D),
        low(D, shard),
        low(shard, D),
        low(F, 16, own_rows),
        low(F, 2 * tok, D),
        low(F, 2 * tok, D),
        low(F, 2 * tok, shard),
        low(F, 2 * tok, shard),
        wide(tok, D),
        wide(tok, 1),
        low(tok, D),
        *pair,
        *pair,
        pltpu.SemaphoreType.DMA((7,)),
        pltpu.SMEM((sequences,), jnp.int32),
    ]
    sizes = dict(zip(HEAD_SCRATCH + TAIL_SCRATCH, first + scratch))
    fits = all(sizes[k].shape == sizes[AGAIN[k]].shape for k in ("gq_ref", "dn1", "dq")) and tok == 2 * HS and own_rows == 2 * tok
    scratch = [ref for name, ref in zip(TAIL_SCRATCH, scratch) if name not in AGAIN]
    fits = fits and vmem_bytes(first + scratch) + 4 * 2**20 < LIMIT
    return outs + (jax.ShapeDtypeStruct((tok, D), BF),), first + scratch, fits


def vmem_bytes(scratch):
    total = 0
    for ref in scratch:
        shape = getattr(ref, "shape", ())
        if len(shape) >= 2:
            lanes = -(-shape[-1] // 128) * 128
            rows = -(-shape[-2] // 8) * 8
            total += math.prod(shape[:-2]) * rows * lanes * jnp.dtype(ref.dtype).itemsize
    return total


def layer(dims, lengths, groups, tokens, gains, w_key, w_value, cotangent, w_query, w_out, w_up, w_down, outs, scratch):
    tok, D = tokens.shape
    hbm = pl.BlockSpec(memory_space=pltpu.HBM)
    names = HEAD_IN + TAIL_OUT[:5] + ("grad_hbm", "out_hbm") + HEAD_SCRATCH + tuple(n for n in TAIL_SCRATCH if n not in AGAIN)
    return pl.pallas_call(
        functools.partial(tail_kernel, dims, head, names),
        out_shape=outs,
        in_specs=[SMEM] * 2 + [VMEM] * 4 + [hbm] * 5,
        out_specs=(hbm,) * 7,
        scratch_shapes=scratch,
        compiler_params=pltpu.CompilerParams(vmem_limit_bytes=LIMIT, collective_id=2, has_side_effects=True),
        cost_estimate=pl.CostEstimate(flops=2**35, bytes_accessed=2**25, transcendentals=2**24),
        name="layer",
    )(lengths, groups, tokens, gains, w_key, w_value, cotangent, w_query, w_out, w_up, w_down)


def after(value, *others):
    return lax.optimization_barrier((value, *others))[0]


class Grid:
    def __init__(self):
        seq = lax.axis_size("seq")
        self.F = lax.axis_size("fsdp")
        self.C = 2
        chips = seq // 2
        self.B = 2 if chips == 8 else chips // 2
        self.A = chips // self.B
        self.s = lax.axis_index("seq")
        self.f = lax.axis_index("fsdp")
        self.c = self.s % 2
        self.b = self.s // 2 % self.B
        self.a = self.s // (2 * self.B)

    def size(self, axis):
        return {"a": self.A, "b": self.B, "c": self.C, "f": self.F}[axis]

    def place(self, axis):
        return {"a": self.a, "b": self.b, "c": self.c, "f": self.f}[axis]

    def send(self, value, axis, step, upward=False):
        pairs = []
        for a in range(self.A):
            for b in range(self.B):
                for c in range(2):
                    for f in range(self.F):
                        at = {"a": a, "b": b, "c": c, "f": f}
                        to = dict(at)
                        to[axis] += step
                        if upward and not 0 <= to[axis] < self.size(axis):
                            continue
                        to[axis] %= self.size(axis)
                        line = [((d["a"] * self.B + d["b"]) * 2 + d["c"]) * self.F + d["f"] for d in (at, to)]
                        pairs.append(tuple(line))
        return lax.ppermute(value, ("seq", "fsdp"), pairs)

    def stack(self, parts, axis):
        n, me = len(parts), self.place(axis)
        if n == 2:
            low = me == 0
            return jnp.stack([jnp.where(low, parts[0], parts[1]), jnp.where(low, parts[1], parts[0])])
        twice = jnp.stack(parts + parts)
        return lax.dynamic_slice_in_dim(twice, (n - me) % n, n, 0)

    def gather(self, value, axis):
        n = self.size(axis)
        return self.stack([value] + [self.send(value, axis, -k) for k in range(1, n)], axis)

    def scatter(self, parts, axis):
        n, me = self.size(axis), self.place(axis)

        def pick(k):
            return lax.dynamic_index_in_dim(parts, (me + k) % n, 0, keepdims=False)

        got = [self.send(pick(k).astype(BF), axis, k) for k in range(1, n)]
        total = pick(0).astype(F32)
        for piece in got:
            total = total + piece.astype(F32)
        return total

    def plane_sum(self, parts):
        half = self.scatter(parts, "b").astype(BF)
        return self.scatter(half, "a")

    def plane_gather(self, share):
        rows = self.gather(share.astype(BF), "a")
        return self.gather(rows, "b")


def local(
    tokens,
    cotangent,
    seq_lengths,
    group_of_shard,
    gain_attn,
    w_query,
    w_key,
    w_value,
    w_out,
    gain_ffn,
    w_up,
    w_down,
):
    g = Grid()
    A, B, C, F = g.A, g.B, g.C, g.F
    tok, D = tokens.shape[1:]
    FF = w_up.shape[1]
    own_rows = D // F
    seq_parts = A * B * C
    shard = FF // (2 * F)

    outs, scratch, fits = layer_shapes((A, B, F), tok, D, shard, seq_parts * tok, seq_lengths.shape[1])
    if fits:
        row = lax.broadcasted_iota(jnp.int32, (16, own_rows), 0)
        gains = jnp.where(row == 0, gain_attn[None], gain_ffn[None])
        *grads, grad_tokens, output = layer(
            (A, B, F),
            seq_lengths,
            group_of_shard,
            tokens[0],
            gains,
            w_key,
            w_value,
            cotangent[0],
            w_query,
            w_out,
            w_up,
            w_down,
            outs,
            scratch,
        )
        return results(output, grad_tokens, *grads)

    group = lax.dynamic_index_in_dim(group_of_shard, g.f, 0, keepdims=False)
    lengths = lax.dynamic_index_in_dim(seq_lengths, group, 0, keepdims=False)
    running, ends = jnp.int32(0), []
    for i in range(seq_lengths.shape[1]):
        running = running + lengths[i]
        ends.append(running)
    scal = jnp.stack([g.s.astype(jnp.int32), *ends])

    gains = jnp.stack([gain_attn, gain_ffn])
    full_gains = g.gather(gains, "f").transpose(1, 0, 2).reshape(2, D).astype(F32)
    gain_first, gain_second = full_gains[0], full_gains[1]
    own_kv = jnp.concatenate([w_key, w_value], axis=1)
    full_kv = g.gather(own_kv, "f").reshape(D, 2 * HS)

    def gather_weight(weight, *late):
        half = own_rows // 2
        mine = lax.dynamic_slice_in_dim(weight, g.c * half, half, 0)
        if late:
            mine = after(mine, *late)
        pieces = [g.gather(g.send(mine, "f", -k), "c").reshape(weight.shape) for k in range(1, F)]
        return g.stack([weight] + pieces, "f").reshape(F * own_rows, -1)

    full_query = gather_weight(w_query)

    stream = tokens[0].astype(F32)
    inverse_first = lax.rsqrt(jnp.mean(stream * stream, axis=1, keepdims=True) + EPS)
    unit_first = stream * inverse_first
    normed_first = (unit_first * gain_first).astype(BF)
    key_value = nn(normed_first, full_kv).astype(BF)
    queries = nn(normed_first, full_query).astype(BF)

    column = [key_value] + [g.send(key_value, "a", k, upward=True) for k in range(1, A)]
    twice = jnp.stack(column[::-1] + column[::-1])
    column = lax.dynamic_slice_in_dim(twice, A - 1 - g.a, A, 0)
    plane = g.gather(column, "b")
    whole = g.gather(plane, "c")
    window_kv = whole.transpose(2, 1, 0, 3, 4).reshape(seq_parts * tok, 2 * HS)

    full_out = gather_weight(w_out, full_query)
    upstream = cotangent[0]
    cot = []
    for k in range(F):
        mine = upstream if k == 0 else g.send(after(upstream, full_query), "f", k)
        cot.append(jnp.concatenate([mine, g.send(mine, "c", 1)], axis=0))
    ups = w_up.reshape(own_rows, F, 2, shard)
    up_parts = []
    for k in range(F):
        block = lax.dynamic_slice(ups, (0, (g.f + k) % F, g.c, 0), (own_rows, 1, 1, shard)).reshape(own_rows, shard)
        up_parts.append(block if k == 0 else g.send(after(block, full_out), "f", k))
    up_parts = [up_parts[0]] + up_parts[1:][::-1]
    up = g.stack(up_parts, "f").reshape(D, shard)
    down = lax.dynamic_slice_in_dim(w_down, g.c * shard, shard, 0)

    attended, lse = attend(scal, queries, window_kv)

    residual = stream + nn(attended, full_out)
    inverse_second = lax.rsqrt(jnp.mean(residual * residual, axis=1, keepdims=True) + EPS)
    unit_second = residual * inverse_second
    normed_second = (unit_second * gain_second).astype(BF)

    out_sum, back_sum = residual, jnp.zeros((tok, D), F32)
    hiddens, d_pres, norms = [], [], []
    backs, outs = [], []
    for k in range(F):
        mine = normed_second if k == 0 else g.send(normed_second, "f", k)
        norm = jnp.concatenate([mine, g.send(mine, "c", 1)], axis=0)
        before = nn(norm, up)
        d_hidden = nt(cot[k], down)
        sig = jax.nn.sigmoid(before)
        hidden = (before * sig).astype(BF)
        d_pre = (d_hidden * sig * (1.0 + before * (1.0 - sig))).astype(BF)
        back = nt(d_pre, up)
        out = nn(hidden, down)
        hiddens.append(hidden)
        d_pres.append(d_pre)
        norms.append(norm)
        backs.append(back)
        outs.append(out)

    def give_back(parts):
        total = 0.0
        for k, part in enumerate(parts):
            other = g.send(part[tok:].astype(BF), "c", 1)
            chip = part[:tok] + other.astype(F32)
            if k:
                chip = g.send(chip.astype(BF), "f", -k).astype(F32)
            total = total + chip
        return total

    d_normed_second = give_back(backs)
    output = (residual + give_back(outs)).astype(BF)

    grad_down = sum(tn(h, c) for h, c in zip(hiddens, cot)).astype(BF)
    grad_up = sum(tn(n, d) for n, d in zip(norms, d_pres)).astype(BF)

    def norm_back(gradient, unit_rows, inverse, gain_vec):
        scaled = gradient * gain_vec
        gain_grad = jnp.sum(gradient * unit_rows, axis=0)
        return gain_grad, inverse * (scaled - unit_rows * jnp.mean(scaled * unit_rows, axis=1, keepdims=True))

    gain_second_grad, d_from_norm = norm_back(d_normed_second, unit_second, inverse_second, gain_second)
    d_residual = upstream.astype(F32) + d_from_norm
    d_branch = d_residual.astype(BF)
    d_attended = nt(d_branch, full_out).astype(BF)
    grad_out = tn(attended, d_branch).astype(BF)

    down_all, up_all, out_all, query_all, kv_all, grad_tokens = tail(
        (A, B, F),
        scal[1:],
        queries,
        window_kv,
        d_attended,
        attended,
        lse,
        grad_down,
        grad_up.reshape(F, own_rows, shard),
        grad_out.reshape(F, own_rows, D),
        normed_first,
        full_query,
        full_kv,
        tokens[0],
        inverse_first,
        gain_first[None],
        d_residual,
        gain_second_grad[None],
    )
    return results(output, grad_tokens, down_all, up_all, out_all, query_all, kv_all)


def widen_kernel(
    low_ref, grad_ref, down_ref, up_ref, o_ref, q_ref, kv_ref, output, grad_tokens, grad_down, grad_up, grad_o, grad_q, grad_k, grad_v, gains
):
    output[0] = low_ref[...]
    grad_tokens[0] = grad_ref[...]
    grad_down[...] = down_ref[...].astype(F32)
    width = up_ref.shape[2]
    for i in range(up_ref.shape[0]):
        grad_up[:, i * width : (i + 1) * width] = up_ref[i].astype(F32)
    grad_o[...] = o_ref[...].astype(F32)
    grad_q[...] = q_ref[...].astype(F32)

    @pl.when(pl.program_id(0) == 0)
    def _():
        rows = kv_ref.shape[2] - 16
        for i in range(kv_ref.shape[1]):
            grad_k[i * rows : (i + 1) * rows, :] = kv_ref[0, i, :rows, :].astype(F32)
            grad_v[i * rows : (i + 1) * rows, :] = kv_ref[1, i, :rows, :].astype(F32)
        for i in range(2):
            gains[i] = kv_ref[i, 0, rows:, :].astype(F32)


def results(output, grad_tokens, down_all, up_all, out_all, query_all, kv_all):
    tok, D = output.shape
    F, own_rows, width = up_all.shape
    steps = max(1, own_rows // 256)

    def rows(n, cols):
        return pl.BlockSpec((n // steps, cols), lambda i: (i, 0))

    def whole(*shape):
        return pl.BlockSpec(shape, lambda i: (0,) * len(shape))

    def first(n, cols):
        return pl.BlockSpec((1, n // steps, cols), lambda i: (0, i, 0))

    down_rows = down_all.shape[0]
    shapes = [(down_rows, D), (own_rows, F * width), (own_rows, D), (own_rows, D), (own_rows, HS), (own_rows, HS), (2, 16, HS)]
    out, grad_tokens, down, up, o, q, k, v, gains = pl.pallas_call(
        widen_kernel,
        grid=(steps,),
        out_shape=[jax.ShapeDtypeStruct((1, tok, D), BF), jax.ShapeDtypeStruct((1, tok, D), F32)]
        + [jax.ShapeDtypeStruct(shape, F32) for shape in shapes],
        in_specs=[
            rows(tok, D),
            rows(tok, D),
            rows(down_rows, D),
            pl.BlockSpec((F, own_rows // steps, width), lambda i: (0, i, 0)),
            rows(own_rows, D),
            rows(own_rows, D),
            whole(*kv_all.shape),
        ],
        out_specs=[
            first(tok, D),
            first(tok, D),
            rows(down_rows, D),
            rows(own_rows, F * width),
            rows(own_rows, D),
            rows(own_rows, D),
            whole(own_rows, HS),
            whole(own_rows, HS),
            whole(2, 16, HS),
        ],
        compiler_params=pltpu.CompilerParams(vmem_limit_bytes=LIMIT),
        name="widen",
    )(output, grad_tokens, down_all, up_all, out_all, query_all, kv_all)
    gains = gains[:, : own_rows // HS].reshape(2, own_rows)
    return out, grad_tokens, gains[0], q, k, v, o, gains[1], up, down


def solution(mesh):
    placed = (
        P("fsdp", "seq", None),
        P("fsdp", "seq", None),
        P(),
        P(),
        P("fsdp"),
        P("fsdp", None),
        P("fsdp", None),
        P("fsdp", None),
        P("fsdp", None),
        P("fsdp"),
        P("fsdp", None),
        P("fsdp", None),
    )
    return jax.shard_map(
        local,
        mesh=mesh,
        in_specs=placed,
        out_specs=(
            P("fsdp", "seq", None),
            P("fsdp", "seq", None),
            P("fsdp"),
            P("fsdp", None),
            P("fsdp", None),
            P("fsdp", None),
            P("fsdp", None),
            P("fsdp"),
            P("fsdp", None),
            P("fsdp", None),
        ),
        check_vma=False,
    )
```

```python
import functools
import math
import types

import jax
import jax.numpy as jnp
from jax import lax
from jax.experimental import pallas as pl
from jax.experimental.pallas import tpu as pltpu
from jax.sharding import PartitionSpec as P

H = 8
HS = 128
EPS = 1e-05
NEG = -1e30
LIMIT = 60 * 2**20
CHUNK = 512
BF = jnp.bfloat16
F32 = jnp.float32


def nt(a, b):
    return lax.dot_general(a, b, (((1,), (1,)), ((), ())), preferred_element_type=F32)


def nn(a, b):
    return lax.dot_general(a, b, (((1,), (0,)), ((), ())), preferred_element_type=F32)


def tn(a, b):
    return lax.dot_general(a, b, (((0,), (0,)), ((), ())), preferred_element_type=F32)


def query_range(scal, tok):
    first = scal[0] * tok
    pos = first + lax.broadcasted_iota(jnp.int32, (1, tok), 1)
    start = jnp.zeros((1, tok), jnp.int32)
    latest = jnp.int32(0)
    for i in range(1, scal.shape[0]):
        end = scal[i]
        start = jnp.maximum(start, jnp.where(end <= pos, end, 0))
        latest = jnp.maximum(latest, jnp.where(end <= first + tok - 1, end, 0))
    return first, pos, start, latest


def chunk_loop(scal, tok, window, step):
    first, pos, start, latest = query_range(scal, tok)
    chunks = (first + tok + CHUNK - 1) // CHUNK

    def body(j, carry):
        low = j * CHUNK
        whole = jnp.logical_and(low >= latest, low + CHUNK - 1 <= first)

        @pl.when(whole)
        def _():
            step(j, None)

        @pl.when(jnp.logical_not(whole))
        def _():
            keys = low + lax.broadcasted_iota(jnp.int32, (CHUNK, tok), 0)
            step(j, jnp.logical_and(keys >= start, keys <= pos))

        return carry

    lax.fori_loop(0, chunks, body, 0)
    return chunks


def attend_kernel(scal, q_ref, kv_ref, out_ref, lse_ref, acc, top, total):
    tok = q_ref.shape[0]
    factor = math.log2(math.e) / math.sqrt(HS)
    top[...] = jnp.full(top.shape, -3e38, F32)
    total[...] = jnp.zeros(total.shape, F32)
    acc[...] = jnp.zeros(acc.shape, F32)

    def step(j, mask):
        rows = pl.ds(pl.multiple_of(j * CHUNK, CHUNK), CHUNK)
        keys = kv_ref[rows, :HS]
        values_t = kv_ref[rows, HS:].T
        for h in range(H):
            scores = nt(keys, q_ref[:, h * HS : (h + 1) * HS])
            if mask is not None:
                scores = jnp.where(mask, scores, NEG)
            old = top[h : h + 1, :]
            new = jnp.maximum(old, jnp.max(scores, axis=0, keepdims=True) * factor)
            shrink = jnp.exp2(old - new)
            probs = jnp.exp2(scores * factor - new)
            total[h : h + 1, :] = total[h : h + 1, :] * shrink + jnp.sum(probs, axis=0, keepdims=True)
            acc[h] = acc[h] * shrink + nn(values_t, probs.astype(BF))
            top[h : h + 1, :] = new

    chunk_loop(scal, tok, kv_ref.shape[0], step)
    for h in range(H):
        mixed = acc[h] * (1.0 / total[h : h + 1, :])
        out_ref[:, h * HS : (h + 1) * HS] = mixed.T.astype(BF)
    lse_ref[...] = top[...] + jnp.log2(total[...])


VMEM = pl.BlockSpec(memory_space=pltpu.VMEM)
SMEM = pl.BlockSpec(memory_space=pltpu.SMEM)
PARAMS = pltpu.CompilerParams(vmem_limit_bytes=40 * 2**20)


def attend(scal, queries, window_kv):
    tok = queries.shape[0]
    window = window_kv.shape[0]
    return pl.pallas_call(
        attend_kernel,
        out_shape=(
            jax.ShapeDtypeStruct((tok, H * HS), BF),
            jax.ShapeDtypeStruct((H, tok), F32),
        ),
        in_specs=[SMEM, VMEM, VMEM],
        out_specs=(VMEM, VMEM),
        scratch_shapes=[
            pltpu.VMEM((H, HS, tok), F32),
            pltpu.VMEM((H, tok), F32),
            pltpu.VMEM((H, tok), F32),
        ],
        compiler_params=PARAMS,
        cost_estimate=pl.CostEstimate(
            flops=8 * tok * window * H * HS, bytes_accessed=4 * window * HS, transcendentals=tok * window * H
        ),
        name="attend",
    )(scal, queries, window_kv)


MESH = pl.DeviceIdType.MESH


TAIL_IN = (
    "ends",
    "q_ref",
    "kv_ref",
    "d_ref",
    "att_ref",
    "lse_ref",
    "gd_ref",
    "gu_ref",
    "go_ref",
    "n1_ref",
    "wq_ref",
    "wkv_ref",
    "tok_ref",
    "inv_ref",
    "gain_ref",
    "dres_ref",
    "gain2_ref",
)
TAIL_OUT = (
    "out_down",
    "out_up",
    "out_o",
    "out_q",
    "out_kv",
    "grad_tokens",
)
TAIL_SCRATCH = (
    "acc",
    "delta",
    "dq",
    "dkv",
    "dkv_c",
    "dkv_x",
    "dkv_z",
    "d_kv",
    "dn1",
    "gq_ref",
    "gkv_ref",
    "xr_d",
    "xr_u",
    "zs_d",
    "zs_u",
    "zr_d",
    "zr_u",
    "sh_d",
    "sh_u",
    "yr_u",
    "o_c",
    "o_y",
    "o_x",
    "o_z",
    "o_s",
    "q_c",
    "q_y",
    "q_x",
    "q_z",
    "q_s",
    "kv_c",
    "kv_y",
    "kv_x",
    "kv_z",
    "kv_s",
    "gain_rows",
    "send_sem",
    "recv_sem",
    "copy_sem",
)


def head_block(h, tok):
    return slice(h % 2 * HS, (h % 2 + 1) * HS), slice(h // 2 * tok, (h // 2 + 1) * tok)


def tail_kernel(dims, head, names, *refs):
    A, B, F = dims
    r = types.SimpleNamespace(**dict(zip(names, refs, strict=True)))
    if head is not None:
        for name, held in AGAIN.items():
            setattr(r, name, getattr(r, held))
    ends = r.ends
    q_ref = r.q_ref
    kv_ref = r.kv_ref
    d_ref = r.d_ref
    att_ref = r.att_ref
    lse_ref = r.lse_ref
    gd_ref = r.gd_ref
    gu_ref = r.gu_ref
    go_ref = r.go_ref
    n1_ref = r.n1_ref
    wq_ref = r.wq_ref
    wkv_ref = r.wkv_ref
    tok_ref = r.tok_ref
    inv_ref = r.inv_ref
    gain_ref = r.gain_ref
    dres_ref = r.dres_ref
    gain2_ref = r.gain2_ref
    out_down = r.out_down
    out_up = r.out_up
    out_o = r.out_o
    out_q = r.out_q
    out_kv = r.out_kv
    grad_tokens = r.grad_tokens
    acc = r.acc
    delta = r.delta
    dq = r.dq
    dkv = r.dkv
    dkv_c = r.dkv_c
    dkv_x = r.dkv_x
    dkv_z = r.dkv_z
    d_kv = r.d_kv
    dn1 = r.dn1
    gq_ref = r.gq_ref
    gkv_ref = r.gkv_ref
    xr_d = r.xr_d
    xr_u = r.xr_u
    zs_d = r.zs_d
    zs_u = r.zs_u
    zr_d = r.zr_d
    zr_u = r.zr_u
    sh_d = r.sh_d
    sh_u = r.sh_u
    yr_u = r.yr_u
    o_c = r.o_c
    o_y = r.o_y
    o_x = r.o_x
    o_z = r.o_z
    o_s = r.o_s
    q_c = r.q_c
    q_y = r.q_y
    q_x = r.q_x
    q_z = r.q_z
    q_s = r.q_s
    kv_c = r.kv_c
    kv_y = r.kv_y
    kv_x = r.kv_x
    kv_z = r.kv_z
    kv_s = r.kv_s
    gain_rows = r.gain_rows
    send_sem = r.send_sem
    recv_sem = r.recv_sem
    copy_sem = r.copy_sem
    tok = q_ref.shape[0]
    window = kv_ref.shape[0]
    D = n1_ref.shape[1]
    own_rows = D // F
    shard = gd_ref.shape[0]
    s = lax.axis_index("seq")
    f = lax.axis_index("fsdp")
    c = lax.rem(s, 2)
    b = lax.rem(s // 2, B)
    a = s // (2 * B)

    def device(axis, step):
        at = {"a": a, "b": b, "c": c, "f": f}
        at[axis] = lax.rem(at[axis] + step, {"a": A, "b": B, "c": 2, "f": F}[axis])
        return ((at["a"] * B + at["b"]) * 2 + at["c"], at["f"])

    def lower(axis, step):
        return lax.rem({"a": a + A, "b": b + B, "f": f + F}[axis] - step, {"a": A, "b": B, "f": F}[axis])

    def flip(axis_bit, place=None):
        place = a if place is None else place
        return place + axis_bit - 2 * axis_bit * lax.rem(place // axis_bit, 2) if axis_bit else place

    def offset(o):
        place = a
        for bit in bits:
            if o // bit % 2:
                place = flip(bit, place)
        return place

    def along_a(bit):
        return ((flip(bit) * B + b) * 2 + c, f)

    bits = [2**i for i in range(A.bit_length() - 1)]
    assert 2 ** len(bits) == A
    order = [o for bit in bits for o in range(A) if o // bit % 2 and o % bit == 0] + [0]

    def low_bit(o):
        return next((bit for bit in bits if o // bit % 2), A)

    used = [0]

    def slots(n=1):
        used[0] += n
        assert used[0] <= send_sem.shape[0]
        return used[0] - n

    def remote(src, dst, slot, to):
        return pltpu.make_async_remote_copy(
            src_ref=src, dst_ref=dst, send_sem=send_sem.at[slot], recv_sem=recv_sem.at[slot], device_id=to, device_id_type=MESH
        )

    pending = []

    def start(src, dst, slot, to):
        copy = remote(src, dst, slot, to)
        copy.start()
        pending.append(copy)
        return copy

    barrier = pltpu.get_barrier_semaphore()
    partners = [("a", k) for k in range(1, A)] + [("b", k) for k in range(1, B)] + [("c", 1)] + [("f", k) for k in range(1, F)]
    for axis, k in partners:
        pl.semaphore_signal(barrier, inc=1, device_id=device(axis, k), device_id_type=MESH)
    pl.semaphore_wait(barrier, len(partners))

    r_d = shard // (A * B)
    r_u = own_rows // B
    w_u = shard // A
    x_d = slots(A * (B - 1))
    x_u = slots(A * (B - 1))
    z_d = slots(A - 1)
    z_u = slots(A - 1)

    def down_copies(i):
        at = offset(order[i])
        copies = []
        for kb in range(B - 1):
            other = lax.rem(b + kb + 1, B)
            rows = pl.ds(pl.multiple_of((other * A + at) * r_d, r_d), r_d)
            copies.append(remote(gd_ref.at[rows, :], xr_d.at[kb, i], x_d + kb * A + i, device("b", kb + 1)))
        return copies

    def up_copies(i):
        at = offset(order[i])
        copies = []
        for kb in range(B - 1):
            rows = pl.ds(pl.multiple_of(lax.rem(b + kb + 1, B) * r_u, r_u), r_u)
            cols = pl.ds(pl.multiple_of(at * w_u, w_u), w_u)
            copies.append(remote(gu_ref.at[:, rows, cols], xr_u.at[kb, i], x_u + kb * A + i, device("b", kb + 1)))
        return copies

    def send_down(first, last):
        for i in range(first, last):
            for copy in down_copies(i):
                copy.start()

    def send_up(first, last):
        for i in range(first, last):
            for copy in up_copies(i):
                copy.start()

    def down_sum(i):
        for copy in down_copies(i):
            copy.wait()
        at = offset(order[i])
        rows = pl.ds(pl.multiple_of((b * A + at) * r_d, r_d), r_d)
        total = gd_ref[rows, :].astype(F32)
        for kb in range(B - 1):
            total = total + xr_d[kb, i].astype(F32)
        return total

    def up_sum(i):
        for copy in up_copies(i):
            copy.wait()
        at = offset(order[i])
        rows = pl.ds(pl.multiple_of(b * r_u, r_u), r_u)
        cols = pl.ds(pl.multiple_of(at * w_u, w_u), w_u)
        total = gu_ref[:, rows, cols].astype(F32)
        for kb in range(B - 1):
            total = total + xr_u[kb, i].astype(F32)
        return total

    def z_index(o, bit):
        return order.index(o + bit)

    def down_z(i):
        return remote(zs_d.at[i], zr_d.at[i], z_d + i, along_a(low_bit(order[i])))

    def up_z(i):
        return remote(zs_u.at[i], zr_u.at[i], z_u + i, along_a(low_bit(order[i])))

    def z_added(i, total, copy, got):
        o = order[i]
        for bit in bits:
            if bit < low_bit(o):
                k = z_index(o, bit)
                copy(k).wait()
                total = total + got[k].astype(F32)
        return total

    def down_step(i):
        zs_d[i] = z_added(i, down_sum(i), down_z, zr_d).astype(BF)
        down_z(i).start()

    def up_step(i):
        zs_u[i] = z_added(i, up_sum(i), up_z, zr_u).astype(BF)
        up_z(i).start()

    def down_share():
        sh_d[...] = z_added(A - 1, down_sum(A - 1), down_z, zr_d).astype(BF)
        gather_down.begin()

    up_y = slots(F - 1)

    def up_y_copy(kf):
        return remote(yr_u.at[lax.rem(f + kf + 1, F)], sh_u.at[f], up_y + kf, device("f", kf + 1))

    def up_share():
        total = z_added(A - 1, up_sum(A - 1), up_z, zr_u)
        yr_u[...] = total.astype(BF)
        for kf in range(F - 1):
            up_y_copy(kf).start()
        sh_u[f] = yr_u[f]

    def up_gather():
        for kf in range(F - 1):
            up_y_copy(kf).wait()
        gather_up.begin()

    gathers = []

    class Gather:
        def __init__(self, share, view, planes=True):
            self.share, self.view, self.n = share, view, B if planes else 1
            self.z_slot = slots(A)
            self.x_slot = slots((self.n - 1) * A)
            self.c_slot = slots(self.n * A)
            self.place = len(gathers)
            gathers.append(self)

        def local(self):
            return pltpu.make_async_copy(self.share, self.view(c, b, a), copy_sem.at[self.place])

        def at(self, o, kb=0):
            return self.view(c, lower("b", kb) if kb else b, offset(o))

        def z(self, bit, o):
            here = self.at(o)
            return remote(here if o else self.share, here, self.z_slot + A - A // bit + o // (2 * bit), along_a(bit))

        def x(self, kb, o):
            here = self.at(o)
            return remote(here if o else self.share, here, self.x_slot + kb * A + o, device("b", kb + 1))

        def c(self, kb, o):
            here = self.at(o, kb)
            return remote(here if kb or o else self.share, here, self.c_slot + kb * A + o, device("c", 1))

        def begin(self):
            self.local().start()
            for bit in bits[::-1]:
                self.z(bit, 0).start()
            self.pass_on(0)

        def pass_on(self, o):
            for kb in range(self.n - 1):
                self.x(kb, o).start()
            self.c(0, o).start()

        def from_a(self, stages=None):
            for i, bit in enumerate(bits[::-1]):
                if stages is not None and i not in stages:
                    continue
                for o in range(0, A, 2 * bit):
                    self.z(bit, o).wait_recv()
                    for lower_bit in bits[: len(bits) - 1 - i][::-1]:
                        self.z(lower_bit, o + bit).start()
                    self.pass_on(o + bit)

        def from_b(self):
            for kb in range(self.n - 1):
                for o in self.offsets():
                    self.x(kb, o).wait_recv()
                    self.c(kb + 1, o).start()

        def offsets(self):
            found = [0]
            for bit in bits[::-1]:
                found += [o + bit for o in found]
            return found

        def end(self):
            self.local().wait()
            for bit in bits:
                for o in range(0, A, 2 * bit):
                    self.z(bit, o).wait_send()
            for o in range(A):
                for kb in range(self.n - 1):
                    self.x(kb, o).wait_send()
                for kb in range(self.n):
                    self.c(kb, o).wait()

    def view_down(c_, b_, a_):
        return out_down.at[pl.ds(pl.multiple_of(((c_ * B + b_) * A + a_) * r_d, r_d), r_d), :]

    def view_up(c_, b_, a_):
        rows = pl.ds(pl.multiple_of(b_ * r_u, r_u), r_u)
        return out_up.at[:, rows, pl.ds(pl.multiple_of(c_ * shard + a_ * w_u, w_u), w_u)]

    half = D // 2
    w_o = half // A

    def view_square(out):
        def view(c_, b_, a_):
            rows = pl.ds(pl.multiple_of(b_ * r_u, r_u), r_u)
            return out.at[rows, pl.ds(pl.multiple_of(c_ * half + a_ * w_o, w_o), w_o)]

        return view

    gather_down = Gather(sh_d, view_down)
    gather_up = Gather(sh_u, view_up)
    gather_o = Gather(o_s, view_square(out_o))
    gather_q = Gather(q_s, view_square(out_q))
    gather_kv = Gather(kv_s, lambda c_, b_, a_: out_kv.at[c_, a_], planes=False)

    if head is None:
        send_down(0, A)
        send_up(0, A)
    else:
        own = types.SimpleNamespace(
            A=A, B=B, F=F, a=a, b=b, c=c, f=f, s=s, slots=slots, remote=remote, device=device, lower=lower,
            send_down=send_down, send_up=send_up, down_step=down_step, offset=offset, order=order,
        )
        finish_output, finish_head = head(r, own)

    def reduce_y(ref, got, sent, width):
        mine = pl.ds(pl.multiple_of(c * width, width), width)

        def add(i, carry):
            sent[i] = (ref[i, :, mine].astype(F32) + got[i].astype(F32)).astype(BF)
            return carry

        lax.fori_loop(0, F, add, 0)

    class Square:
        def __init__(self, grad, got_c, got_y, got_x, got_z, share, gather):
            self.grad, self.got_c, self.got_y, self.got_x, self.got_z = grad, got_c, got_y, got_x, got_z
            self.share, self.gather = share, gather
            self.c_slot, self.y_slot, self.x_slot = slots(), slots(F - 1), slots(B - 1)

        def c(self):
            other = pl.ds(pl.multiple_of((1 - c) * half, half), half)
            return remote(self.grad.at[:, :, other], self.got_c, self.c_slot, device("c", 1))

        def y(self, kf):
            return remote(self.got_c.at[lax.rem(f + kf + 1, F)], self.got_y.at[kf], self.y_slot + kf, device("f", kf + 1))

        def over_c(self):
            self.c().start()

        def over_f(self):
            self.c().wait()
            reduce_y(self.grad, self.got_c, self.got_c, half)
            for kf in range(F - 1):
                self.y(kf).start()

        def over_b(self):
            total = self.got_c[f].astype(F32)
            for kf in range(F - 1):
                self.y(kf).wait()
                total = total + self.got_y[kf].astype(F32)
            self.got_y[F - 1] = total.astype(BF)
            for kb in range(B - 1):
                self.x(kb).start()

        def x(self, kb):
            rows = pl.ds(pl.multiple_of(lax.rem(b + kb + 1, B) * r_u, r_u), r_u)
            return remote(self.got_y.at[F - 1, rows, :], self.got_x.at[kb], self.x_slot + kb, device("b", kb + 1))

        def over_a(self):
            rows = pl.ds(pl.multiple_of(b * r_u, r_u), r_u)
            total = self.got_y[F - 1, rows, :].astype(F32)
            for kb in range(B - 1):
                self.x(kb).wait()
                total = total + self.got_x[kb].astype(F32)
            self.got_x[B - 1] = total.astype(BF)
            self.copies = []
            for ka in range(A - 1):
                cols = pl.ds(pl.multiple_of(lax.rem(a + ka + 1, A) * w_o, w_o), w_o)
                self.copies.append(start(self.got_x.at[B - 1, :, cols], self.got_z.at[ka], slots(), device("a", ka + 1)))

        def finish(self):
            cols = pl.ds(pl.multiple_of(a * w_o, w_o), w_o)
            total = self.got_x[B - 1, :, cols].astype(F32)
            for ka in range(A - 1):
                self.copies[ka].wait()
                total = total + self.got_z[ka].astype(F32)
            self.share[...] = total.astype(BF)
            self.gather.begin()

    square_o = Square(go_ref, o_c, o_y, o_x, o_z, o_s, gather_o)
    square_q = Square(gq_ref, q_c, q_y, q_x, q_z, q_s, gather_q)

    square_o.over_c()

    scale = 1.0 / math.sqrt(HS)
    factor = math.log2(math.e) * scale
    acc[...] = jnp.zeros(acc.shape, F32)
    for h in range(H):
        cols = slice(h * HS, (h + 1) * HS)
        both = d_ref[:, cols].astype(F32) * att_ref[:, cols].astype(F32)
        delta[h : h + 1, :] = jnp.sum(both.T, axis=0, keepdims=True)
    first = s * tok
    pos = first + lax.broadcasted_iota(jnp.int32, (1, tok), 1)
    begin = jnp.zeros((1, tok), jnp.int32)
    for i in range(ends.shape[0]):
        begin = jnp.maximum(begin, jnp.where(ends[i] <= pos, ends[i], 0))

    def step(j, masked):
        rows = pl.ds(pl.multiple_of(j * CHUNK, CHUNK), CHUNK)
        keys = kv_ref[rows, :HS]
        values = kv_ref[rows, HS:]
        keys_t = keys.T
        if masked:
            at = j * CHUNK + lax.broadcasted_iota(jnp.int32, (CHUNK, tok), 0)
            mask = jnp.logical_and(at >= begin, at <= pos)
        else:
            seen = begin <= j * CHUNK
        d_keys = jnp.zeros((CHUNK, HS), F32)
        d_values = jnp.zeros((CHUNK, HS), F32)
        for h in range(H):
            cols = slice(h * HS, (h + 1) * HS)
            q = q_ref[:, cols]
            d = d_ref[:, cols]
            scores = nt(keys, q)
            if masked:
                scores = jnp.where(mask, scores, NEG)
            lse = lse_ref[h : h + 1, :]
            if not masked:
                lse = jnp.where(seen, lse, 3e38)
            probs = jnp.exp2(scores * factor - lse)
            d_probs = nt(values, d)
            d_scores = (probs * (d_probs - delta[h : h + 1, :])).astype(BF)
            d_values = d_values + nn(probs.astype(BF), d)
            d_keys = d_keys + nn(d_scores, q)
            acc[head_block(h, tok)] += nn(keys_t, d_scores)
        for i in range(2):
            part = slice(i * tok, (i + 1) * tok)
            dkv[j, i, :, :HS] = (d_keys[part] * scale).astype(BF)
            dkv[j, i, :, HS:] = d_values[part].astype(BF)

    chunks = s // 2 + 1
    def attention_chunk(j, carry):
        plain = jnp.logical_and(j > 0, j < chunks - 1)

        @pl.when(plain)
        def _():
            step(j, False)

        @pl.when(jnp.logical_not(plain))
        def _():
            step(j, True)

        return carry

    first = 0 if head is None else min(3, A - 1)
    steps = [functools.partial(down_step, i) for i in range(first, A - 1)]
    steps += [functools.partial(up_step, i) for i in range(A - 2)] + [down_share, functools.partial(up_step, A - 2), square_o.over_b]
    if A == 4 and head is not None:
        acts = [(1, steps[0]), (3, steps[1]), (4, steps[2]), (5, steps[4]), (2, square_o.over_f)]
    else:
        acts = [(0, square_o.over_f), *((1, act) for act in steps)]

    def chunk_and_step(j, carry):
        @pl.when(j < chunks)
        def _():
            attention_chunk(j, 0)

        for time, act in acts:
            pl.when(j == time)(act)
        return carry

    lax.fori_loop(0, window // CHUNK, chunk_and_step, 0)

    def clear(j, carry):
        dkv[j] = jnp.zeros(dkv.shape[1:], BF)
        return carry

    lax.fori_loop(chunks, window // CHUNK, clear, 0)

    dkv_c_copy = start(dkv.at[:, 1 - c], dkv_c, slots(), device("c", 1))


    if head is not None:
        finish_output()
    for h in range(H):
        dq[:, h * HS : (h + 1) * HS] = (acc[head_block(h, tok)] * scale).T.astype(BF)
    n_rows = 128

    def query_grad(i, carry):
        col = pl.ds(pl.multiple_of(i * n_rows, n_rows), n_rows)
        fi = i // (own_rows // n_rows)
        row = lax.rem(i, own_rows // n_rows) * n_rows
        gq_ref[fi, pl.ds(pl.multiple_of(row, n_rows), n_rows), :] = nn(n1_ref[:, col].T, dq[...]).astype(BF)
        return carry

    lax.fori_loop(0, D // n_rows, query_grad, 0)
    square_q.over_c()

    dkv_c_copy.wait()

    def add_c(j, carry):
        dkv_c[j] = (dkv_c[j].astype(F32) + dkv[j, c].astype(F32)).astype(BF)
        return carry

    lax.fori_loop(0, A * B, add_c, 0)
    x_kv = []
    for kb in range(B - 1):
        other = lax.rem(b + kb + 1, B)
        for j in range(A):
            x_kv.append(start(dkv_c.at[j * B + other], dkv_x.at[kb, j], slots(), device("b", kb + 1)))

    if A == 4 and head is not None:
        steps[3]()
    square_q.over_f()
    gather_down.from_a((0,))
    up_share()
    square_q.over_b()
    for i in range(1, len(bits)):
        gather_down.from_a((i,))
    square_o.over_a()

    for copy in x_kv:
        copy.wait()

    def add_x(j, carry):
        total = dkv_c[j * B + b].astype(F32)
        for kb in range(B - 1):
            total = total + dkv_x[kb, j].astype(F32)
        dkv_x[0, j] = total.astype(BF)
        return carry

    lax.fori_loop(0, A, add_x, 0)
    z_kv = slots(A - 1)
    for k in range(A - 1, 0, -1):

        @pl.when(a - k >= 0)
        def _():
            to = (((a - k) * B + b) * 2 + c, f)
            remote(dkv_x.at[0, jnp.maximum(a - k, 0)], dkv_z.at[k - 1], z_kv + k - 1, to).start()

    up_gather()

    total = dkv_x[0, a].astype(F32)
    d_kv[...] = total
    for k in range(1, A):
        copy = remote(dkv_x.at[0, jnp.maximum(a - k, 0)], dkv_z.at[k - 1], z_kv + k - 1, device("a", A - k))

        @pl.when(a - k >= 0)
        def _():
            copy.wait_send()

        @pl.when(a + k < A)
        def _():
            copy.wait_recv()
            d_kv[...] = d_kv[...] + dkv_z[k - 1].astype(F32)

    d_kv_low = d_kv[...].astype(BF)

    n_cols = 256
    mean = jnp.zeros((tok, 1), F32)
    for i in range(D // n_cols):
        cols = slice(i * n_cols, (i + 1) * n_cols)
        part = nt(dq[...], wq_ref[cols, :]) + nt(d_kv_low, wkv_ref[cols, :])
        dn1[:, cols] = part
        weighted = part * (tok_ref[:, cols].astype(F32) * inv_ref[...])
        gain_rows[0:1, cols] = jnp.sum(weighted, axis=0, keepdims=True)
        mean = mean + jnp.sum(weighted * gain_ref[:, cols], axis=1, keepdims=True)
    if head is None:
        gain_rows[1:2, :] = gain2_ref[...]
    mean = mean * (1.0 / D)

    r_kv = own_rows // A
    rows_kv = r_kv + 16
    for fi in range(F):
        for i in range(A):
            at = fi * own_rows + i * r_kv
            part = tn(n1_ref[:, at : at + r_kv], d_kv_low).astype(BF)
            gkv_ref[0, fi, i, :r_kv, :] = part[:, :HS]
            gkv_ref[1, fi, i, :r_kv, :] = part[:, HS:]
            for ci in range(2):
                rows = [gain_rows[ci : ci + 1, fi * own_rows + k * 128 : fi * own_rows + (k + 1) * 128] for k in range(own_rows // 128)]
                block = jnp.concatenate(rows + [jnp.zeros((16 - len(rows), 128), F32)], axis=0)
                gkv_ref[ci, fi, i, r_kv:, :] = block.astype(BF)
    kv_c_copy = start(gkv_ref.at[1 - c], kv_c, slots(), device("c", 1))

    square_q.over_a()
    for i in range(D // n_cols):
        cols = slice(i * n_cols, (i + 1) * n_cols)
        grad_tokens[:, cols] = dres_ref[:, cols] + inv_ref[...] * (
            dn1[:, cols] * gain_ref[:, cols] - tok_ref[:, cols].astype(F32) * inv_ref[...] * mean
        )
    kv_c_copy.wait()
    kv_c[...] = (kv_c[...].astype(F32) + gkv_ref[c].astype(F32)).astype(BF)
    kv_f = [start(kv_c.at[lax.rem(f + kf + 1, F)], kv_y.at[kf], slots(), device("f", kf + 1)) for kf in range(F - 1)]
    square_o.finish()
    gather_up.from_a((0,))
    total = kv_c[f].astype(F32)
    for kf in range(F - 1):
        kv_f[kf].wait()
        total = total + kv_y[kf].astype(F32)
    kv_y[F - 1] = total.astype(BF)
    kv_b = [start(kv_y.at[F - 1], kv_x.at[kb], slots(), device("b", kb + 1)) for kb in range(B - 1)]
    square_q.finish()
    for i in range(1, len(bits)):
        gather_up.from_a((i,))
    total = kv_y[F - 1].astype(F32)
    for kb in range(B - 1):
        kv_b[kb].wait()
        total = total + kv_x[kb].astype(F32)
    kv_x[B - 1] = total.astype(BF)
    kv_a = [start(kv_x.at[B - 1, lax.rem(a + ka + 1, A)], kv_z.at[ka], slots(), device("a", ka + 1)) for ka in range(A - 1)]
    gather_o.from_a()
    gather_q.from_a((0,))
    total = kv_x[B - 1, a].astype(F32)
    for ka in range(A - 1):
        kv_a[ka].wait()
        total = total + kv_z[ka].astype(F32)
    kv_s[...] = total.astype(BF)
    gather_kv.begin()
    for i in range(1, len(bits)):
        gather_q.from_a((i,))
    gather_down.from_b()
    gather_up.from_b()
    gather_kv.from_a()
    gather_o.from_b()
    gather_q.from_b()
    for gather in gathers:
        gather.end()
    if head is not None:
        finish_head()


def tail_shapes(dims, tok, D, shard, window, extra):
    A, B, F = dims
    own_rows = D // F
    half, r_d, r_u, w_u = D // 2, shard // (A * B), own_rows // B, shard // A
    w_o, r_kv = half // A, own_rows // A + 16

    def low(*shape):
        return pltpu.VMEM(shape, BF)

    square = [low(F, own_rows, half), low(F, own_rows, half), low(B, r_u, half), low(A - 1, r_u, w_o), low(r_u, w_o)]
    n_sems = extra + 2 * (A * (B - 1) + A - 1) + 4 * (A + (B - 1) * A + B * A) + 2 * A
    n_sems += 2 * (F + B + A) + 2 * F + (B - 1) * A + A + F + B + A + 8
    outs = (
        jax.ShapeDtypeStruct((2 * shard, D), BF),
        jax.ShapeDtypeStruct((F, own_rows, 2 * shard), BF),
        jax.ShapeDtypeStruct((own_rows, D), BF),
        jax.ShapeDtypeStruct((own_rows, D), BF),
        jax.ShapeDtypeStruct((2, A, r_kv, HS), BF),
        jax.ShapeDtypeStruct((tok, D), F32),
    )
    scratch = [
        pltpu.VMEM((2 * HS, H // 2 * tok), F32),
        pltpu.VMEM((H, tok), F32),
        low(tok, D),
        low(A * B, 2, tok, 2 * HS),
        low(A * B, tok, 2 * HS),
        low(max(1, B - 1), A, tok, 2 * HS),
        low(max(1, A - 1), tok, 2 * HS),
        pltpu.VMEM((tok, 2 * HS), F32),
        pltpu.VMEM((tok, D), F32),
        low(F, own_rows, D),
        low(2, F, A, r_kv, HS),
        low(B - 1, A, r_d, D),
        low(B - 1, A, F, r_u, w_u),
        low(A - 1, r_d, D),
        low(A - 1, F, r_u, w_u),
        low(A - 1, r_d, D),
        low(A - 1, F, r_u, w_u),
        low(r_d, D),
        low(F, r_u, w_u),
        low(F, r_u, w_u),
        *square,
        *square,
        low(F, A, r_kv, HS),
        low(F, A, r_kv, HS),
        low(B, A, r_kv, HS),
        low(A - 1, r_kv, HS),
        low(r_kv, HS),
        pltpu.VMEM((8, D), F32),
        pltpu.SemaphoreType.DMA((n_sems,)),
        pltpu.SemaphoreType.DMA((n_sems,)),
        pltpu.SemaphoreType.DMA((5,)),
    ]
    return outs, scratch


def tail(dims, ends, queries, window_kv, d_attended, attended, lse, grad_down, grad_up, grad_out, n1, wq, wkv, tokens, inv, gain, dres, gain2):
    A, B, F = dims
    tok, D = n1.shape
    window = window_kv.shape[0]
    outs, scratch = tail_shapes(dims, tok, D, grad_down.shape[0], window, 0)
    hbm = pl.BlockSpec(memory_space=pltpu.HBM)
    return pl.pallas_call(
        functools.partial(tail_kernel, dims, None, TAIL_IN + TAIL_OUT + TAIL_SCRATCH),
        out_shape=outs,
        in_specs=[SMEM] + [VMEM] * 16,
        out_specs=(hbm,) * 5 + (VMEM,),
        scratch_shapes=scratch,
        compiler_params=pltpu.CompilerParams(vmem_limit_bytes=56 * 2**20, collective_id=1, has_side_effects=True),
        cost_estimate=pl.CostEstimate(flops=20 * tok * window * D, bytes_accessed=2**25, transcendentals=tok * window * H),
        name="tail",
    )(ends, queries, window_kv, d_attended, attended, lse, grad_down, grad_up, grad_out, n1, wq, wkv, tokens, inv, gain, dres, gain2)


HEAD_IN = (
    "lengths",
    "groups",
    "tokens",
    "gain_a_in",
    "gain_f_in",
    "wk_in",
    "wv_in",
    "cot_in",
    "wq_in",
    "wo_in",
    "up_in",
    "down_in",
)
HEAD_SCRATCH = (
    "q_ref",
    "kv_ref",
    "d_ref",
    "att_ref",
    "lse_ref",
    "gd_ref",
    "gu_ref",
    "n1_ref",
    "wq_ref",
    "wkv_ref",
    "inv_ref",
    "gain_ref",
    "dres_ref",
    "gain2_ref",
    "wo_ref",
    "up_ref",
    "down_ref",
    "gains_all",
    "cot_all",
    "n2_all",
    "hid_all",
    "dp_all",
    "res_ref",
    "inv2_ref",
    "dbr_ref",
    "back_s",
    "back_c",
    "back_y",
    "back_r",
    "out_s",
    "out_c",
    "out_y",
    "out_r",
    "loc_sem",
    "ends",
)


def head(r, x):
    A, B, F, a, b, c, f, s = x.A, x.B, x.F, x.a, x.b, x.c, x.f, x.s
    slots, remote, device, lower = x.slots, x.remote, x.device, x.lower
    tok, D = r.tokens.shape
    own_rows = D // F
    shard = r.down_ref.shape[0]
    half = own_rows // 2
    sent = []

    def start(src, dst, to, slot=None):
        copy = remote(src, dst, slots() if slot is None else slot, to)
        copy.start()
        sent.append(copy)
        return copy

    def done(copies):
        for copy in copies:
            copy.wait_send()
            sent[:] = [other for other in sent if other is not copy]

    def span(at, n):
        return pl.ds(pl.multiple_of(at, n), n)

    sibling = device("c", 1)
    mine, mine_half = span(f * own_rows, own_rows), span(c * half, half)
    full_half = span((f * 2 + c) * half, half)

    def to_f(src, dst):
        return [start(src(kf), dst(kf), device("f", kf)) for kf in range(1, F)]

    row = lax.broadcasted_iota(jnp.int32, (16, own_rows), 0)
    both = [ref[...].astype(F32).reshape(1, own_rows) for ref in (r.gain_a_in, r.gain_f_in)]
    r.gains_all[f] = jnp.where(row == 0, *both).astype(BF)
    gains_f = to_f(lambda kf: r.gains_all.at[f], lambda kf: r.gains_all.at[f])
    wk_f = to_f(lambda kf: r.wk_in.at[mine_half, :], lambda kf: r.wkv_ref.at[full_half, :HS])
    wv_f = to_f(lambda kf: r.wv_in.at[mine_half, :], lambda kf: r.wkv_ref.at[full_half, HS:])
    part, up_part = half // B, own_rows // B

    def wo_rows(f_, c_, b_):
        return span(((f_ * 2 + c_) * B + b_) * part, part)

    def up_rows(f_, b_):
        return span((f_ * B + b_) * up_part, up_part)

    wq_f = to_f(lambda kf: r.wq_in.at[span((c * B + b) * part, part), :], lambda kf: r.wq_ref.at[wo_rows(f, c, b), :])
    wo_f = to_f(lambda kf: r.wo_in.at[span((c * B + b) * part, part), :], lambda kf: r.wo_ref.at[wo_rows(f, c, b), :])
    up_f = to_f(
        lambda kf: r.up_in.at[span(b * up_part, up_part), span((lax.rem(f + kf, F) * 2 + c) * shard, shard)],
        lambda kf: r.up_ref.at[up_rows(f, b), :],
    )
    cot_f = to_f(lambda kf: r.cot_in, lambda kf: r.cot_all.at[kf, :tok])
    cot_c = [start(r.cot_in, r.cot_all.at[0, tok:], sibling)]

    local = [
        pltpu.make_async_copy(src, dst, r.loc_sem.at[i])
        for i, (src, dst) in enumerate(
            (
                (r.wq_in, r.wq_ref.at[mine, :]),
                (r.wo_in, r.wo_ref.at[mine, :]),
                (r.up_in.at[:, span((f * 2 + c) * shard, shard)], r.up_ref.at[mine, :]),
                (r.cot_in, r.cot_all.at[0, :tok]),
                (r.down_in.at[span(c * shard, shard), :], r.down_ref),
            )
        )
    ]
    for copy in local:
        copy.start()

    def weight_halves(copies, ref, cols):
        passed = []
        for kf in range(1, F):
            copies[kf - 1].wait_recv()
            rows = span((lower("f", kf) * 2 + c) * half, half)
            passed.append(start(ref.at[rows, cols], ref.at[rows, cols], sibling))
        return passed

    def along_b(copies, ref, rows):
        passed = []
        for kf in range(1, F):
            copies[kf - 1].wait_recv()
            here = ref.at[rows(lower("f", kf)), :]
            passed += [start(here, here, device("b", kb)) for kb in range(1, B)]
        return passed

    group = r.groups[f]
    end = jnp.int32(0)
    for i in range(r.ends.shape[0]):
        end = end + r.lengths[group, i]
        r.ends[i] = end
    n_rows = 64

    def unit_rows(i, carry):
        rows = span(i * n_rows, n_rows)
        stream = r.tokens[rows, :].astype(F32)
        inverse = lax.rsqrt(jnp.mean(stream * stream, axis=1, keepdims=True) + EPS)
        r.inv_ref[rows, :] = inverse
        return carry

    lax.fori_loop(0, tok // n_rows, unit_rows, 0)
    r.wkv_ref[mine, :HS] = r.wk_in[...]
    r.wkv_ref[mine, HS:] = r.wv_in[...]
    for copy in gains_f:
        copy.wait_recv()
    for i in range(F):
        both = r.gains_all[i].astype(F32)
        cols = slice(i * own_rows, (i + 1) * own_rows)
        r.gain_ref[0:1, cols] = both[0:1, :]
        r.gain2_ref[0:1, cols] = both[1:2, :]

    def normed_rows(i, carry):
        rows = span(i * n_rows, n_rows)
        r.n1_ref[rows, :] = (r.tokens[rows, :].astype(F32) * r.inv_ref[rows, :] * r.gain_ref[...]).astype(BF)
        return carry

    lax.fori_loop(0, tok // n_rows, normed_rows, 0)

    wkv_c = weight_halves(wk_f, r.wkv_ref, slice(0, HS)) + weight_halves(wv_f, r.wkv_ref, slice(HS, 2 * HS))
    for copy in wkv_c:
        copy.wait_recv()
    kv = r.kv_ref

    def block(a_, b_, c_):
        return kv.at[span(((a_ * B + b_) * 2 + c_) * tok, tok), :]

    kv[span(s * tok, tok), :] = nn(r.n1_ref[...], r.wkv_ref[...]).astype(BF)
    kv_z, kv_x, kv_c = slots(A - 1), slots((B - 1) * A), slots(B * A)
    own = block(a, b, c)
    z_copies = [remote(own, own, kv_z + k - 1, device("a", k)) for k in range(1, A)]

    def guarded(k, ok, act):
        if k == 0:
            act()
        else:
            pl.when(ok)(act)

    for k in range(1, A):
        guarded(k, a + k < A, z_copies[k - 1].start)

    def x_copy(kb, k):
        here = block(jnp.maximum(a - k, 0), b, c)
        return remote(here, here, kv_x + (kb - 1) * A + k, device("b", kb))

    def c_copy(kb, k):
        here = block(jnp.maximum(a - k, 0), lower("b", kb) if kb else b, c)
        return remote(here, here, kv_c + kb * A + k, sibling)

    def pass_on(k):
        for kb in range(1, B):
            x_copy(kb, k).start()
        c_copy(0, k).start()

    pass_on(0)

    def from_a(k):
        z_copies[k - 1].wait_recv()
        pass_on(k)

    wq_b = along_b(wq_f, r.wq_ref, lambda f_: wo_rows(f_, c, b))
    if A > 2:
        guarded(1, a >= 1, functools.partial(from_a, 1))

    local[0].wait()
    for copy in wq_b:
        copy.wait_recv()
    wq_c = []
    for kf in range(1, F):
        here = r.wq_ref.at[span((lower("f", kf) * 2 + c) * half, half), :]
        wq_c.append(start(here, here, sibling))
    for copy in wq_c:
        copy.wait_recv()
    n_cols = 256

    def columns(n, act):
        def body(i, carry):
            act(span(i * n_cols, n_cols))
            return carry

        lax.fori_loop(0, n // n_cols, body, 0)

    def query_cols(cols):
        r.q_ref[:, cols] = nn(r.n1_ref[...], r.wq_ref[:, cols]).astype(BF)

    columns(D, query_cols)

    for k in range(2 if A > 2 else 1, A):
        guarded(k, a - k >= 0, functools.partial(from_a, k))
    wo_b = along_b(wo_f, r.wo_ref, lambda f_: wo_rows(f_, c, b))

    factor = math.log2(math.e) / math.sqrt(HS)
    top, mixed, total = r.dres_ref, r.res_ref, r.acc
    top[...] = jnp.full(top.shape, -3e38, F32)
    mixed[...] = jnp.zeros(mixed.shape, F32)
    total[...] = jnp.zeros(total.shape, F32)
    pos = s * tok + lax.broadcasted_iota(jnp.int32, (tok, 1), 0)
    begin = jnp.zeros((tok, 1), jnp.int32)
    for i in range(r.ends.shape[0]):
        begin = jnp.maximum(begin, jnp.where(r.ends[i] <= pos, r.ends[i], 0))

    def step(j, masked):
        rows = span(j * CHUNK, CHUNK)
        keys = kv[rows, :HS]
        values = jnp.concatenate([kv[rows, HS:], jnp.ones((CHUNK, HS), BF)], axis=1)
        if masked:
            at = j * CHUNK + lax.broadcasted_iota(jnp.int32, (tok, CHUNK), 1)
            mask = jnp.logical_and(at >= begin, at <= pos)
        else:
            seen = begin <= j * CHUNK
        for h in range(H):
            cols = slice(h * HS, (h + 1) * HS)
            scores = nt(r.q_ref[:, cols], keys)
            if masked:
                scores = jnp.where(mask, scores, NEG)
            old = top[:, cols]
            new = jnp.maximum(old, jnp.max(scores, axis=1, keepdims=True) * factor)
            if not masked:
                new = jnp.where(seen, new, old)
            shrink = jnp.exp2(old - new)
            probs = jnp.exp2(scores * factor - jnp.concatenate([new] * (CHUNK // HS), axis=1))
            both = nn(probs.astype(BF), values)
            if not masked:
                both = jnp.where(seen, both, 0.0)
            mixed[:, cols] = mixed[:, cols] * shrink + both[:, :HS]
            total[:, cols] = total[:, cols] * shrink + both[:, HS:]
            top[:, cols] = new

    last = s // 2
    c_copy(0, 0).wait_recv()
    step(last, True)

    def from_b(k):
        for kb in range(1, B):
            x_copy(kb, k).wait_recv()
            c_copy(kb, k).start()

    def from_c(k):
        for kb in range(B):
            if kb or k:
                c_copy(kb, k).wait_recv()

    wo_c, up_b = [], []
    for kf in range(1, F):
        here = r.wo_ref.at[span((lower("f", kf) * 2 + c) * half, half), :]
        wo_c.append(remote(here, here, slots(), sibling))
        here = r.up_ref.at[up_rows(lower("f", kf), b), :]
        up_b += [remote(here, here, slots(), device("b", kb)) for kb in range(1, B)]
    sent.extend(wo_c + up_b)

    def pass_weights():
        for copy in wo_b:
            copy.wait_recv()
        for copy in wo_c:
            copy.start()
        for copy in up_f:
            copy.wait_recv()
        for copy in up_b:
            copy.start()

    from_b(0)
    guarded(1, a >= 1, functools.partial(from_b, 1))
    from_c(0)

    def begin_group(k):
        if k + 1 < A:
            guarded(k + 1, a - (k + 1) >= 0, functools.partial(from_b, k + 1))
        from_c(k)
        if k == A - 1:
            pass_weights()

    def attention_chunk(j, carry):
        @pl.when(j > 0)
        def _():
            step(j, False)

        @pl.when(j == 0)
        def _():
            step(j, True)

        return carry

    def attention_part(i, carry):
        j = last - 1 - i
        for k in range(1, A):
            pl.when(j == (a - k) * B + B - 1)(functools.partial(begin_group, k))
        return attention_chunk(j, carry)

    lax.fori_loop(0, last, attention_part, 0)
    guarded(1, a < A - 1, pass_weights)
    for h in range(H):
        cols = slice(h * HS, (h + 1) * HS)
        r.att_ref[:, cols] = (mixed[:, cols] * (1.0 / total[:, cols])).astype(BF)
        r.lse_ref[h : h + 1, :] = (top[:, cols] + jnp.log2(total[:, cols])).T[0:1, :]

    local[1].wait()
    for copy in wo_c:
        copy.wait_recv()
    squares = jnp.zeros((tok, 1), F32)
    for i in range(D // n_cols):
        cols = slice(i * n_cols, (i + 1) * n_cols)
        part = r.tokens[:, cols].astype(F32) + nn(r.att_ref[...], r.wo_ref[:, cols])
        r.res_ref[:, cols] = part
        squares = squares + jnp.sum(part * part, axis=1, keepdims=True)
    r.inv2_ref[...] = lax.rsqrt(squares * (1.0 / D) + EPS)

    def second_norm(i, carry):
        rows = span(i * n_rows, n_rows)
        r.n2_all[0, rows, :] = (r.res_ref[rows, :] * r.inv2_ref[rows, :] * r.gain2_ref[...]).astype(BF)
        return carry

    lax.fori_loop(0, tok // n_rows, second_norm, 0)

    n2_f = to_f(lambda kf: r.n2_all.at[0, :tok], lambda kf: r.n2_all.at[kf, :tok])
    n2_c = [start(r.n2_all.at[0, :tok], r.n2_all.at[0, tok:], sibling)]
    local[2].wait()
    local[3].wait()
    local[4].wait()
    for copy in up_b:
        copy.wait_recv()
    for kf in range(1, F):
        cot_f[kf - 1].wait_recv()
        cot_c.append(start(r.cot_all.at[kf, :tok], r.cot_all.at[kf, tok:], sibling))

    def feed_forward(kf):
        def hidden_cols(cols):
            before = nn(r.n2_all[kf], r.up_ref[:, cols])
            d_hidden = nt(r.cot_all[kf], r.down_ref[cols, :])
            sig = 1.0 / (1.0 + jnp.exp(-before))
            r.hid_all[kf, :, cols] = (before * sig).astype(BF)
            r.dp_all[kf, :, cols] = (d_hidden * sig * (1.0 + before * (1.0 - sig))).astype(BF)

        columns(shard, hidden_cols)

    def back_part(kf):
        def back_cols(cols):
            r.back_s[kf, :, cols] = nt(r.dp_all[kf], r.up_ref[cols, :]).astype(BF)

        columns(D, back_cols)
        return start(r.back_s.at[kf, tok:], r.back_c.at[kf], sibling)

    def out_part(kf):
        def out_cols(cols):
            r.out_s[kf, :, cols] = nn(r.hid_all[kf], r.down_ref[:, cols]).astype(BF)

        columns(D, out_cols)
        return start(r.out_s.at[kf, tok:], r.out_c.at[kf], sibling)

    def chip_sum(kf, part, other, ref):
        def rows_sum(i, carry):
            rows = span(i * n_rows, n_rows)
            ref[kf - 1, rows, :] = (part[kf, rows, :].astype(F32) + other[kf, rows, :].astype(F32)).astype(BF)
            return carry

        lax.fori_loop(0, tok // n_rows, rows_sum, 0)

    n_out = 128

    r_d = shard // (A * B)

    def down_rows(kfs, place):
        cols = span(place * r_d, r_d)
        grad = sum(tn(r.hid_all[kf, :, cols], r.cot_all[kf]) for kf in kfs)
        if 0 not in kfs:
            grad = grad + r.gd_ref[cols, :].astype(F32)
        r.gd_ref[cols, :] = grad.astype(BF)

    def down_grad(kf):
        for i in range(A):
            for kb in range(1, B):
                down_rows((kf,), lax.rem(b + kb, B) * A + x.offset(x.order[i]))
            if kf == F - 1:
                x.send_down(i, i + 1)

    def down_grad_own():
        def rows_of(i, carry):
            down_rows(range(F), b * A + i)
            return carry

        lax.fori_loop(0, A, rows_of, 0)

    def up_grad():
        def rows_of(i, carry):
            cols = span(i * n_out, n_out)
            rows = span(lax.rem(i, own_rows // n_out) * n_out, n_out)
            grad = sum(tn(r.n2_all[kf, :, cols], r.dp_all[kf]) for kf in range(F))
            r.gu_ref[i // (own_rows // n_out), rows, :] = grad.astype(BF)
            return carry

        lax.fori_loop(0, D // n_out, rows_of, 0)

    back_copies, out_copies, back_back, out_back = [None] * F, [None] * F, [], []
    n2_c[0].wait_recv()
    cot_c[0].wait_recv()
    feed_forward(0)
    down_grad(0)
    back_copies[0] = back_part(0)
    for kf in range(1, F):
        n2_f[kf - 1].wait_recv()
        n2_c.append(start(r.n2_all.at[kf, :tok], r.n2_all.at[kf, tok:], sibling))
    for kf in range(1, F):
        n2_c[kf].wait_recv()
        cot_c[kf].wait_recv()
        feed_forward(kf)
        down_grad(kf)
        back_copies[kf] = back_part(kf)
        if kf == F - 1:
            down_grad_own()
        back_copies[kf].wait_recv()
        chip_sum(kf, r.back_s, r.back_c, r.back_y)
        back_back.append(start(r.back_y.at[kf - 1], r.back_r.at[kf - 1], device("f", F - kf)))
        if kf == F - 1:
            up_grad()
            x.send_up(0, A)
            x.down_step(0)
        out_copies[kf] = out_part(kf)
    for kf in range(1, F):
        out_copies[kf].wait_recv()
        chip_sum(kf, r.out_s, r.out_c, r.out_y)
        out_back.append(start(r.out_y.at[kf - 1], r.out_r.at[kf - 1], device("f", F - kf)))
    if A > 2:
        x.down_step(1)
    out_copies[0] = out_part(0)
    if A > 2:
        x.down_step(2)

    back_copies[0].wait_recv()
    for copy in back_back:
        copy.wait_recv()

    def norm_back(i, gain_grad):
        rows = span(i * n_rows, n_rows)
        d_normed = r.back_s[0, rows, :].astype(F32) + r.back_c[0, rows, :].astype(F32)
        for kf in range(1, F):
            d_normed = d_normed + r.back_r[kf - 1, rows, :].astype(F32)
        inverse = r.inv2_ref[rows, :]
        unit = r.res_ref[rows, :] * inverse
        weighted = d_normed * unit
        scaled = d_normed * r.gain2_ref[...]
        mean = jnp.mean(scaled * unit, axis=1, keepdims=True)
        d_residual = r.cot_all[0, rows, :].astype(F32) + inverse * (scaled - unit * mean)
        r.dres_ref[rows, :] = d_residual
        r.dbr_ref[rows, :] = d_residual.astype(BF)
        return gain_grad + jnp.sum(weighted, axis=0, keepdims=True)

    r.gain_rows[1:2, :] = lax.fori_loop(0, tok // n_rows, norm_back, jnp.zeros((1, D), F32))

    def attended_cols(cols):
        r.d_ref[:, cols] = nt(r.dbr_ref[...], r.wo_ref[cols, :]).astype(BF)

    columns(D, attended_cols)

    done(n2_f + n2_c)

    def out_grad(i, carry):
        cols = span(i * n_out, n_out)
        rows = span(lax.rem(i, own_rows // n_out) * n_out, n_out)
        r.go_ref[i // (own_rows // n_out), rows, :] = tn(r.att_ref[:, cols], r.dbr_ref[...]).astype(BF)
        return carry

    lax.fori_loop(0, D // n_out, out_grad, 0)

    def finish_output():
        out_copies[0].wait_recv()
        for copy in out_back:
            copy.wait_recv()

        def output_rows(i, carry):
            rows = span(i * n_rows, n_rows)
            value = r.res_ref[rows, :] + r.out_s[0, rows, :].astype(F32) + r.out_c[0, rows, :].astype(F32)
            for kf in range(1, F):
                value = value + r.out_r[kf - 1, rows, :].astype(F32)
            r.out_ref[rows, :] = value.astype(BF)
            return carry

        lax.fori_loop(0, tok // n_rows, output_rows, 0)
        done(out_copies)
        results[0].start()

    results = [
        pltpu.make_async_copy(src, dst, r.loc_sem.at[5 + i])
        for i, (src, dst) in enumerate(((r.out_ref, r.out_hbm), (r.grad_tokens, r.grad_hbm)))
    ]

    def finish():
        results[1].start()
        for copy in results:
            copy.wait()
        for copy in sent:
            copy.wait_send()
        for k in range(1, A):
            guarded(k, a + k < A, z_copies[k - 1].wait_send)
        for k in range(A):
            for kb in range(B):
                if kb:
                    guarded(k, a - k >= 0, x_copy(kb, k).wait_send)
                guarded(k, a - k >= 0, c_copy(kb, k).wait_send)

    return finish_output, finish


AGAIN = {
    "go_ref": "n2_all",
    "gq_ref": "out_s",
    "dn1": "res_ref",
    "grad_tokens": "res_ref",
    "dq": "d_ref",
    "out_ref": "dbr_ref",
    "tok_ref": "tokens",
}


def layer_shapes(dims, tok, D, shard, window, sequences):
    A, B, F = dims
    own_rows = D // F
    outs, scratch = tail_shapes(dims, tok, D, shard, window, 16 * F + A - 1 + (B - 1) * A + B * A)

    def low(*shape):
        return pltpu.VMEM(shape, BF)

    def wide(*shape):
        return pltpu.VMEM(shape, F32)

    pair = [low(F, 2 * tok, D), low(F, tok, D), low(F - 1, tok, D), low(F - 1, tok, D)]
    first = [
        low(tok, D),
        low(window, 2 * HS),
        low(tok, D),
        low(tok, D),
        wide(H, tok),
        low(shard, D),
        low(F, own_rows, shard),
        low(tok, D),
        low(D, D),
        low(D, 2 * HS),
        wide(tok, 1),
        wide(1, D),
        wide(tok, D),
        wide(1, D),
        low(D, D),
        low(D, shard),
        low(shard, D),
        low(F, 16, own_rows),
        low(F, 2 * tok, D),
        low(F, 2 * tok, D),
        low(F, 2 * tok, shard),
        low(F, 2 * tok, shard),
        wide(tok, D),
        wide(tok, 1),
        low(tok, D),
        *pair,
        *pair,
        pltpu.SemaphoreType.DMA((7,)),
        pltpu.SMEM((sequences,), jnp.int32),
    ]
    sizes = dict(zip(HEAD_SCRATCH + TAIL_SCRATCH, first + scratch))
    fits = all(sizes[k].shape == sizes[AGAIN[k]].shape for k in ("gq_ref", "dn1", "dq")) and tok == 2 * HS and own_rows == 2 * tok
    scratch = [ref for name, ref in zip(TAIL_SCRATCH, scratch) if name not in AGAIN]
    fits = fits and vmem_bytes(first + scratch) + 4 * 2**20 < LIMIT
    return outs + (jax.ShapeDtypeStruct((tok, D), BF),), first + scratch, fits


def vmem_bytes(scratch):
    total = 0
    for ref in scratch:
        shape = getattr(ref, "shape", ())
        if len(shape) >= 2:
            lanes = -(-shape[-1] // 128) * 128
            rows = -(-shape[-2] // 8) * 8
            total += math.prod(shape[:-2]) * rows * lanes * jnp.dtype(ref.dtype).itemsize
    return total


def layer(dims, lengths, groups, tokens, gain_a, gain_f, w_key, w_value, cotangent, w_query, w_out, w_up, w_down, outs, scratch):
    tok, D = tokens.shape
    hbm = pl.BlockSpec(memory_space=pltpu.HBM)
    names = HEAD_IN + TAIL_OUT[:5] + ("grad_hbm", "out_hbm") + HEAD_SCRATCH + tuple(n for n in TAIL_SCRATCH if n not in AGAIN)
    return pl.pallas_call(
        functools.partial(tail_kernel, dims, head, names),
        out_shape=outs,
        in_specs=[SMEM] * 2 + [VMEM] * 5 + [hbm] * 5,
        out_specs=(hbm,) * 7,
        scratch_shapes=scratch,
        compiler_params=pltpu.CompilerParams(vmem_limit_bytes=LIMIT, collective_id=2, has_side_effects=True),
        cost_estimate=pl.CostEstimate(flops=2**35, bytes_accessed=2**25, transcendentals=2**24),
        name="layer",
    )(lengths, groups, tokens, gain_a, gain_f, w_key, w_value, cotangent, w_query, w_out, w_up, w_down)


def after(value, *others):
    return lax.optimization_barrier((value, *others))[0]


class Grid:
    def __init__(self):
        seq = lax.axis_size("seq")
        self.F = lax.axis_size("fsdp")
        self.C = 2
        chips = seq // 2
        self.B = 2 if chips == 8 else chips // 2
        self.A = chips // self.B
        self.s = lax.axis_index("seq")
        self.f = lax.axis_index("fsdp")
        self.c = self.s % 2
        self.b = self.s // 2 % self.B
        self.a = self.s // (2 * self.B)

    def size(self, axis):
        return {"a": self.A, "b": self.B, "c": self.C, "f": self.F}[axis]

    def place(self, axis):
        return {"a": self.a, "b": self.b, "c": self.c, "f": self.f}[axis]

    def send(self, value, axis, step, upward=False):
        pairs = []
        for a in range(self.A):
            for b in range(self.B):
                for c in range(2):
                    for f in range(self.F):
                        at = {"a": a, "b": b, "c": c, "f": f}
                        to = dict(at)
                        to[axis] += step
                        if upward and not 0 <= to[axis] < self.size(axis):
                            continue
                        to[axis] %= self.size(axis)
                        line = [((d["a"] * self.B + d["b"]) * 2 + d["c"]) * self.F + d["f"] for d in (at, to)]
                        pairs.append(tuple(line))
        return lax.ppermute(value, ("seq", "fsdp"), pairs)

    def stack(self, parts, axis):
        n, me = len(parts), self.place(axis)
        if n == 2:
            low = me == 0
            return jnp.stack([jnp.where(low, parts[0], parts[1]), jnp.where(low, parts[1], parts[0])])
        twice = jnp.stack(parts + parts)
        return lax.dynamic_slice_in_dim(twice, (n - me) % n, n, 0)

    def gather(self, value, axis):
        n = self.size(axis)
        return self.stack([value] + [self.send(value, axis, -k) for k in range(1, n)], axis)

    def scatter(self, parts, axis):
        n, me = self.size(axis), self.place(axis)

        def pick(k):
            return lax.dynamic_index_in_dim(parts, (me + k) % n, 0, keepdims=False)

        got = [self.send(pick(k).astype(BF), axis, k) for k in range(1, n)]
        total = pick(0).astype(F32)
        for piece in got:
            total = total + piece.astype(F32)
        return total

    def plane_sum(self, parts):
        half = self.scatter(parts, "b").astype(BF)
        return self.scatter(half, "a")

    def plane_gather(self, share):
        rows = self.gather(share.astype(BF), "a")
        return self.gather(rows, "b")


def local(
    tokens,
    cotangent,
    seq_lengths,
    group_of_shard,
    gain_attn,
    w_query,
    w_key,
    w_value,
    w_out,
    gain_ffn,
    w_up,
    w_down,
):
    g = Grid()
    A, B, C, F = g.A, g.B, g.C, g.F
    tok, D = tokens.shape[1:]
    FF = w_up.shape[1]
    own_rows = D // F
    seq_parts = A * B * C
    shard = FF // (2 * F)

    outs, scratch, fits = layer_shapes((A, B, F), tok, D, shard, seq_parts * tok, seq_lengths.shape[1])
    if fits:
        *grads, grad_tokens, output = layer(
            (A, B, F),
            seq_lengths,
            group_of_shard,
            tokens[0],
            gain_attn,
            gain_ffn,
            w_key,
            w_value,
            cotangent[0],
            w_query,
            w_out,
            w_up,
            w_down,
            outs,
            scratch,
        )
        return results(output, grad_tokens, *grads)

    group = lax.dynamic_index_in_dim(group_of_shard, g.f, 0, keepdims=False)
    lengths = lax.dynamic_index_in_dim(seq_lengths, group, 0, keepdims=False)
    running, ends = jnp.int32(0), []
    for i in range(seq_lengths.shape[1]):
        running = running + lengths[i]
        ends.append(running)
    scal = jnp.stack([g.s.astype(jnp.int32), *ends])

    gains = jnp.stack([gain_attn, gain_ffn])
    full_gains = g.gather(gains, "f").transpose(1, 0, 2).reshape(2, D).astype(F32)
    gain_first, gain_second = full_gains[0], full_gains[1]
    own_kv = jnp.concatenate([w_key, w_value], axis=1)
    full_kv = g.gather(own_kv, "f").reshape(D, 2 * HS)

    def gather_weight(weight, *late):
        half = own_rows // 2
        mine = lax.dynamic_slice_in_dim(weight, g.c * half, half, 0)
        if late:
            mine = after(mine, *late)
        pieces = [g.gather(g.send(mine, "f", -k), "c").reshape(weight.shape) for k in range(1, F)]
        return g.stack([weight] + pieces, "f").reshape(F * own_rows, -1)

    full_query = gather_weight(w_query)

    stream = tokens[0].astype(F32)
    inverse_first = lax.rsqrt(jnp.mean(stream * stream, axis=1, keepdims=True) + EPS)
    unit_first = stream * inverse_first
    normed_first = (unit_first * gain_first).astype(BF)
    key_value = nn(normed_first, full_kv).astype(BF)
    queries = nn(normed_first, full_query).astype(BF)

    column = [key_value] + [g.send(key_value, "a", k, upward=True) for k in range(1, A)]
    twice = jnp.stack(column[::-1] + column[::-1])
    column = lax.dynamic_slice_in_dim(twice, A - 1 - g.a, A, 0)
    plane = g.gather(column, "b")
    whole = g.gather(plane, "c")
    window_kv = whole.transpose(2, 1, 0, 3, 4).reshape(seq_parts * tok, 2 * HS)

    full_out = gather_weight(w_out, full_query)
    upstream = cotangent[0]
    cot = []
    for k in range(F):
        mine = upstream if k == 0 else g.send(after(upstream, full_query), "f", k)
        cot.append(jnp.concatenate([mine, g.send(mine, "c", 1)], axis=0))
    ups = w_up.reshape(own_rows, F, 2, shard)
    up_parts = []
    for k in range(F):
        block = lax.dynamic_slice(ups, (0, (g.f + k) % F, g.c, 0), (own_rows, 1, 1, shard)).reshape(own_rows, shard)
        up_parts.append(block if k == 0 else g.send(after(block, full_out), "f", k))
    up_parts = [up_parts[0]] + up_parts[1:][::-1]
    up = g.stack(up_parts, "f").reshape(D, shard)
    down = lax.dynamic_slice_in_dim(w_down, g.c * shard, shard, 0)

    attended, lse = attend(scal, queries, window_kv)

    residual = stream + nn(attended, full_out)
    inverse_second = lax.rsqrt(jnp.mean(residual * residual, axis=1, keepdims=True) + EPS)
    unit_second = residual * inverse_second
    normed_second = (unit_second * gain_second).astype(BF)

    out_sum, back_sum = residual, jnp.zeros((tok, D), F32)
    hiddens, d_pres, norms = [], [], []
    backs, outs = [], []
    for k in range(F):
        mine = normed_second if k == 0 else g.send(normed_second, "f", k)
        norm = jnp.concatenate([mine, g.send(mine, "c", 1)], axis=0)
        before = nn(norm, up)
        d_hidden = nt(cot[k], down)
        sig = jax.nn.sigmoid(before)
        hidden = (before * sig).astype(BF)
        d_pre = (d_hidden * sig * (1.0 + before * (1.0 - sig))).astype(BF)
        back = nt(d_pre, up)
        out = nn(hidden, down)
        hiddens.append(hidden)
        d_pres.append(d_pre)
        norms.append(norm)
        backs.append(back)
        outs.append(out)

    def give_back(parts):
        total = 0.0
        for k, part in enumerate(parts):
            other = g.send(part[tok:].astype(BF), "c", 1)
            chip = part[:tok] + other.astype(F32)
            if k:
                chip = g.send(chip.astype(BF), "f", -k).astype(F32)
            total = total + chip
        return total

    d_normed_second = give_back(backs)
    output = (residual + give_back(outs)).astype(BF)

    grad_down = sum(tn(h, c) for h, c in zip(hiddens, cot)).astype(BF)
    grad_up = sum(tn(n, d) for n, d in zip(norms, d_pres)).astype(BF)

    def norm_back(gradient, unit_rows, inverse, gain_vec):
        scaled = gradient * gain_vec
        gain_grad = jnp.sum(gradient * unit_rows, axis=0)
        return gain_grad, inverse * (scaled - unit_rows * jnp.mean(scaled * unit_rows, axis=1, keepdims=True))

    gain_second_grad, d_from_norm = norm_back(d_normed_second, unit_second, inverse_second, gain_second)
    d_residual = upstream.astype(F32) + d_from_norm
    d_branch = d_residual.astype(BF)
    d_attended = nt(d_branch, full_out).astype(BF)
    grad_out = tn(attended, d_branch).astype(BF)

    down_all, up_all, out_all, query_all, kv_all, grad_tokens = tail(
        (A, B, F),
        scal[1:],
        queries,
        window_kv,
        d_attended,
        attended,
        lse,
        grad_down,
        grad_up.reshape(F, own_rows, shard),
        grad_out.reshape(F, own_rows, D),
        normed_first,
        full_query,
        full_kv,
        tokens[0],
        inverse_first,
        gain_first[None],
        d_residual,
        gain_second_grad[None],
    )
    return results(output, grad_tokens, down_all, up_all, out_all, query_all, kv_all)


def widen_kernel(
    low_ref, grad_ref, down_ref, up_ref, o_ref, q_ref, kv_ref, output, grad_tokens, grad_down, grad_up, grad_o, grad_q, grad_k, grad_v, gain_a, gain_f
):
    output[0] = low_ref[...]
    grad_tokens[0] = grad_ref[...]
    grad_down[...] = down_ref[...].astype(F32)
    width = up_ref.shape[2]
    for i in range(up_ref.shape[0]):
        grad_up[:, i * width : (i + 1) * width] = up_ref[i].astype(F32)
    grad_o[...] = o_ref[...].astype(F32)
    grad_q[...] = q_ref[...].astype(F32)

    @pl.when(pl.program_id(0) == 0)
    def _():
        rows = kv_ref.shape[2] - 16
        for i in range(kv_ref.shape[1]):
            grad_k[i * rows : (i + 1) * rows, :] = kv_ref[0, i, :rows, :].astype(F32)
            grad_v[i * rows : (i + 1) * rows, :] = kv_ref[1, i, :rows, :].astype(F32)
        for i, gain in enumerate((gain_a, gain_f)):
            block = kv_ref[i, 0, rows:, :].astype(F32)
            for k in range(gain.shape[0] // HS):
                gain[k * HS : (k + 1) * HS] = block[k]


def results(output, grad_tokens, down_all, up_all, out_all, query_all, kv_all):
    tok, D = output.shape
    F, own_rows, width = up_all.shape
    steps = max(1, own_rows // 256)

    def rows(n, cols):
        return pl.BlockSpec((n // steps, cols), lambda i: (i, 0))

    def whole(*shape):
        return pl.BlockSpec(shape, lambda i: (0,) * len(shape))

    def first(n, cols):
        return pl.BlockSpec((1, n // steps, cols), lambda i: (0, i, 0))

    down_rows = down_all.shape[0]
    shapes = [(down_rows, D), (own_rows, F * width), (own_rows, D), (own_rows, D), (own_rows, HS), (own_rows, HS), (own_rows,), (own_rows,)]
    out, grad_tokens, down, up, o, q, k, v, gain_a, gain_f = pl.pallas_call(
        widen_kernel,
        grid=(steps,),
        out_shape=[jax.ShapeDtypeStruct((1, tok, D), BF), jax.ShapeDtypeStruct((1, tok, D), F32)]
        + [jax.ShapeDtypeStruct(shape, F32) for shape in shapes],
        in_specs=[
            rows(tok, D),
            rows(tok, D),
            rows(down_rows, D),
            pl.BlockSpec((F, own_rows // steps, width), lambda i: (0, i, 0)),
            rows(own_rows, D),
            rows(own_rows, D),
            whole(*kv_all.shape),
        ],
        out_specs=[
            first(tok, D),
            first(tok, D),
            rows(down_rows, D),
            rows(own_rows, F * width),
            rows(own_rows, D),
            rows(own_rows, D),
            whole(own_rows, HS),
            whole(own_rows, HS),
            whole(own_rows),
            whole(own_rows),
        ],
        compiler_params=pltpu.CompilerParams(vmem_limit_bytes=LIMIT),
        name="widen",
    )(output, grad_tokens, down_all, up_all, out_all, query_all, kv_all)
    return out, grad_tokens, gain_a, q, k, v, o, gain_f, up, down


def solution(mesh):
    placed = (
        P("fsdp", "seq", None),
        P("fsdp", "seq", None),
        P(),
        P(),
        P("fsdp"),
        P("fsdp", None),
        P("fsdp", None),
        P("fsdp", None),
        P("fsdp", None),
        P("fsdp"),
        P("fsdp", None),
        P("fsdp", None),
    )
    return jax.shard_map(
        local,
        mesh=mesh,
        in_specs=placed,
        out_specs=(
            P("fsdp", "seq", None),
            P("fsdp", "seq", None),
            P("fsdp"),
            P("fsdp", None),
            P("fsdp", None),
            P("fsdp", None),
            P("fsdp", None),
            P("fsdp"),
            P("fsdp", None),
            P("fsdp", None),
        ),
        check_vma=False,
    )
```

```python
import functools
import math
import types

import jax
import jax.numpy as jnp
from jax import lax
from jax.experimental import pallas as pl
from jax.experimental.pallas import tpu as pltpu
from jax.sharding import PartitionSpec as P

H = 8
HS = 128
EPS = 1e-05
NEG = -1e30
LIMIT = 60 * 2**20
CHUNK = 512
BF = jnp.bfloat16
F32 = jnp.float32


def nt(a, b):
    return lax.dot_general(a, b, (((1,), (1,)), ((), ())), preferred_element_type=F32)


def nn(a, b):
    return lax.dot_general(a, b, (((1,), (0,)), ((), ())), preferred_element_type=F32)


def tn(a, b):
    return lax.dot_general(a, b, (((0,), (0,)), ((), ())), preferred_element_type=F32)


def query_range(scal, tok):
    first = scal[0] * tok
    pos = first + lax.broadcasted_iota(jnp.int32, (1, tok), 1)
    start = jnp.zeros((1, tok), jnp.int32)
    latest = jnp.int32(0)
    for i in range(1, scal.shape[0]):
        end = scal[i]
        start = jnp.maximum(start, jnp.where(end <= pos, end, 0))
        latest = jnp.maximum(latest, jnp.where(end <= first + tok - 1, end, 0))
    return first, pos, start, latest


def chunk_loop(scal, tok, window, step):
    first, pos, start, latest = query_range(scal, tok)
    chunks = (first + tok + CHUNK - 1) // CHUNK

    def body(j, carry):
        low = j * CHUNK
        whole = jnp.logical_and(low >= latest, low + CHUNK - 1 <= first)

        @pl.when(whole)
        def _():
            step(j, None)

        @pl.when(jnp.logical_not(whole))
        def _():
            keys = low + lax.broadcasted_iota(jnp.int32, (CHUNK, tok), 0)
            step(j, jnp.logical_and(keys >= start, keys <= pos))

        return carry

    lax.fori_loop(0, chunks, body, 0)
    return chunks


def attend_kernel(scal, q_ref, kv_ref, out_ref, lse_ref, acc, top, total):
    tok = q_ref.shape[0]
    factor = math.log2(math.e) / math.sqrt(HS)
    top[...] = jnp.full(top.shape, -3e38, F32)
    total[...] = jnp.zeros(total.shape, F32)
    acc[...] = jnp.zeros(acc.shape, F32)

    def step(j, mask):
        rows = pl.ds(pl.multiple_of(j * CHUNK, CHUNK), CHUNK)
        keys = kv_ref[rows, :HS]
        values_t = kv_ref[rows, HS:].T
        for h in range(H):
            scores = nt(keys, q_ref[:, h * HS : (h + 1) * HS])
            if mask is not None:
                scores = jnp.where(mask, scores, NEG)
            old = top[h : h + 1, :]
            new = jnp.maximum(old, jnp.max(scores, axis=0, keepdims=True) * factor)
            shrink = jnp.exp2(old - new)
            probs = jnp.exp2(scores * factor - new)
            total[h : h + 1, :] = total[h : h + 1, :] * shrink + jnp.sum(probs, axis=0, keepdims=True)
            acc[h] = acc[h] * shrink + nn(values_t, probs.astype(BF))
            top[h : h + 1, :] = new

    chunk_loop(scal, tok, kv_ref.shape[0], step)
    for h in range(H):
        mixed = acc[h] * (1.0 / total[h : h + 1, :])
        out_ref[:, h * HS : (h + 1) * HS] = mixed.T.astype(BF)
    lse_ref[...] = top[...] + jnp.log2(total[...])


VMEM = pl.BlockSpec(memory_space=pltpu.VMEM)
SMEM = pl.BlockSpec(memory_space=pltpu.SMEM)
PARAMS = pltpu.CompilerParams(vmem_limit_bytes=40 * 2**20)


def attend(scal, queries, window_kv):
    tok = queries.shape[0]
    window = window_kv.shape[0]
    return pl.pallas_call(
        attend_kernel,
        out_shape=(
            jax.ShapeDtypeStruct((tok, H * HS), BF),
            jax.ShapeDtypeStruct((H, tok), F32),
        ),
        in_specs=[SMEM, VMEM, VMEM],
        out_specs=(VMEM, VMEM),
        scratch_shapes=[
            pltpu.VMEM((H, HS, tok), F32),
            pltpu.VMEM((H, tok), F32),
            pltpu.VMEM((H, tok), F32),
        ],
        compiler_params=PARAMS,
        cost_estimate=pl.CostEstimate(
            flops=8 * tok * window * H * HS, bytes_accessed=4 * window * HS, transcendentals=tok * window * H
        ),
        name="attend",
    )(scal, queries, window_kv)


MESH = pl.DeviceIdType.MESH


TAIL_IN = (
    "ends",
    "q_ref",
    "kv_ref",
    "d_ref",
    "att_ref",
    "lse_ref",
    "gd_ref",
    "gu_ref",
    "go_ref",
    "n1_ref",
    "wq_ref",
    "wkv_ref",
    "tok_ref",
    "inv_ref",
    "gain_ref",
    "dres_ref",
    "gain2_ref",
)
TAIL_OUT = (
    "out_down",
    "out_up",
    "out_o",
    "out_q",
    "out_kv",
    "grad_tokens",
)
TAIL_SCRATCH = (
    "acc",
    "delta",
    "dq",
    "dkv",
    "dkv_c",
    "dkv_x",
    "dkv_z",
    "d_kv",
    "dn1",
    "gq_ref",
    "gkv_ref",
    "xr_d",
    "xr_u",
    "zs_d",
    "zs_u",
    "zr_d",
    "zr_u",
    "sh_d",
    "sh_u",
    "yr_u",
    "o_c",
    "o_y",
    "o_x",
    "o_z",
    "o_s",
    "q_c",
    "q_y",
    "q_x",
    "q_z",
    "q_s",
    "kv_c",
    "kv_y",
    "kv_x",
    "kv_z",
    "kv_s",
    "gain_rows",
    "send_sem",
    "recv_sem",
    "copy_sem",
)


def head_block(h, tok):
    return slice(h % 2 * HS, (h % 2 + 1) * HS), slice(h // 2 * tok, (h // 2 + 1) * tok)


def tail_kernel(dims, head, names, *refs):
    A, B, F = dims
    r = types.SimpleNamespace(**dict(zip(names, refs, strict=True)))
    if head is not None:
        for name, held in AGAIN.items():
            setattr(r, name, getattr(r, held))
    ends = r.ends
    q_ref = r.q_ref
    kv_ref = r.kv_ref
    d_ref = r.d_ref
    att_ref = r.att_ref
    lse_ref = r.lse_ref
    gd_ref = r.gd_ref
    gu_ref = r.gu_ref
    go_ref = r.go_ref
    n1_ref = r.n1_ref
    wq_ref = r.wq_ref
    wkv_ref = r.wkv_ref
    tok_ref = r.tok_ref
    inv_ref = r.inv_ref
    gain_ref = r.gain_ref
    dres_ref = r.dres_ref
    gain2_ref = r.gain2_ref
    out_down = r.out_down
    out_up = r.out_up
    out_o = r.out_o
    out_q = r.out_q
    out_kv = r.out_kv
    grad_tokens = r.grad_tokens
    acc = r.acc
    delta = r.delta
    dq = r.dq
    dkv = r.dkv
    dkv_c = r.dkv_c
    dkv_x = r.dkv_x
    dkv_z = r.dkv_z
    d_kv = r.d_kv
    dn1 = r.dn1
    gq_ref = r.gq_ref
    gkv_ref = r.gkv_ref
    xr_d = r.xr_d
    xr_u = r.xr_u
    zs_d = r.zs_d
    zs_u = r.zs_u
    zr_d = r.zr_d
    zr_u = r.zr_u
    sh_d = r.sh_d
    sh_u = r.sh_u
    yr_u = r.yr_u
    o_c = r.o_c
    o_y = r.o_y
    o_x = r.o_x
    o_z = r.o_z
    o_s = r.o_s
    q_c = r.q_c
    q_y = r.q_y
    q_x = r.q_x
    q_z = r.q_z
    q_s = r.q_s
    kv_c = r.kv_c
    kv_y = r.kv_y
    kv_x = r.kv_x
    kv_z = r.kv_z
    kv_s = r.kv_s
    gain_rows = r.gain_rows
    send_sem = r.send_sem
    recv_sem = r.recv_sem
    copy_sem = r.copy_sem
    tok = q_ref.shape[0]
    window = kv_ref.shape[0]
    D = n1_ref.shape[1]
    own_rows = D // F
    shard = gd_ref.shape[0]
    s = lax.axis_index("seq")
    f = lax.axis_index("fsdp")
    c = lax.rem(s, 2)
    b = lax.rem(s // 2, B)
    a = s // (2 * B)

    def device(axis, step):
        at = {"a": a, "b": b, "c": c, "f": f}
        at[axis] = lax.rem(at[axis] + step, {"a": A, "b": B, "c": 2, "f": F}[axis])
        return ((at["a"] * B + at["b"]) * 2 + at["c"], at["f"])

    def lower(axis, step):
        return lax.rem({"a": a + A, "b": b + B, "f": f + F}[axis] - step, {"a": A, "b": B, "f": F}[axis])

    def flip(axis_bit, place=None):
        place = a if place is None else place
        return place + axis_bit - 2 * axis_bit * lax.rem(place // axis_bit, 2) if axis_bit else place

    def offset(o):
        place = a
        for bit in bits:
            if o // bit % 2:
                place = flip(bit, place)
        return place

    def along_a(bit):
        return ((flip(bit) * B + b) * 2 + c, f)

    bits = [2**i for i in range(A.bit_length() - 1)]
    assert 2 ** len(bits) == A
    order = [o for bit in bits for o in range(A) if o // bit % 2 and o % bit == 0] + [0]

    def low_bit(o):
        return next((bit for bit in bits if o // bit % 2), A)

    used = [0]

    def slots(n=1):
        used[0] += n
        assert used[0] <= send_sem.shape[0]
        return used[0] - n

    def remote(src, dst, slot, to):
        return pltpu.make_async_remote_copy(
            src_ref=src, dst_ref=dst, send_sem=send_sem.at[slot], recv_sem=recv_sem.at[slot], device_id=to, device_id_type=MESH
        )

    pending = []

    def start(src, dst, slot, to):
        copy = remote(src, dst, slot, to)
        copy.start()
        pending.append(copy)
        return copy

    barrier = pltpu.get_barrier_semaphore()
    partners = [("a", k) for k in range(1, A)] + [("b", k) for k in range(1, B)] + [("c", 1)] + [("f", k) for k in range(1, F)]
    for axis, k in partners:
        pl.semaphore_signal(barrier, inc=1, device_id=device(axis, k), device_id_type=MESH)
    pl.semaphore_wait(barrier, len(partners))

    r_d = shard // (A * B)
    r_u = own_rows // B
    w_u = shard // A
    x_d = slots(A * (B - 1))
    x_u = slots(A * (B - 1))
    z_d = slots(A - 1)
    z_u = slots(A - 1)

    def down_copies(i):
        at = offset(order[i])
        copies = []
        for kb in range(B - 1):
            other = lax.rem(b + kb + 1, B)
            rows = pl.ds(pl.multiple_of((other * A + at) * r_d, r_d), r_d)
            copies.append(remote(gd_ref.at[rows, :], xr_d.at[kb, i], x_d + kb * A + i, device("b", kb + 1)))
        return copies

    def up_copies(i):
        at = offset(order[i])
        copies = []
        for kb in range(B - 1):
            rows = pl.ds(pl.multiple_of(lax.rem(b + kb + 1, B) * r_u, r_u), r_u)
            cols = pl.ds(pl.multiple_of(at * w_u, w_u), w_u)
            copies.append(remote(gu_ref.at[:, rows, cols], xr_u.at[kb, i], x_u + kb * A + i, device("b", kb + 1)))
        return copies

    def send_down(first, last):
        for i in range(first, last):
            for copy in down_copies(i):
                copy.start()

    def send_up(first, last):
        for i in range(first, last):
            for copy in up_copies(i):
                copy.start()

    def down_sum(i):
        for copy in down_copies(i):
            copy.wait()
        at = offset(order[i])
        rows = pl.ds(pl.multiple_of((b * A + at) * r_d, r_d), r_d)
        total = gd_ref[rows, :].astype(F32)
        for kb in range(B - 1):
            total = total + xr_d[kb, i].astype(F32)
        return total

    def up_sum(i):
        for copy in up_copies(i):
            copy.wait()
        at = offset(order[i])
        rows = pl.ds(pl.multiple_of(b * r_u, r_u), r_u)
        cols = pl.ds(pl.multiple_of(at * w_u, w_u), w_u)
        total = gu_ref[:, rows, cols].astype(F32)
        for kb in range(B - 1):
            total = total + xr_u[kb, i].astype(F32)
        return total

    def z_index(o, bit):
        return order.index(o + bit)

    def down_z(i):
        return remote(zs_d.at[i], zr_d.at[i], z_d + i, along_a(low_bit(order[i])))

    def up_z(i):
        return remote(zs_u.at[i], zr_u.at[i], z_u + i, along_a(low_bit(order[i])))

    def z_added(i, total, copy, got):
        o = order[i]
        for bit in bits:
            if bit < low_bit(o):
                k = z_index(o, bit)
                copy(k).wait()
                total = total + got[k].astype(F32)
        return total

    def down_step(i):
        zs_d[i] = z_added(i, down_sum(i), down_z, zr_d).astype(BF)
        down_z(i).start()

    def up_step(i):
        zs_u[i] = z_added(i, up_sum(i), up_z, zr_u).astype(BF)
        up_z(i).start()

    def down_share():
        sh_d[...] = z_added(A - 1, down_sum(A - 1), down_z, zr_d).astype(BF)
        gather_down.begin()

    up_y = slots(F - 1)

    def up_y_copy(kf):
        return remote(yr_u.at[lax.rem(f + kf + 1, F)], sh_u.at[f], up_y + kf, device("f", kf + 1))

    def up_share():
        total = z_added(A - 1, up_sum(A - 1), up_z, zr_u)
        yr_u[...] = total.astype(BF)
        for kf in range(F - 1):
            up_y_copy(kf).start()
        sh_u[f] = yr_u[f]

    def up_gather():
        for kf in range(F - 1):
            up_y_copy(kf).wait()
        gather_up.begin()

    gathers = []

    class Gather:
        def __init__(self, share, view, planes=True):
            self.share, self.view, self.n = share, view, B if planes else 1
            self.z_slot = slots(A)
            self.x_slot = slots((self.n - 1) * A)
            self.c_slot = slots(self.n * A)
            self.place = len(gathers)
            gathers.append(self)

        def local(self):
            return pltpu.make_async_copy(self.share, self.view(c, b, a), copy_sem.at[self.place])

        def at(self, o, kb=0):
            return self.view(c, lower("b", kb) if kb else b, offset(o))

        def z(self, bit, o):
            here = self.at(o)
            return remote(here if o else self.share, here, self.z_slot + A - A // bit + o // (2 * bit), along_a(bit))

        def x(self, kb, o):
            here = self.at(o)
            return remote(here if o else self.share, here, self.x_slot + kb * A + o, device("b", kb + 1))

        def c(self, kb, o):
            here = self.at(o, kb)
            return remote(here if kb or o else self.share, here, self.c_slot + kb * A + o, device("c", 1))

        def begin(self):
            self.local().start()
            for bit in bits[::-1]:
                self.z(bit, 0).start()
            self.pass_on(0)

        def pass_on(self, o):
            for kb in range(self.n - 1):
                self.x(kb, o).start()
            self.c(0, o).start()

        def from_a(self, stages=None):
            for i, bit in enumerate(bits[::-1]):
                if stages is not None and i not in stages:
                    continue
                for o in range(0, A, 2 * bit):
                    self.z(bit, o).wait_recv()
                    for lower_bit in bits[: len(bits) - 1 - i][::-1]:
                        self.z(lower_bit, o + bit).start()
                    self.pass_on(o + bit)

        def from_b(self):
            for kb in range(self.n - 1):
                for o in self.offsets():
                    self.x(kb, o).wait_recv()
                    self.c(kb + 1, o).start()

        def offsets(self):
            found = [0]
            for bit in bits[::-1]:
                found += [o + bit for o in found]
            return found

        def end(self):
            self.local().wait()
            for bit in bits:
                for o in range(0, A, 2 * bit):
                    self.z(bit, o).wait_send()
            for o in range(A):
                for kb in range(self.n - 1):
                    self.x(kb, o).wait_send()
                for kb in range(self.n):
                    self.c(kb, o).wait()

    def view_down(c_, b_, a_):
        return out_down.at[pl.ds(pl.multiple_of(((c_ * B + b_) * A + a_) * r_d, r_d), r_d), :]

    def view_up(c_, b_, a_):
        rows = pl.ds(pl.multiple_of(b_ * r_u, r_u), r_u)
        return out_up.at[:, rows, pl.ds(pl.multiple_of(c_ * shard + a_ * w_u, w_u), w_u)]

    half = D // 2
    w_o = half // A

    def view_square(out):
        def view(c_, b_, a_):
            rows = pl.ds(pl.multiple_of(b_ * r_u, r_u), r_u)
            return out.at[rows, pl.ds(pl.multiple_of(c_ * half + a_ * w_o, w_o), w_o)]

        return view

    gather_down = Gather(sh_d, view_down)
    gather_up = Gather(sh_u, view_up)
    gather_o = Gather(o_s, view_square(out_o))
    gather_q = Gather(q_s, view_square(out_q))
    gather_kv = Gather(kv_s, lambda c_, b_, a_: out_kv.at[c_, a_], planes=False)

    if head is None:
        send_down(0, A)
        send_up(0, A)
    else:
        own = types.SimpleNamespace(
            A=A, B=B, F=F, a=a, b=b, c=c, f=f, s=s, slots=slots, remote=remote, device=device, lower=lower,
            send_down=send_down, send_up=send_up, down_step=down_step, offset=offset, order=order,
        )
        finish_output, send_tokens, finish_head = head(r, own)

    def reduce_y(ref, got, sent, width):
        mine = pl.ds(pl.multiple_of(c * width, width), width)

        def add(i, carry):
            sent[i] = (ref[i, :, mine].astype(F32) + got[i].astype(F32)).astype(BF)
            return carry

        lax.fori_loop(0, F, add, 0)

    class Square:
        def __init__(self, grad, got_c, got_y, got_x, got_z, share, gather):
            self.grad, self.got_c, self.got_y, self.got_x, self.got_z = grad, got_c, got_y, got_x, got_z
            self.share, self.gather = share, gather
            self.c_slot, self.y_slot, self.x_slot = slots(), slots(F - 1), slots(B - 1)

        def c(self):
            other = pl.ds(pl.multiple_of((1 - c) * half, half), half)
            return remote(self.grad.at[:, :, other], self.got_c, self.c_slot, device("c", 1))

        def y(self, kf):
            return remote(self.got_c.at[lax.rem(f + kf + 1, F)], self.got_y.at[kf], self.y_slot + kf, device("f", kf + 1))

        def over_c(self):
            self.c().start()

        def over_f(self):
            self.c().wait()
            reduce_y(self.grad, self.got_c, self.got_c, half)
            for kf in range(F - 1):
                self.y(kf).start()

        def over_b(self):
            total = self.got_c[f].astype(F32)
            for kf in range(F - 1):
                self.y(kf).wait()
                total = total + self.got_y[kf].astype(F32)
            self.got_y[F - 1] = total.astype(BF)
            for kb in range(B - 1):
                self.x(kb).start()

        def x(self, kb):
            rows = pl.ds(pl.multiple_of(lax.rem(b + kb + 1, B) * r_u, r_u), r_u)
            return remote(self.got_y.at[F - 1, rows, :], self.got_x.at[kb], self.x_slot + kb, device("b", kb + 1))

        def over_a(self):
            rows = pl.ds(pl.multiple_of(b * r_u, r_u), r_u)
            total = self.got_y[F - 1, rows, :].astype(F32)
            for kb in range(B - 1):
                self.x(kb).wait()
                total = total + self.got_x[kb].astype(F32)
            self.got_x[B - 1] = total.astype(BF)
            self.copies = []
            for ka in range(A - 1):
                cols = pl.ds(pl.multiple_of(lax.rem(a + ka + 1, A) * w_o, w_o), w_o)
                self.copies.append(start(self.got_x.at[B - 1, :, cols], self.got_z.at[ka], slots(), device("a", ka + 1)))

        def finish(self):
            cols = pl.ds(pl.multiple_of(a * w_o, w_o), w_o)
            total = self.got_x[B - 1, :, cols].astype(F32)
            for ka in range(A - 1):
                self.copies[ka].wait()
                total = total + self.got_z[ka].astype(F32)
            self.share[...] = total.astype(BF)
            self.gather.begin()

    square_o = Square(go_ref, o_c, o_y, o_x, o_z, o_s, gather_o)
    square_q = Square(gq_ref, q_c, q_y, q_x, q_z, q_s, gather_q)

    square_o.over_c()

    scale = 1.0 / math.sqrt(HS)
    factor = math.log2(math.e) * scale
    acc[...] = jnp.zeros(acc.shape, F32)
    for h in range(H):
        cols = slice(h * HS, (h + 1) * HS)
        both = d_ref[:, cols].astype(F32) * att_ref[:, cols].astype(F32)
        delta[h : h + 1, :] = jnp.sum(both.T, axis=0, keepdims=True)
    first = s * tok
    pos = first + lax.broadcasted_iota(jnp.int32, (1, tok), 1)
    begin = jnp.zeros((1, tok), jnp.int32)
    for i in range(ends.shape[0]):
        begin = jnp.maximum(begin, jnp.where(ends[i] <= pos, ends[i], 0))

    def step(j, masked):
        rows = pl.ds(pl.multiple_of(j * CHUNK, CHUNK), CHUNK)
        keys = kv_ref[rows, :HS]
        values = kv_ref[rows, HS:]
        keys_t = keys.T
        if masked:
            at = j * CHUNK + lax.broadcasted_iota(jnp.int32, (CHUNK, tok), 0)
            mask = jnp.logical_and(at >= begin, at <= pos)
        else:
            seen = begin <= j * CHUNK
        d_keys = jnp.zeros((CHUNK, HS), F32)
        d_values = jnp.zeros((CHUNK, HS), F32)
        for h in range(H):
            cols = slice(h * HS, (h + 1) * HS)
            q = q_ref[:, cols]
            d = d_ref[:, cols]
            scores = nt(keys, q)
            if masked:
                scores = jnp.where(mask, scores, NEG)
            lse = lse_ref[h : h + 1, :]
            if not masked:
                lse = jnp.where(seen, lse, 3e38)
            probs = jnp.exp2(scores * factor - lse)
            d_probs = nt(values, d)
            d_scores = (probs * (d_probs - delta[h : h + 1, :])).astype(BF)
            d_values = d_values + nn(probs.astype(BF), d)
            d_keys = d_keys + nn(d_scores, q)
            acc[head_block(h, tok)] += nn(keys_t, d_scores)
        for i in range(2):
            part = slice(i * tok, (i + 1) * tok)
            dkv[j, i, :, :HS] = (d_keys[part] * scale).astype(BF)
            dkv[j, i, :, HS:] = d_values[part].astype(BF)

    chunks = s // 2 + 1
    def attention_chunk(j, carry):
        plain = jnp.logical_and(j > 0, j < chunks - 1)

        @pl.when(plain)
        def _():
            step(j, False)

        @pl.when(jnp.logical_not(plain))
        def _():
            step(j, True)

        return carry

    first = 0 if head is None else min(3, A - 1)
    steps = [functools.partial(down_step, i) for i in range(first, A - 1)]
    steps += [functools.partial(up_step, i) for i in range(A - 2)] + [down_share, functools.partial(up_step, A - 2), square_o.over_b]
    if A == 4 and head is not None:
        acts = [(1, steps[0]), (3, steps[1]), (4, steps[2]), (5, steps[4]), (2, square_o.over_f)]
    else:
        acts = [(0, square_o.over_f), *((1, act) for act in steps)]

    def chunk_and_step(j, carry):
        @pl.when(j < chunks)
        def _():
            attention_chunk(j, 0)

        for time, act in acts:
            pl.when(j == time)(act)
        return carry

    lax.fori_loop(0, window // CHUNK, chunk_and_step, 0)

    def clear(j, carry):
        dkv[j] = jnp.zeros(dkv.shape[1:], BF)
        return carry

    lax.fori_loop(chunks, window // CHUNK, clear, 0)

    dkv_c_copy = start(dkv.at[:, 1 - c], dkv_c, slots(), device("c", 1))


    if head is not None:
        finish_output()
    for h in range(H):
        dq[:, h * HS : (h + 1) * HS] = (acc[head_block(h, tok)] * scale).T.astype(BF)
    n_rows = 128

    def query_grad(i, carry):
        col = pl.ds(pl.multiple_of(i * n_rows, n_rows), n_rows)
        fi = i // (own_rows // n_rows)
        row = lax.rem(i, own_rows // n_rows) * n_rows
        gq_ref[fi, pl.ds(pl.multiple_of(row, n_rows), n_rows), :] = nn(n1_ref[:, col].T, dq[...]).astype(BF)
        return carry

    lax.fori_loop(0, D // n_rows, query_grad, 0)
    square_q.over_c()

    dkv_c_copy.wait()

    def add_c(j, carry):
        dkv_c[j] = (dkv_c[j].astype(F32) + dkv[j, c].astype(F32)).astype(BF)
        return carry

    lax.fori_loop(0, A * B, add_c, 0)
    x_kv = []
    for kb in range(B - 1):
        other = lax.rem(b + kb + 1, B)
        for j in range(A):
            x_kv.append(start(dkv_c.at[j * B + other], dkv_x.at[kb, j], slots(), device("b", kb + 1)))

    if A == 4 and head is not None:
        steps[3]()
    square_q.over_f()
    gather_down.from_a((0,))
    up_share()
    square_q.over_b()
    for i in range(1, len(bits)):
        gather_down.from_a((i,))
    square_o.over_a()

    for copy in x_kv:
        copy.wait()

    def add_x(j, carry):
        total = dkv_c[j * B + b].astype(F32)
        for kb in range(B - 1):
            total = total + dkv_x[kb, j].astype(F32)
        dkv_x[0, j] = total.astype(BF)
        return carry

    lax.fori_loop(0, A, add_x, 0)
    z_kv = slots(A - 1)
    for k in range(A - 1, 0, -1):

        @pl.when(a - k >= 0)
        def _():
            to = (((a - k) * B + b) * 2 + c, f)
            remote(dkv_x.at[0, jnp.maximum(a - k, 0)], dkv_z.at[k - 1], z_kv + k - 1, to).start()

    up_gather()

    total = dkv_x[0, a].astype(F32)
    d_kv[...] = total
    for k in range(1, A):
        copy = remote(dkv_x.at[0, jnp.maximum(a - k, 0)], dkv_z.at[k - 1], z_kv + k - 1, device("a", A - k))

        @pl.when(a - k >= 0)
        def _():
            copy.wait_send()

        @pl.when(a + k < A)
        def _():
            copy.wait_recv()
            d_kv[...] = d_kv[...] + dkv_z[k - 1].astype(F32)

    d_kv_low = d_kv[...].astype(BF)

    n_cols = 256
    mean = jnp.zeros((tok, 1), F32)
    for i in range(D // n_cols):
        cols = slice(i * n_cols, (i + 1) * n_cols)
        part = nt(dq[...], wq_ref[cols, :]) + nt(d_kv_low, wkv_ref[cols, :])
        dn1[:, cols] = part
        weighted = part * (tok_ref[:, cols].astype(F32) * inv_ref[...])
        gain_rows[0:1, cols] = jnp.sum(weighted, axis=0, keepdims=True)
        mean = mean + jnp.sum(weighted * gain_ref[:, cols], axis=1, keepdims=True)
    if head is None:
        gain_rows[1:2, :] = gain2_ref[...]
    mean = mean * (1.0 / D)

    r_kv = own_rows // A
    rows_kv = r_kv + 16
    for fi in range(F):
        for i in range(A):
            at = fi * own_rows + i * r_kv
            part = tn(n1_ref[:, at : at + r_kv], d_kv_low).astype(BF)
            gkv_ref[0, fi, i, :r_kv, :] = part[:, :HS]
            gkv_ref[1, fi, i, :r_kv, :] = part[:, HS:]
            for ci in range(2):
                rows = [gain_rows[ci : ci + 1, fi * own_rows + k * 128 : fi * own_rows + (k + 1) * 128] for k in range(own_rows // 128)]
                block = jnp.concatenate(rows + [jnp.zeros((16 - len(rows), 128), F32)], axis=0)
                gkv_ref[ci, fi, i, r_kv:, :] = block.astype(BF)
    kv_c_copy = start(gkv_ref.at[1 - c], kv_c, slots(), device("c", 1))

    square_q.over_a()
    for i in range(D // n_cols):
        cols = slice(i * n_cols, (i + 1) * n_cols)
        grad_tokens[:, cols] = dres_ref[:, cols] + inv_ref[...] * (
            dn1[:, cols] * gain_ref[:, cols] - tok_ref[:, cols].astype(F32) * inv_ref[...] * mean
        )
    if head is not None:
        send_tokens()
    kv_c_copy.wait()
    kv_c[...] = (kv_c[...].astype(F32) + gkv_ref[c].astype(F32)).astype(BF)
    kv_f = [start(kv_c.at[lax.rem(f + kf + 1, F)], kv_y.at[kf], slots(), device("f", kf + 1)) for kf in range(F - 1)]
    square_o.finish()
    gather_up.from_a((0,))
    total = kv_c[f].astype(F32)
    for kf in range(F - 1):
        kv_f[kf].wait()
        total = total + kv_y[kf].astype(F32)
    kv_y[F - 1] = total.astype(BF)
    kv_b = [start(kv_y.at[F - 1], kv_x.at[kb], slots(), device("b", kb + 1)) for kb in range(B - 1)]
    square_q.finish()
    for i in range(1, len(bits)):
        gather_up.from_a((i,))
    total = kv_y[F - 1].astype(F32)
    for kb in range(B - 1):
        kv_b[kb].wait()
        total = total + kv_x[kb].astype(F32)
    kv_x[B - 1] = total.astype(BF)
    kv_a = [start(kv_x.at[B - 1, lax.rem(a + ka + 1, A)], kv_z.at[ka], slots(), device("a", ka + 1)) for ka in range(A - 1)]
    gather_o.from_a()
    gather_q.from_a((0,))
    total = kv_x[B - 1, a].astype(F32)
    for ka in range(A - 1):
        kv_a[ka].wait()
        total = total + kv_z[ka].astype(F32)
    kv_s[...] = total.astype(BF)
    gather_kv.begin()
    for i in range(1, len(bits)):
        gather_q.from_a((i,))
    gather_down.from_b()
    gather_up.from_b()
    gather_kv.from_a()
    gather_o.from_b()
    gather_q.from_b()
    for gather in gathers:
        gather.end()
    if head is not None:
        finish_head()


def tail_shapes(dims, tok, D, shard, window, extra):
    A, B, F = dims
    own_rows = D // F
    half, r_d, r_u, w_u = D // 2, shard // (A * B), own_rows // B, shard // A
    w_o, r_kv = half // A, own_rows // A + 16

    def low(*shape):
        return pltpu.VMEM(shape, BF)

    square = [low(F, own_rows, half), low(F, own_rows, half), low(B, r_u, half), low(A - 1, r_u, w_o), low(r_u, w_o)]
    n_sems = extra + 2 * (A * (B - 1) + A - 1) + 4 * (A + (B - 1) * A + B * A) + 2 * A
    n_sems += 2 * (F + B + A) + 2 * F + (B - 1) * A + A + F + B + A + 8
    outs = (
        jax.ShapeDtypeStruct((2 * shard, D), BF),
        jax.ShapeDtypeStruct((F, own_rows, 2 * shard), BF),
        jax.ShapeDtypeStruct((own_rows, D), BF),
        jax.ShapeDtypeStruct((own_rows, D), BF),
        jax.ShapeDtypeStruct((2, A, r_kv, HS), BF),
        jax.ShapeDtypeStruct((tok, D), F32),
    )
    scratch = [
        pltpu.VMEM((2 * HS, H // 2 * tok), F32),
        pltpu.VMEM((H, tok), F32),
        low(tok, D),
        low(A * B, 2, tok, 2 * HS),
        low(A * B, tok, 2 * HS),
        low(max(1, B - 1), A, tok, 2 * HS),
        low(max(1, A - 1), tok, 2 * HS),
        pltpu.VMEM((tok, 2 * HS), F32),
        pltpu.VMEM((tok, D), F32),
        low(F, own_rows, D),
        low(2, F, A, r_kv, HS),
        low(B - 1, A, r_d, D),
        low(B - 1, A, F, r_u, w_u),
        low(A - 1, r_d, D),
        low(A - 1, F, r_u, w_u),
        low(A - 1, r_d, D),
        low(A - 1, F, r_u, w_u),
        low(r_d, D),
        low(F, r_u, w_u),
        low(F, r_u, w_u),
        *square,
        *square,
        low(F, A, r_kv, HS),
        low(F, A, r_kv, HS),
        low(B, A, r_kv, HS),
        low(A - 1, r_kv, HS),
        low(r_kv, HS),
        pltpu.VMEM((8, D), F32),
        pltpu.SemaphoreType.DMA((n_sems,)),
        pltpu.SemaphoreType.DMA((n_sems,)),
        pltpu.SemaphoreType.DMA((5,)),
    ]
    return outs, scratch


def tail(dims, ends, queries, window_kv, d_attended, attended, lse, grad_down, grad_up, grad_out, n1, wq, wkv, tokens, inv, gain, dres, gain2):
    A, B, F = dims
    tok, D = n1.shape
    window = window_kv.shape[0]
    outs, scratch = tail_shapes(dims, tok, D, grad_down.shape[0], window, 0)
    hbm = pl.BlockSpec(memory_space=pltpu.HBM)
    return pl.pallas_call(
        functools.partial(tail_kernel, dims, None, TAIL_IN + TAIL_OUT + TAIL_SCRATCH),
        out_shape=outs,
        in_specs=[SMEM] + [VMEM] * 16,
        out_specs=(hbm,) * 5 + (VMEM,),
        scratch_shapes=scratch,
        compiler_params=pltpu.CompilerParams(vmem_limit_bytes=56 * 2**20, collective_id=1, has_side_effects=True),
        cost_estimate=pl.CostEstimate(flops=20 * tok * window * D, bytes_accessed=2**25, transcendentals=tok * window * H),
        name="tail",
    )(ends, queries, window_kv, d_attended, attended, lse, grad_down, grad_up, grad_out, n1, wq, wkv, tokens, inv, gain, dres, gain2)


HEAD_IN = (
    "lengths",
    "groups",
    "tokens",
    "gain_a_in",
    "gain_f_in",
    "wk_in",
    "wv_in",
    "cot_in",
    "wq_in",
    "wo_in",
    "up_in",
    "down_in",
)
HEAD_SCRATCH = (
    "q_ref",
    "kv_ref",
    "d_ref",
    "att_ref",
    "lse_ref",
    "gd_ref",
    "gu_ref",
    "n1_ref",
    "wq_ref",
    "wkv_ref",
    "inv_ref",
    "gain_ref",
    "dres_ref",
    "gain2_ref",
    "wo_ref",
    "up_ref",
    "down_ref",
    "gains_all",
    "cot_all",
    "n2_all",
    "hid_all",
    "dp_all",
    "res_ref",
    "inv2_ref",
    "dbr_ref",
    "back_s",
    "back_c",
    "back_y",
    "back_r",
    "out_s",
    "out_c",
    "out_y",
    "out_r",
    "loc_sem",
    "ends",
)


def head(r, x):
    A, B, F, a, b, c, f, s = x.A, x.B, x.F, x.a, x.b, x.c, x.f, x.s
    slots, remote, device, lower = x.slots, x.remote, x.device, x.lower
    tok, D = r.tokens.shape
    own_rows = D // F
    shard = r.down_ref.shape[0]
    half = own_rows // 2
    sent = []

    def start(src, dst, to, slot=None):
        copy = remote(src, dst, slots() if slot is None else slot, to)
        copy.start()
        sent.append(copy)
        return copy

    def done(copies):
        for copy in copies:
            copy.wait_send()
            sent[:] = [other for other in sent if other is not copy]

    def span(at, n):
        return pl.ds(pl.multiple_of(at, n), n)

    sibling = device("c", 1)
    mine, mine_half = span(f * own_rows, own_rows), span(c * half, half)
    full_half = span((f * 2 + c) * half, half)

    def to_f(src, dst):
        return [start(src(kf), dst(kf), device("f", kf)) for kf in range(1, F)]

    row = lax.broadcasted_iota(jnp.int32, (16, own_rows), 0)
    both = [ref[...].astype(F32).reshape(1, own_rows) for ref in (r.gain_a_in, r.gain_f_in)]
    r.gains_all[f] = jnp.where(row == 0, *both).astype(BF)
    gains_f = to_f(lambda kf: r.gains_all.at[f], lambda kf: r.gains_all.at[f])
    wk_f = to_f(lambda kf: r.wk_in.at[mine_half, :], lambda kf: r.wkv_ref.at[full_half, :HS])
    wv_f = to_f(lambda kf: r.wv_in.at[mine_half, :], lambda kf: r.wkv_ref.at[full_half, HS:])
    part, up_part = half // B, own_rows // B

    def wo_rows(f_, c_, b_):
        return span(((f_ * 2 + c_) * B + b_) * part, part)

    def up_rows(f_, b_):
        return span((f_ * B + b_) * up_part, up_part)

    wq_f = to_f(lambda kf: r.wq_in.at[span((c * B + b) * part, part), :], lambda kf: r.wq_ref.at[wo_rows(f, c, b), :])
    wo_f = to_f(lambda kf: r.wo_in.at[span((c * B + b) * part, part), :], lambda kf: r.wo_ref.at[wo_rows(f, c, b), :])
    up_f = to_f(
        lambda kf: r.up_in.at[span(b * up_part, up_part), span((lax.rem(f + kf, F) * 2 + c) * shard, shard)],
        lambda kf: r.up_ref.at[up_rows(f, b), :],
    )
    cot_f = to_f(lambda kf: r.cot_in, lambda kf: r.cot_all.at[kf, :tok])
    cot_c = [start(r.cot_in, r.cot_all.at[0, tok:], sibling)]

    local = [
        pltpu.make_async_copy(src, dst, r.loc_sem.at[i])
        for i, (src, dst) in enumerate(
            (
                (r.wq_in, r.wq_ref.at[mine, :]),
                (r.wo_in, r.wo_ref.at[mine, :]),
                (r.up_in.at[:, span((f * 2 + c) * shard, shard)], r.up_ref.at[mine, :]),
                (r.cot_in, r.cot_all.at[0, :tok]),
                (r.down_in.at[span(c * shard, shard), :], r.down_ref),
            )
        )
    ]
    for copy in local:
        copy.start()

    def weight_halves(copies, ref, cols):
        passed = []
        for kf in range(1, F):
            copies[kf - 1].wait_recv()
            rows = span((lower("f", kf) * 2 + c) * half, half)
            passed.append(start(ref.at[rows, cols], ref.at[rows, cols], sibling))
        return passed

    def along_b(copies, ref, rows):
        passed = []
        for kf in range(1, F):
            copies[kf - 1].wait_recv()
            here = ref.at[rows(lower("f", kf)), :]
            passed += [start(here, here, device("b", kb)) for kb in range(1, B)]
        return passed

    group = r.groups[f]
    end = jnp.int32(0)
    for i in range(r.ends.shape[0]):
        end = end + r.lengths[group, i]
        r.ends[i] = end
    n_rows = 64

    def unit_rows(i, carry):
        rows = span(i * n_rows, n_rows)
        stream = r.tokens[rows, :].astype(F32)
        inverse = lax.rsqrt(jnp.mean(stream * stream, axis=1, keepdims=True) + EPS)
        r.inv_ref[rows, :] = inverse
        return carry

    lax.fori_loop(0, tok // n_rows, unit_rows, 0)
    r.wkv_ref[mine, :HS] = r.wk_in[...]
    r.wkv_ref[mine, HS:] = r.wv_in[...]
    for copy in gains_f:
        copy.wait_recv()
    for i in range(F):
        both = r.gains_all[i].astype(F32)
        cols = slice(i * own_rows, (i + 1) * own_rows)
        r.gain_ref[0:1, cols] = both[0:1, :]
        r.gain2_ref[0:1, cols] = both[1:2, :]

    def normed_rows(i, carry):
        rows = span(i * n_rows, n_rows)
        r.n1_ref[rows, :] = (r.tokens[rows, :].astype(F32) * r.inv_ref[rows, :] * r.gain_ref[...]).astype(BF)
        return carry

    lax.fori_loop(0, tok // n_rows, normed_rows, 0)

    wkv_c = weight_halves(wk_f, r.wkv_ref, slice(0, HS)) + weight_halves(wv_f, r.wkv_ref, slice(HS, 2 * HS))
    for copy in wkv_c:
        copy.wait_recv()
    kv = r.kv_ref

    def block(a_, b_, c_):
        return kv.at[span(((a_ * B + b_) * 2 + c_) * tok, tok), :]

    kv[span(s * tok, tok), :] = nn(r.n1_ref[...], r.wkv_ref[...]).astype(BF)
    kv_z, kv_x, kv_c = slots(A - 1), slots((B - 1) * A), slots(B * A)
    own = block(a, b, c)
    z_copies = [remote(own, own, kv_z + k - 1, device("a", k)) for k in range(1, A)]

    def guarded(k, ok, act):
        if k == 0:
            act()
        else:
            pl.when(ok)(act)

    for k in range(1, A):
        guarded(k, a + k < A, z_copies[k - 1].start)

    def x_copy(kb, k):
        here = block(jnp.maximum(a - k, 0), b, c)
        return remote(here, here, kv_x + (kb - 1) * A + k, device("b", kb))

    def c_copy(kb, k):
        here = block(jnp.maximum(a - k, 0), lower("b", kb) if kb else b, c)
        return remote(here, here, kv_c + kb * A + k, sibling)

    def pass_on(k):
        for kb in range(1, B):
            x_copy(kb, k).start()
        c_copy(0, k).start()

    pass_on(0)

    def from_a(k):
        z_copies[k - 1].wait_recv()
        pass_on(k)

    wq_b = along_b(wq_f, r.wq_ref, lambda f_: wo_rows(f_, c, b))
    if A > 2:
        guarded(1, a >= 1, functools.partial(from_a, 1))

    local[0].wait()
    for copy in wq_b:
        copy.wait_recv()
    wq_c = []
    for kf in range(1, F):
        here = r.wq_ref.at[span((lower("f", kf) * 2 + c) * half, half), :]
        wq_c.append(start(here, here, sibling))
    for copy in wq_c:
        copy.wait_recv()
    n_cols = 256

    def columns(n, act):
        def body(i, carry):
            act(span(i * n_cols, n_cols))
            return carry

        lax.fori_loop(0, n // n_cols, body, 0)

    def query_cols(cols):
        r.q_ref[:, cols] = nn(r.n1_ref[...], r.wq_ref[:, cols]).astype(BF)

    columns(D, query_cols)

    for k in range(2 if A > 2 else 1, A):
        guarded(k, a - k >= 0, functools.partial(from_a, k))
    wo_b = along_b(wo_f, r.wo_ref, lambda f_: wo_rows(f_, c, b))

    factor = math.log2(math.e) / math.sqrt(HS)
    top, mixed, total = r.dres_ref, r.res_ref, r.acc
    top[...] = jnp.full(top.shape, -3e38, F32)
    mixed[...] = jnp.zeros(mixed.shape, F32)
    total[...] = jnp.zeros(total.shape, F32)
    pos = s * tok + lax.broadcasted_iota(jnp.int32, (tok, 1), 0)
    begin = jnp.zeros((tok, 1), jnp.int32)
    for i in range(r.ends.shape[0]):
        begin = jnp.maximum(begin, jnp.where(r.ends[i] <= pos, r.ends[i], 0))

    def step(j, masked):
        rows = span(j * CHUNK, CHUNK)
        keys = kv[rows, :HS]
        values = jnp.concatenate([kv[rows, HS:], jnp.ones((CHUNK, HS), BF)], axis=1)
        if masked:
            at = j * CHUNK + lax.broadcasted_iota(jnp.int32, (tok, CHUNK), 1)
            mask = jnp.logical_and(at >= begin, at <= pos)
        else:
            seen = begin <= j * CHUNK
        for h in range(H):
            cols = slice(h * HS, (h + 1) * HS)
            scores = nt(r.q_ref[:, cols], keys)
            if masked:
                scores = jnp.where(mask, scores, NEG)
            old = top[:, cols]
            new = jnp.maximum(old, jnp.max(scores, axis=1, keepdims=True) * factor)
            if not masked:
                new = jnp.where(seen, new, old)
            shrink = jnp.exp2(old - new)
            probs = jnp.exp2(scores * factor - jnp.concatenate([new] * (CHUNK // HS), axis=1))
            both = nn(probs.astype(BF), values)
            if not masked:
                both = jnp.where(seen, both, 0.0)
            mixed[:, cols] = mixed[:, cols] * shrink + both[:, :HS]
            total[:, cols] = total[:, cols] * shrink + both[:, HS:]
            top[:, cols] = new

    last = s // 2
    c_copy(0, 0).wait_recv()
    step(last, True)

    def from_b(k):
        for kb in range(1, B):
            x_copy(kb, k).wait_recv()
            c_copy(kb, k).start()

    def from_c(k):
        for kb in range(B):
            if kb or k:
                c_copy(kb, k).wait_recv()

    wo_c, up_b = [], []
    for kf in range(1, F):
        here = r.wo_ref.at[span((lower("f", kf) * 2 + c) * half, half), :]
        wo_c.append(remote(here, here, slots(), sibling))
        here = r.up_ref.at[up_rows(lower("f", kf), b), :]
        up_b += [remote(here, here, slots(), device("b", kb)) for kb in range(1, B)]
    sent.extend(wo_c + up_b)

    def pass_weights():
        for copy in wo_b:
            copy.wait_recv()
        for copy in wo_c:
            copy.start()
        for copy in up_f:
            copy.wait_recv()
        for copy in up_b:
            copy.start()

    from_b(0)
    guarded(1, a >= 1, functools.partial(from_b, 1))
    from_c(0)

    def begin_group(k):
        if k + 1 < A:
            guarded(k + 1, a - (k + 1) >= 0, functools.partial(from_b, k + 1))
        from_c(k)
        if k == A - 1:
            pass_weights()

    def attention_chunk(j, carry):
        @pl.when(j > 0)
        def _():
            step(j, False)

        @pl.when(j == 0)
        def _():
            step(j, True)

        return carry

    def attention_part(i, carry):
        j = last - 1 - i
        for k in range(1, A):
            pl.when(j == (a - k) * B + B - 1)(functools.partial(begin_group, k))
        return attention_chunk(j, carry)

    lax.fori_loop(0, last, attention_part, 0)
    guarded(1, a < A - 1, pass_weights)
    for h in range(H):
        cols = slice(h * HS, (h + 1) * HS)
        r.att_ref[:, cols] = (mixed[:, cols] * (1.0 / total[:, cols])).astype(BF)
        r.lse_ref[h : h + 1, :] = (top[:, cols] + jnp.log2(total[:, cols])).T[0:1, :]

    local[1].wait()
    for copy in wo_c:
        copy.wait_recv()
    squares = jnp.zeros((tok, 1), F32)
    for i in range(D // n_cols):
        cols = slice(i * n_cols, (i + 1) * n_cols)
        part = r.tokens[:, cols].astype(F32) + nn(r.att_ref[...], r.wo_ref[:, cols])
        r.res_ref[:, cols] = part
        squares = squares + jnp.sum(part * part, axis=1, keepdims=True)
    r.inv2_ref[...] = lax.rsqrt(squares * (1.0 / D) + EPS)

    def second_norm(i, carry):
        rows = span(i * n_rows, n_rows)
        r.n2_all[0, rows, :] = (r.res_ref[rows, :] * r.inv2_ref[rows, :] * r.gain2_ref[...]).astype(BF)
        return carry

    lax.fori_loop(0, tok // n_rows, second_norm, 0)

    n2_f = to_f(lambda kf: r.n2_all.at[0, :tok], lambda kf: r.n2_all.at[kf, :tok])
    n2_c = [start(r.n2_all.at[0, :tok], r.n2_all.at[0, tok:], sibling)]
    local[2].wait()
    local[3].wait()
    local[4].wait()
    for copy in up_b:
        copy.wait_recv()
    for kf in range(1, F):
        cot_f[kf - 1].wait_recv()
        cot_c.append(start(r.cot_all.at[kf, :tok], r.cot_all.at[kf, tok:], sibling))

    def feed_forward(kf):
        def hidden_cols(cols):
            before = nn(r.n2_all[kf], r.up_ref[:, cols])
            d_hidden = nt(r.cot_all[kf], r.down_ref[cols, :])
            sig = 1.0 / (1.0 + jnp.exp(-before))
            r.hid_all[kf, :, cols] = (before * sig).astype(BF)
            r.dp_all[kf, :, cols] = (d_hidden * sig * (1.0 + before * (1.0 - sig))).astype(BF)

        columns(shard, hidden_cols)

    def back_part(kf):
        def back_cols(cols):
            r.back_s[kf, :, cols] = nt(r.dp_all[kf], r.up_ref[cols, :]).astype(BF)

        columns(D, back_cols)
        return start(r.back_s.at[kf, tok:], r.back_c.at[kf], sibling)

    def out_part(kf):
        def out_cols(cols):
            r.out_s[kf, :, cols] = nn(r.hid_all[kf], r.down_ref[:, cols]).astype(BF)

        columns(D, out_cols)
        return start(r.out_s.at[kf, tok:], r.out_c.at[kf], sibling)

    def chip_sum(kf, part, other, ref):
        def rows_sum(i, carry):
            rows = span(i * n_rows, n_rows)
            ref[kf - 1, rows, :] = (part[kf, rows, :].astype(F32) + other[kf, rows, :].astype(F32)).astype(BF)
            return carry

        lax.fori_loop(0, tok // n_rows, rows_sum, 0)

    n_out = 128

    r_d = shard // (A * B)

    def down_rows(kfs, place):
        cols = span(place * r_d, r_d)
        grad = sum(tn(r.hid_all[kf, :, cols], r.cot_all[kf]) for kf in kfs)
        if 0 not in kfs:
            grad = grad + r.gd_ref[cols, :].astype(F32)
        r.gd_ref[cols, :] = grad.astype(BF)

    def down_grad(kf):
        for i in range(A):
            for kb in range(1, B):
                down_rows((kf,), lax.rem(b + kb, B) * A + x.offset(x.order[i]))
            if kf == F - 1:
                x.send_down(i, i + 1)

    def down_grad_own():
        def rows_of(i, carry):
            down_rows(range(F), b * A + i)
            return carry

        lax.fori_loop(0, A, rows_of, 0)

    def up_grad():
        def rows_of(i, carry):
            cols = span(i * n_out, n_out)
            rows = span(lax.rem(i, own_rows // n_out) * n_out, n_out)
            grad = sum(tn(r.n2_all[kf, :, cols], r.dp_all[kf]) for kf in range(F))
            r.gu_ref[i // (own_rows // n_out), rows, :] = grad.astype(BF)
            return carry

        lax.fori_loop(0, D // n_out, rows_of, 0)

    back_copies, out_copies, back_back, out_back = [None] * F, [None] * F, [], []
    n2_c[0].wait_recv()
    cot_c[0].wait_recv()
    feed_forward(0)
    down_grad(0)
    back_copies[0] = back_part(0)
    for kf in range(1, F):
        n2_f[kf - 1].wait_recv()
        n2_c.append(start(r.n2_all.at[kf, :tok], r.n2_all.at[kf, tok:], sibling))
    for kf in range(1, F):
        n2_c[kf].wait_recv()
        cot_c[kf].wait_recv()
        feed_forward(kf)
        down_grad(kf)
        back_copies[kf] = back_part(kf)
        if kf == F - 1:
            down_grad_own()
        back_copies[kf].wait_recv()
        chip_sum(kf, r.back_s, r.back_c, r.back_y)
        back_back.append(start(r.back_y.at[kf - 1], r.back_r.at[kf - 1], device("f", F - kf)))
        if kf == F - 1:
            up_grad()
            x.send_up(0, A)
            x.down_step(0)
        out_copies[kf] = out_part(kf)
    for kf in range(1, F):
        out_copies[kf].wait_recv()
        chip_sum(kf, r.out_s, r.out_c, r.out_y)
        out_back.append(start(r.out_y.at[kf - 1], r.out_r.at[kf - 1], device("f", F - kf)))
    if A > 2:
        x.down_step(1)
    out_copies[0] = out_part(0)
    if A > 2:
        x.down_step(2)

    back_copies[0].wait_recv()
    for copy in back_back:
        copy.wait_recv()

    def norm_back(i, gain_grad):
        rows = span(i * n_rows, n_rows)
        d_normed = r.back_s[0, rows, :].astype(F32) + r.back_c[0, rows, :].astype(F32)
        for kf in range(1, F):
            d_normed = d_normed + r.back_r[kf - 1, rows, :].astype(F32)
        inverse = r.inv2_ref[rows, :]
        unit = r.res_ref[rows, :] * inverse
        weighted = d_normed * unit
        scaled = d_normed * r.gain2_ref[...]
        mean = jnp.mean(scaled * unit, axis=1, keepdims=True)
        d_residual = r.cot_all[0, rows, :].astype(F32) + inverse * (scaled - unit * mean)
        r.dres_ref[rows, :] = d_residual
        r.dbr_ref[rows, :] = d_residual.astype(BF)
        return gain_grad + jnp.sum(weighted, axis=0, keepdims=True)

    r.gain_rows[1:2, :] = lax.fori_loop(0, tok // n_rows, norm_back, jnp.zeros((1, D), F32))

    def attended_cols(cols):
        r.d_ref[:, cols] = nt(r.dbr_ref[...], r.wo_ref[cols, :]).astype(BF)

    columns(D, attended_cols)

    done(n2_f + n2_c)

    def out_grad(i, carry):
        cols = span(i * n_out, n_out)
        rows = span(lax.rem(i, own_rows // n_out) * n_out, n_out)
        r.go_ref[i // (own_rows // n_out), rows, :] = tn(r.att_ref[:, cols], r.dbr_ref[...]).astype(BF)
        return carry

    lax.fori_loop(0, D // n_out, out_grad, 0)

    def finish_output():
        out_copies[0].wait_recv()
        for copy in out_back:
            copy.wait_recv()

        def output_rows(i, carry):
            rows = span(i * n_rows, n_rows)
            value = r.res_ref[rows, :] + r.out_s[0, rows, :].astype(F32) + r.out_c[0, rows, :].astype(F32)
            for kf in range(1, F):
                value = value + r.out_r[kf - 1, rows, :].astype(F32)
            r.out_ref[rows, :] = value.astype(BF)
            return carry

        lax.fori_loop(0, tok // n_rows, output_rows, 0)
        done(out_copies)
        results[0].start()

    results = [
        pltpu.make_async_copy(src, dst, r.loc_sem.at[5 + i])
        for i, (src, dst) in enumerate(((r.out_ref, r.out_hbm), (r.grad_tokens, r.grad_hbm)))
    ]

    def finish():
        for copy in results:
            copy.wait()
        for copy in sent:
            copy.wait_send()
        for k in range(1, A):
            guarded(k, a + k < A, z_copies[k - 1].wait_send)
        for k in range(A):
            for kb in range(B):
                if kb:
                    guarded(k, a - k >= 0, x_copy(kb, k).wait_send)
                guarded(k, a - k >= 0, c_copy(kb, k).wait_send)

    return finish_output, results[1].start, finish


AGAIN = {
    "go_ref": "n2_all",
    "gq_ref": "out_s",
    "dn1": "res_ref",
    "grad_tokens": "res_ref",
    "dq": "d_ref",
    "out_ref": "dbr_ref",
    "tok_ref": "tokens",
}


def layer_shapes(dims, tok, D, shard, window, sequences):
    A, B, F = dims
    own_rows = D // F
    outs, scratch = tail_shapes(dims, tok, D, shard, window, 16 * F + A - 1 + (B - 1) * A + B * A)

    def low(*shape):
        return pltpu.VMEM(shape, BF)

    def wide(*shape):
        return pltpu.VMEM(shape, F32)

    pair = [low(F, 2 * tok, D), low(F, tok, D), low(F - 1, tok, D), low(F - 1, tok, D)]
    first = [
        low(tok, D),
        low(window, 2 * HS),
        low(tok, D),
        low(tok, D),
        wide(H, tok),
        low(shard, D),
        low(F, own_rows, shard),
        low(tok, D),
        low(D, D),
        low(D, 2 * HS),
        wide(tok, 1),
        wide(1, D),
        wide(tok, D),
        wide(1, D),
        low(D, D),
        low(D, shard),
        low(shard, D),
        low(F, 16, own_rows),
        low(F, 2 * tok, D),
        low(F, 2 * tok, D),
        low(F, 2 * tok, shard),
        low(F, 2 * tok, shard),
        wide(tok, D),
        wide(tok, 1),
        low(tok, D),
        *pair,
        *pair,
        pltpu.SemaphoreType.DMA((7,)),
        pltpu.SMEM((sequences,), jnp.int32),
    ]
    sizes = dict(zip(HEAD_SCRATCH + TAIL_SCRATCH, first + scratch))
    fits = all(sizes[k].shape == sizes[AGAIN[k]].shape for k in ("gq_ref", "dn1", "dq")) and tok == 2 * HS and own_rows == 2 * tok
    scratch = [ref for name, ref in zip(TAIL_SCRATCH, scratch) if name not in AGAIN]
    fits = fits and vmem_bytes(first + scratch) + 4 * 2**20 < LIMIT
    return outs + (jax.ShapeDtypeStruct((tok, D), BF),), first + scratch, fits


def vmem_bytes(scratch):
    total = 0
    for ref in scratch:
        shape = getattr(ref, "shape", ())
        if len(shape) >= 2:
            lanes = -(-shape[-1] // 128) * 128
            rows = -(-shape[-2] // 8) * 8
            total += math.prod(shape[:-2]) * rows * lanes * jnp.dtype(ref.dtype).itemsize
    return total


def layer(dims, lengths, groups, tokens, gain_a, gain_f, w_key, w_value, cotangent, w_query, w_out, w_up, w_down, outs, scratch):
    tok, D = tokens.shape
    hbm = pl.BlockSpec(memory_space=pltpu.HBM)
    names = HEAD_IN + TAIL_OUT[:5] + ("grad_hbm", "out_hbm") + HEAD_SCRATCH + tuple(n for n in TAIL_SCRATCH if n not in AGAIN)
    return pl.pallas_call(
        functools.partial(tail_kernel, dims, head, names),
        out_shape=outs,
        in_specs=[SMEM] * 2 + [VMEM] * 5 + [hbm] * 5,
        out_specs=(hbm,) * 7,
        scratch_shapes=scratch,
        compiler_params=pltpu.CompilerParams(vmem_limit_bytes=LIMIT, collective_id=2, has_side_effects=True),
        cost_estimate=pl.CostEstimate(flops=2**35, bytes_accessed=2**25, transcendentals=2**24),
        name="layer",
    )(lengths, groups, tokens, gain_a, gain_f, w_key, w_value, cotangent, w_query, w_out, w_up, w_down)


def after(value, *others):
    return lax.optimization_barrier((value, *others))[0]


class Grid:
    def __init__(self):
        seq = lax.axis_size("seq")
        self.F = lax.axis_size("fsdp")
        self.C = 2
        chips = seq // 2
        self.B = 2 if chips == 8 else chips // 2
        self.A = chips // self.B
        self.s = lax.axis_index("seq")
        self.f = lax.axis_index("fsdp")
        self.c = self.s % 2
        self.b = self.s // 2 % self.B
        self.a = self.s // (2 * self.B)

    def size(self, axis):
        return {"a": self.A, "b": self.B, "c": self.C, "f": self.F}[axis]

    def place(self, axis):
        return {"a": self.a, "b": self.b, "c": self.c, "f": self.f}[axis]

    def send(self, value, axis, step, upward=False):
        pairs = []
        for a in range(self.A):
            for b in range(self.B):
                for c in range(2):
                    for f in range(self.F):
                        at = {"a": a, "b": b, "c": c, "f": f}
                        to = dict(at)
                        to[axis] += step
                        if upward and not 0 <= to[axis] < self.size(axis):
                            continue
                        to[axis] %= self.size(axis)
                        line = [((d["a"] * self.B + d["b"]) * 2 + d["c"]) * self.F + d["f"] for d in (at, to)]
                        pairs.append(tuple(line))
        return lax.ppermute(value, ("seq", "fsdp"), pairs)

    def stack(self, parts, axis):
        n, me = len(parts), self.place(axis)
        if n == 2:
            low = me == 0
            return jnp.stack([jnp.where(low, parts[0], parts[1]), jnp.where(low, parts[1], parts[0])])
        twice = jnp.stack(parts + parts)
        return lax.dynamic_slice_in_dim(twice, (n - me) % n, n, 0)

    def gather(self, value, axis):
        n = self.size(axis)
        return self.stack([value] + [self.send(value, axis, -k) for k in range(1, n)], axis)

    def scatter(self, parts, axis):
        n, me = self.size(axis), self.place(axis)

        def pick(k):
            return lax.dynamic_index_in_dim(parts, (me + k) % n, 0, keepdims=False)

        got = [self.send(pick(k).astype(BF), axis, k) for k in range(1, n)]
        total = pick(0).astype(F32)
        for piece in got:
            total = total + piece.astype(F32)
        return total

    def plane_sum(self, parts):
        half = self.scatter(parts, "b").astype(BF)
        return self.scatter(half, "a")

    def plane_gather(self, share):
        rows = self.gather(share.astype(BF), "a")
        return self.gather(rows, "b")


def local(
    tokens,
    cotangent,
    seq_lengths,
    group_of_shard,
    gain_attn,
    w_query,
    w_key,
    w_value,
    w_out,
    gain_ffn,
    w_up,
    w_down,
):
    g = Grid()
    A, B, C, F = g.A, g.B, g.C, g.F
    tok, D = tokens.shape[1:]
    FF = w_up.shape[1]
    own_rows = D // F
    seq_parts = A * B * C
    shard = FF // (2 * F)

    outs, scratch, fits = layer_shapes((A, B, F), tok, D, shard, seq_parts * tok, seq_lengths.shape[1])
    if fits:
        *grads, grad_tokens, output = layer(
            (A, B, F),
            seq_lengths,
            group_of_shard,
            tokens[0],
            gain_attn,
            gain_ffn,
            w_key,
            w_value,
            cotangent[0],
            w_query,
            w_out,
            w_up,
            w_down,
            outs,
            scratch,
        )
        return results(output, grad_tokens, *grads)

    group = lax.dynamic_index_in_dim(group_of_shard, g.f, 0, keepdims=False)
    lengths = lax.dynamic_index_in_dim(seq_lengths, group, 0, keepdims=False)
    running, ends = jnp.int32(0), []
    for i in range(seq_lengths.shape[1]):
        running = running + lengths[i]
        ends.append(running)
    scal = jnp.stack([g.s.astype(jnp.int32), *ends])

    gains = jnp.stack([gain_attn, gain_ffn])
    full_gains = g.gather(gains, "f").transpose(1, 0, 2).reshape(2, D).astype(F32)
    gain_first, gain_second = full_gains[0], full_gains[1]
    own_kv = jnp.concatenate([w_key, w_value], axis=1)
    full_kv = g.gather(own_kv, "f").reshape(D, 2 * HS)

    def gather_weight(weight, *late):
        half = own_rows // 2
        mine = lax.dynamic_slice_in_dim(weight, g.c * half, half, 0)
        if late:
            mine = after(mine, *late)
        pieces = [g.gather(g.send(mine, "f", -k), "c").reshape(weight.shape) for k in range(1, F)]
        return g.stack([weight] + pieces, "f").reshape(F * own_rows, -1)

    full_query = gather_weight(w_query)

    stream = tokens[0].astype(F32)
    inverse_first = lax.rsqrt(jnp.mean(stream * stream, axis=1, keepdims=True) + EPS)
    unit_first = stream * inverse_first
    normed_first = (unit_first * gain_first).astype(BF)
    key_value = nn(normed_first, full_kv).astype(BF)
    queries = nn(normed_first, full_query).astype(BF)

    column = [key_value] + [g.send(key_value, "a", k, upward=True) for k in range(1, A)]
    twice = jnp.stack(column[::-1] + column[::-1])
    column = lax.dynamic_slice_in_dim(twice, A - 1 - g.a, A, 0)
    plane = g.gather(column, "b")
    whole = g.gather(plane, "c")
    window_kv = whole.transpose(2, 1, 0, 3, 4).reshape(seq_parts * tok, 2 * HS)

    full_out = gather_weight(w_out, full_query)
    upstream = cotangent[0]
    cot = []
    for k in range(F):
        mine = upstream if k == 0 else g.send(after(upstream, full_query), "f", k)
        cot.append(jnp.concatenate([mine, g.send(mine, "c", 1)], axis=0))
    ups = w_up.reshape(own_rows, F, 2, shard)
    up_parts = []
    for k in range(F):
        block = lax.dynamic_slice(ups, (0, (g.f + k) % F, g.c, 0), (own_rows, 1, 1, shard)).reshape(own_rows, shard)
        up_parts.append(block if k == 0 else g.send(after(block, full_out), "f", k))
    up_parts = [up_parts[0]] + up_parts[1:][::-1]
    up = g.stack(up_parts, "f").reshape(D, shard)
    down = lax.dynamic_slice_in_dim(w_down, g.c * shard, shard, 0)

    attended, lse = attend(scal, queries, window_kv)

    residual = stream + nn(attended, full_out)
    inverse_second = lax.rsqrt(jnp.mean(residual * residual, axis=1, keepdims=True) + EPS)
    unit_second = residual * inverse_second
    normed_second = (unit_second * gain_second).astype(BF)

    out_sum, back_sum = residual, jnp.zeros((tok, D), F32)
    hiddens, d_pres, norms = [], [], []
    backs, outs = [], []
    for k in range(F):
        mine = normed_second if k == 0 else g.send(normed_second, "f", k)
        norm = jnp.concatenate([mine, g.send(mine, "c", 1)], axis=0)
        before = nn(norm, up)
        d_hidden = nt(cot[k], down)
        sig = jax.nn.sigmoid(before)
        hidden = (before * sig).astype(BF)
        d_pre = (d_hidden * sig * (1.0 + before * (1.0 - sig))).astype(BF)
        back = nt(d_pre, up)
        out = nn(hidden, down)
        hiddens.append(hidden)
        d_pres.append(d_pre)
        norms.append(norm)
        backs.append(back)
        outs.append(out)

    def give_back(parts):
        total = 0.0
        for k, part in enumerate(parts):
            other = g.send(part[tok:].astype(BF), "c", 1)
            chip = part[:tok] + other.astype(F32)
            if k:
                chip = g.send(chip.astype(BF), "f", -k).astype(F32)
            total = total + chip
        return total

    d_normed_second = give_back(backs)
    output = (residual + give_back(outs)).astype(BF)

    grad_down = sum(tn(h, c) for h, c in zip(hiddens, cot)).astype(BF)
    grad_up = sum(tn(n, d) for n, d in zip(norms, d_pres)).astype(BF)

    def norm_back(gradient, unit_rows, inverse, gain_vec):
        scaled = gradient * gain_vec
        gain_grad = jnp.sum(gradient * unit_rows, axis=0)
        return gain_grad, inverse * (scaled - unit_rows * jnp.mean(scaled * unit_rows, axis=1, keepdims=True))

    gain_second_grad, d_from_norm = norm_back(d_normed_second, unit_second, inverse_second, gain_second)
    d_residual = upstream.astype(F32) + d_from_norm
    d_branch = d_residual.astype(BF)
    d_attended = nt(d_branch, full_out).astype(BF)
    grad_out = tn(attended, d_branch).astype(BF)

    down_all, up_all, out_all, query_all, kv_all, grad_tokens = tail(
        (A, B, F),
        scal[1:],
        queries,
        window_kv,
        d_attended,
        attended,
        lse,
        grad_down,
        grad_up.reshape(F, own_rows, shard),
        grad_out.reshape(F, own_rows, D),
        normed_first,
        full_query,
        full_kv,
        tokens[0],
        inverse_first,
        gain_first[None],
        d_residual,
        gain_second_grad[None],
    )
    return results(output, grad_tokens, down_all, up_all, out_all, query_all, kv_all)


def widen_kernel(
    low_ref, grad_ref, down_ref, up_ref, o_ref, q_ref, kv_ref, output, grad_tokens, grad_down, grad_up, grad_o, grad_q, grad_k, grad_v, gain_a, gain_f
):
    output[0] = low_ref[...]
    grad_tokens[0] = grad_ref[...]
    grad_down[...] = down_ref[...].astype(F32)
    width = up_ref.shape[2]
    for i in range(up_ref.shape[0]):
        grad_up[:, i * width : (i + 1) * width] = up_ref[i].astype(F32)
    grad_o[...] = o_ref[...].astype(F32)
    grad_q[...] = q_ref[...].astype(F32)

    @pl.when(pl.program_id(0) == 0)
    def _():
        rows = kv_ref.shape[2] - 16
        for i in range(kv_ref.shape[1]):
            grad_k[i * rows : (i + 1) * rows, :] = kv_ref[0, i, :rows, :].astype(F32)
            grad_v[i * rows : (i + 1) * rows, :] = kv_ref[1, i, :rows, :].astype(F32)
        for i, gain in enumerate((gain_a, gain_f)):
            block = kv_ref[i, 0, rows:, :].astype(F32)
            for k in range(gain.shape[0] // HS):
                gain[k * HS : (k + 1) * HS] = block[k]


def results(output, grad_tokens, down_all, up_all, out_all, query_all, kv_all):
    tok, D = output.shape
    F, own_rows, width = up_all.shape
    steps = max(1, own_rows // 256)

    def rows(n, cols):
        return pl.BlockSpec((n // steps, cols), lambda i: (i, 0))

    def whole(*shape):
        return pl.BlockSpec(shape, lambda i: (0,) * len(shape))

    def first(n, cols):
        return pl.BlockSpec((1, n // steps, cols), lambda i: (0, i, 0))

    down_rows = down_all.shape[0]
    shapes = [(down_rows, D), (own_rows, F * width), (own_rows, D), (own_rows, D), (own_rows, HS), (own_rows, HS), (own_rows,), (own_rows,)]
    out, grad_tokens, down, up, o, q, k, v, gain_a, gain_f = pl.pallas_call(
        widen_kernel,
        grid=(steps,),
        out_shape=[jax.ShapeDtypeStruct((1, tok, D), BF), jax.ShapeDtypeStruct((1, tok, D), F32)]
        + [jax.ShapeDtypeStruct(shape, F32) for shape in shapes],
        in_specs=[
            rows(tok, D),
            rows(tok, D),
            rows(down_rows, D),
            pl.BlockSpec((F, own_rows // steps, width), lambda i: (0, i, 0)),
            rows(own_rows, D),
            rows(own_rows, D),
            whole(*kv_all.shape),
        ],
        out_specs=[
            first(tok, D),
            first(tok, D),
            rows(down_rows, D),
            rows(own_rows, F * width),
            rows(own_rows, D),
            rows(own_rows, D),
            whole(own_rows, HS),
            whole(own_rows, HS),
            whole(own_rows),
            whole(own_rows),
        ],
        compiler_params=pltpu.CompilerParams(vmem_limit_bytes=LIMIT),
        name="widen",
    )(output, grad_tokens, down_all, up_all, out_all, query_all, kv_all)
    return out, grad_tokens, gain_a, q, k, v, o, gain_f, up, down


def solution(mesh):
    placed = (
        P("fsdp", "seq", None),
        P("fsdp", "seq", None),
        P(),
        P(),
        P("fsdp"),
        P("fsdp", None),
        P("fsdp", None),
        P("fsdp", None),
        P("fsdp", None),
        P("fsdp"),
        P("fsdp", None),
        P("fsdp", None),
    )
    return jax.shard_map(
        local,
        mesh=mesh,
        in_specs=placed,
        out_specs=(
            P("fsdp", "seq", None),
            P("fsdp", "seq", None),
            P("fsdp"),
            P("fsdp", None),
            P("fsdp", None),
            P("fsdp", None),
            P("fsdp", None),
            P("fsdp"),
            P("fsdp", None),
            P("fsdp", None),
        ),
        check_vma=False,
    )
```
